32 devices in a mesh: seq: 16 (over z, x, core), head: 2 (over y).
Axes of the slice: x: 2, y: 2, z: 4, core: 2. Of those that a mesh axis runs over, the one named last changes fastest.
Arguments:
- queries: bfloat16 [1024, 16384], P('seq', 'head'), may hold values from -12 to 12
- keys: bfloat16 [1024, 1024], P('seq', 'head'), may hold values from -12 to 12
- values: bfloat16 [1024, 1024], P('seq', 'head'), may hold values from -6 to 6
- q_feature: bfloat16 [128, 128, 64], P('head'), may hold values from -1.1953125 to 1.1953125
- k_feature: bfloat16 [128, 128, 64], P('head'), may hold values from -1.1953125 to 1.1953125
- window_factor: float32 [128], P('head'), may hold values from 0.3 to 0.9
Outputs:
- mixed: bfloat16 [1024, 16384], P(('seq', 'head'))
The draws below stay inside these ranges and needn't reach their ends.
All inputs are finite; a program needn't handle non-finite values.
Results may differ from the reference program's by a relative error of at most 0.005.
Values may be sent and summed in bfloat16 or wider, within the bound.
No kernel may reach another device: no remote copies, remote signals or barrier semaphores. Data moves between devices by JAX's collectives and lax.ppermute only.
A program may use at most 192 MiB of HBM per device.

```python
import math
import jax
import jax.numpy as jnp
from jax import lax

HEADS = 128
KV_HEADS = 8
DH = 128
FEAT = 64
WINDOW = 64
TOK_DEV = 64
TOKENS = 1024


def shared_keys(key):
    base = jax.random.normal(jax.random.fold_in(key, 7), (TOKENS, KV_HEADS * DH), jnp.float32)
    return jnp.clip(base, -12.0, 12.0)


def draw_keys(key, part):
    keys_drawn = shared_keys(key)
    return keys_drawn.astype(jnp.bfloat16)


def draw_queries(key, part):
    drawn = jax.random.normal(jax.random.fold_in(key, 13), (TOKENS, HEADS * DH), jnp.float32)
    return jnp.clip(drawn, -12.0, 12.0).astype(jnp.bfloat16)


def shard_levels(stream_key, shape, shards, least, high):
    def one(axis_at, shards_of):
        steps = jax.random.uniform(jax.random.fold_in(jax.random.fold_in(stream_key, 6), axis_at), (shards_of,), jnp.float32, least / len(shards), high / len(shards))
        return jnp.repeat(jnp.exp(steps), shape[axis_at] // shards_of).reshape((-1,) + (1,) * (len(shape) - axis_at - 1))

    loudness = one(*shards[0])
    for cut in shards[1:]:
        loudness = loudness * one(*cut)
    return loudness


def gaussian(key, extent, scale, reach, shards=(), held_as=jnp.bfloat16):
    array = scale * jax.random.normal(key, extent, jnp.float32)
    if shards:
        array = array * shard_levels(key, extent, shards, -0.22, 0.18)
    return jnp.clip(array, -reach, reach).astype(held_as)


def setup_inputs(seed: int = 0) -> dict:
    arg_keys = jax.random.split(jax.random.key(seed), 7)
    return {
        "queries": draw_queries(jax.random.fold_in(arg_keys[6], 71), 0),
        "keys": draw_keys(jax.random.fold_in(arg_keys[6], 71), 0),
        "values": gaussian(arg_keys[2], (TOKENS, KV_HEADS * DH), 1.0, 6.0, ((0, 16), (1, 2))),
        "q_feature": gaussian(arg_keys[3], (HEADS, DH, FEAT), 0.2, 1.1953125, ((0, 2),)),
        "k_feature": gaussian(arg_keys[4], (HEADS, DH, FEAT), 0.2, 1.1953125, ((0, 2),)),
        "window_factor": jnp.clip(0.3 + 0.59999996 * jax.random.uniform(arg_keys[5], (HEADS,), jnp.float32) ** shard_levels(arg_keys[5], (HEADS,), ((0, 2),), -0.2, 0.2), 0.3, 0.9),
    }


def features(rows, weight):
    logits = jnp.dot(rows, weight, preferred_element_type=jnp.float32)
    return jnp.concatenate([jax.nn.softmax(logits, axis=-1), jax.nn.softmax(-logits, axis=-1)], axis=-1)

def mix_block(query, fq, keys_ext, values_ext, fk_ext, valid, state, total, factor):
    size = query.shape[0]
    width = keys_ext.shape[0] - size
    scores = jnp.dot(query, keys_ext.T, preferred_element_type=jnp.float32) / math.sqrt(query.shape[1])
    row = lax.broadcasted_iota(jnp.int32, (size, size + width), 0)
    col = lax.broadcasted_iota(jnp.int32, (size, size + width), 1)
    inside = (col > row) & (col <= row + width) & valid[None, :]
    masked = jnp.where(inside, scores, -jnp.inf)
    top = lax.optimization_barrier(jnp.max(masked, axis=1, keepdims=True))
    soft = jnp.exp(masked - top)
    causal = row[:, :size] >= col[:, :size]
    linear = jnp.where(causal, jnp.einsum('if,jf->ij', fq, fk_ext[:size], precision=lax.Precision.HIGHEST), 0.0)
    values_wide = values_ext.astype(jnp.float32)
    numer = factor * jnp.dot(soft, values_wide, precision=lax.Precision.HIGHEST) + (1.0 - factor) * (jnp.dot(linear, values_wide[:size], precision=lax.Precision.HIGHEST) + jnp.dot(fq, state, precision=lax.Precision.HIGHEST))
    denom = factor * lax.optimization_barrier(jnp.sum(soft, axis=1, keepdims=True)) + (1.0 - factor) * (lax.optimization_barrier(jnp.sum(linear, axis=1, keepdims=True)) + lax.optimization_barrier(jnp.sum(fq * total[None, :], axis=1, keepdims=True)))
    return numer / denom

def reference(queries, keys, values, q_feature, k_feature, window_factor):
    tokens = queries.shape[0]
    blocks = tokens // TOK_DEV
    group = HEADS // KV_HEADS
    padding = jnp.zeros((WINDOW, DH), jnp.bfloat16)
    valid_all = jnp.concatenate([jnp.zeros((WINDOW,), bool), jnp.ones((tokens,), bool)])

    def one_head(head):
        kv_head = head // group
        q_rows = lax.dynamic_slice_in_dim(queries, (head * DH).astype(jnp.int32), DH, 1)
        k_rows = jnp.concatenate([padding, lax.dynamic_slice_in_dim(keys, (kv_head * DH).astype(jnp.int32), DH, 1)])
        v_rows = jnp.concatenate([padding, lax.dynamic_slice_in_dim(values, (kv_head * DH).astype(jnp.int32), DH, 1)])
        fq_all = features(q_rows, q_feature[head])
        fk_all = features(k_rows, k_feature[head]) * valid_all[:, None].astype(jnp.float32)
        factor = window_factor[head]

        def step(carry, index):
            state, total = carry
            start = (index * TOK_DEV).astype(jnp.int32)
            query = lax.dynamic_slice_in_dim(q_rows, start, TOK_DEV, 0)
            fq = lax.dynamic_slice_in_dim(fq_all, start, TOK_DEV, 0)
            keys_ext = lax.dynamic_slice_in_dim(k_rows, start, TOK_DEV + WINDOW, 0)
            values_ext = lax.dynamic_slice_in_dim(v_rows, start, TOK_DEV + WINDOW, 0)
            fk_ext = lax.dynamic_slice_in_dim(fk_all, start, TOK_DEV + WINDOW, 0)
            valid = lax.dynamic_slice_in_dim(valid_all, start, TOK_DEV + WINDOW, 0)
            result = mix_block(query, fq, keys_ext, values_ext, fk_ext, valid, state, total, factor)
            shifted = fk_ext[:TOK_DEV]
            state = state + jnp.dot(shifted.T, values_ext[:TOK_DEV].astype(jnp.float32), precision=lax.Precision.HIGHEST)
            total = total + lax.optimization_barrier(jnp.sum(shifted, axis=0))
            return ((state, total), result)
        init = (jnp.zeros((2 * FEAT, DH), jnp.float32), jnp.zeros((2 * FEAT,), jnp.float32))
        carry, outs = lax.scan(step, init, jnp.arange(blocks, dtype=jnp.int32))
        return outs.reshape(tokens, DH)
    result = lax.map(one_head, jnp.arange(HEADS, dtype=jnp.int32))
    return result.transpose(1, 0, 2).reshape(tokens, HEADS * DH).astype(jnp.bfloat16)
```

```python
import math

import jax
import jax.numpy as jnp
from jax import lax
from jax.experimental import pallas as pl
from jax.experimental.pallas import tpu as pltpu
from jax.sharding import PartitionSpec as P

DH = 128
WINDOW = 64
F32 = jnp.float32
BF16 = jnp.bfloat16


def dot_t(a, b):
    return lax.dot_general(a, b, (((1,), (1,)), ((), ())), preferred_element_type=F32)


def features_t(logits):
    top = jnp.max(logits, axis=0, keepdims=True)
    low = jnp.min(logits, axis=0, keepdims=True)
    up = jnp.exp(logits - top)
    down = jnp.exp(low - logits)
    up = up * (1.0 / jnp.sum(up, axis=0, keepdims=True))
    down = down * (1.0 / jnp.sum(down, axis=0, keepdims=True))
    return jnp.concatenate([up.astype(BF16), down.astype(BF16)], axis=0)


def mix_kernel(
    place_ref, q_ref, k_ref, v_ref, wq_ref, wk_ref, ratio_ref, out_ref, fk_scr, state_scr
):
    tok = q_ref.shape[0]
    heads, feat, dh = wq_ref.shape
    seen = fk_scr.shape[1]
    place = place_ref[0]
    first_head = pl.program_id(0) * heads

    weights = wk_ref[...].reshape(heads * feat, dh)
    for start in range(0, seen, 256):
        size = min(256, seen - start)
        logits = dot_t(weights, k_ref[start : start + size, :])
        for h in range(heads):
            fk_scr[h * 2 * feat : (h + 1) * 2 * feat, start : start + size] = features_t(
                logits[h * feat : (h + 1) * feat]
            )
    row = lax.broadcasted_iota(jnp.int32, (seen, dh), 0)
    kept = row < (place - 1) * tok
    v_seen = jnp.where(kept, v_ref[:seen, :].astype(F32), 0.0).astype(BF16)
    ones_seen = jnp.where(kept, 1.0, 0.0).astype(BF16)
    v_seen = jnp.concatenate([v_seen, ones_seen], axis=1)
    state_scr[...] = jnp.dot(fk_scr[...], v_seen, preferred_element_type=F32).astype(BF16)

    before = pl.multiple_of(jnp.maximum(place - 1, 0) * tok, tok)
    own = pl.multiple_of(place * tok, tok)
    k_ext = jnp.concatenate([k_ref[pl.ds(before, tok), :], k_ref[pl.ds(own, tok), :]], axis=0)
    v_ext = jnp.concatenate([v_ref[pl.ds(before, tok), :], v_ref[pl.ds(own, tok), :]], axis=0)
    v_ext = jnp.concatenate([v_ext, jnp.ones_like(v_ext)], axis=1)
    row = lax.broadcasted_iota(jnp.int32, (tok, 2 * tok), 0)
    col = lax.broadcasted_iota(jnp.int32, (tok, 2 * tok), 1)
    valid = (col >= tok) | (place > 0)
    inside = (col > row) & (col <= row + WINDOW) & valid
    causal = (col <= row) & valid
    lane = lax.broadcasted_iota(jnp.int32, (tok, 2 * feat), 1)
    left = lane < feat
    side_r = lax.broadcasted_iota(jnp.int32, (2 * feat, 2 * feat), 0) < feat
    side_c = lax.broadcasted_iota(jnp.int32, (2 * feat, 2 * feat), 1) < feat
    halves = jnp.where(side_r == side_c, 1.0, 0.0).astype(BF16)

    for h in range(heads):
        q = q_ref[:, h * dh : (h + 1) * dh]
        wq = wq_ref[h]
        logits = dot_t(q, jnp.concatenate([wq, -wq], axis=0))
        top_l = jnp.max(jnp.where(left, logits, -jnp.inf), axis=1, keepdims=True)
        top_r = jnp.max(jnp.where(left, -jnp.inf, logits), axis=1, keepdims=True)
        expd = jnp.exp(logits - jnp.where(left, top_l, top_r)).astype(BF16)
        total = jnp.dot(expd, halves, preferred_element_type=F32)
        fq = (expd.astype(F32) / total).astype(BF16)
        fk = features_t(dot_t(wk_ref[h], k_ext))
        linear = jnp.dot(fq, fk, preferred_element_type=F32)
        scores = dot_t(q, k_ext) * (1.0 / math.sqrt(dh))
        masked = jnp.where(inside, scores, -jnp.inf)
        top = jnp.max(masked, axis=1, keepdims=True)
        soft = jnp.exp(masked - top) * ratio_ref[first_head + h]
        weight = jnp.where(causal, linear, soft).astype(BF16)
        both = jnp.dot(weight, v_ext, preferred_element_type=F32) + jnp.dot(
            fq, state_scr[h * 2 * feat : (h + 1) * 2 * feat, :], preferred_element_type=F32
        )
        out_ref[:, h * dh : (h + 1) * dh] = (both[:, :dh] / both[:, dh:]).astype(BF16)


def mix(place, queries, kv, wq, wk, ratio, group):
    tok = queries.shape[0]
    local_heads, feat, dh = wq.shape
    groups = local_heads // group
    tokens = kv.shape[0]
    seen = tokens - 2 * tok
    return pl.pallas_call(
        mix_kernel,
        grid_spec=pltpu.PrefetchScalarGridSpec(
            num_scalar_prefetch=1,
            grid=(groups,),
            in_specs=[
                pl.BlockSpec((tok, group * dh), lambda g, p: (0, g)),
                pl.BlockSpec((tokens, dh), lambda g, p: (0, g)),
                pl.BlockSpec((tokens, dh), lambda g, p: (0, groups + g)),
                pl.BlockSpec((group, feat, dh), lambda g, p: (g, 0, 0)),
                pl.BlockSpec((group, feat, dh), lambda g, p: (g, 0, 0)),
                pl.BlockSpec(memory_space=pltpu.SMEM),
            ],
            out_specs=pl.BlockSpec((tok, group * dh), lambda g, p: (0, g)),
            scratch_shapes=[
                pltpu.VMEM((group * 2 * feat, seen), BF16),
                pltpu.VMEM((group * 2 * feat, 2 * dh), BF16),
            ],
        ),
        out_shape=jax.ShapeDtypeStruct(queries.shape, BF16),
        compiler_params=pltpu.CompilerParams(vmem_limit_bytes=48 * 2**20),
        cost_estimate=pl.CostEstimate(
            flops=2 * local_heads * tokens * 3 * feat * 2 * dh,
            bytes_accessed=8 * 2**20,
            transcendentals=local_heads * tokens * 2 * feat,
        ),
    )(place, queries, kv, kv, wq, wk, ratio)


def local(queries, keys, values, q_feature, k_feature, window_factor):
    tok = queries.shape[0]
    local_heads = q_feature.shape[0]
    group = local_heads // (keys.shape[1] // DH)
    place = lax.axis_index("seq").astype(jnp.int32).reshape(1)
    kv = lax.all_gather(jnp.concatenate([keys, values], axis=1), "seq", tiled=True)
    out = mix(
        place,
        queries,
        kv,
        jnp.swapaxes(q_feature, 1, 2),
        jnp.swapaxes(k_feature, 1, 2),
        window_factor / (1.0 - window_factor),
        group,
    )
    return lax.all_to_all(out, "head", split_axis=0, concat_axis=1, tiled=True)


def solution(mesh):
    return jax.shard_map(
        local,
        mesh=mesh,
        in_specs=(
            P("seq", "head"),
            P("seq", "head"),
            P("seq", "head"),
            P("head", None, None),
            P("head", None, None),
            P("head"),
        ),
        out_specs=P(("seq", "head"), None),
        check_vma=False,
    )
```

```python
import math

import jax
import jax.numpy as jnp
from jax import lax
from jax.experimental import pallas as pl
from jax.experimental.pallas import tpu as pltpu
from jax.sharding import PartitionSpec as P

DH = 128
WINDOW = 64
F32 = jnp.float32
BF16 = jnp.bfloat16


def dot_t(a, b):
    return lax.dot_general(a, b, (((1,), (1,)), ((), ())), preferred_element_type=F32)


def features_t(logits):
    top = jnp.max(logits, axis=0, keepdims=True)
    low = jnp.min(logits, axis=0, keepdims=True)
    up = jnp.exp(logits - top)
    down = jnp.exp(low - logits)
    up = up * (1.0 / jnp.sum(up, axis=0, keepdims=True))
    down = down * (1.0 / jnp.sum(down, axis=0, keepdims=True))
    return jnp.concatenate([up.astype(BF16), down.astype(BF16)], axis=0)


def mix_kernel(
    place_ref, q_ref, k_ref, v_ref, wq_ref, wk_ref, ratio_ref, out_ref, fk_scr, state_scr
):
    tok = q_ref.shape[0]
    heads, feat, dh = wq_ref.shape
    seen = fk_scr.shape[1]
    place = place_ref[0]
    first_head = pl.program_id(0) * heads

    weights = wk_ref[...].reshape(heads * feat, dh)
    for start in range(0, seen, 256):
        size = min(256, seen - start)
        logits = dot_t(weights, k_ref[start : start + size, :])
        for h in range(heads):
            fk_scr[h * 2 * feat : (h + 1) * 2 * feat, start : start + size] = features_t(
                logits[h * feat : (h + 1) * feat]
            )
    row = lax.broadcasted_iota(jnp.int32, (seen, dh), 0)
    kept = row < (place - 1) * tok
    v_seen = jnp.where(kept, v_ref[:seen, :].astype(F32), 0.0).astype(BF16)
    ones_seen = jnp.where(kept, 1.0, 0.0).astype(BF16)
    v_seen = jnp.concatenate([v_seen, ones_seen], axis=1)
    state_scr[...] = jnp.dot(fk_scr[...], v_seen, preferred_element_type=F32).astype(BF16)

    before = pl.multiple_of(jnp.maximum(place - 1, 0) * tok, tok)
    own = pl.multiple_of(place * tok, tok)
    k_ext = jnp.concatenate([k_ref[pl.ds(before, tok), :], k_ref[pl.ds(own, tok), :]], axis=0)
    v_ext = jnp.concatenate([v_ref[pl.ds(before, tok), :], v_ref[pl.ds(own, tok), :]], axis=0)
    v_ext = jnp.concatenate([v_ext, jnp.ones_like(v_ext)], axis=1)
    row = lax.broadcasted_iota(jnp.int32, (tok, 2 * tok), 0)
    col = lax.broadcasted_iota(jnp.int32, (tok, 2 * tok), 1)
    valid = (col >= tok) | (place > 0)
    inside = (col > row) & (col <= row + WINDOW) & valid
    causal = (col <= row) & valid
    lane = lax.broadcasted_iota(jnp.int32, (tok, 2 * feat), 1)
    left = lane < feat
    side_r = lax.broadcasted_iota(jnp.int32, (2 * feat, 2 * feat), 0) < feat
    side_c = lax.broadcasted_iota(jnp.int32, (2 * feat, 2 * feat), 1) < feat
    halves = jnp.where(side_r == side_c, 1.0, 0.0).astype(BF16)

    for h in range(heads):
        q = q_ref[:, h * dh : (h + 1) * dh]
        wq = wq_ref[h]
        logits = dot_t(q, jnp.concatenate([wq, -wq], axis=0))
        top_l = jnp.max(jnp.where(left, logits, -jnp.inf), axis=1, keepdims=True)
        top_r = jnp.max(jnp.where(left, -jnp.inf, logits), axis=1, keepdims=True)
        expd = jnp.exp(logits - jnp.where(left, top_l, top_r)).astype(BF16)
        total = jnp.dot(expd, halves, preferred_element_type=F32)
        fq = (expd.astype(F32) / total).astype(BF16)
        fk = features_t(dot_t(wk_ref[h], k_ext))
        linear = jnp.dot(fq, fk, preferred_element_type=F32)
        scores = dot_t(q, k_ext) * (1.0 / math.sqrt(dh))
        masked = jnp.where(inside, scores, -jnp.inf)
        top = jnp.max(masked, axis=1, keepdims=True)
        soft = jnp.exp(masked - top) * ratio_ref[first_head + h]
        weight = jnp.where(causal, linear, soft).astype(BF16)
        both = jnp.dot(weight, v_ext, preferred_element_type=F32) + jnp.dot(
            fq, state_scr[h * 2 * feat : (h + 1) * 2 * feat, :], preferred_element_type=F32
        )
        out_ref[:, h * dh : (h + 1) * dh] = (both[:, :dh] / both[:, dh:]).astype(BF16)


def mix(place, queries, kv, wq, wk, ratio, group):
    tok = queries.shape[0]
    local_heads, feat, dh = wq.shape
    groups = local_heads // group
    tokens = kv.shape[0]
    seen = tokens - 2 * tok
    return pl.pallas_call(
        mix_kernel,
        grid_spec=pltpu.PrefetchScalarGridSpec(
            num_scalar_prefetch=1,
            grid=(groups,),
            in_specs=[
                pl.BlockSpec((tok, group * dh), lambda g, p: (0, g)),
                pl.BlockSpec((tokens, dh), lambda g, p: (0, g)),
                pl.BlockSpec((tokens, dh), lambda g, p: (0, groups + g)),
                pl.BlockSpec((group, feat, dh), lambda g, p: (g, 0, 0)),
                pl.BlockSpec((group, feat, dh), lambda g, p: (g, 0, 0)),
                pl.BlockSpec(memory_space=pltpu.SMEM),
            ],
            out_specs=pl.BlockSpec((tok, group * dh), lambda g, p: (0, g)),
            scratch_shapes=[
                pltpu.VMEM((group * 2 * feat, seen), BF16),
                pltpu.VMEM((group * 2 * feat, 2 * dh), BF16),
            ],
        ),
        out_shape=jax.ShapeDtypeStruct(queries.shape, BF16),
        compiler_params=pltpu.CompilerParams(vmem_limit_bytes=48 * 2**20),
        cost_estimate=pl.CostEstimate(
            flops=2 * local_heads * tokens * 3 * feat * 2 * dh,
            bytes_accessed=8 * 2**20,
            transcendentals=local_heads * tokens * 2 * feat,
        ),
    )(place, queries, kv, kv, wq, wk, ratio)


def pack_kv_kernel(k_ref, v_ref, kv_ref):
    for g in range(k_ref.shape[1] // DH):
        kv_ref[:, 2 * g * DH : (2 * g + 1) * DH] = k_ref[:, g * DH : (g + 1) * DH]
        kv_ref[:, (2 * g + 1) * DH : (2 * g + 2) * DH] = v_ref[:, g * DH : (g + 1) * DH]


def pack_q_kernel(place_ref, q_ref, *out_refs):
    width = out_refs[0].shape[1]
    for d, ref in enumerate(out_refs):
        at = pl.multiple_of((place_ref[0] ^ d) * width, width)
        ref[...] = q_ref[:, pl.ds(at, width)]


def pick_kernel(levels, place_ref, *refs):
    for d, ref in enumerate(refs[levels:]):
        at = pl.multiple_of((place_ref[0] ^ d) * 2 * DH, 2 * DH)
        for s in range(levels):
            ref[:, s * 2 * DH : (s + 1) * 2 * DH] = refs[s][:, pl.ds(at, 2 * DH)]


def join_kernel(ways, sides, place_ref, *refs):
    width = refs[0].shape[1]
    for n, ref in enumerate(refs[:-1]):
        dr, dy = divmod(n, sides)
        block = (place_ref[2] ^ dy) * ways + (place_ref[0] ^ dr)
        refs[-1][:, pl.ds(pl.multiple_of(block * width, width), width)] = ref[...]


def level_kernel(levels, ways, sides, place_ref, ratio_ref, wq_ref, wk_ref, *refs):
    q_refs, kv_refs = refs[:ways], refs[ways : 2 * ways]
    out_refs = refs[2 * ways : 2 * ways + ways * sides]
    q_scr, k_scr, v_scr, fk_scr, state_scr, out_scr = refs[2 * ways + ways * sides :]
    tok = q_refs[0].shape[0]
    heads, feat, dh = wq_ref.shape
    size = ways * tok
    half = size // 2
    past = (levels - 1) * size
    place, level, side = place_ref[0], place_ref[1], place_ref[2]
    first_head = place * heads

    for d in range(ways):
        at = pl.multiple_of((place ^ d) * tok, tok)
        q_scr[pl.ds(at, tok), :] = q_refs[d][...]
        for s in range(levels):
            row = (levels - 1 - s) * size + at
            k_scr[pl.ds(row, tok), :] = kv_refs[d][:, s * 2 * dh : s * 2 * dh + dh]
            v_scr[pl.ds(row, tok), :dh] = kv_refs[d][:, s * 2 * dh + dh : (s + 1) * 2 * dh]
    for s in range(levels):
        here = jnp.where(level >= s, 1.0, 0.0).astype(BF16)
        v_scr[(levels - 1 - s) * size : (levels - s) * size, dh:] = jnp.full((size, dh), here)

    weights = wk_ref[...].reshape(heads * feat, dh)
    for start in range(0, past + size, 256):
        logits = dot_t(weights, k_scr[start : start + 256, :])
        for h in range(heads):
            fk_scr[h * 2 * feat : (h + 1) * 2 * feat, start : start + 256] = features_t(
                logits[h * feat : (h + 1) * feat]
            )
    state = jnp.dot(
        fk_scr[:, : past - half], v_scr[: past - half, :], preferred_element_type=F32
    )
    state_scr[0] = state.astype(BF16)
    state_scr[1] = (
        state
        + jnp.dot(
            fk_scr[:, past - half : past],
            v_scr[past - half : past, :],
            preferred_element_type=F32,
        )
    ).astype(BF16)

    row = lax.broadcasted_iota(jnp.int32, (half, 2 * half), 0)
    col = lax.broadcasted_iota(jnp.int32, (half, 2 * half), 1)
    lane = lax.broadcasted_iota(jnp.int32, (half, 2 * feat), 1)
    left = lane < feat
    side_r = lax.broadcasted_iota(jnp.int32, (2 * feat, 2 * feat), 0) < feat
    side_c = lax.broadcasted_iota(jnp.int32, (2 * feat, 2 * feat), 1) < feat
    halves = jnp.where(side_r == side_c, 1.0, 0.0).astype(BF16)
    for u in range(2):
        valid = (col >= half) | (level > 0) | (u > 0)
        split = row + (half - WINDOW)
        inside = (col > split) & (col <= row + half) & valid
        causal = (col <= split) & valid
        keys = pl.ds(past - half + u * half, 2 * half)
        k_ext, v_ext = k_scr[keys, :], v_scr[keys, :]
        for h in range(heads):
            q = q_scr[u * half : (u + 1) * half, h * dh : (h + 1) * dh]
            wq = wq_ref[h]
            logits = dot_t(q, jnp.concatenate([wq, -wq], axis=0))
            top_l = jnp.max(jnp.where(left, logits, -jnp.inf), axis=1, keepdims=True)
            top_r = jnp.max(jnp.where(left, -jnp.inf, logits), axis=1, keepdims=True)
            expd = jnp.exp(logits - jnp.where(left, top_l, top_r)).astype(BF16)
            total = jnp.dot(expd, halves, preferred_element_type=F32)
            fq = (expd.astype(F32) / total).astype(BF16)
            feats = slice(h * 2 * feat, (h + 1) * 2 * feat)
            linear = jnp.dot(fq, fk_scr[feats, keys], preferred_element_type=F32)
            scores = dot_t(q, k_ext) * (1.0 / math.sqrt(dh))
            masked = jnp.where(inside, scores, -jnp.inf)
            top = jnp.max(masked, axis=1, keepdims=True)
            soft = jnp.exp(masked - top) * ratio_ref[first_head + h]
            weight = jnp.where(causal, linear, soft).astype(BF16)
            both = jnp.dot(weight, v_ext, preferred_element_type=F32) + jnp.dot(
                fq, state_scr[u, feats, :], preferred_element_type=F32
            )
            out_scr[u * half : (u + 1) * half, h * dh : (h + 1) * dh] = (
                both[:, :dh] / both[:, dh:]
            ).astype(BF16)

    part = tok // sides
    for n, ref in enumerate(out_refs):
        dr, dy = divmod(n, sides)
        at = pl.multiple_of((place ^ dr) * tok + (side ^ dy) * part, part)
        ref[...] = out_scr[pl.ds(at, part), :]


def whole_spec():
    return pl.BlockSpec(memory_space=pltpu.VMEM)


def call(kernel, place, ins, outs, name):
    return pl.pallas_call(
        kernel,
        in_specs=[pl.BlockSpec(memory_space=pltpu.SMEM)] + [whole_spec() for _ in ins],
        out_specs=[whole_spec() for _ in outs],
        out_shape=[jax.ShapeDtypeStruct(s, BF16) for s in outs],
        compiler_params=pltpu.CompilerParams(vmem_limit_bytes=16 * 2**20),
        name=name,
    )(place, *ins)


def by_levels(queries, keys, values, wq, wk, ratio):
    tok, width = queries.shape
    local_heads, feat, dh = wq.shape
    ways = keys.shape[1] // dh
    heads = local_heads // ways
    seq, sides = lax.axis_size("seq"), lax.axis_size("head")
    levels = seq // ways
    at = lax.axis_index("seq").astype(jnp.int32)
    side = lax.axis_index("head").astype(jnp.int32)
    place = jnp.stack([at % ways, at // ways, side])

    def partner(x, d):
        return lax.ppermute(x, "seq", [(i, i // ways * ways + (i % ways ^ d)) for i in range(seq)])

    def partner_of_both(x, dr, dy):
        pairs = [
            (i * sides + j, (i // ways * ways + (i % ways ^ dr)) * sides + (j ^ dy))
            for i in range(seq)
            for j in range(sides)
        ]
        return lax.ppermute(x, ("seq", "head"), pairs)

    (kv,) = pl.pallas_call(
        pack_kv_kernel,
        in_specs=[whole_spec(), whole_spec()],
        out_specs=[whole_spec()],
        out_shape=[jax.ShapeDtypeStruct((tok, 2 * keys.shape[1]), BF16)],
        name="pack_kv",
    )(keys, values)
    raw = [kv] + [
        lax.ppermute(kv, "seq", [(i, i + s * ways) for i in range(seq - s * ways)])
        for s in range(1, levels)
    ]
    q_parts = call(
        pack_q_kernel, place, [queries], [(tok, width // ways)] * ways, "pack_q"
    )
    q_parts = [q_parts[0]] + [partner(q_parts[d], d) for d in range(1, ways)]
    kv_parts = call(
        lambda *refs: pick_kernel(levels, *refs),
        place,
        raw,
        [(tok, levels * 2 * dh)] * ways,
        "pick_kv",
    )
    kv_parts = [kv_parts[0]] + [partner(kv_parts[d], d) for d in range(1, ways)]

    size = ways * tok
    part = (tok // sides, heads * dh)
    picked = pl.BlockSpec((heads, feat, dh), lambda i, p: (p[0], 0, 0))
    outs = pl.pallas_call(
        lambda *refs: level_kernel(levels, ways, sides, *refs),
        grid_spec=pltpu.PrefetchScalarGridSpec(
            num_scalar_prefetch=1,
            grid=(1,),
            in_specs=[pl.BlockSpec(memory_space=pltpu.SMEM), picked, picked]
            + [whole_spec() for _ in range(2 * ways)],
            out_specs=[whole_spec() for _ in range(ways * sides)],
            scratch_shapes=[
                pltpu.VMEM((size, heads * dh), BF16),
                pltpu.VMEM((levels * size, dh), BF16),
                pltpu.VMEM((levels * size, 2 * dh), BF16),
                pltpu.VMEM((heads * 2 * feat, levels * size), BF16),
                pltpu.VMEM((2, heads * 2 * feat, 2 * dh), BF16),
                pltpu.VMEM((size, heads * dh), BF16),
            ],
        ),
        out_shape=[jax.ShapeDtypeStruct(part, BF16)] * (ways * sides),
        compiler_params=pltpu.CompilerParams(vmem_limit_bytes=40 * 2**20),
        name="level_mix",
    )(place, ratio, wq, wk, *q_parts, *kv_parts)
    outs = [
        o if n == 0 else partner_of_both(o, *divmod(n, sides)) for n, o in enumerate(outs)
    ]
    (joined,) = call(
        lambda *refs: join_kernel(ways, sides, *refs),
        place,
        outs,
        [(part[0], sides * ways * part[1])],
        "join",
    )
    return joined


def by_blocks(queries, keys, values, wq, wk, ratio):
    group = wq.shape[0] // (keys.shape[1] // DH)
    place = lax.axis_index("seq").astype(jnp.int32).reshape(1)
    kv = lax.all_gather(jnp.concatenate([keys, values], axis=1), "seq", tiled=True)
    out = mix(place, queries, kv, wq, wk, ratio, group)
    return lax.all_to_all(out, "head", split_axis=0, concat_axis=1, tiled=True)


def local(queries, keys, values, q_feature, k_feature, window_factor):
    tok = queries.shape[0]
    ways = keys.shape[1] // DH
    seq, sides = lax.axis_size("seq"), lax.axis_size("head")
    wq, wk = jnp.swapaxes(q_feature, 1, 2), jnp.swapaxes(k_feature, 1, 2)
    ratio = window_factor / (1.0 - window_factor)
    levels = seq // ways
    fits = ways in (2, 4) and sides in (1, 2) and seq == levels * ways and 2 <= levels <= 4
    if fits and ways * tok == 256 and tok == WINDOW:
        return by_levels(queries, keys, values, wq, wk, ratio)
    return by_blocks(queries, keys, values, wq, wk, ratio)


def solution(mesh):
    return jax.shard_map(
        local,
        mesh=mesh,
        in_specs=(
            P("seq", "head"),
            P("seq", "head"),
            P("seq", "head"),
            P("head", None, None),
            P("head", None, None),
            P("head"),
        ),
        out_specs=P(("seq", "head"), None),
        check_vma=False,
    )
```

```python
import math

import jax
import jax.numpy as jnp
from jax import lax
from jax.experimental import pallas as pl
from jax.experimental.pallas import tpu as pltpu
from jax.sharding import PartitionSpec as P

DH = 128
WINDOW = 64
F32 = jnp.float32
BF16 = jnp.bfloat16


def dot_t(a, b):
    return lax.dot_general(a, b, (((1,), (1,)), ((), ())), preferred_element_type=F32)


def features_t(logits):
    top = jnp.max(logits, axis=0, keepdims=True)
    low = jnp.min(logits, axis=0, keepdims=True)
    up = jnp.exp(logits - top)
    down = jnp.exp(low - logits)
    up = up * (1.0 / jnp.sum(up, axis=0, keepdims=True))
    down = down * (1.0 / jnp.sum(down, axis=0, keepdims=True))
    return jnp.concatenate([up.astype(BF16), down.astype(BF16)], axis=0)


def mix_kernel(
    place_ref, q_ref, k_ref, v_ref, wq_ref, wk_ref, ratio_ref, out_ref, fk_scr, state_scr
):
    tok = q_ref.shape[0]
    heads, feat, dh = wq_ref.shape
    seen = fk_scr.shape[1]
    place = place_ref[0]
    first_head = pl.program_id(0) * heads

    weights = wk_ref[...].reshape(heads * feat, dh)
    for start in range(0, seen, 256):
        size = min(256, seen - start)
        logits = dot_t(weights, k_ref[start : start + size, :])
        for h in range(heads):
            fk_scr[h * 2 * feat : (h + 1) * 2 * feat, start : start + size] = features_t(
                logits[h * feat : (h + 1) * feat]
            )
    row = lax.broadcasted_iota(jnp.int32, (seen, dh), 0)
    kept = row < (place - 1) * tok
    v_seen = jnp.where(kept, v_ref[:seen, :].astype(F32), 0.0).astype(BF16)
    ones_seen = jnp.where(kept, 1.0, 0.0).astype(BF16)
    v_seen = jnp.concatenate([v_seen, ones_seen], axis=1)
    state_scr[...] = jnp.dot(fk_scr[...], v_seen, preferred_element_type=F32).astype(BF16)

    before = pl.multiple_of(jnp.maximum(place - 1, 0) * tok, tok)
    own = pl.multiple_of(place * tok, tok)
    k_ext = jnp.concatenate([k_ref[pl.ds(before, tok), :], k_ref[pl.ds(own, tok), :]], axis=0)
    v_ext = jnp.concatenate([v_ref[pl.ds(before, tok), :], v_ref[pl.ds(own, tok), :]], axis=0)
    v_ext = jnp.concatenate([v_ext, jnp.ones_like(v_ext)], axis=1)
    row = lax.broadcasted_iota(jnp.int32, (tok, 2 * tok), 0)
    col = lax.broadcasted_iota(jnp.int32, (tok, 2 * tok), 1)
    valid = (col >= tok) | (place > 0)
    inside = (col > row) & (col <= row + WINDOW) & valid
    causal = (col <= row) & valid
    lane = lax.broadcasted_iota(jnp.int32, (tok, 2 * feat), 1)
    left = lane < feat
    side_r = lax.broadcasted_iota(jnp.int32, (2 * feat, 2 * feat), 0) < feat
    side_c = lax.broadcasted_iota(jnp.int32, (2 * feat, 2 * feat), 1) < feat
    halves = jnp.where(side_r == side_c, 1.0, 0.0).astype(BF16)

    for h in range(heads):
        q = q_ref[:, h * dh : (h + 1) * dh]
        wq = wq_ref[h]
        logits = dot_t(q, jnp.concatenate([wq, -wq], axis=0))
        top_l = jnp.max(jnp.where(left, logits, -jnp.inf), axis=1, keepdims=True)
        top_r = jnp.max(jnp.where(left, -jnp.inf, logits), axis=1, keepdims=True)
        expd = jnp.exp(logits - jnp.where(left, top_l, top_r)).astype(BF16)
        total = jnp.dot(expd, halves, preferred_element_type=F32)
        fq = (expd.astype(F32) / total).astype(BF16)
        fk = features_t(dot_t(wk_ref[h], k_ext))
        linear = jnp.dot(fq, fk, preferred_element_type=F32)
        scores = dot_t(q, k_ext) * (1.0 / math.sqrt(dh))
        masked = jnp.where(inside, scores, -jnp.inf)
        top = jnp.max(masked, axis=1, keepdims=True)
        soft = jnp.exp(masked - top) * ratio_ref[first_head + h]
        weight = jnp.where(causal, linear, soft).astype(BF16)
        both = jnp.dot(weight, v_ext, preferred_element_type=F32) + jnp.dot(
            fq, state_scr[h * 2 * feat : (h + 1) * 2 * feat, :], preferred_element_type=F32
        )
        out_ref[:, h * dh : (h + 1) * dh] = (both[:, :dh] / both[:, dh:]).astype(BF16)


def mix(place, queries, kv, wq, wk, ratio, group):
    tok = queries.shape[0]
    local_heads, feat, dh = wq.shape
    groups = local_heads // group
    tokens = kv.shape[0]
    seen = tokens - 2 * tok
    return pl.pallas_call(
        mix_kernel,
        grid_spec=pltpu.PrefetchScalarGridSpec(
            num_scalar_prefetch=1,
            grid=(groups,),
            in_specs=[
                pl.BlockSpec((tok, group * dh), lambda g, p: (0, g)),
                pl.BlockSpec((tokens, dh), lambda g, p: (0, g)),
                pl.BlockSpec((tokens, dh), lambda g, p: (0, groups + g)),
                pl.BlockSpec((group, feat, dh), lambda g, p: (g, 0, 0)),
                pl.BlockSpec((group, feat, dh), lambda g, p: (g, 0, 0)),
                pl.BlockSpec(memory_space=pltpu.SMEM),
            ],
            out_specs=pl.BlockSpec((tok, group * dh), lambda g, p: (0, g)),
            scratch_shapes=[
                pltpu.VMEM((group * 2 * feat, seen), BF16),
                pltpu.VMEM((group * 2 * feat, 2 * dh), BF16),
            ],
        ),
        out_shape=jax.ShapeDtypeStruct(queries.shape, BF16),
        compiler_params=pltpu.CompilerParams(vmem_limit_bytes=48 * 2**20),
        cost_estimate=pl.CostEstimate(
            flops=2 * local_heads * tokens * 3 * feat * 2 * dh,
            bytes_accessed=8 * 2**20,
            transcendentals=local_heads * tokens * 2 * feat,
        ),
    )(place, queries, kv, kv, wq, wk, ratio)


def copy_all(pairs, sems):
    copies = [pltpu.make_async_copy(a, b, sems.at[n]) for n, (a, b) in enumerate(pairs)]
    for copy in copies:
        copy.start()
    for copy in copies:
        copy.wait()


def pack_kv_kernel(place_ref, k_ref, v_ref, *refs):
    pairs = []
    for d, out in enumerate(refs[:-1]):
        at = pl.ds(pl.multiple_of((place_ref[0] ^ d) * DH, DH), DH)
        pairs += [(k_ref.at[:, at], out.at[:, :DH]), (v_ref.at[:, at], out.at[:, DH:])]
    copy_all(pairs, refs[-1])


def pack_q_kernel(place_ref, q_ref, wq_ref, wk_ref, *refs):
    out_refs, own_wq, own_wk, sems = refs[:-3], *refs[-3:]
    width = out_refs[0].shape[1]
    heads = own_wq.shape[0]
    own = pl.ds(place_ref[0] * heads, heads)
    pairs = []
    for d, out in enumerate(out_refs):
        at = pl.multiple_of((place_ref[0] ^ d) * width, width)
        pairs.append((q_ref.at[:, pl.ds(at, width)], out))
    pairs += [(wk_ref.at[own], own_wk), (wq_ref.at[own], own_wq)]
    copy_all(pairs, sems)


def stack_kernel(place_ref, *refs):
    tok = refs[0].shape[0]
    for d, ref in enumerate(refs[:-1]):
        at = pl.multiple_of((place_ref[0] ^ d) * tok, tok)
        refs[-1][pl.ds(at, tok), :] = ref[...]


def join_kernel(ways, sides, place_ref, *refs):
    width = refs[0].shape[1]
    for n, ref in enumerate(refs[:-1]):
        dr, dy = divmod(n, sides)
        block = (place_ref[2] ^ dy) * ways + (place_ref[0] ^ dr)
        refs[-1][:, pl.ds(pl.multiple_of(block * width, width), width)] = ref[...]


def key_features_kernel(kv_ref, wk_ref, fk_ref):
    heads, feat, dh = wk_ref.shape
    logits = dot_t(wk_ref[...].reshape(heads * feat, dh), kv_ref[:, :dh])
    for h in range(heads):
        part = logits[h * feat : (h + 1) * feat]
        top = jnp.max(part, axis=0, keepdims=True)
        low = jnp.min(part, axis=0, keepdims=True)
        for n, shifted in enumerate((part - top, low - part)):
            row = (2 * h + n) * feat
            expd = jnp.exp(shifted.astype(BF16))
            total = expd[: feat // 4]
            for q in range(1, 4):
                total = total + expd[q * feat // 4 : (q + 1) * feat // 4]
            total = jnp.sum(total.astype(F32), axis=0, keepdims=True)
            fk_ref[row : row + feat, :] = expd * pl.reciprocal(total).astype(BF16)


def level_kernel(levels, ways, sides, place_ref, ratio_ref, wq_ref, *refs):
    q_refs, kv_refs, fk_refs = refs[:ways], refs[ways:][:levels], refs[ways + levels :][:levels]
    refs = refs[ways + 2 * levels :]
    out_refs = refs[: ways * sides]
    q_scr, v_scr, fk_scr, state_scr, out_scr = refs[ways * sides :]
    tok = q_refs[0].shape[0]
    heads, feat, dh = wq_ref.shape
    size = ways * tok
    half = size // 2
    place, level, side = place_ref[0], place_ref[1], place_ref[2]
    first_head = place * heads

    for d in range(ways):
        at = pl.multiple_of((place ^ d) * tok, tok)
        q_scr[pl.ds(at, tok), :] = q_refs[d][...]
    for s in range(levels):
        here = jnp.where(level >= s, 1.0, 0.0).astype(BF16)
        v_scr[s, :, :dh] = kv_refs[s][:, dh:]
        v_scr[s, :, dh:] = jnp.full((size, dh), here)

    state = jnp.dot(fk_refs[1][:, :half], v_scr[1, :half], preferred_element_type=F32)
    for s in range(2, levels):
        state = state + jnp.dot(fk_refs[s][...], v_scr[s], preferred_element_type=F32)
    state_scr[0] = state.astype(BF16)
    state_scr[1] = (
        state + jnp.dot(fk_refs[1][:, half:], v_scr[1, half:], preferred_element_type=F32)
    ).astype(BF16)
    fk_scr[:, :half] = fk_refs[1][:, half:]
    fk_scr[:, half:] = fk_refs[0][:, :half]

    row = lax.broadcasted_iota(jnp.int32, (half, 2 * half), 0)
    col = lax.broadcasted_iota(jnp.int32, (half, 2 * half), 1)
    lane = lax.broadcasted_iota(jnp.int32, (half, 2 * feat), 1)
    left = lane < feat
    side_r = lax.broadcasted_iota(jnp.int32, (2 * feat, 2 * feat), 0) < feat
    side_c = lax.broadcasted_iota(jnp.int32, (2 * feat, 2 * feat), 1) < feat
    halves = jnp.where(side_r == side_c, 1.0, 0.0).astype(BF16)
    for u in range(2):
        valid = (col >= half) | (level > 0) | (u > 0)
        split = row + (half - WINDOW)
        inside = (col > split) & (col <= row + half) & valid
        causal = (col <= split) & valid
        if u == 0:
            k_ext = jnp.concatenate([kv_refs[1][half:, :dh], kv_refs[0][:half, :dh]], axis=0)
            v_ext = jnp.concatenate([v_scr[1, half:], v_scr[0, :half]], axis=0)
        else:
            k_ext, v_ext = kv_refs[0][:, :dh], v_scr[0]
        for h in range(heads):
            q = q_scr[u * half : (u + 1) * half, h * dh : (h + 1) * dh]
            wq = wq_ref[h]
            logits = dot_t(q, jnp.concatenate([wq, -wq], axis=0))
            top_l = jnp.max(jnp.where(left, logits, -jnp.inf), axis=1, keepdims=True)
            top_r = jnp.max(jnp.where(left, -jnp.inf, logits), axis=1, keepdims=True)
            expd = jnp.exp((logits - jnp.where(left, top_l, top_r)).astype(BF16))
            total = jnp.dot(expd, halves, preferred_element_type=F32)
            fq = (expd.astype(F32) * pl.reciprocal(total, approx=True)).astype(BF16)
            feats = slice(h * 2 * feat, (h + 1) * 2 * feat)
            fk = fk_refs[0][feats, :] if u else fk_scr[feats, :]
            linear = jnp.dot(fq, fk, preferred_element_type=F32)
            scores = dot_t(q, k_ext) * (1.0 / math.sqrt(dh))
            masked = jnp.where(inside, scores, -jnp.inf)
            top = jnp.max(masked, axis=1, keepdims=True)
            soft = jnp.exp(masked - top) * ratio_ref[first_head + h]
            weight = jnp.where(causal, linear, soft).astype(BF16)
            both = jnp.dot(weight, v_ext, preferred_element_type=F32) + jnp.dot(
                fq, state_scr[u, feats, :], preferred_element_type=F32
            )
            out_scr[u * half : (u + 1) * half, h * dh : (h + 1) * dh] = (
                both[:, :dh] * pl.reciprocal(both[:, dh:])
            ).astype(BF16)

    part = tok // sides
    for n, ref in enumerate(out_refs):
        dr, dy = divmod(n, sides)
        at = pl.multiple_of((place ^ dr) * tok + (side ^ dy) * part, part)
        ref[...] = out_scr[pl.ds(at, part), :]


def whole_spec(space=pltpu.VMEM):
    return pl.BlockSpec(memory_space=space)


def call(kernel, place, ins, outs, name, space=pltpu.VMEM, copies=0, flops=0):
    return pl.pallas_call(
        kernel,
        in_specs=[whole_spec(pltpu.SMEM)] + [whole_spec(space) for _ in ins],
        out_specs=[whole_spec() for _ in outs],
        out_shape=[jax.ShapeDtypeStruct(s, BF16) for s in outs],
        scratch_shapes=[pltpu.SemaphoreType.DMA((copies,))] if copies else [],
        compiler_params=pltpu.CompilerParams(vmem_limit_bytes=8 * 2**20),
        name=name,
    )(place, *ins)


def by_levels(queries, keys, values, wq, wk, ratio):
    tok, width = queries.shape
    local_heads, feat, dh = wq.shape
    ways = keys.shape[1] // dh
    heads = local_heads // ways
    seq, sides = lax.axis_size("seq"), lax.axis_size("head")
    levels = seq // ways
    size = ways * tok
    at = lax.axis_index("seq").astype(jnp.int32)
    side = lax.axis_index("head").astype(jnp.int32)
    place = jnp.stack([lax.rem(at, ways), lax.div(at, ways), side])

    def partner(x, d):
        return lax.ppermute(x, "seq", [(i, i // ways * ways + (i % ways ^ d)) for i in range(seq)])

    def partner_of_both(x, dr, dy):
        pairs = [
            (i * sides + j, (i // ways * ways + (i % ways ^ dr)) * sides + (j ^ dy))
            for i in range(seq)
            for j in range(sides)
        ]
        return lax.ppermute(x, ("seq", "head"), pairs)

    def exchanged(parts):
        got = {d: partner(parts[d], d) for d in reversed(range(1, ways))}
        return [parts[0]] + [got[d] for d in range(1, ways)]

    hbm = pltpu.HBM
    kv_parts = call(
        pack_kv_kernel, place, [keys, values], [(tok, 2 * dh)] * ways, "pack_kv", hbm, 2 * ways
    )
    kv_parts = exchanged(kv_parts)
    *q_parts, own_wq, own_wk = call(
        pack_q_kernel,
        place,
        [queries, wq, wk],
        [(tok, width // ways)] * ways + [(heads, feat, dh)] * 2,
        "pack_q",
        hbm,
        ways + 2,
    )
    (kv,) = call(stack_kernel, place, kv_parts, [(size, 2 * dh)], "stack_kv")
    kvs = [kv] + [
        lax.ppermute(kv, "seq", [(i, i + s * ways) for i in range(seq - s * ways)])
        for s in range(1, levels)
    ]
    q_parts = exchanged(q_parts)

    def key_features(x):
        return pl.pallas_call(
            key_features_kernel,
            in_specs=[whole_spec()] * 2,
            out_specs=whole_spec(),
            out_shape=jax.ShapeDtypeStruct((heads * 2 * feat, size), BF16),
            compiler_params=pltpu.CompilerParams(vmem_limit_bytes=16 * 2**20),
            cost_estimate=pl.CostEstimate(
                flops=2 * heads * feat * dh * size,
                bytes_accessed=2**23,
                transcendentals=2 * heads * feat * size,
            ),
            name="key_features",
        )(x, own_wk)

    fks = [key_features(x) for x in kvs]
    part = (tok // sides, heads * dh)
    outs = pl.pallas_call(
        lambda *refs: level_kernel(levels, ways, sides, *refs),
        in_specs=[whole_spec(pltpu.SMEM)] * 2 + [whole_spec() for _ in range(1 + ways + 2 * levels)],
        out_specs=[whole_spec() for _ in range(ways * sides)],
        scratch_shapes=[
            pltpu.VMEM((size, heads * dh), BF16),
            pltpu.VMEM((levels, size, 2 * dh), BF16),
            pltpu.VMEM((heads * 2 * feat, size), BF16),
            pltpu.VMEM((2, heads * 2 * feat, 2 * dh), BF16),
            pltpu.VMEM((size, heads * dh), BF16),
        ],
        out_shape=[jax.ShapeDtypeStruct(part, BF16)] * (ways * sides),
        compiler_params=pltpu.CompilerParams(vmem_limit_bytes=32 * 2**20),
        name="level_mix",
    )(place, ratio, own_wq, *q_parts, *kvs, *fks)
    order = sorted(range(1, ways * sides), key=lambda n: (-(n % sides), -(n // sides)))
    got = {0: outs[0]}
    for n in order:
        got[n] = partner_of_both(outs[n], *divmod(n, sides))
    (joined,) = call(
        lambda *refs: join_kernel(ways, sides, *refs),
        place,
        [got[n] for n in range(ways * sides)],
        [(part[0], sides * ways * part[1])],
        "join",
    )
    return joined


def by_blocks(queries, keys, values, wq, wk, ratio):
    group = wq.shape[0] // (keys.shape[1] // DH)
    place = lax.axis_index("seq").astype(jnp.int32).reshape(1)
    kv = lax.all_gather(jnp.concatenate([keys, values], axis=1), "seq", tiled=True)
    out = mix(place, queries, kv, wq, wk, ratio, group)
    return lax.all_to_all(out, "head", split_axis=0, concat_axis=1, tiled=True)


def local(queries, keys, values, q_feature, k_feature, window_factor):
    tok = queries.shape[0]
    ways = keys.shape[1] // DH
    seq, sides = lax.axis_size("seq"), lax.axis_size("head")
    wq, wk = jnp.swapaxes(q_feature, 1, 2), jnp.swapaxes(k_feature, 1, 2)
    ratio = window_factor / (1.0 - window_factor)
    levels = seq // ways
    fits = ways in (2, 4) and sides in (1, 2) and seq == levels * ways and 2 <= levels <= 4
    if fits and ways * tok == 256 and tok == WINDOW:
        return by_levels(queries, keys, values, wq, wk, ratio)
    return by_blocks(queries, keys, values, wq, wk, ratio)


def solution(mesh):
    return jax.shard_map(
        local,
        mesh=mesh,
        in_specs=(
            P("seq", "head"),
            P("seq", "head"),
            P("seq", "head"),
            P("head", None, None),
            P("head", None, None),
            P("head"),
        ),
        out_specs=P(("seq", "head"), None),
        check_vma=False,
    )
```

```python
import math

import jax
import jax.numpy as jnp
from jax import lax
from jax.experimental import pallas as pl
from jax.experimental.pallas import tpu as pltpu
from jax.sharding import PartitionSpec as P

DH = 128
WINDOW = 64
F32 = jnp.float32
BF16 = jnp.bfloat16


def dot_t(a, b):
    return lax.dot_general(a, b, (((1,), (1,)), ((), ())), preferred_element_type=F32)


def features_t(logits):
    top = jnp.max(logits, axis=0, keepdims=True)
    low = jnp.min(logits, axis=0, keepdims=True)
    up = jnp.exp(logits - top)
    down = jnp.exp(low - logits)
    up = up * (1.0 / jnp.sum(up, axis=0, keepdims=True))
    down = down * (1.0 / jnp.sum(down, axis=0, keepdims=True))
    return jnp.concatenate([up.astype(BF16), down.astype(BF16)], axis=0)


def mix_kernel(
    place_ref, q_ref, k_ref, v_ref, wq_ref, wk_ref, ratio_ref, out_ref, fk_scr, state_scr
):
    tok = q_ref.shape[0]
    heads, feat, dh = wq_ref.shape
    seen = fk_scr.shape[1]
    place = place_ref[0]
    first_head = pl.program_id(0) * heads

    weights = wk_ref[...].reshape(heads * feat, dh)
    for start in range(0, seen, 256):
        size = min(256, seen - start)
        logits = dot_t(weights, k_ref[start : start + size, :])
        for h in range(heads):
            fk_scr[h * 2 * feat : (h + 1) * 2 * feat, start : start + size] = features_t(
                logits[h * feat : (h + 1) * feat]
            )
    row = lax.broadcasted_iota(jnp.int32, (seen, dh), 0)
    kept = row < (place - 1) * tok
    v_seen = jnp.where(kept, v_ref[:seen, :].astype(F32), 0.0).astype(BF16)
    ones_seen = jnp.where(kept, 1.0, 0.0).astype(BF16)
    v_seen = jnp.concatenate([v_seen, ones_seen], axis=1)
    state_scr[...] = jnp.dot(fk_scr[...], v_seen, preferred_element_type=F32).astype(BF16)

    before = pl.multiple_of(jnp.maximum(place - 1, 0) * tok, tok)
    own = pl.multiple_of(place * tok, tok)
    k_ext = jnp.concatenate([k_ref[pl.ds(before, tok), :], k_ref[pl.ds(own, tok), :]], axis=0)
    v_ext = jnp.concatenate([v_ref[pl.ds(before, tok), :], v_ref[pl.ds(own, tok), :]], axis=0)
    v_ext = jnp.concatenate([v_ext, jnp.ones_like(v_ext)], axis=1)
    row = lax.broadcasted_iota(jnp.int32, (tok, 2 * tok), 0)
    col = lax.broadcasted_iota(jnp.int32, (tok, 2 * tok), 1)
    valid = (col >= tok) | (place > 0)
    inside = (col > row) & (col <= row + WINDOW) & valid
    causal = (col <= row) & valid
    lane = lax.broadcasted_iota(jnp.int32, (tok, 2 * feat), 1)
    left = lane < feat
    side_r = lax.broadcasted_iota(jnp.int32, (2 * feat, 2 * feat), 0) < feat
    side_c = lax.broadcasted_iota(jnp.int32, (2 * feat, 2 * feat), 1) < feat
    halves = jnp.where(side_r == side_c, 1.0, 0.0).astype(BF16)

    for h in range(heads):
        q = q_ref[:, h * dh : (h + 1) * dh]
        wq = wq_ref[h]
        logits = dot_t(q, jnp.concatenate([wq, -wq], axis=0))
        top_l = jnp.max(jnp.where(left, logits, -jnp.inf), axis=1, keepdims=True)
        top_r = jnp.max(jnp.where(left, -jnp.inf, logits), axis=1, keepdims=True)
        expd = jnp.exp(logits - jnp.where(left, top_l, top_r)).astype(BF16)
        total = jnp.dot(expd, halves, preferred_element_type=F32)
        fq = (expd.astype(F32) / total).astype(BF16)
        fk = features_t(dot_t(wk_ref[h], k_ext))
        linear = jnp.dot(fq, fk, preferred_element_type=F32)
        scores = dot_t(q, k_ext) * (1.0 / math.sqrt(dh))
        masked = jnp.where(inside, scores, -jnp.inf)
        top = jnp.max(masked, axis=1, keepdims=True)
        soft = jnp.exp(masked - top) * ratio_ref[first_head + h]
        weight = jnp.where(causal, linear, soft).astype(BF16)
        both = jnp.dot(weight, v_ext, preferred_element_type=F32) + jnp.dot(
            fq, state_scr[h * 2 * feat : (h + 1) * 2 * feat, :], preferred_element_type=F32
        )
        out_ref[:, h * dh : (h + 1) * dh] = (both[:, :dh] / both[:, dh:]).astype(BF16)


def mix(place, queries, kv, wq, wk, ratio, group):
    tok = queries.shape[0]
    local_heads, feat, dh = wq.shape
    groups = local_heads // group
    tokens = kv.shape[0]
    seen = tokens - 2 * tok
    return pl.pallas_call(
        mix_kernel,
        grid_spec=pltpu.PrefetchScalarGridSpec(
            num_scalar_prefetch=1,
            grid=(groups,),
            in_specs=[
                pl.BlockSpec((tok, group * dh), lambda g, p: (0, g)),
                pl.BlockSpec((tokens, dh), lambda g, p: (0, g)),
                pl.BlockSpec((tokens, dh), lambda g, p: (0, groups + g)),
                pl.BlockSpec((group, feat, dh), lambda g, p: (g, 0, 0)),
                pl.BlockSpec((group, feat, dh), lambda g, p: (g, 0, 0)),
                pl.BlockSpec(memory_space=pltpu.SMEM),
            ],
            out_specs=pl.BlockSpec((tok, group * dh), lambda g, p: (0, g)),
            scratch_shapes=[
                pltpu.VMEM((group * 2 * feat, seen), BF16),
                pltpu.VMEM((group * 2 * feat, 2 * dh), BF16),
            ],
        ),
        out_shape=jax.ShapeDtypeStruct(queries.shape, BF16),
        compiler_params=pltpu.CompilerParams(vmem_limit_bytes=48 * 2**20),
        cost_estimate=pl.CostEstimate(
            flops=2 * local_heads * tokens * 3 * feat * 2 * dh,
            bytes_accessed=8 * 2**20,
            transcendentals=local_heads * tokens * 2 * feat,
        ),
    )(place, queries, kv, kv, wq, wk, ratio)


def spot(ways):
    at = lax.axis_index("seq")
    return lax.rem(at, ways), lax.div(at, ways)


def copy_all(pairs, sems):
    copies = [pltpu.make_async_copy(a, b, sems.at[n]) for n, (a, b) in enumerate(pairs)]
    for copy in copies:
        copy.start()
    for copy in copies:
        copy.wait()


def pack_kernel(k_ref, v_ref, q_ref, *refs):
    outs, sems = refs[:-1], refs[-1]
    ways = k_ref.shape[1] // DH
    width = q_ref.shape[1] // ways
    place = spot(ways)[0]
    pairs = []
    for d, out in enumerate(outs[: ways - 1], 1):
        at = pl.ds(pl.multiple_of((place ^ d) * DH, DH), DH)
        pairs += [(k_ref.at[:, at], out.at[:, :DH]), (v_ref.at[:, at], out.at[:, DH:])]
    for d, out in enumerate(outs[ways - 1 :]):
        at = pl.multiple_of((place ^ d) * width, width)
        pairs.append((q_ref.at[:, pl.ds(at, width)], out))
    copy_all(pairs, sems)


def stack_kernel(k_ref, v_ref, *refs):
    got, out_ref = refs[:-1], refs[-1]
    tok = k_ref.shape[0]
    place = spot(len(got) + 1)[0]
    group = pl.ds(pl.multiple_of(place * DH, DH), DH)
    own = pl.ds(pl.multiple_of(place * tok, tok), tok)
    out_ref[own, :DH] = k_ref[:, group]
    out_ref[own, DH:] = v_ref[:, group]
    for d, ref in enumerate(got, 1):
        out_ref[pl.ds(pl.multiple_of((place ^ d) * tok, tok), tok), :] = ref[...]


def weights_kernel(ways, wq_ref, wk_ref, both_ref, own_wk_ref):
    heads = own_wk_ref.shape[0]
    first = spot(ways)[0] * heads
    for h in range(heads):
        wq = wq_ref[first + h].T
        both_ref[h] = jnp.concatenate([wq, -wq], axis=1)
        own_wk_ref[h] = wk_ref[first + h]


def join_kernel(ways, sides, got_ref, out_ref, sems):
    width = got_ref.shape[2]
    pairs = []
    for n in range(ways * sides):
        block = n % sides * ways + n // sides
        pairs.append((got_ref.at[n], out_ref.at[:, block * width : (block + 1) * width]))
    copy_all(pairs, sems)


def key_features_kernel(kv_ref, wk_ref, fk_ref):
    heads, feat, dh = wk_ref.shape
    logits = dot_t(wk_ref[...].reshape(heads * feat, dh), kv_ref[:, :dh])
    for h in range(heads):
        part = logits[h * feat : (h + 1) * feat]
        top = jnp.max(part, axis=0, keepdims=True)
        low = jnp.min(part, axis=0, keepdims=True)
        for n, shifted in enumerate((part - top, low - part)):
            row = (2 * h + n) * feat
            expd = jnp.exp(shifted.astype(BF16))
            total = expd[: feat // 4]
            for q in range(1, 4):
                total = total + expd[q * feat // 4 : (q + 1) * feat // 4]
            total = jnp.sum(total.astype(F32), axis=0, keepdims=True)
            fk_ref[row : row + feat, :] = expd * pl.reciprocal(total).astype(BF16)


def query_features_kernel(ways, *refs):
    q_refs, w_ref, q_out, fq_out, exp_scr = refs[:ways], *refs[ways:]
    tok = q_refs[0].shape[0]
    heads, dh, both = w_ref.shape
    half = ways * tok // 2
    blocks = half // tok
    place = spot(ways)[0]
    for d, ref in enumerate(q_refs):
        at = place ^ d
        u = at // blocks
        row = pl.multiple_of((at % blocks) * tok, tok)
        for h in range(heads):
            q_out[u, pl.ds(h * half + row, tok), :] = ref[:, h * dh : (h + 1) * dh]
    left = lax.broadcasted_iota(jnp.int32, (half, both), 1) < both // 2
    side_r = lax.broadcasted_iota(jnp.int32, (both, both), 0) < both // 2
    side_c = lax.broadcasted_iota(jnp.int32, (both, both), 1) < both // 2
    halves = jnp.where(side_r == side_c, 1.0, 0.0).astype(BF16)
    for u in range(2):
        for h in range(heads):
            rows = slice(h * half, (h + 1) * half)
            logits = jnp.dot(q_out[u, rows, :], w_ref[h], preferred_element_type=F32)
            top_l = jnp.max(jnp.where(left, logits, -jnp.inf), axis=1, keepdims=True)
            top_r = jnp.max(jnp.where(left, -jnp.inf, logits), axis=1, keepdims=True)
            exp_scr[rows, :] = jnp.exp((logits - jnp.where(left, top_l, top_r)).astype(BF16))
        total = jnp.dot(exp_scr[...], halves, preferred_element_type=F32)
        fq_out[u] = (exp_scr[...].astype(F32) * pl.reciprocal(total, approx=True)).astype(BF16)


def weights_of_pairs_kernel(
    ways, ratio_ref, q_ref, fq_ref, own_ref, last_ref, fk_own_ref, fk_last_ref, w_ref
):
    half, rows = own_ref.shape[0] // 2, q_ref.shape[1]
    heads = rows // half
    dh = q_ref.shape[2]
    feats = fq_ref.shape[2]
    place, level = spot(ways)
    row = lax.broadcasted_iota(jnp.int32, (half, 2 * half), 0)
    col = lax.broadcasted_iota(jnp.int32, (half, 2 * half), 1)
    split = row + (half - WINDOW)
    for u in range(2):
        valid = (col >= half) | (level > 0) | (u > 0)
        inside = (col > split) & (col <= row + half) & valid
        causal = (col <= split) & valid
        if u == 0:
            keys = jnp.concatenate([last_ref[half:, :dh], own_ref[:half, :dh]], axis=0)
        else:
            keys = own_ref[:, :dh]
        scores = dot_t(q_ref[u], keys) * (1.0 / math.sqrt(dh))
        for h in range(heads):
            here = slice(h * half, (h + 1) * half)
            f = slice(h * feats, (h + 1) * feats)
            if u == 0:
                fk = jnp.concatenate([fk_last_ref[f, half:], fk_own_ref[f, :half]], axis=1)
            else:
                fk = fk_own_ref[f, :]
            linear = jnp.dot(fq_ref[u, here, :], fk, preferred_element_type=F32)
            masked = jnp.where(inside, scores[here], -jnp.inf)
            top = jnp.max(masked, axis=1, keepdims=True)
            soft = jnp.exp(masked - top) * ratio_ref[place * heads + h]
            w_ref[u, here, :] = jnp.where(causal, linear, soft).astype(BF16)


def mix_level_kernel(ways, levels, w_ref, fq_ref, *refs):
    kv_refs, fk_refs = refs[:levels], refs[levels : 2 * levels - 1]
    out_ref, near_scr, state_scr = refs[2 * levels - 1 :]
    size, dh = kv_refs[0].shape[0], kv_refs[0].shape[1] // 2
    half = size // 2
    rows = w_ref.shape[1]
    heads = rows // half
    feats = fq_ref.shape[2]
    level = spot(ways)[1]
    part = out_ref.shape[1]

    def with_ones(s, at):
        v = kv_refs[s][at, dh:]
        here = jnp.where(level >= s, 1.0, 0.0).astype(BF16)
        return jnp.concatenate([v, jnp.full(v.shape, here)], axis=1)

    first, second, every = slice(0, half), slice(half, size), slice(0, size)
    fk = jnp.concatenate([fk_refs[0][:, first]] + [ref[...] for ref in fk_refs[1:]], axis=1)
    v = jnp.concatenate(
        [with_ones(1, first)] + [with_ones(s, every) for s in range(2, levels)], axis=0
    )
    state = jnp.dot(fk, v, preferred_element_type=F32)
    state_scr[0] = state.astype(BF16)
    state_scr[1] = (
        state + jnp.dot(fk_refs[0][:, second], with_ones(1, second), preferred_element_type=F32)
    ).astype(BF16)
    near_scr[0] = jnp.dot(
        w_ref[0],
        jnp.concatenate([with_ones(1, second), with_ones(0, first)], axis=0),
        preferred_element_type=F32,
    )
    near_scr[1] = jnp.dot(w_ref[1], with_ones(0, every), preferred_element_type=F32)
    for h in range(heads):
        for u in range(2):
            here = slice(h * half, (h + 1) * half)
            far = jnp.dot(
                fq_ref[u, here, :],
                state_scr[u, h * feats : (h + 1) * feats, :],
                preferred_element_type=F32,
            )
            both = near_scr[u, here, :] + far
            out = (both[:, :dh] * pl.reciprocal(both[:, dh:], approx=True)).astype(BF16)
            for n in range(half // part):
                out_ref[u * (half // part) + n, :, h * dh : (h + 1) * dh] = out[
                    n * part : (n + 1) * part
                ]


def whole_spec(space=pltpu.VMEM):
    return pl.BlockSpec(memory_space=space)


def call(kernel, ins, outs, name, scratch=(), limit=8, flops=0, space=pltpu.VMEM):
    return pl.pallas_call(
        kernel,
        in_specs=[whole_spec(space) for _ in ins],
        out_specs=[whole_spec(space) for _ in outs],
        out_shape=[jax.ShapeDtypeStruct(s, BF16) for s in outs],
        scratch_shapes=list(scratch),
        compiler_params=pltpu.CompilerParams(vmem_limit_bytes=limit * 2**20),
        cost_estimate=pl.CostEstimate(flops=flops, bytes_accessed=2**20, transcendentals=0),
        name=name,
    )(*ins)


def by_levels(queries, keys, values, wq, wk, ratio):
    tok, width = queries.shape
    local_heads, feat, dh = wq.shape
    ways = keys.shape[1] // dh
    heads = local_heads // ways
    seq, sides = lax.axis_size("seq"), lax.axis_size("head")
    levels = seq // ways
    size = ways * tok
    half = size // 2
    rows = heads * half
    def partner(x, d):
        return lax.ppermute(x, "seq", [(i, i // ways * ways + (i % ways ^ d)) for i in range(seq)])

    parts = call(
        pack_kernel,
        [keys, values, queries],
        [(tok, 2 * dh)] * (ways - 1) + [(tok, width // ways)] * ways,
        "pack",
        [pltpu.SemaphoreType.DMA((3 * ways - 2,))],
        60,
        space=pltpu.HBM,
    )
    kv_parts, q_parts = [None, *parts[: ways - 1]], parts[ways - 1 :]
    got = {d: partner(kv_parts[d], d) for d in reversed(range(1, ways))}
    kv_parts = [got[d] for d in range(1, ways)]
    got = {d: partner(q_parts[d], d) for d in reversed(range(1, ways))}
    q_parts = [q_parts[0]] + [got[d] for d in range(1, ways)]
    (kv,) = call(
        stack_kernel,
        [keys, values, *kv_parts],
        [(size, 2 * dh)],
        "stack_kv",
    )
    kvs = [kv] + [
        lax.ppermute(kv, "seq", [(i, i + s * ways) for i in range(seq - s * ways)])
        for s in range(1, levels)
    ]

    both_wq, own_wk = call(
        lambda *refs: weights_kernel(ways, *refs),
        [wq, wk],
        [(heads, dh, 2 * feat), (heads, feat, dh)],
        "weights",
    )

    def key_features(x):
        return pl.pallas_call(
            key_features_kernel,
            in_specs=[whole_spec()] * 2,
            out_specs=whole_spec(),
            out_shape=jax.ShapeDtypeStruct((heads * 2 * feat, size), BF16),
            compiler_params=pltpu.CompilerParams(vmem_limit_bytes=16 * 2**20),
            cost_estimate=pl.CostEstimate(
                flops=2 * heads * feat * dh * size,
                bytes_accessed=2**20,
                transcendentals=2 * heads * feat * size,
            ),
            name="key_features",
        )(x, own_wk)

    fks = [key_features(x) for x in kvs]
    q_all, fq = call(
        lambda *refs: query_features_kernel(ways, *refs),
        [*q_parts, both_wq],
        [(2, rows, dh), (2, rows, 2 * feat)],
        "query_features",
        [pltpu.VMEM((rows, 2 * feat), BF16)],
        16,
        4 * rows * dh * 2 * feat,
    )
    (pair_weights,) = pl.pallas_call(
        lambda *refs: weights_of_pairs_kernel(ways, *refs),
        in_specs=[whole_spec(pltpu.SMEM)] + [whole_spec() for _ in range(6)],
        out_specs=[whole_spec()],
        out_shape=[jax.ShapeDtypeStruct((2, rows, size), BF16)],
        compiler_params=pltpu.CompilerParams(vmem_limit_bytes=24 * 2**20),
        cost_estimate=pl.CostEstimate(
            flops=8 * rows * dh * size, bytes_accessed=2**20, transcendentals=2 * rows * size
        ),
        name="pair_weights",
    )(ratio, q_all, fq, kvs[0], kvs[1], fks[0], fks[1])
    part = tok // sides
    (outs,) = call(
        lambda *refs: mix_level_kernel(ways, levels, *refs),
        [pair_weights, fq, *kvs, *fks[1:]],
        [(ways * sides, part, heads * dh)],
        "mix_level",
        [pltpu.VMEM((2, rows, 2 * dh), F32), pltpu.VMEM((2, heads * 2 * feat, 2 * dh), BF16)],
        32,
        16 * rows * dh * size,
    )
    groups = [
        [(z * ways + r) * sides + y for r in range(ways) for y in range(sides)]
        for z in range(levels)
    ]
    got = lax.all_to_all(
        outs, ("seq", "head"), split_axis=0, concat_axis=0, axis_index_groups=groups, tiled=True
    )
    (joined,) = pl.pallas_call(
        lambda *refs: join_kernel(ways, sides, *refs),
        in_specs=[whole_spec()],
        out_specs=[whole_spec(pltpu.HBM)],
        out_shape=[jax.ShapeDtypeStruct((part, sides * ways * heads * dh), BF16)],
        scratch_shapes=[pltpu.SemaphoreType.DMA((ways * sides,))],
        compiler_params=pltpu.CompilerParams(vmem_limit_bytes=4 * 2**20),
        name="join",
    )(got)
    return joined


def by_blocks(queries, keys, values, wq, wk, ratio):
    group = wq.shape[0] // (keys.shape[1] // DH)
    place = lax.axis_index("seq").astype(jnp.int32).reshape(1)
    kv = lax.all_gather(jnp.concatenate([keys, values], axis=1), "seq", tiled=True)
    out = mix(place, queries, kv, wq, wk, ratio, group)
    return lax.all_to_all(out, "head", split_axis=0, concat_axis=1, tiled=True)


def local(queries, keys, values, q_feature, k_feature, window_factor):
    tok = queries.shape[0]
    ways = keys.shape[1] // DH
    seq, sides = lax.axis_size("seq"), lax.axis_size("head")
    wq, wk = jnp.swapaxes(q_feature, 1, 2), jnp.swapaxes(k_feature, 1, 2)
    ratio = window_factor / (1.0 - window_factor)
    levels = seq // ways
    fits = ways in (2, 4) and sides in (1, 2) and seq == levels * ways and 2 <= levels <= 4
    if fits and ways * tok == 256 and tok == WINDOW:
        return by_levels(queries, keys, values, wq, wk, ratio)
    return by_blocks(queries, keys, values, wq, wk, ratio)


def solution(mesh):
    return jax.shard_map(
        local,
        mesh=mesh,
        in_specs=(
            P("seq", "head"),
            P("seq", "head"),
            P("seq", "head"),
            P("head", None, None),
            P("head", None, None),
            P("head"),
        ),
        out_specs=P(("seq", "head"), None),
        check_vma=False,
    )
```

```python
import math

import jax
import jax.numpy as jnp
from jax import lax
from jax.experimental import pallas as pl
from jax.experimental.pallas import tpu as pltpu
from jax.sharding import PartitionSpec as P

DH = 128
WINDOW = 64
F32 = jnp.float32
BF16 = jnp.bfloat16


def dot_t(a, b):
    return lax.dot_general(a, b, (((1,), (1,)), ((), ())), preferred_element_type=F32)


def features_t(logits):
    top = jnp.max(logits, axis=0, keepdims=True)
    low = jnp.min(logits, axis=0, keepdims=True)
    up = jnp.exp(logits - top)
    down = jnp.exp(low - logits)
    up = up * (1.0 / jnp.sum(up, axis=0, keepdims=True))
    down = down * (1.0 / jnp.sum(down, axis=0, keepdims=True))
    return jnp.concatenate([up.astype(BF16), down.astype(BF16)], axis=0)


def mix_kernel(
    place_ref, q_ref, k_ref, v_ref, wq_ref, wk_ref, ratio_ref, out_ref, fk_scr, state_scr
):
    tok = q_ref.shape[0]
    heads, feat, dh = wq_ref.shape
    seen = fk_scr.shape[1]
    place = place_ref[0]
    first_head = pl.program_id(0) * heads

    weights = wk_ref[...].reshape(heads * feat, dh)
    for start in range(0, seen, 256):
        size = min(256, seen - start)
        logits = dot_t(weights, k_ref[start : start + size, :])
        for h in range(heads):
            fk_scr[h * 2 * feat : (h + 1) * 2 * feat, start : start + size] = features_t(
                logits[h * feat : (h + 1) * feat]
            )
    row = lax.broadcasted_iota(jnp.int32, (seen, dh), 0)
    kept = row < (place - 1) * tok
    v_seen = jnp.where(kept, v_ref[:seen, :].astype(F32), 0.0).astype(BF16)
    ones_seen = jnp.where(kept, 1.0, 0.0).astype(BF16)
    v_seen = jnp.concatenate([v_seen, ones_seen], axis=1)
    state_scr[...] = jnp.dot(fk_scr[...], v_seen, preferred_element_type=F32).astype(BF16)

    before = pl.multiple_of(jnp.maximum(place - 1, 0) * tok, tok)
    own = pl.multiple_of(place * tok, tok)
    k_ext = jnp.concatenate([k_ref[pl.ds(before, tok), :], k_ref[pl.ds(own, tok), :]], axis=0)
    v_ext = jnp.concatenate([v_ref[pl.ds(before, tok), :], v_ref[pl.ds(own, tok), :]], axis=0)
    v_ext = jnp.concatenate([v_ext, jnp.ones_like(v_ext)], axis=1)
    row = lax.broadcasted_iota(jnp.int32, (tok, 2 * tok), 0)
    col = lax.broadcasted_iota(jnp.int32, (tok, 2 * tok), 1)
    valid = (col >= tok) | (place > 0)
    inside = (col > row) & (col <= row + WINDOW) & valid
    causal = (col <= row) & valid
    lane = lax.broadcasted_iota(jnp.int32, (tok, 2 * feat), 1)
    left = lane < feat
    side_r = lax.broadcasted_iota(jnp.int32, (2 * feat, 2 * feat), 0) < feat
    side_c = lax.broadcasted_iota(jnp.int32, (2 * feat, 2 * feat), 1) < feat
    halves = jnp.where(side_r == side_c, 1.0, 0.0).astype(BF16)

    for h in range(heads):
        q = q_ref[:, h * dh : (h + 1) * dh]
        wq = wq_ref[h]
        logits = dot_t(q, jnp.concatenate([wq, -wq], axis=0))
        top_l = jnp.max(jnp.where(left, logits, -jnp.inf), axis=1, keepdims=True)
        top_r = jnp.max(jnp.where(left, -jnp.inf, logits), axis=1, keepdims=True)
        expd = jnp.exp(logits - jnp.where(left, top_l, top_r)).astype(BF16)
        total = jnp.dot(expd, halves, preferred_element_type=F32)
        fq = (expd.astype(F32) / total).astype(BF16)
        fk = features_t(dot_t(wk_ref[h], k_ext))
        linear = jnp.dot(fq, fk, preferred_element_type=F32)
        scores = dot_t(q, k_ext) * (1.0 / math.sqrt(dh))
        masked = jnp.where(inside, scores, -jnp.inf)
        top = jnp.max(masked, axis=1, keepdims=True)
        soft = jnp.exp(masked - top) * ratio_ref[first_head + h]
        weight = jnp.where(causal, linear, soft).astype(BF16)
        both = jnp.dot(weight, v_ext, preferred_element_type=F32) + jnp.dot(
            fq, state_scr[h * 2 * feat : (h + 1) * 2 * feat, :], preferred_element_type=F32
        )
        out_ref[:, h * dh : (h + 1) * dh] = (both[:, :dh] / both[:, dh:]).astype(BF16)


def mix(place, queries, kv, wq, wk, ratio, group):
    tok = queries.shape[0]
    local_heads, feat, dh = wq.shape
    groups = local_heads // group
    tokens = kv.shape[0]
    seen = tokens - 2 * tok
    return pl.pallas_call(
        mix_kernel,
        grid_spec=pltpu.PrefetchScalarGridSpec(
            num_scalar_prefetch=1,
            grid=(groups,),
            in_specs=[
                pl.BlockSpec((tok, group * dh), lambda g, p: (0, g)),
                pl.BlockSpec((tokens, dh), lambda g, p: (0, g)),
                pl.BlockSpec((tokens, dh), lambda g, p: (0, groups + g)),
                pl.BlockSpec((group, feat, dh), lambda g, p: (g, 0, 0)),
                pl.BlockSpec((group, feat, dh), lambda g, p: (g, 0, 0)),
                pl.BlockSpec(memory_space=pltpu.SMEM),
            ],
            out_specs=pl.BlockSpec((tok, group * dh), lambda g, p: (0, g)),
            scratch_shapes=[
                pltpu.VMEM((group * 2 * feat, seen), BF16),
                pltpu.VMEM((group * 2 * feat, 2 * dh), BF16),
            ],
        ),
        out_shape=jax.ShapeDtypeStruct(queries.shape, BF16),
        compiler_params=pltpu.CompilerParams(vmem_limit_bytes=48 * 2**20),
        cost_estimate=pl.CostEstimate(
            flops=2 * local_heads * tokens * 3 * feat * 2 * dh,
            bytes_accessed=8 * 2**20,
            transcendentals=local_heads * tokens * 2 * feat,
        ),
    )(place, queries, kv, kv, wq, wk, ratio)


def spot(ways):
    at = lax.axis_index("seq")
    return lax.rem(at, ways), lax.div(at, ways)


def copy_all(pairs, sems):
    copies = [pltpu.make_async_copy(a, b, sems.at[n]) for n, (a, b) in enumerate(pairs)]
    for copy in copies:
        copy.start()
    for copy in copies:
        copy.wait()


def pack_kernel(q_ref, *out_refs):
    width = out_refs[0].shape[1]
    place = spot(len(out_refs))[0]
    for d, out in enumerate(out_refs):
        out[...] = q_ref[:, pl.ds(pl.multiple_of((place ^ d) * width, width), width)]


def pack_kv_kernel(k_ref, v_ref, out_ref):
    for g in range(out_ref.shape[0]):
        out_ref[g, :, :DH] = k_ref[:, g * DH : (g + 1) * DH]
        out_ref[g, :, DH:] = v_ref[:, g * DH : (g + 1) * DH]


def weights_kernel(ways, wq_ref, wk_ref, both_ref, own_wk_ref):
    heads = own_wk_ref.shape[0]
    first = spot(ways)[0] * heads
    for h in range(heads):
        wq = wq_ref[first + h].T
        both_ref[h] = jnp.concatenate([wq, -wq], axis=1)
        own_wk_ref[h] = wk_ref[first + h]


def join_kernel(ways, sides, got_ref, out_ref, sems):
    width = got_ref.shape[2]
    pairs = []
    for n in range(ways * sides):
        block = n % sides * ways + n // sides
        pairs.append((got_ref.at[n], out_ref.at[:, block * width : (block + 1) * width]))
    copy_all(pairs, sems)


def key_features_kernel(kv_ref, wk_ref, fk_ref):
    heads, feat, dh = wk_ref.shape
    logits = dot_t(wk_ref[...].reshape(heads * feat, dh), kv_ref[:, :dh])
    for h in range(heads):
        part = logits[h * feat : (h + 1) * feat]
        top = jnp.max(part, axis=0, keepdims=True)
        low = jnp.min(part, axis=0, keepdims=True)
        for n, shifted in enumerate((part - top, low - part)):
            row = (2 * h + n) * feat
            expd = jnp.exp(shifted.astype(BF16))
            total = expd[: feat // 4]
            for q in range(1, 4):
                total = total + expd[q * feat // 4 : (q + 1) * feat // 4]
            total = jnp.sum(total.astype(F32), axis=0, keepdims=True)
            fk_ref[row : row + feat, :] = expd * pl.reciprocal(total).astype(BF16)


def query_features_kernel(ways, *refs):
    q_refs, w_ref, q_out, fq_out, exp_scr = refs[:ways], *refs[ways:]
    tok = q_refs[0].shape[0]
    heads, dh, both = w_ref.shape
    half = ways * tok // 2
    blocks = half // tok
    place = spot(ways)[0]
    for d, ref in enumerate(q_refs):
        at = place ^ d
        u = at // blocks
        row = pl.multiple_of((at % blocks) * tok, tok)
        for h in range(heads):
            q_out[u, pl.ds(h * half + row, tok), :] = ref[:, h * dh : (h + 1) * dh]
    left = lax.broadcasted_iota(jnp.int32, (half, both), 1) < both // 2
    side_r = lax.broadcasted_iota(jnp.int32, (both, both), 0) < both // 2
    side_c = lax.broadcasted_iota(jnp.int32, (both, both), 1) < both // 2
    halves = jnp.where(side_r == side_c, 1.0, 0.0).astype(BF16)
    for u in range(2):
        for h in range(heads):
            rows = slice(h * half, (h + 1) * half)
            logits = jnp.dot(q_out[u, rows, :], w_ref[h], preferred_element_type=F32)
            top_l = jnp.max(jnp.where(left, logits, -jnp.inf), axis=1, keepdims=True)
            top_r = jnp.max(jnp.where(left, -jnp.inf, logits), axis=1, keepdims=True)
            exp_scr[rows, :] = jnp.exp((logits - jnp.where(left, top_l, top_r)).astype(BF16))
        total = jnp.dot(exp_scr[...], halves, preferred_element_type=F32)
        fq_out[u] = (exp_scr[...].astype(F32) * pl.reciprocal(total, approx=True)).astype(BF16)


def weights_of_pairs_kernel(
    ways, ratio_ref, q_ref, fq_ref, own_ref, last_ref, fk_own_ref, fk_last_ref, w_ref
):
    half, rows = own_ref.shape[0] // 2, q_ref.shape[1]
    heads = rows // half
    dh = q_ref.shape[2]
    feats = fq_ref.shape[2]
    place, level = spot(ways)
    row = lax.broadcasted_iota(jnp.int32, (half, 2 * half), 0)
    col = lax.broadcasted_iota(jnp.int32, (half, 2 * half), 1)
    split = row + (half - WINDOW)
    for u in range(2):
        valid = (col >= half) | (level > 0) | (u > 0)
        inside = (col > split) & (col <= row + half) & valid
        causal = (col <= split) & valid
        if u == 0:
            keys = jnp.concatenate([last_ref[half:, :dh], own_ref[:half, :dh]], axis=0)
        else:
            keys = own_ref[:, :dh]
        scores = dot_t(q_ref[u], keys) * (1.0 / math.sqrt(dh))
        for h in range(heads):
            here = slice(h * half, (h + 1) * half)
            f = slice(h * feats, (h + 1) * feats)
            if u == 0:
                fk = jnp.concatenate([fk_last_ref[f, half:], fk_own_ref[f, :half]], axis=1)
            else:
                fk = fk_own_ref[f, :]
            linear = jnp.dot(fq_ref[u, here, :], fk, preferred_element_type=F32)
            masked = jnp.where(inside, scores[here], -jnp.inf)
            top = jnp.max(masked, axis=1, keepdims=True)
            soft = jnp.exp(masked - top) * ratio_ref[place * heads + h]
            w_ref[u, here, :] = jnp.where(causal, linear, soft).astype(BF16)


def mix_level_kernel(ways, levels, w_ref, fq_ref, *refs):
    kv_refs, fk_refs = refs[:levels], refs[levels : 2 * levels - 1]
    out_ref, near_scr, state_scr = refs[2 * levels - 1 :]
    size, dh = kv_refs[0].shape[0], kv_refs[0].shape[1] // 2
    half = size // 2
    rows = w_ref.shape[1]
    heads = rows // half
    feats = fq_ref.shape[2]
    level = spot(ways)[1]
    part = out_ref.shape[1]

    def with_ones(s, at):
        v = kv_refs[s][at, dh:]
        here = jnp.where(level >= s, 1.0, 0.0).astype(BF16)
        return jnp.concatenate([v, jnp.full(v.shape, here)], axis=1)

    first, second, every = slice(0, half), slice(half, size), slice(0, size)
    fk = jnp.concatenate([fk_refs[0][:, first]] + [ref[...] for ref in fk_refs[1:]], axis=1)
    v = jnp.concatenate(
        [with_ones(1, first)] + [with_ones(s, every) for s in range(2, levels)], axis=0
    )
    state = jnp.dot(fk, v, preferred_element_type=F32)
    state_scr[0] = state.astype(BF16)
    state_scr[1] = (
        state + jnp.dot(fk_refs[0][:, second], with_ones(1, second), preferred_element_type=F32)
    ).astype(BF16)
    near_scr[0] = jnp.dot(
        w_ref[0],
        jnp.concatenate([with_ones(1, second), with_ones(0, first)], axis=0),
        preferred_element_type=F32,
    )
    near_scr[1] = jnp.dot(w_ref[1], with_ones(0, every), preferred_element_type=F32)
    for h in range(heads):
        for u in range(2):
            here = slice(h * half, (h + 1) * half)
            far = jnp.dot(
                fq_ref[u, here, :],
                state_scr[u, h * feats : (h + 1) * feats, :],
                preferred_element_type=F32,
            )
            both = near_scr[u, here, :] + far
            out = (both[:, :dh] * pl.reciprocal(both[:, dh:], approx=True)).astype(BF16)
            for n in range(half // part):
                out_ref[u * (half // part) + n, :, h * dh : (h + 1) * dh] = out[
                    n * part : (n + 1) * part
                ]


def whole_spec(space=pltpu.VMEM):
    return pl.BlockSpec(memory_space=space)


def call(kernel, ins, outs, name, scratch=(), limit=8, flops=0, space=pltpu.VMEM):
    return pl.pallas_call(
        kernel,
        in_specs=[whole_spec(space) for _ in ins],
        out_specs=[whole_spec(space) for _ in outs],
        out_shape=[jax.ShapeDtypeStruct(s, BF16) for s in outs],
        scratch_shapes=list(scratch),
        compiler_params=pltpu.CompilerParams(vmem_limit_bytes=limit * 2**20),
        name=name,
    )(*ins)


def by_levels(queries, keys, values, wq, wk, ratio):
    tok, width = queries.shape
    local_heads, feat, dh = wq.shape
    ways = keys.shape[1] // dh
    heads = local_heads // ways
    seq, sides = lax.axis_size("seq"), lax.axis_size("head")
    levels = seq // ways
    size = ways * tok
    half = size // 2
    rows = heads * half
    def partner(x, d):
        return lax.ppermute(x, "seq", [(i, i // ways * ways + (i % ways ^ d)) for i in range(seq)])

    q_parts = call(pack_kernel, [queries], [(tok, width // ways)] * ways, "pack_q", limit=4)
    got = {d: partner(q_parts[d], d) for d in reversed(range(1, ways))}
    q_parts = [q_parts[0]] + [got[d] for d in range(1, ways)]
    keys, values, q_parts[1] = lax.optimization_barrier((keys, values, q_parts[1]))
    (raw,) = call(pack_kv_kernel, [keys, values], [(ways, tok, 2 * dh)], "pack_kv", limit=4)
    groups = [[z * ways + r for r in range(ways)] for z in range(levels)]
    kv = lax.all_to_all(
        raw, "seq", split_axis=0, concat_axis=0, axis_index_groups=groups, tiled=True
    ).reshape(size, 2 * dh)
    kvs = [kv] + [
        lax.ppermute(kv, "seq", [(i, i + s * ways) for i in range(seq - s * ways)])
        for s in range(1, levels)
    ]
    wq, wk, kv = lax.optimization_barrier((wq, wk, kv))
    both_wq, own_wk = call(
        lambda *refs: weights_kernel(ways, *refs),
        [wq, wk],
        [(heads, dh, 2 * feat), (heads, feat, dh)],
        "weights",
    )

    def key_features(x):
        return pl.pallas_call(
            key_features_kernel,
            in_specs=[whole_spec()] * 2,
            out_specs=whole_spec(),
            out_shape=jax.ShapeDtypeStruct((heads * 2 * feat, size), BF16),
            compiler_params=pltpu.CompilerParams(vmem_limit_bytes=16 * 2**20),
            name="key_features",
        )(x, own_wk)

    fks = [key_features(x) for x in kvs]
    q_all, fq = call(
        lambda *refs: query_features_kernel(ways, *refs),
        [*q_parts, both_wq],
        [(2, rows, dh), (2, rows, 2 * feat)],
        "query_features",
        [pltpu.VMEM((rows, 2 * feat), BF16)],
        16,
        4 * rows * dh * 2 * feat,
    )
    (pair_weights,) = pl.pallas_call(
        lambda *refs: weights_of_pairs_kernel(ways, *refs),
        in_specs=[whole_spec(pltpu.SMEM)] + [whole_spec() for _ in range(6)],
        out_specs=[whole_spec()],
        out_shape=[jax.ShapeDtypeStruct((2, rows, size), BF16)],
        compiler_params=pltpu.CompilerParams(vmem_limit_bytes=24 * 2**20),
        name="pair_weights",
    )(ratio, q_all, fq, kvs[0], kvs[1], fks[0], fks[1])
    part = tok // sides
    (outs,) = call(
        lambda *refs: mix_level_kernel(ways, levels, *refs),
        [pair_weights, fq, *kvs, *fks[1:]],
        [(ways * sides, part, heads * dh)],
        "mix_level",
        [pltpu.VMEM((2, rows, 2 * dh), F32), pltpu.VMEM((2, heads * 2 * feat, 2 * dh), BF16)],
        32,
        16 * rows * dh * size,
    )
    groups = [
        [(z * ways + r) * sides + y for r in range(ways) for y in range(sides)]
        for z in range(levels)
    ]
    got = lax.all_to_all(
        outs, ("seq", "head"), split_axis=0, concat_axis=0, axis_index_groups=groups, tiled=True
    )
    (joined,) = pl.pallas_call(
        lambda *refs: join_kernel(ways, sides, *refs),
        in_specs=[whole_spec()],
        out_specs=[whole_spec(pltpu.HBM)],
        out_shape=[jax.ShapeDtypeStruct((part, sides * ways * heads * dh), BF16)],
        scratch_shapes=[pltpu.SemaphoreType.DMA((ways * sides,))],
        compiler_params=pltpu.CompilerParams(vmem_limit_bytes=4 * 2**20),
        name="join",
    )(got)
    return joined


def by_blocks(queries, keys, values, wq, wk, ratio):
    group = wq.shape[0] // (keys.shape[1] // DH)
    place = lax.axis_index("seq").astype(jnp.int32).reshape(1)
    kv = lax.all_gather(jnp.concatenate([keys, values], axis=1), "seq", tiled=True)
    out = mix(place, queries, kv, wq, wk, ratio, group)
    return lax.all_to_all(out, "head", split_axis=0, concat_axis=1, tiled=True)


def local(queries, keys, values, q_feature, k_feature, window_factor):
    tok = queries.shape[0]
    ways = keys.shape[1] // DH
    seq, sides = lax.axis_size("seq"), lax.axis_size("head")
    wq, wk = jnp.swapaxes(q_feature, 1, 2), jnp.swapaxes(k_feature, 1, 2)
    ratio = window_factor / (1.0 - window_factor)
    levels = seq // ways
    fits = ways in (2, 4) and sides in (1, 2) and seq == levels * ways and 2 <= levels <= 4
    if fits and ways * tok == 256 and tok == WINDOW:
        return by_levels(queries, keys, values, wq, wk, ratio)
    return by_blocks(queries, keys, values, wq, wk, ratio)


def solution(mesh):
    return jax.shard_map(
        local,
        mesh=mesh,
        in_specs=(
            P("seq", "head"),
            P("seq", "head"),
            P("seq", "head"),
            P("head", None, None),
            P("head", None, None),
            P("head"),
        ),
        out_specs=P(("seq", "head"), None),
        check_vma=False,
    )
```

```python
import math

import jax
import jax.numpy as jnp
from jax import lax
from jax.experimental import pallas as pl
from jax.experimental.pallas import tpu as pltpu
from jax.sharding import PartitionSpec as P

DH = 128
WINDOW = 64
F32 = jnp.float32
BF16 = jnp.bfloat16


def dot_t(a, b):
    return lax.dot_general(a, b, (((1,), (1,)), ((), ())), preferred_element_type=F32)


def features_t(logits):
    top = jnp.max(logits, axis=0, keepdims=True)
    low = jnp.min(logits, axis=0, keepdims=True)
    up = jnp.exp(logits - top)
    down = jnp.exp(low - logits)
    up = up * (1.0 / jnp.sum(up, axis=0, keepdims=True))
    down = down * (1.0 / jnp.sum(down, axis=0, keepdims=True))
    return jnp.concatenate([up.astype(BF16), down.astype(BF16)], axis=0)


def mix_kernel(
    place_ref, q_ref, k_ref, v_ref, wq_ref, wk_ref, ratio_ref, out_ref, fk_scr, state_scr
):
    tok = q_ref.shape[0]
    heads, feat, dh = wq_ref.shape
    seen = fk_scr.shape[1]
    place = place_ref[0]
    first_head = pl.program_id(0) * heads

    weights = wk_ref[...].reshape(heads * feat, dh)
    for start in range(0, seen, 256):
        size = min(256, seen - start)
        logits = dot_t(weights, k_ref[start : start + size, :])
        for h in range(heads):
            fk_scr[h * 2 * feat : (h + 1) * 2 * feat, start : start + size] = features_t(
                logits[h * feat : (h + 1) * feat]
            )
    row = lax.broadcasted_iota(jnp.int32, (seen, dh), 0)
    kept = row < (place - 1) * tok
    v_seen = jnp.where(kept, v_ref[:seen, :].astype(F32), 0.0).astype(BF16)
    ones_seen = jnp.where(kept, 1.0, 0.0).astype(BF16)
    v_seen = jnp.concatenate([v_seen, ones_seen], axis=1)
    state_scr[...] = jnp.dot(fk_scr[...], v_seen, preferred_element_type=F32).astype(BF16)

    before = pl.multiple_of(jnp.maximum(place - 1, 0) * tok, tok)
    own = pl.multiple_of(place * tok, tok)
    k_ext = jnp.concatenate([k_ref[pl.ds(before, tok), :], k_ref[pl.ds(own, tok), :]], axis=0)
    v_ext = jnp.concatenate([v_ref[pl.ds(before, tok), :], v_ref[pl.ds(own, tok), :]], axis=0)
    v_ext = jnp.concatenate([v_ext, jnp.ones_like(v_ext)], axis=1)
    row = lax.broadcasted_iota(jnp.int32, (tok, 2 * tok), 0)
    col = lax.broadcasted_iota(jnp.int32, (tok, 2 * tok), 1)
    valid = (col >= tok) | (place > 0)
    inside = (col > row) & (col <= row + WINDOW) & valid
    causal = (col <= row) & valid
    lane = lax.broadcasted_iota(jnp.int32, (tok, 2 * feat), 1)
    left = lane < feat
    side_r = lax.broadcasted_iota(jnp.int32, (2 * feat, 2 * feat), 0) < feat
    side_c = lax.broadcasted_iota(jnp.int32, (2 * feat, 2 * feat), 1) < feat
    halves = jnp.where(side_r == side_c, 1.0, 0.0).astype(BF16)

    for h in range(heads):
        q = q_ref[:, h * dh : (h + 1) * dh]
        wq = wq_ref[h]
        logits = dot_t(q, jnp.concatenate([wq, -wq], axis=0))
        top_l = jnp.max(jnp.where(left, logits, -jnp.inf), axis=1, keepdims=True)
        top_r = jnp.max(jnp.where(left, -jnp.inf, logits), axis=1, keepdims=True)
        expd = jnp.exp(logits - jnp.where(left, top_l, top_r)).astype(BF16)
        total = jnp.dot(expd, halves, preferred_element_type=F32)
        fq = (expd.astype(F32) / total).astype(BF16)
        fk = features_t(dot_t(wk_ref[h], k_ext))
        linear = jnp.dot(fq, fk, preferred_element_type=F32)
        scores = dot_t(q, k_ext) * (1.0 / math.sqrt(dh))
        masked = jnp.where(inside, scores, -jnp.inf)
        top = jnp.max(masked, axis=1, keepdims=True)
        soft = jnp.exp(masked - top) * ratio_ref[first_head + h]
        weight = jnp.where(causal, linear, soft).astype(BF16)
        both = jnp.dot(weight, v_ext, preferred_element_type=F32) + jnp.dot(
            fq, state_scr[h * 2 * feat : (h + 1) * 2 * feat, :], preferred_element_type=F32
        )
        out_ref[:, h * dh : (h + 1) * dh] = (both[:, :dh] / both[:, dh:]).astype(BF16)


def mix(place, queries, kv, wq, wk, ratio, group):
    tok = queries.shape[0]
    local_heads, feat, dh = wq.shape
    groups = local_heads // group
    tokens = kv.shape[0]
    seen = tokens - 2 * tok
    return pl.pallas_call(
        mix_kernel,
        grid_spec=pltpu.PrefetchScalarGridSpec(
            num_scalar_prefetch=1,
            grid=(groups,),
            in_specs=[
                pl.BlockSpec((tok, group * dh), lambda g, p: (0, g)),
                pl.BlockSpec((tokens, dh), lambda g, p: (0, g)),
                pl.BlockSpec((tokens, dh), lambda g, p: (0, groups + g)),
                pl.BlockSpec((group, feat, dh), lambda g, p: (g, 0, 0)),
                pl.BlockSpec((group, feat, dh), lambda g, p: (g, 0, 0)),
                pl.BlockSpec(memory_space=pltpu.SMEM),
            ],
            out_specs=pl.BlockSpec((tok, group * dh), lambda g, p: (0, g)),
            scratch_shapes=[
                pltpu.VMEM((group * 2 * feat, seen), BF16),
                pltpu.VMEM((group * 2 * feat, 2 * dh), BF16),
            ],
        ),
        out_shape=jax.ShapeDtypeStruct(queries.shape, BF16),
        compiler_params=pltpu.CompilerParams(vmem_limit_bytes=48 * 2**20),
        cost_estimate=pl.CostEstimate(
            flops=2 * local_heads * tokens * 3 * feat * 2 * dh,
            bytes_accessed=8 * 2**20,
            transcendentals=local_heads * tokens * 2 * feat,
        ),
    )(place, queries, kv, kv, wq, wk, ratio)


def spot(ways):
    at = lax.axis_index("seq")
    return lax.rem(at, ways), lax.div(at, ways)


def copy_all(pairs, sems):
    copies = [pltpu.make_async_copy(a, b, sems.at[n]) for n, (a, b) in enumerate(pairs)]
    for copy in copies:
        copy.start()
    for copy in copies:
        copy.wait()


def pack_kernel(q_ref, k_ref, v_ref, *out_refs):
    ways = len(out_refs) // 2
    width = q_ref.shape[1] // ways
    place = spot(ways)[0]
    for d in range(ways):
        group = place ^ d
        out_refs[d][...] = q_ref[:, pl.ds(pl.multiple_of(group * width, width), width)]
        at = pl.ds(pl.multiple_of(group * DH, DH), DH)
        out_refs[ways + d][:, :DH] = k_ref[:, at]
        out_refs[ways + d][:, DH:] = v_ref[:, at]


def stack_kernel(*refs):
    tok = refs[0].shape[0]
    place = spot(len(refs) - 1)[0]
    for d, ref in enumerate(refs[:-1]):
        refs[-1][pl.ds(pl.multiple_of((place ^ d) * tok, tok), tok), :] = ref[...]


def weights_kernel(ways, wq_ref, wk_ref, both_ref, own_wk_ref):
    heads = own_wk_ref.shape[0]
    first = spot(ways)[0] * heads
    for h in range(heads):
        wq = wq_ref[first + h].T
        both_ref[h] = jnp.concatenate([wq, -wq], axis=1)
        own_wk_ref[h] = wk_ref[first + h]


def join_kernel(ways, sides, got_ref, out_ref, sems):
    width = got_ref.shape[2]
    pairs = []
    for n in range(ways * sides):
        block = n % sides * ways + n // sides
        pairs.append((got_ref.at[n], out_ref.at[:, block * width : (block + 1) * width]))
    copy_all(pairs, sems)


def key_features_kernel(kv_ref, wk_ref, fk_ref):
    heads, feat, dh = wk_ref.shape
    logits = dot_t(wk_ref[...].reshape(heads * feat, dh), kv_ref[:, :dh])
    for h in range(heads):
        part = logits[h * feat : (h + 1) * feat]
        top = jnp.max(part, axis=0, keepdims=True)
        low = jnp.min(part, axis=0, keepdims=True)
        for n, shifted in enumerate((part - top, low - part)):
            row = (2 * h + n) * feat
            expd = jnp.exp(shifted.astype(BF16))
            total = expd[: feat // 4]
            for q in range(1, 4):
                total = total + expd[q * feat // 4 : (q + 1) * feat // 4]
            total = jnp.sum(total.astype(F32), axis=0, keepdims=True)
            fk_ref[row : row + feat, :] = expd * pl.reciprocal(total).astype(BF16)


def query_features_kernel(ways, *refs):
    q_refs, w_ref, q_out, fq_out, exp_scr = refs[:ways], *refs[ways:]
    tok = q_refs[0].shape[0]
    heads, dh, both = w_ref.shape
    half = ways * tok // 2
    blocks = half // tok
    place = spot(ways)[0]
    for d, ref in enumerate(q_refs):
        at = place ^ d
        u = at // blocks
        row = pl.multiple_of((at % blocks) * tok, tok)
        for h in range(heads):
            q_out[u, pl.ds(h * half + row, tok), :] = ref[:, h * dh : (h + 1) * dh]
    left = lax.broadcasted_iota(jnp.int32, (half, both), 1) < both // 2
    side_r = lax.broadcasted_iota(jnp.int32, (both, both), 0) < both // 2
    side_c = lax.broadcasted_iota(jnp.int32, (both, both), 1) < both // 2
    halves = jnp.where(side_r == side_c, 1.0, 0.0).astype(BF16)
    for u in range(2):
        for h in range(heads):
            rows = slice(h * half, (h + 1) * half)
            logits = jnp.dot(q_out[u, rows, :], w_ref[h], preferred_element_type=F32)
            top_l = jnp.max(jnp.where(left, logits, -jnp.inf), axis=1, keepdims=True)
            top_r = jnp.max(jnp.where(left, -jnp.inf, logits), axis=1, keepdims=True)
            exp_scr[rows, :] = jnp.exp((logits - jnp.where(left, top_l, top_r)).astype(BF16))
        total = jnp.dot(exp_scr[...], halves, preferred_element_type=F32)
        fq_out[u] = (exp_scr[...].astype(F32) * pl.reciprocal(total, approx=True)).astype(BF16)


def near_kernel(
    ways, factor_ref, q_ref, fq_ref, own_ref, last_ref, fk_own_ref, fk_last_ref, *outs
):
    near_ref, first_ref, second_ref, w_scr = outs
    half, rows = own_ref.shape[0] // 2, q_ref.shape[1]
    heads = rows // half
    dh = q_ref.shape[2]
    feats = fq_ref.shape[2]
    place, level = spot(ways)
    row = lax.broadcasted_iota(jnp.int32, (half, 2 * half), 0)
    col = lax.broadcasted_iota(jnp.int32, (half, 2 * half), 1)
    split = row + (half - WINDOW)
    for u in range(2):
        valid = (col >= half) | (level > 0) | (u > 0)
        inside = (col > split) & (col <= row + half) & valid
        causal = (col <= split) & valid
        if u == 0:
            pairs = jnp.concatenate([last_ref[half:, :], own_ref[:half, :]], axis=0)
        else:
            pairs = own_ref[...]
        keys, values = pairs[:, :dh], pairs[:, dh:]
        scores = dot_t(q_ref[u], keys) * (1.0 / math.sqrt(dh))
        for h in range(heads):
            here = slice(h * half, (h + 1) * half)
            f = slice(h * feats, (h + 1) * feats)
            if u == 0:
                fk = jnp.concatenate([fk_last_ref[f, half:], fk_own_ref[f, :half]], axis=1)
            else:
                fk = fk_own_ref[f, :]
            linear = jnp.dot(fq_ref[u, here, :], fk, preferred_element_type=F32)
            masked = jnp.where(inside, scores[here], -jnp.inf)
            top = jnp.max(masked, axis=1, keepdims=True)
            factor = jnp.full((1, 2 * half), factor_ref[place * heads + h])
            soft = jnp.exp(masked - top) * (factor / (1.0 - factor))
            w_scr[here, :] = jnp.where(causal, linear, soft).astype(BF16)
        near_ref[u] = jnp.dot(
            w_scr[...],
            jnp.concatenate([values, jnp.ones_like(values)], axis=1),
            preferred_element_type=F32,
        )
    here = jnp.where(level > 0, 1.0, 0.0).astype(BF16)
    for at, ref in ((0, first_ref), (half, second_ref)):
        v = last_ref[at : at + half, dh:]
        v = jnp.concatenate([v, jnp.full(v.shape, here)], axis=1)
        ref[...] = jnp.dot(fk_last_ref[:, at : at + half], v, preferred_element_type=F32)


def mix_level_kernel(ways, near_ref, fq_ref, first_ref, second_ref, *refs):
    kv_refs, fk_refs = refs[: len(refs) // 2 - 1], refs[len(refs) // 2 - 1 : -2]
    out_ref, state_scr = refs[-2:]
    dh = kv_refs[0].shape[1] // 2
    rows = near_ref.shape[1]
    feats = fq_ref.shape[2]
    heads = first_ref.shape[0] // feats
    half = rows // heads
    level = spot(ways)[1]
    part = out_ref.shape[1]

    state = first_ref[...]
    if kv_refs:
        v = []
        for s, ref in enumerate(kv_refs, 2):
            here = jnp.where(level >= s, 1.0, 0.0).astype(BF16)
            v.append(jnp.concatenate([ref[:, dh:], jnp.full((ref.shape[0], dh), here)], axis=1))
        fk = jnp.concatenate([ref[...] for ref in fk_refs], axis=1)
        state = state + jnp.dot(fk, jnp.concatenate(v, axis=0), preferred_element_type=F32)
    state_scr[0] = state.astype(BF16)
    state_scr[1] = (state + second_ref[...]).astype(BF16)
    for h in range(heads):
        for u in range(2):
            here = slice(h * half, (h + 1) * half)
            far = jnp.dot(
                fq_ref[u, here, :],
                state_scr[u, h * feats : (h + 1) * feats, :],
                preferred_element_type=F32,
            )
            both = near_ref[u, here, :] + far
            out = (both[:, :dh] * pl.reciprocal(both[:, dh:], approx=True)).astype(BF16)
            for n in range(half // part):
                out_ref[u * (half // part) + n, :, h * dh : (h + 1) * dh] = out[
                    n * part : (n + 1) * part
                ]


def whole_spec(space=pltpu.VMEM):
    return pl.BlockSpec(memory_space=space)


def call(kernel, ins, outs, name, scratch=(), limit=8, flops=0, space=pltpu.VMEM):
    return pl.pallas_call(
        kernel,
        in_specs=[whole_spec(space) for _ in ins],
        out_specs=[whole_spec(space) for _ in outs],
        out_shape=[jax.ShapeDtypeStruct(s, BF16) for s in outs],
        scratch_shapes=list(scratch),
        compiler_params=pltpu.CompilerParams(vmem_limit_bytes=limit * 2**20),
        name=name,
    )(*ins)


def by_levels(queries, keys, values, wq, wk, factor):
    tok, width = queries.shape
    local_heads, feat, dh = wq.shape
    ways = keys.shape[1] // dh
    heads = local_heads // ways
    seq, sides = lax.axis_size("seq"), lax.axis_size("head")
    levels = seq // ways
    size = ways * tok
    half = size // 2
    rows = heads * half
    def partner(x, d):
        return lax.ppermute(x, "seq", [(i, i // ways * ways + (i % ways ^ d)) for i in range(seq)])

    parts = call(
        pack_kernel,
        [queries, keys, values],
        [(tok, width // ways)] * ways + [(tok, 2 * dh)] * ways,
        "pack",
        limit=4,
    )
    q_parts, kv_parts = list(parts[:ways]), list(parts[ways:])
    for d in reversed(range(1, ways)):
        q_parts[d] = partner(q_parts[d], d)
    *kv_parts, q_parts[1] = lax.optimization_barrier((*kv_parts, q_parts[1]))
    for d in reversed(range(1, ways)):
        kv_parts[d] = partner(kv_parts[d], d)
    (kv,) = call(stack_kernel, kv_parts, [(size, 2 * dh)], "stack_kv", limit=4)
    kvs = [kv] + [
        lax.ppermute(kv, "seq", [(i, i + s * ways) for i in range(seq - s * ways)])
        for s in range(1, levels)
    ]
    wq, wk, kv = lax.optimization_barrier((wq, wk, kv))
    both_wq, own_wk = call(
        lambda *refs: weights_kernel(ways, *refs),
        [wq, wk],
        [(heads, dh, 2 * feat), (heads, feat, dh)],
        "weights",
    )

    def key_features(x):
        return pl.pallas_call(
            key_features_kernel,
            in_specs=[whole_spec()] * 2,
            out_specs=whole_spec(),
            out_shape=jax.ShapeDtypeStruct((heads * 2 * feat, size), BF16),
            compiler_params=pltpu.CompilerParams(vmem_limit_bytes=16 * 2**20),
            name="key_features",
        )(x, own_wk)

    fks = [key_features(x) for x in kvs[:2]]
    q_all, fq = call(
        lambda *refs: query_features_kernel(ways, *refs),
        [*q_parts, both_wq],
        [(2, rows, dh), (2, rows, 2 * feat)],
        "query_features",
        [pltpu.VMEM((rows, 2 * feat), BF16)],
        16,
        4 * rows * dh * 2 * feat,
    )
    near, first, second = pl.pallas_call(
        lambda *refs: near_kernel(ways, *refs),
        in_specs=[whole_spec(pltpu.SMEM)] + [whole_spec() for _ in range(6)],
        out_specs=[whole_spec()] * 3,
        out_shape=[
            jax.ShapeDtypeStruct((2, rows, 2 * dh), F32),
            jax.ShapeDtypeStruct((heads * 2 * feat, 2 * dh), F32),
            jax.ShapeDtypeStruct((heads * 2 * feat, 2 * dh), F32),
        ],
        scratch_shapes=[pltpu.VMEM((rows, size), BF16)],
        compiler_params=pltpu.CompilerParams(vmem_limit_bytes=20 * 2**20),
        name="near",
    )(factor, q_all, fq, kvs[0], kvs[1], fks[0], fks[1])
    part = tok // sides
    *kvs[2:], near = lax.optimization_barrier((*kvs[2:], near))
    fks += [key_features(x) for x in kvs[2:]]
    (outs,) = call(
        lambda *refs: mix_level_kernel(ways, *refs),
        [near, fq, first, second, *kvs[2:], *fks[2:]],
        [(ways * sides, part, heads * dh)],
        "mix_level",
        [pltpu.VMEM((2, heads * 2 * feat, 2 * dh), BF16)],
        20,
    )
    groups = [
        [(z * ways + r) * sides + y for r in range(ways) for y in range(sides)]
        for z in range(levels)
    ]
    got = lax.all_to_all(
        outs, ("seq", "head"), split_axis=0, concat_axis=0, axis_index_groups=groups, tiled=True
    )
    (joined,) = pl.pallas_call(
        lambda *refs: join_kernel(ways, sides, *refs),
        in_specs=[whole_spec()],
        out_specs=[whole_spec(pltpu.HBM)],
        out_shape=[jax.ShapeDtypeStruct((part, sides * ways * heads * dh), BF16)],
        scratch_shapes=[pltpu.SemaphoreType.DMA((ways * sides,))],
        compiler_params=pltpu.CompilerParams(vmem_limit_bytes=4 * 2**20),
        name="join",
    )(got)
    return joined


def by_blocks(queries, keys, values, wq, wk, ratio):
    group = wq.shape[0] // (keys.shape[1] // DH)
    place = lax.axis_index("seq").astype(jnp.int32).reshape(1)
    kv = lax.all_gather(jnp.concatenate([keys, values], axis=1), "seq", tiled=True)
    out = mix(place, queries, kv, wq, wk, ratio, group)
    return lax.all_to_all(out, "head", split_axis=0, concat_axis=1, tiled=True)


def local(queries, keys, values, q_feature, k_feature, window_factor):
    tok = queries.shape[0]
    ways = keys.shape[1] // DH
    seq, sides = lax.axis_size("seq"), lax.axis_size("head")
    wq, wk = jnp.swapaxes(q_feature, 1, 2), jnp.swapaxes(k_feature, 1, 2)
    levels = seq // ways
    fits = ways in (2, 4) and sides in (1, 2) and seq == levels * ways and 2 <= levels <= 4
    if fits and ways * tok == 256 and tok == WINDOW:
        return by_levels(queries, keys, values, wq, wk, window_factor)
    ratio = window_factor / (1.0 - window_factor)
    return by_blocks(queries, keys, values, wq, wk, ratio)


def solution(mesh):
    return jax.shard_map(
        local,
        mesh=mesh,
        in_specs=(
            P("seq", "head"),
            P("seq", "head"),
            P("seq", "head"),
            P("head", None, None),
            P("head", None, None),
            P("head"),
        ),
        out_specs=P(("seq", "head"), None),
        check_vma=False,
    )
```

```python
import math

import jax
import jax.numpy as jnp
from jax import lax
from jax.experimental import pallas as pl
from jax.experimental.pallas import tpu as pltpu
from jax.sharding import PartitionSpec as P

DH = 128
WINDOW = 64
F32 = jnp.float32
BF16 = jnp.bfloat16


def dot_t(a, b):
    return lax.dot_general(a, b, (((1,), (1,)), ((), ())), preferred_element_type=F32)


def features_t(logits):
    top = jnp.max(logits, axis=0, keepdims=True)
    low = jnp.min(logits, axis=0, keepdims=True)
    up = jnp.exp(logits - top)
    down = jnp.exp(low - logits)
    up = up * (1.0 / jnp.sum(up, axis=0, keepdims=True))
    down = down * (1.0 / jnp.sum(down, axis=0, keepdims=True))
    return jnp.concatenate([up.astype(BF16), down.astype(BF16)], axis=0)


def mix_kernel(
    place_ref, q_ref, k_ref, v_ref, wq_ref, wk_ref, ratio_ref, out_ref, fk_scr, state_scr
):
    tok = q_ref.shape[0]
    heads, feat, dh = wq_ref.shape
    seen = fk_scr.shape[1]
    place = place_ref[0]
    first_head = pl.program_id(0) * heads

    weights = wk_ref[...].reshape(heads * feat, dh)
    for start in range(0, seen, 256):
        size = min(256, seen - start)
        logits = dot_t(weights, k_ref[start : start + size, :])
        for h in range(heads):
            fk_scr[h * 2 * feat : (h + 1) * 2 * feat, start : start + size] = features_t(
                logits[h * feat : (h + 1) * feat]
            )
    row = lax.broadcasted_iota(jnp.int32, (seen, dh), 0)
    kept = row < (place - 1) * tok
    v_seen = jnp.where(kept, v_ref[:seen, :].astype(F32), 0.0).astype(BF16)
    ones_seen = jnp.where(kept, 1.0, 0.0).astype(BF16)
    v_seen = jnp.concatenate([v_seen, ones_seen], axis=1)
    state_scr[...] = jnp.dot(fk_scr[...], v_seen, preferred_element_type=F32).astype(BF16)

    before = pl.multiple_of(jnp.maximum(place - 1, 0) * tok, tok)
    own = pl.multiple_of(place * tok, tok)
    k_ext = jnp.concatenate([k_ref[pl.ds(before, tok), :], k_ref[pl.ds(own, tok), :]], axis=0)
    v_ext = jnp.concatenate([v_ref[pl.ds(before, tok), :], v_ref[pl.ds(own, tok), :]], axis=0)
    v_ext = jnp.concatenate([v_ext, jnp.ones_like(v_ext)], axis=1)
    row = lax.broadcasted_iota(jnp.int32, (tok, 2 * tok), 0)
    col = lax.broadcasted_iota(jnp.int32, (tok, 2 * tok), 1)
    valid = (col >= tok) | (place > 0)
    inside = (col > row) & (col <= row + WINDOW) & valid
    causal = (col <= row) & valid
    lane = lax.broadcasted_iota(jnp.int32, (tok, 2 * feat), 1)
    left = lane < feat
    side_r = lax.broadcasted_iota(jnp.int32, (2 * feat, 2 * feat), 0) < feat
    side_c = lax.broadcasted_iota(jnp.int32, (2 * feat, 2 * feat), 1) < feat
    halves = jnp.where(side_r == side_c, 1.0, 0.0).astype(BF16)

    for h in range(heads):
        q = q_ref[:, h * dh : (h + 1) * dh]
        wq = wq_ref[h]
        logits = dot_t(q, jnp.concatenate([wq, -wq], axis=0))
        top_l = jnp.max(jnp.where(left, logits, -jnp.inf), axis=1, keepdims=True)
        top_r = jnp.max(jnp.where(left, -jnp.inf, logits), axis=1, keepdims=True)
        expd = jnp.exp(logits - jnp.where(left, top_l, top_r)).astype(BF16)
        total = jnp.dot(expd, halves, preferred_element_type=F32)
        fq = (expd.astype(F32) / total).astype(BF16)
        fk = features_t(dot_t(wk_ref[h], k_ext))
        linear = jnp.dot(fq, fk, preferred_element_type=F32)
        scores = dot_t(q, k_ext) * (1.0 / math.sqrt(dh))
        masked = jnp.where(inside, scores, -jnp.inf)
        top = jnp.max(masked, axis=1, keepdims=True)
        soft = jnp.exp(masked - top) * ratio_ref[first_head + h]
        weight = jnp.where(causal, linear, soft).astype(BF16)
        both = jnp.dot(weight, v_ext, preferred_element_type=F32) + jnp.dot(
            fq, state_scr[h * 2 * feat : (h + 1) * 2 * feat, :], preferred_element_type=F32
        )
        out_ref[:, h * dh : (h + 1) * dh] = (both[:, :dh] / both[:, dh:]).astype(BF16)


def mix(place, queries, kv, wq, wk, ratio, group):
    tok = queries.shape[0]
    local_heads, feat, dh = wq.shape
    groups = local_heads // group
    tokens = kv.shape[0]
    seen = tokens - 2 * tok
    return pl.pallas_call(
        mix_kernel,
        grid_spec=pltpu.PrefetchScalarGridSpec(
            num_scalar_prefetch=1,
            grid=(groups,),
            in_specs=[
                pl.BlockSpec((tok, group * dh), lambda g, p: (0, g)),
                pl.BlockSpec((tokens, dh), lambda g, p: (0, g)),
                pl.BlockSpec((tokens, dh), lambda g, p: (0, groups + g)),
                pl.BlockSpec((group, feat, dh), lambda g, p: (g, 0, 0)),
                pl.BlockSpec((group, feat, dh), lambda g, p: (g, 0, 0)),
                pl.BlockSpec(memory_space=pltpu.SMEM),
            ],
            out_specs=pl.BlockSpec((tok, group * dh), lambda g, p: (0, g)),
            scratch_shapes=[
                pltpu.VMEM((group * 2 * feat, seen), BF16),
                pltpu.VMEM((group * 2 * feat, 2 * dh), BF16),
            ],
        ),
        out_shape=jax.ShapeDtypeStruct(queries.shape, BF16),
        compiler_params=pltpu.CompilerParams(vmem_limit_bytes=48 * 2**20),
        cost_estimate=pl.CostEstimate(
            flops=2 * local_heads * tokens * 3 * feat * 2 * dh,
            bytes_accessed=8 * 2**20,
            transcendentals=local_heads * tokens * 2 * feat,
        ),
    )(place, queries, kv, kv, wq, wk, ratio)


def spot(ways):
    at = lax.axis_index("seq")
    return lax.rem(at, ways), lax.div(at, ways)


def copy_all(pairs, sems):
    copies = [pltpu.make_async_copy(a, b, sems.at[n]) for n, (a, b) in enumerate(pairs)]
    for copy in copies:
        copy.start()
    for copy in copies:
        copy.wait()


def pack_q_kernel(q_ref, *out_refs):
    width = out_refs[0].shape[1]
    place = spot(len(out_refs))[0]
    for d, out in enumerate(out_refs):
        out[...] = q_ref[:, pl.ds(pl.multiple_of((place ^ d) * width, width), width)]


def pack_kv_kernel(k_ref, v_ref, *out_refs):
    place = spot(len(out_refs))[0]
    for d, out in enumerate(out_refs):
        at = pl.ds(pl.multiple_of((place ^ d) * DH, DH), DH)
        out[:, :DH] = k_ref[:, at]
        out[:, DH:] = v_ref[:, at]


def stack_kernel(*refs):
    tok = refs[0].shape[0]
    place = spot(len(refs) - 1)[0]
    for d, ref in enumerate(refs[:-1]):
        refs[-1][pl.ds(pl.multiple_of((place ^ d) * tok, tok), tok), :] = ref[...]


def weights_kernel(ways, wq_ref, wk_ref, both_ref, own_wk_ref):
    heads = own_wk_ref.shape[0]
    first = spot(ways)[0] * heads
    for h in range(heads):
        wq = wq_ref[first + h].T
        both_ref[h] = jnp.concatenate([wq, -wq], axis=1)
        own_wk_ref[h] = wk_ref[first + h]


def join_kernel(ways, sides, *refs):
    got, out_ref, sems = refs[:-2], *refs[-2:]
    width = got[0].shape[1]
    place, side = spot(ways)[0], lax.axis_index("head")
    pairs = []
    for n, ref in enumerate(got):
        dr, dy = divmod(n, sides)
        block = (side ^ dy) * ways + (place ^ dr)
        at = pl.ds(pl.multiple_of(block * width, width), width)
        pairs.append((ref, out_ref.at[:, at]))
    copy_all(pairs, sems)


def key_features_kernel(kv_ref, wk_ref, fk_ref):
    heads, feat, dh = wk_ref.shape
    logits = dot_t(wk_ref[...].reshape(heads * feat, dh), kv_ref[:, :dh])
    for h in range(heads):
        part = logits[h * feat : (h + 1) * feat]
        top = jnp.max(part, axis=0, keepdims=True)
        low = jnp.min(part, axis=0, keepdims=True)
        for n, shifted in enumerate((part - top, low - part)):
            row = (2 * h + n) * feat
            expd = jnp.exp(shifted.astype(BF16))
            total = expd[: feat // 4]
            for q in range(1, 4):
                total = total + expd[q * feat // 4 : (q + 1) * feat // 4]
            total = jnp.sum(total.astype(F32), axis=0, keepdims=True)
            fk_ref[row : row + feat, :] = expd * pl.reciprocal(total).astype(BF16)


def query_features_kernel(ways, *refs):
    q_refs, w_ref, q_out, fq_out, exp_scr = refs[:ways], *refs[ways:]
    tok = q_refs[0].shape[0]
    heads, dh, both = w_ref.shape
    half = ways * tok // 2
    blocks = half // tok
    place = spot(ways)[0]
    for d, ref in enumerate(q_refs):
        at = place ^ d
        u = at // blocks
        row = pl.multiple_of((at % blocks) * tok, tok)
        for h in range(heads):
            q_out[u, pl.ds(h * half + row, tok), :] = ref[:, h * dh : (h + 1) * dh]
    left = lax.broadcasted_iota(jnp.int32, (half, both), 1) < both // 2
    side_r = lax.broadcasted_iota(jnp.int32, (both, both), 0) < both // 2
    side_c = lax.broadcasted_iota(jnp.int32, (both, both), 1) < both // 2
    halves = jnp.where(side_r == side_c, 1.0, 0.0).astype(BF16)
    for u in range(2):
        for h in range(heads):
            rows = slice(h * half, (h + 1) * half)
            logits = jnp.dot(q_out[u, rows, :], w_ref[h], preferred_element_type=F32)
            top_l = jnp.max(jnp.where(left, logits, -jnp.inf), axis=1, keepdims=True)
            top_r = jnp.max(jnp.where(left, -jnp.inf, logits), axis=1, keepdims=True)
            exp_scr[rows, :] = jnp.exp((logits - jnp.where(left, top_l, top_r)).astype(BF16))
        total = jnp.dot(exp_scr[...], halves, preferred_element_type=F32)
        fq_out[u] = (exp_scr[...].astype(F32) * pl.reciprocal(total, approx=True)).astype(BF16)


def near_kernel(
    ways, factor_ref, q_ref, fq_ref, own_ref, last_ref, fk_own_ref, fk_last_ref, *outs
):
    near_ref, first_ref, second_ref, w_scr = outs
    half, rows = own_ref.shape[0] // 2, q_ref.shape[1]
    heads = rows // half
    dh = q_ref.shape[2]
    feats = fq_ref.shape[2]
    place, level = spot(ways)
    row = lax.broadcasted_iota(jnp.int32, (half, 2 * half), 0)
    col = lax.broadcasted_iota(jnp.int32, (half, 2 * half), 1)
    split = row + (half - WINDOW)
    for u in range(2):
        valid = (col >= half) | (level > 0) | (u > 0)
        inside = (col > split) & (col <= row + half) & valid
        causal = (col <= split) & valid
        if u == 0:
            pairs = jnp.concatenate([last_ref[half:, :], own_ref[:half, :]], axis=0)
        else:
            pairs = own_ref[...]
        keys, values = pairs[:, :dh], pairs[:, dh:]
        scores = dot_t(q_ref[u], keys) * (1.0 / math.sqrt(dh))
        for h in range(heads):
            here = slice(h * half, (h + 1) * half)
            f = slice(h * feats, (h + 1) * feats)
            if u == 0:
                fk = jnp.concatenate([fk_last_ref[f, half:], fk_own_ref[f, :half]], axis=1)
            else:
                fk = fk_own_ref[f, :]
            linear = jnp.dot(fq_ref[u, here, :], fk, preferred_element_type=F32)
            masked = jnp.where(inside, scores[here], -jnp.inf)
            top = jnp.max(masked, axis=1, keepdims=True)
            factor = jnp.full((1, 2 * half), factor_ref[place * heads + h])
            soft = jnp.exp(masked - top) * (factor / (1.0 - factor))
            w_scr[here, :] = jnp.where(causal, linear, soft).astype(BF16)
        near_ref[u] = jnp.dot(
            w_scr[...],
            jnp.concatenate([values, jnp.ones_like(values)], axis=1),
            preferred_element_type=F32,
        )
    here = jnp.where(level > 0, 1.0, 0.0).astype(BF16)
    for at, ref in ((0, first_ref), (half, second_ref)):
        v = last_ref[at : at + half, dh:]
        v = jnp.concatenate([v, jnp.full(v.shape, here)], axis=1)
        ref[...] = jnp.dot(fk_last_ref[:, at : at + half], v, preferred_element_type=F32)


def mix_level_kernel(ways, sides, far, near_ref, fq_ref, first_ref, second_ref, *refs):
    kv_refs, fk_refs = refs[:far], refs[far : 2 * far]
    out_refs, state_scr, out_scr = refs[-2 - ways * sides : -2], *refs[-2:]
    rows, dh = near_ref.shape[1], near_ref.shape[2] // 2
    feats = fq_ref.shape[2]
    heads = first_ref.shape[0] // feats
    half = rows // heads
    place, level = spot(ways)
    side = lax.axis_index("head")

    state = first_ref[...]
    if kv_refs:
        v = []
        for s, ref in enumerate(kv_refs, 2):
            here = jnp.where(level >= s, 1.0, 0.0).astype(BF16)
            v.append(jnp.concatenate([ref[:, dh:], jnp.full((ref.shape[0], dh), here)], axis=1))
        fk = jnp.concatenate([ref[...] for ref in fk_refs], axis=1)
        state = state + jnp.dot(fk, jnp.concatenate(v, axis=0), preferred_element_type=F32)
    state_scr[0] = state.astype(BF16)
    state_scr[1] = (state + second_ref[...]).astype(BF16)
    for h in range(heads):
        for u in range(2):
            here = slice(h * half, (h + 1) * half)
            far = jnp.dot(
                fq_ref[u, here, :],
                state_scr[u, h * feats : (h + 1) * feats, :],
                preferred_element_type=F32,
            )
            both = near_ref[u, here, :] + far
            out_scr[u * half : (u + 1) * half, h * dh : (h + 1) * dh] = (
                both[:, :dh] * pl.reciprocal(both[:, dh:], approx=True)
            ).astype(BF16)
    part = out_refs[0].shape[0]
    for n, ref in enumerate(out_refs):
        dr, dy = divmod(n, sides)
        at = ((place ^ dr) * sides + (side ^ dy)) * part
        ref[...] = out_scr[pl.ds(pl.multiple_of(at, part), part), :]


def whole_spec(space=pltpu.VMEM):
    return pl.BlockSpec(memory_space=space)


def call(kernel, ins, outs, name, scratch=(), limit=8, flops=0, space=pltpu.VMEM):
    return pl.pallas_call(
        kernel,
        in_specs=[whole_spec(space) for _ in ins],
        out_specs=[whole_spec(space) for _ in outs],
        out_shape=[jax.ShapeDtypeStruct(s, BF16) for s in outs],
        scratch_shapes=list(scratch),
        compiler_params=pltpu.CompilerParams(vmem_limit_bytes=limit * 2**20),
        name=name,
    )(*ins)


def by_levels(queries, keys, values, wq, wk, factor):
    tok, width = queries.shape
    local_heads, feat, dh = wq.shape
    ways = keys.shape[1] // dh
    heads = local_heads // ways
    seq, sides = lax.axis_size("seq"), lax.axis_size("head")
    levels = seq // ways
    size = ways * tok
    half = size // 2
    rows = heads * half
    def partner(x, d):
        return lax.ppermute(x, "seq", [(i, i // ways * ways + (i % ways ^ d)) for i in range(seq)])

    def partner_of_both(x, dr, dy):
        pairs = [
            (i * sides + j, (i // ways * ways + (i % ways ^ dr)) * sides + (j ^ dy))
            for i in range(seq)
            for j in range(sides)
        ]
        return lax.ppermute(x, ("seq", "head"), pairs)

    kv_parts = call(pack_kv_kernel, [keys, values], [(tok, 2 * dh)] * ways, "pack_kv", limit=4)
    kv_parts = list(kv_parts)
    for d in reversed(range(1, ways)):
        kv_parts[d] = partner(kv_parts[d], d)
    queries, kv_parts[1] = lax.optimization_barrier((queries, kv_parts[1]))
    q_parts = call(pack_q_kernel, [queries], [(tok, width // ways)] * ways, "pack_q", limit=4)
    q_parts = list(q_parts)
    for d in reversed(range(1, ways)):
        q_parts[d] = partner(q_parts[d], d)
    (kv,) = call(stack_kernel, kv_parts, [(size, 2 * dh)], "stack_kv", limit=4)
    kv, q_parts[1] = lax.optimization_barrier((kv, q_parts[1]))
    kvs = [kv] + [
        lax.ppermute(kv, "seq", [(i, i + s * ways) for i in range(seq - s * ways)])
        for s in range(1, levels)
    ]
    wq, wk, kv = lax.optimization_barrier((wq, wk, kv))
    both_wq, own_wk = call(
        lambda *refs: weights_kernel(ways, *refs),
        [wq, wk],
        [(heads, dh, 2 * feat), (heads, feat, dh)],
        "weights",
    )

    def key_features(x):
        return pl.pallas_call(
            key_features_kernel,
            in_specs=[whole_spec()] * 2,
            out_specs=whole_spec(),
            out_shape=jax.ShapeDtypeStruct((heads * 2 * feat, size), BF16),
            compiler_params=pltpu.CompilerParams(vmem_limit_bytes=16 * 2**20),
            name="key_features",
        )(x, own_wk)

    fks = [key_features(x) for x in kvs[:2]]
    q_all, fq = call(
        lambda *refs: query_features_kernel(ways, *refs),
        [*q_parts, both_wq],
        [(2, rows, dh), (2, rows, 2 * feat)],
        "query_features",
        [pltpu.VMEM((rows, 2 * feat), BF16)],
        16,
        4 * rows * dh * 2 * feat,
    )
    near, first, second = pl.pallas_call(
        lambda *refs: near_kernel(ways, *refs),
        in_specs=[whole_spec(pltpu.SMEM)] + [whole_spec() for _ in range(6)],
        out_specs=[whole_spec()] * 3,
        out_shape=[
            jax.ShapeDtypeStruct((2, rows, 2 * dh), F32),
            jax.ShapeDtypeStruct((heads * 2 * feat, 2 * dh), F32),
            jax.ShapeDtypeStruct((heads * 2 * feat, 2 * dh), F32),
        ],
        scratch_shapes=[pltpu.VMEM((rows, size), BF16)],
        compiler_params=pltpu.CompilerParams(vmem_limit_bytes=20 * 2**20),
        name="near",
    )(factor, q_all, fq, kvs[0], kvs[1], fks[0], fks[1])
    part = tok // sides
    *kvs[2:], near = lax.optimization_barrier((*kvs[2:], near))
    fks += [key_features(x) for x in kvs[2:]]
    outs = call(
        lambda *refs: mix_level_kernel(ways, sides, levels - 2, *refs),
        [near, fq, first, second, *kvs[2:], *fks[2:]],
        [(part, heads * dh)] * (ways * sides),
        "mix_level",
        [
            pltpu.VMEM((2, heads * 2 * feat, 2 * dh), BF16),
            pltpu.VMEM((size, heads * dh), BF16),
        ],
        20,
    )
    def turn(n):
        dr, dy = divmod(n, sides)
        return (0, dr, 0) if dr > 1 and dy else (1, dr % 2, dy) if dr > 1 or dy else (2, 0, 0)

    order = sorted(range(1, ways * sides), key=turn)
    got = list(outs)
    for n in order:
        got[n] = partner_of_both(outs[n], *divmod(n, sides))
    (joined,) = pl.pallas_call(
        lambda *refs: join_kernel(ways, sides, *refs),
        in_specs=[whole_spec()] * (ways * sides),
        out_specs=[whole_spec(pltpu.HBM)],
        out_shape=[jax.ShapeDtypeStruct((part, sides * ways * heads * dh), BF16)],
        scratch_shapes=[pltpu.SemaphoreType.DMA((ways * sides,))],
        compiler_params=pltpu.CompilerParams(vmem_limit_bytes=4 * 2**20),
        name="join",
    )(*got)
    return joined


def by_blocks(queries, keys, values, wq, wk, ratio):
    group = wq.shape[0] // (keys.shape[1] // DH)
    place = lax.axis_index("seq").astype(jnp.int32).reshape(1)
    kv = lax.all_gather(jnp.concatenate([keys, values], axis=1), "seq", tiled=True)
    out = mix(place, queries, kv, wq, wk, ratio, group)
    return lax.all_to_all(out, "head", split_axis=0, concat_axis=1, tiled=True)


def local(queries, keys, values, q_feature, k_feature, window_factor):
    tok = queries.shape[0]
    ways = keys.shape[1] // DH
    seq, sides = lax.axis_size("seq"), lax.axis_size("head")
    wq, wk = jnp.swapaxes(q_feature, 1, 2), jnp.swapaxes(k_feature, 1, 2)
    levels = seq // ways
    fits = ways in (2, 4) and sides in (1, 2) and seq == levels * ways and 2 <= levels <= 4
    if fits and ways * tok == 256 and tok == WINDOW:
        return by_levels(queries, keys, values, wq, wk, window_factor)
    ratio = window_factor / (1.0 - window_factor)
    return by_blocks(queries, keys, values, wq, wk, ratio)


def solution(mesh):
    return jax.shard_map(
        local,
        mesh=mesh,
        in_specs=(
            P("seq", "head"),
            P("seq", "head"),
            P("seq", "head"),
            P("head", None, None),
            P("head", None, None),
            P("head"),
        ),
        out_specs=P(("seq", "head"), None),
        check_vma=False,
    )
```

```python
import math

import jax
import jax.numpy as jnp
from jax import lax
from jax.experimental import pallas as pl
from jax.experimental.pallas import tpu as pltpu
from jax.sharding import PartitionSpec as P

DH = 128
WINDOW = 64
F32 = jnp.float32
BF16 = jnp.bfloat16


def dot_t(a, b):
    return lax.dot_general(a, b, (((1,), (1,)), ((), ())), preferred_element_type=F32)


def features_t(logits):
    top = jnp.max(logits, axis=0, keepdims=True)
    low = jnp.min(logits, axis=0, keepdims=True)
    up = jnp.exp(logits - top)
    down = jnp.exp(low - logits)
    up = up * (1.0 / jnp.sum(up, axis=0, keepdims=True))
    down = down * (1.0 / jnp.sum(down, axis=0, keepdims=True))
    return jnp.concatenate([up.astype(BF16), down.astype(BF16)], axis=0)


def mix_kernel(
    place_ref, q_ref, k_ref, v_ref, wq_ref, wk_ref, ratio_ref, out_ref, fk_scr, state_scr
):
    tok = q_ref.shape[0]
    heads, feat, dh = wq_ref.shape
    seen = fk_scr.shape[1]
    place = place_ref[0]
    first_head = pl.program_id(0) * heads

    weights = wk_ref[...].reshape(heads * feat, dh)
    for start in range(0, seen, 256):
        size = min(256, seen - start)
        logits = dot_t(weights, k_ref[start : start + size, :])
        for h in range(heads):
            fk_scr[h * 2 * feat : (h + 1) * 2 * feat, start : start + size] = features_t(
                logits[h * feat : (h + 1) * feat]
            )
    row = lax.broadcasted_iota(jnp.int32, (seen, dh), 0)
    kept = row < (place - 1) * tok
    v_seen = jnp.where(kept, v_ref[:seen, :].astype(F32), 0.0).astype(BF16)
    ones_seen = jnp.where(kept, 1.0, 0.0).astype(BF16)
    v_seen = jnp.concatenate([v_seen, ones_seen], axis=1)
    state_scr[...] = jnp.dot(fk_scr[...], v_seen, preferred_element_type=F32).astype(BF16)

    before = pl.multiple_of(jnp.maximum(place - 1, 0) * tok, tok)
    own = pl.multiple_of(place * tok, tok)
    k_ext = jnp.concatenate([k_ref[pl.ds(before, tok), :], k_ref[pl.ds(own, tok), :]], axis=0)
    v_ext = jnp.concatenate([v_ref[pl.ds(before, tok), :], v_ref[pl.ds(own, tok), :]], axis=0)
    v_ext = jnp.concatenate([v_ext, jnp.ones_like(v_ext)], axis=1)
    row = lax.broadcasted_iota(jnp.int32, (tok, 2 * tok), 0)
    col = lax.broadcasted_iota(jnp.int32, (tok, 2 * tok), 1)
    valid = (col >= tok) | (place > 0)
    inside = (col > row) & (col <= row + WINDOW) & valid
    causal = (col <= row) & valid
    lane = lax.broadcasted_iota(jnp.int32, (tok, 2 * feat), 1)
    left = lane < feat
    side_r = lax.broadcasted_iota(jnp.int32, (2 * feat, 2 * feat), 0) < feat
    side_c = lax.broadcasted_iota(jnp.int32, (2 * feat, 2 * feat), 1) < feat
    halves = jnp.where(side_r == side_c, 1.0, 0.0).astype(BF16)

    for h in range(heads):
        q = q_ref[:, h * dh : (h + 1) * dh]
        wq = wq_ref[h]
        logits = dot_t(q, jnp.concatenate([wq, -wq], axis=0))
        top_l = jnp.max(jnp.where(left, logits, -jnp.inf), axis=1, keepdims=True)
        top_r = jnp.max(jnp.where(left, -jnp.inf, logits), axis=1, keepdims=True)
        expd = jnp.exp(logits - jnp.where(left, top_l, top_r)).astype(BF16)
        total = jnp.dot(expd, halves, preferred_element_type=F32)
        fq = (expd.astype(F32) / total).astype(BF16)
        fk = features_t(dot_t(wk_ref[h], k_ext))
        linear = jnp.dot(fq, fk, preferred_element_type=F32)
        scores = dot_t(q, k_ext) * (1.0 / math.sqrt(dh))
        masked = jnp.where(inside, scores, -jnp.inf)
        top = jnp.max(masked, axis=1, keepdims=True)
        soft = jnp.exp(masked - top) * ratio_ref[first_head + h]
        weight = jnp.where(causal, linear, soft).astype(BF16)
        both = jnp.dot(weight, v_ext, preferred_element_type=F32) + jnp.dot(
            fq, state_scr[h * 2 * feat : (h + 1) * 2 * feat, :], preferred_element_type=F32
        )
        out_ref[:, h * dh : (h + 1) * dh] = (both[:, :dh] / both[:, dh:]).astype(BF16)


def mix(place, queries, kv, wq, wk, ratio, group):
    tok = queries.shape[0]
    local_heads, feat, dh = wq.shape
    groups = local_heads // group
    tokens = kv.shape[0]
    seen = tokens - 2 * tok
    return pl.pallas_call(
        mix_kernel,
        grid_spec=pltpu.PrefetchScalarGridSpec(
            num_scalar_prefetch=1,
            grid=(groups,),
            in_specs=[
                pl.BlockSpec((tok, group * dh), lambda g, p: (0, g)),
                pl.BlockSpec((tokens, dh), lambda g, p: (0, g)),
                pl.BlockSpec((tokens, dh), lambda g, p: (0, groups + g)),
                pl.BlockSpec((group, feat, dh), lambda g, p: (g, 0, 0)),
                pl.BlockSpec((group, feat, dh), lambda g, p: (g, 0, 0)),
                pl.BlockSpec(memory_space=pltpu.SMEM),
            ],
            out_specs=pl.BlockSpec((tok, group * dh), lambda g, p: (0, g)),
            scratch_shapes=[
                pltpu.VMEM((group * 2 * feat, seen), BF16),
                pltpu.VMEM((group * 2 * feat, 2 * dh), BF16),
            ],
        ),
        out_shape=jax.ShapeDtypeStruct(queries.shape, BF16),
        compiler_params=pltpu.CompilerParams(vmem_limit_bytes=48 * 2**20),
        cost_estimate=pl.CostEstimate(
            flops=2 * local_heads * tokens * 3 * feat * 2 * dh,
            bytes_accessed=8 * 2**20,
            transcendentals=local_heads * tokens * 2 * feat,
        ),
    )(place, queries, kv, kv, wq, wk, ratio)


WAYS = 4


def spot():
    at = lax.axis_index("seq")
    return lax.rem(at, WAYS), lax.div(at, WAYS)


def aligned(at, step):
    return pl.ds(pl.multiple_of(at * step, step), step)


def with_ones(values, kept):
    here = jnp.where(kept, 1.0, 0.0).astype(BF16)
    return jnp.concatenate([values, jnp.full(values.shape, here)], axis=1)


def pack_kv_kernel(k_ref, v_ref, own_ref, away_ref):
    place = spot()[0]
    for d in range(WAYS):
        ref, at = (own_ref, away_ref)[d // 2], d % 2 * 2 * DH
        ref[:, at : at + DH] = k_ref[:, aligned(place ^ d, DH)]
        ref[:, at + DH : at + 2 * DH] = v_ref[:, aligned(place ^ d, DH)]


def pair_kernel(own_ref, got_ref, out_ref):
    tok = own_ref.shape[0]
    out_ref[:tok, :] = own_ref[:, 2 * DH :]
    out_ref[tok:, :] = got_ref[:, 2 * DH :]


def stack_kernel(own_ref, got_ref, pair_ref, out_ref):
    tok = own_ref.shape[0]
    place = spot()[0]
    out_ref[aligned(place, tok), :] = own_ref[:, : 2 * DH]
    out_ref[aligned(place ^ 2, tok), :] = got_ref[:, : 2 * DH]
    out_ref[aligned(place ^ 1, tok), :] = pair_ref[:tok, :]
    out_ref[aligned(place ^ 3, tok), :] = pair_ref[tok:, :]


def pack_q_kernel(q_ref, *out_refs):
    place = spot()[0]
    for d, out in enumerate(out_refs):
        out[...] = q_ref[:, aligned(place ^ d, out.shape[1])]


def weights_kernel(wq_ref, both_ref):
    for h in range(wq_ref.shape[0]):
        wq = wq_ref[h].T
        both_ref[h] = jnp.concatenate([wq, -wq], axis=1)


def join_kernel(sides, *refs):
    got, out_ref, sems = refs[:-2], *refs[-2:]
    width = got[0].shape[1]
    place, side = spot()[0], lax.axis_index("head")
    copies = []
    for n, ref in enumerate(got):
        dr, dy = divmod(n, sides)
        at = aligned((side ^ dy) * WAYS + (place ^ dr), width)
        copies.append(pltpu.make_async_copy(ref, out_ref.at[:, at], sems.at[n]))
    for copy in copies:
        copy.start()
    for copy in copies:
        copy.wait()


def write_key_features(keys, wk_ref, fk_ref):
    heads, feat, dh = wk_ref.shape
    logits = dot_t(wk_ref[...].reshape(heads * feat, dh), keys)
    for h in range(heads):
        part = logits[h * feat : (h + 1) * feat]
        top = jnp.max(part, axis=0, keepdims=True)
        low = jnp.min(part, axis=0, keepdims=True)
        for n, shifted in enumerate((part - top, low - part)):
            row = (2 * h + n) * feat
            expd = jnp.exp(shifted.astype(BF16))
            total = expd[: feat // 4]
            for q in range(1, 4):
                total = total + expd[q * feat // 4 : (q + 1) * feat // 4]
            total = jnp.sum(total.astype(F32), axis=0, keepdims=True)
            fk_ref[row : row + feat, :] = expd * pl.reciprocal(total).astype(BF16)


def near_features_kernel(last_ref, own_ref, wk_ref, fk_ref):
    half = last_ref.shape[0] // 2
    keys = jnp.concatenate([last_ref[half:, :DH], own_ref[:, :DH]], axis=0)
    write_key_features(keys, wk_ref, fk_ref)


def past_kernel(last_ref, before_ref, fk_near_ref, wk_ref, past_ref, step_ref, fk_scr):
    level = spot()[1]
    half = last_ref.shape[0] // 2
    keys = jnp.concatenate([last_ref[:half, :DH], before_ref[:, :DH]], axis=0)
    write_key_features(keys, wk_ref, fk_scr)
    values = jnp.concatenate(
        [with_ones(last_ref[:half, DH:], level >= 1), with_ones(before_ref[:, DH:], level >= 2)],
        axis=0,
    )
    past_ref[...] = jnp.dot(fk_scr[...], values, preferred_element_type=F32)
    step_ref[...] = jnp.dot(
        fk_near_ref[:, :half],
        with_ones(last_ref[half:, DH:], level >= 1),
        preferred_element_type=F32,
    )


def query_features_kernel(a_ref, b_ref, w_ref, q_out, fq_out, exp_scr):
    tok = a_ref.shape[0]
    heads, dh, both = w_ref.shape
    half = 2 * tok
    place = spot()[0]
    for d, ref in enumerate((a_ref, b_ref)):
        row = pl.multiple_of(lax.rem(place ^ d, 2) * tok, tok)
        for h in range(heads):
            q_out[pl.ds(h * half + row, tok), :] = ref[:, h * dh : (h + 1) * dh]
    left = lax.broadcasted_iota(jnp.int32, (half, both), 1) < both // 2
    side_r = lax.broadcasted_iota(jnp.int32, (both, both), 0) < both // 2
    side_c = lax.broadcasted_iota(jnp.int32, (both, both), 1) < both // 2
    halves = jnp.where(side_r == side_c, 1.0, 0.0).astype(BF16)
    for h in range(heads):
        rows = slice(h * half, (h + 1) * half)
        logits = jnp.dot(q_out[rows, :], w_ref[h], preferred_element_type=F32)
        top_l = jnp.max(jnp.where(left, logits, -jnp.inf), axis=1, keepdims=True)
        top_r = jnp.max(jnp.where(left, -jnp.inf, logits), axis=1, keepdims=True)
        exp_scr[rows, :] = jnp.exp((logits - jnp.where(left, top_l, top_r)).astype(BF16))
    total = jnp.dot(exp_scr[...], halves, preferred_element_type=F32)
    fq_out[...] = (exp_scr[...].astype(F32) * pl.reciprocal(total, approx=True)).astype(BF16)


def near_kernel(other, factor_ref, q_ref, fq_ref, last_ref, own_ref, fk_ref, near_ref, *scr):
    kv_scr, w_scr = scr
    half, dh = last_ref.shape[0] // 2, q_ref.shape[1]
    heads = q_ref.shape[0] // half
    feats = fq_ref.shape[1]
    place, level = spot()
    u = lax.div(place, 2) ^ other
    kv_scr[:half, :] = last_ref[half:, :]
    kv_scr[half:, :] = own_ref[...]
    at = pl.ds(pl.multiple_of(u * half, half), 2 * half)
    keys, values = kv_scr[at, :dh], kv_scr[at, dh:]
    row = lax.broadcasted_iota(jnp.int32, (half, 2 * half), 0)
    col = lax.broadcasted_iota(jnp.int32, (half, 2 * half), 1)
    split = row + (half - WINDOW)
    valid = (col >= half) | (level > 0) | (u > 0)
    inside = (col > split) & (col <= row + half) & valid
    causal = (col <= split) & valid
    scores = dot_t(q_ref[...], keys) * (1.0 / math.sqrt(dh))
    for h in range(heads):
        here = slice(h * half, (h + 1) * half)
        linear = jnp.dot(
            fq_ref[here, :],
            fk_ref[h * feats : (h + 1) * feats, at],
            preferred_element_type=F32,
        )
        masked = jnp.where(inside, scores[here], -jnp.inf)
        top = jnp.max(masked, axis=1, keepdims=True)
        factor = jnp.full((1, 2 * half), factor_ref[place * heads + h])
        soft = jnp.exp(masked - top) * (factor / (1.0 - factor))
        w_scr[here, :] = jnp.where(causal, linear, soft).astype(BF16)
    near_ref[...] = jnp.dot(
        w_scr[...], with_ones(values, level >= 0), preferred_element_type=F32
    )


def mix_kernel_of_level(sides, *refs):
    near_refs, fq_refs, (past_ref, step_ref, wk_ref) = refs[:2], refs[2:4], refs[4:7]
    first_ref, refs = refs[7], refs[8:]
    out_refs, (fk_scr, state_scr, out_scr) = refs[:-3], refs[-3:]
    rows, dh = near_refs[0].shape[0], near_refs[0].shape[1] // 2
    feats = fq_refs[0].shape[1]
    heads = past_ref.shape[0] // feats
    half = rows // heads
    place, level = spot()
    side = lax.axis_index("head")
    u = lax.div(place, 2)

    write_key_features(first_ref[:, :dh], wk_ref, fk_scr)
    state = past_ref[...] + jnp.dot(
        fk_scr[...], with_ones(first_ref[:, dh:], level >= 3), preferred_element_type=F32
    )
    state_scr[0] = state.astype(BF16)
    state_scr[1] = (state + step_ref[...]).astype(BF16)
    part = out_refs[0].shape[0]
    for other in (1, 0):
        for h in range(heads):
            here = slice(h * half, (h + 1) * half)
            far = jnp.dot(
                fq_refs[other][here, :],
                state_scr[u ^ other, h * feats : (h + 1) * feats, :],
                preferred_element_type=F32,
            )
            both = near_refs[other][here, :] + far
            out_scr[:, h * dh : (h + 1) * dh] = (
                both[:, :dh] * pl.reciprocal(both[:, dh:], approx=True)
            ).astype(BF16)
        for d in range(2):
            for dy in range(sides):
                at = lax.rem(place ^ d, 2) * sides + (side ^ dy)
                out_refs[(2 * other + d) * sides + dy][...] = out_scr[aligned(at, part), :]


def whole_spec(space=pltpu.VMEM):
    return pl.BlockSpec(memory_space=space)


def call(kernel, ins, outs, name, scratch=(), limit=4, out_type=BF16, scalars=()):
    return pl.pallas_call(
        kernel,
        in_specs=[whole_spec(pltpu.SMEM) for _ in scalars] + [whole_spec() for _ in ins],
        out_specs=[whole_spec() for _ in outs],
        out_shape=[jax.ShapeDtypeStruct(s, out_type) for s in outs],
        scratch_shapes=list(scratch),
        compiler_params=pltpu.CompilerParams(vmem_limit_bytes=limit * 2**20),
        name=name,
    )(*scalars, *ins)


def by_levels(queries, keys, values, wq, wk, factor):
    tok, width = queries.shape
    local_heads, feat, dh = wq.shape
    heads = local_heads // WAYS
    seq, sides = lax.axis_size("seq"), lax.axis_size("head")
    half = 2 * tok
    rows, states = heads * half, heads * 2 * feat

    def partner(x, dr, dy=0):
        pairs = [
            (i * sides + j, (i // WAYS * WAYS + (i % WAYS ^ dr)) * sides + (j ^ dy))
            for i in range(seq)
            for j in range(sides)
        ]
        return lax.ppermute(x, ("seq", "head"), pairs)

    def levels_back(x, by):
        pairs = [(i, i + by * WAYS) for i in range(seq - by * WAYS)]
        return lax.ppermute(x, "seq", pairs)

    own, away = call(pack_kv_kernel, [keys, values], [(tok, 4 * dh)] * 2, "pack_kv")
    got = partner(away, 2)
    q = list(call(pack_q_kernel, [queries], [(tok, width // WAYS)] * WAYS, "pack_q"))
    (pair,) = call(pair_kernel, [own, got], [(half, 2 * dh)], "pair_kv")
    *q, pair = lax.optimization_barrier((*q, pair))
    pair = partner(pair, 1)
    q[1], q[2] = partner(q[1], 1), partner(q[2], 2)
    (kv,) = call(stack_kernel, [own, got, pair], [(2 * half, 2 * dh)], "stack_kv")
    wq, wk, kv, q[1] = lax.optimization_barrier((wq, wk, kv, q[1]))
    last, before, first = [levels_back(kv, by) for by in (1, 2, 3)]

    at = lax.rem(lax.axis_index("seq"), WAYS) * heads
    wk = lax.dynamic_slice_in_dim(wk, at, heads)
    (wq,) = call(
        weights_kernel,
        [lax.dynamic_slice_in_dim(wq, at, heads)],
        [(heads, dh, 2 * feat)],
        "weights",
    )
    wq, q[3] = lax.optimization_barrier((wq, q[3]))
    q[3] = partner(q[3], 3)

    def query_features(a, b):
        return call(
            query_features_kernel,
            [a, b, wq],
            [(rows, dh), (rows, 2 * feat)],
            "query_features",
            [pltpu.VMEM((rows, 2 * feat), BF16)],
            12,
        )

    def near(other, q_rows, fq, fk):
        return call(
            lambda *refs: near_kernel(other, *refs),
            [q_rows, fq, last, kv, fk],
            [(rows, 2 * dh)],
            "near",
            [pltpu.VMEM((3 * half, 2 * dh), BF16), pltpu.VMEM((rows, 2 * half), BF16)],
            16,
            F32,
            [factor],
        )[0]

    q_own, fq_own = query_features(q[0], q[1])
    (fk_near,) = call(
        near_features_kernel, [last, kv, wk], [(states, 3 * half)], "near_features", limit=16
    )
    near_own = near(0, q_own, fq_own, fk_near)
    q[2], q[3], before, near_own = lax.optimization_barrier((q[2], q[3], before, near_own))
    q_other, fq_other = query_features(q[2], q[3])
    near_other = near(1, q_other, fq_other, fk_near)
    past, step = call(
        past_kernel,
        [last, before, fk_near, wk],
        [(states, 2 * dh)] * 2,
        "past",
        [pltpu.VMEM((states, 3 * half), BF16)],
        16,
        F32,
    )
    first, near_other, past = lax.optimization_barrier((first, near_other, past))
    part = tok // sides
    outs = call(
        lambda *refs: mix_kernel_of_level(sides, *refs),
        [near_own, near_other, fq_own, fq_other, past, step, wk, first],
        [(part, heads * dh)] * (WAYS * sides),
        "mix_level",
        [
            pltpu.VMEM((states, 2 * half), BF16),
            pltpu.VMEM((2, states, 2 * dh), BF16),
            pltpu.VMEM((half, heads * dh), BF16),
        ],
        24,
    )

    def turn(n):
        dr, dy = divmod(n, sides)
        return (0, dr, 0) if dr > 1 and dy else (1, dr % 2, dy) if dr > 1 or dy else (2, 0, 0)

    outs = list(outs)
    for n in sorted(range(1, WAYS * sides), key=turn):
        outs[n] = partner(outs[n], *divmod(n, sides))
    return pl.pallas_call(
        lambda *refs: join_kernel(sides, *refs),
        in_specs=[whole_spec()] * (WAYS * sides),
        out_specs=whole_spec(pltpu.HBM),
        out_shape=jax.ShapeDtypeStruct((part, sides * WAYS * heads * dh), BF16),
        scratch_shapes=[pltpu.SemaphoreType.DMA((WAYS * sides,))],
        compiler_params=pltpu.CompilerParams(vmem_limit_bytes=4 * 2**20),
        name="join",
    )(*outs)


def by_blocks(queries, keys, values, wq, wk, ratio):
    group = wq.shape[0] // (keys.shape[1] // DH)
    place = lax.axis_index("seq").astype(jnp.int32).reshape(1)
    kv = lax.all_gather(jnp.concatenate([keys, values], axis=1), "seq", tiled=True)
    out = mix(place, queries, kv, wq, wk, ratio, group)
    return lax.all_to_all(out, "head", split_axis=0, concat_axis=1, tiled=True)


def local(queries, keys, values, q_feature, k_feature, window_factor):
    tok = queries.shape[0]
    seq, sides = lax.axis_size("seq"), lax.axis_size("head")
    wq, wk = jnp.swapaxes(q_feature, 1, 2), jnp.swapaxes(k_feature, 1, 2)
    if keys.shape[1] == WAYS * DH and seq == 4 * WAYS and sides == 2 and tok == WINDOW:
        return by_levels(queries, keys, values, wq, wk, window_factor)
    ratio = window_factor / (1.0 - window_factor)
    return by_blocks(queries, keys, values, wq, wk, ratio)


def solution(mesh):
    return jax.shard_map(
        local,
        mesh=mesh,
        in_specs=(
            P("seq", "head"),
            P("seq", "head"),
            P("seq", "head"),
            P("head", None, None),
            P("head", None, None),
            P("head"),
        ),
        out_specs=P(("seq", "head"), None),
        check_vma=False,
    )
```

```python
import math

import jax
import jax.numpy as jnp
from jax import lax
from jax.experimental import pallas as pl
from jax.experimental.pallas import tpu as pltpu
from jax.sharding import PartitionSpec as P

DH = 128
WINDOW = 64
F32 = jnp.float32
BF16 = jnp.bfloat16


def dot_t(a, b):
    return lax.dot_general(a, b, (((1,), (1,)), ((), ())), preferred_element_type=F32)


def features_t(logits):
    top = jnp.max(logits, axis=0, keepdims=True)
    low = jnp.min(logits, axis=0, keepdims=True)
    up = jnp.exp(logits - top)
    down = jnp.exp(low - logits)
    up = up * (1.0 / jnp.sum(up, axis=0, keepdims=True))
    down = down * (1.0 / jnp.sum(down, axis=0, keepdims=True))
    return jnp.concatenate([up.astype(BF16), down.astype(BF16)], axis=0)


def mix_kernel(
    place_ref, q_ref, k_ref, v_ref, wq_ref, wk_ref, ratio_ref, out_ref, fk_scr, state_scr
):
    tok = q_ref.shape[0]
    heads, feat, dh = wq_ref.shape
    seen = fk_scr.shape[1]
    place = place_ref[0]
    first_head = pl.program_id(0) * heads

    weights = wk_ref[...].reshape(heads * feat, dh)
    for start in range(0, seen, 256):
        size = min(256, seen - start)
        logits = dot_t(weights, k_ref[start : start + size, :])
        for h in range(heads):
            fk_scr[h * 2 * feat : (h + 1) * 2 * feat, start : start + size] = features_t(
                logits[h * feat : (h + 1) * feat]
            )
    row = lax.broadcasted_iota(jnp.int32, (seen, dh), 0)
    kept = row < (place - 1) * tok
    v_seen = jnp.where(kept, v_ref[:seen, :].astype(F32), 0.0).astype(BF16)
    ones_seen = jnp.where(kept, 1.0, 0.0).astype(BF16)
    v_seen = jnp.concatenate([v_seen, ones_seen], axis=1)
    state_scr[...] = jnp.dot(fk_scr[...], v_seen, preferred_element_type=F32).astype(BF16)

    before = pl.multiple_of(jnp.maximum(place - 1, 0) * tok, tok)
    own = pl.multiple_of(place * tok, tok)
    k_ext = jnp.concatenate([k_ref[pl.ds(before, tok), :], k_ref[pl.ds(own, tok), :]], axis=0)
    v_ext = jnp.concatenate([v_ref[pl.ds(before, tok), :], v_ref[pl.ds(own, tok), :]], axis=0)
    v_ext = jnp.concatenate([v_ext, jnp.ones_like(v_ext)], axis=1)
    row = lax.broadcasted_iota(jnp.int32, (tok, 2 * tok), 0)
    col = lax.broadcasted_iota(jnp.int32, (tok, 2 * tok), 1)
    valid = (col >= tok) | (place > 0)
    inside = (col > row) & (col <= row + WINDOW) & valid
    causal = (col <= row) & valid
    lane = lax.broadcasted_iota(jnp.int32, (tok, 2 * feat), 1)
    left = lane < feat
    side_r = lax.broadcasted_iota(jnp.int32, (2 * feat, 2 * feat), 0) < feat
    side_c = lax.broadcasted_iota(jnp.int32, (2 * feat, 2 * feat), 1) < feat
    halves = jnp.where(side_r == side_c, 1.0, 0.0).astype(BF16)

    for h in range(heads):
        q = q_ref[:, h * dh : (h + 1) * dh]
        wq = wq_ref[h]
        logits = dot_t(q, jnp.concatenate([wq, -wq], axis=0))
        top_l = jnp.max(jnp.where(left, logits, -jnp.inf), axis=1, keepdims=True)
        top_r = jnp.max(jnp.where(left, -jnp.inf, logits), axis=1, keepdims=True)
        expd = jnp.exp(logits - jnp.where(left, top_l, top_r)).astype(BF16)
        total = jnp.dot(expd, halves, preferred_element_type=F32)
        fq = (expd.astype(F32) / total).astype(BF16)
        fk = features_t(dot_t(wk_ref[h], k_ext))
        linear = jnp.dot(fq, fk, preferred_element_type=F32)
        scores = dot_t(q, k_ext) * (1.0 / math.sqrt(dh))
        masked = jnp.where(inside, scores, -jnp.inf)
        top = jnp.max(masked, axis=1, keepdims=True)
        soft = jnp.exp(masked - top) * ratio_ref[first_head + h]
        weight = jnp.where(causal, linear, soft).astype(BF16)
        both = jnp.dot(weight, v_ext, preferred_element_type=F32) + jnp.dot(
            fq, state_scr[h * 2 * feat : (h + 1) * 2 * feat, :], preferred_element_type=F32
        )
        out_ref[:, h * dh : (h + 1) * dh] = (both[:, :dh] / both[:, dh:]).astype(BF16)


def mix(place, queries, kv, wq, wk, ratio, group):
    tok = queries.shape[0]
    local_heads, feat, dh = wq.shape
    groups = local_heads // group
    tokens = kv.shape[0]
    seen = tokens - 2 * tok
    return pl.pallas_call(
        mix_kernel,
        grid_spec=pltpu.PrefetchScalarGridSpec(
            num_scalar_prefetch=1,
            grid=(groups,),
            in_specs=[
                pl.BlockSpec((tok, group * dh), lambda g, p: (0, g)),
                pl.BlockSpec((tokens, dh), lambda g, p: (0, g)),
                pl.BlockSpec((tokens, dh), lambda g, p: (0, groups + g)),
                pl.BlockSpec((group, feat, dh), lambda g, p: (g, 0, 0)),
                pl.BlockSpec((group, feat, dh), lambda g, p: (g, 0, 0)),
                pl.BlockSpec(memory_space=pltpu.SMEM),
            ],
            out_specs=pl.BlockSpec((tok, group * dh), lambda g, p: (0, g)),
            scratch_shapes=[
                pltpu.VMEM((group * 2 * feat, seen), BF16),
                pltpu.VMEM((group * 2 * feat, 2 * dh), BF16),
            ],
        ),
        out_shape=jax.ShapeDtypeStruct(queries.shape, BF16),
        compiler_params=pltpu.CompilerParams(vmem_limit_bytes=48 * 2**20),
        cost_estimate=pl.CostEstimate(
            flops=2 * local_heads * tokens * 3 * feat * 2 * dh,
            bytes_accessed=8 * 2**20,
            transcendentals=local_heads * tokens * 2 * feat,
        ),
    )(place, queries, kv, kv, wq, wk, ratio)


WAYS = 4


SLOTS = (
    ((0, 0), (0, 0)),
    ((2, 1), (2, 1)),
    ((2, 0), (0, 1)),
    ((0, 1), (2, 0)),
    ((3, 1), (3, 1)),
    ((3, 0), (1, 1)),
    ((1, 1), (3, 0)),
    ((1, 0), (1, 0)),
)


def slot_of(n, odd):
    return [jnp.where(odd == 1, b, a) if a != b else a for a, b in zip(*SLOTS[n])]


def spot():
    at = lax.axis_index("seq")
    return lax.rem(at, WAYS), lax.div(at, WAYS)


def aligned(at, step):
    return pl.ds(pl.multiple_of(at * step, step), step)


def with_ones(values, kept):
    here = jnp.where(kept, 1.0, 0.0).astype(BF16)
    return jnp.concatenate([values, jnp.full(values.shape, here)], axis=1)


def pack_kv_kernel(k_ref, v_ref, own_ref, away_ref):
    place = spot()[0]
    for d in range(WAYS):
        ref, at = (own_ref, away_ref)[d // 2], d % 2 * 2 * DH
        ref[:, at : at + DH] = k_ref[:, aligned(place ^ d, DH)]
        ref[:, at + DH : at + 2 * DH] = v_ref[:, aligned(place ^ d, DH)]


def pair_kernel(own_ref, got_ref, out_ref):
    tok = own_ref.shape[0]
    out_ref[:tok, :] = own_ref[:, 2 * DH :]
    out_ref[tok:, :] = got_ref[:, 2 * DH :]


def stack_kernel(own_ref, got_ref, pair_ref, out_ref):
    tok = own_ref.shape[0]
    place = spot()[0]
    out_ref[aligned(place, tok), :] = own_ref[:, : 2 * DH]
    out_ref[aligned(place ^ 2, tok), :] = got_ref[:, : 2 * DH]
    out_ref[aligned(place ^ 1, tok), :] = pair_ref[:tok, :]
    out_ref[aligned(place ^ 3, tok), :] = pair_ref[tok:, :]


def pack_q_kernel(q_ref, *out_refs):
    place = spot()[0]
    for d, out in enumerate(out_refs):
        out[...] = q_ref[:, aligned(place ^ d, out.shape[1])]


def weights_kernel(wq_ref, both_ref):
    for h in range(wq_ref.shape[0]):
        wq = wq_ref[h].T
        both_ref[h] = jnp.concatenate([wq, -wq], axis=1)


def join_kernel(*refs):
    got, out_ref, sems = refs[:-2], *refs[-2:]
    width = got[0].shape[1]
    place, side = spot()[0], lax.axis_index("head")
    copies = []
    for n, ref in enumerate(got):
        dr, dy = slot_of(n, lax.rem(place, 2) ^ (SLOTS[n][0][0] & 1))
        at = aligned((side ^ dy) * WAYS + (place ^ dr), width)
        copies.append(pltpu.make_async_copy(ref, out_ref.at[:, at], sems.at[n]))
    for copy in copies:
        copy.start()
    for copy in copies:
        copy.wait()


def write_key_features(keys, wk_ref, fk_ref):
    heads, feat, dh = wk_ref.shape
    logits = dot_t(wk_ref[...].reshape(heads * feat, dh), keys)
    for h in range(heads):
        part = logits[h * feat : (h + 1) * feat]
        top = jnp.max(part, axis=0, keepdims=True)
        low = jnp.min(part, axis=0, keepdims=True)
        for n, shifted in enumerate((part - top, low - part)):
            row = (2 * h + n) * feat
            expd = jnp.exp(shifted.astype(BF16))
            total = expd[: feat // 4]
            for q in range(1, 4):
                total = total + expd[q * feat // 4 : (q + 1) * feat // 4]
            total = jnp.sum(total.astype(F32), axis=0, keepdims=True)
            fk_ref[row : row + feat, :] = expd * pl.reciprocal(total).astype(BF16)


def near_features_kernel(last_ref, own_ref, wk_ref, fk_ref):
    half = last_ref.shape[0] // 2
    keys = jnp.concatenate([last_ref[half:, :DH], own_ref[:, :DH]], axis=0)
    write_key_features(keys, wk_ref, fk_ref)


def past_kernel(last_ref, before_ref, fk_near_ref, wk_ref, past_ref, step_ref, fk_scr):
    level = spot()[1]
    half = last_ref.shape[0] // 2
    keys = jnp.concatenate([last_ref[:half, :DH], before_ref[:, :DH]], axis=0)
    write_key_features(keys, wk_ref, fk_scr)
    values = jnp.concatenate(
        [with_ones(last_ref[:half, DH:], level >= 1), with_ones(before_ref[:, DH:], level >= 2)],
        axis=0,
    )
    past_ref[...] = jnp.dot(fk_scr[...], values, preferred_element_type=F32)
    step_ref[...] = jnp.dot(
        fk_near_ref[:, :half],
        with_ones(last_ref[half:, DH:], level >= 1),
        preferred_element_type=F32,
    )


def query_features_kernel(a_ref, b_ref, w_ref, q_out, fq_out, exp_scr):
    tok = a_ref.shape[0]
    heads, dh, both = w_ref.shape
    half = 2 * tok
    place = spot()[0]
    for d, ref in enumerate((a_ref, b_ref)):
        row = pl.multiple_of(lax.rem(place ^ d, 2) * tok, tok)
        for h in range(heads):
            q_out[pl.ds(h * half + row, tok), :] = ref[:, h * dh : (h + 1) * dh]
    left = lax.broadcasted_iota(jnp.int32, (half, both), 1) < both // 2
    side_r = lax.broadcasted_iota(jnp.int32, (both, both), 0) < both // 2
    side_c = lax.broadcasted_iota(jnp.int32, (both, both), 1) < both // 2
    halves = jnp.where(side_r == side_c, 1.0, 0.0).astype(BF16)
    for h in range(heads):
        rows = slice(h * half, (h + 1) * half)
        logits = jnp.dot(q_out[rows, :], w_ref[h], preferred_element_type=F32)
        top_l = jnp.max(jnp.where(left, logits, -jnp.inf), axis=1, keepdims=True)
        top_r = jnp.max(jnp.where(left, -jnp.inf, logits), axis=1, keepdims=True)
        exp_scr[rows, :] = jnp.exp((logits - jnp.where(left, top_l, top_r)).astype(BF16))
    total = jnp.dot(exp_scr[...], halves, preferred_element_type=F32)
    fq_out[...] = (exp_scr[...].astype(F32) * pl.reciprocal(total, approx=True)).astype(BF16)


def near_kernel(other, factor_ref, q_ref, fq_ref, last_ref, own_ref, fk_ref, near_ref, *scr):
    kv_scr, w_scr = scr
    half, dh = last_ref.shape[0] // 2, q_ref.shape[1]
    heads = q_ref.shape[0] // half
    feats = fq_ref.shape[1]
    place, level = spot()
    u = lax.div(place, 2) ^ other
    kv_scr[:half, :] = last_ref[half:, :]
    kv_scr[half:, :] = own_ref[...]
    at = pl.ds(pl.multiple_of(u * half, half), 2 * half)
    keys, values = kv_scr[at, :dh], kv_scr[at, dh:]
    row = lax.broadcasted_iota(jnp.int32, (half, 2 * half), 0)
    col = lax.broadcasted_iota(jnp.int32, (half, 2 * half), 1)
    split = row + (half - WINDOW)
    valid = (col >= half) | (level > 0) | (u > 0)
    inside = (col > split) & (col <= row + half) & valid
    causal = (col <= split) & valid
    scores = dot_t(q_ref[...], keys) * (1.0 / math.sqrt(dh))
    for h in range(heads):
        here = slice(h * half, (h + 1) * half)
        linear = jnp.dot(
            fq_ref[here, :],
            fk_ref[h * feats : (h + 1) * feats, at],
            preferred_element_type=F32,
        )
        masked = jnp.where(inside, scores[here], -jnp.inf)
        top = jnp.max(masked, axis=1, keepdims=True)
        factor = jnp.full((1, 2 * half), factor_ref[place * heads + h])
        soft = jnp.exp(masked - top) * (factor / (1.0 - factor))
        w_scr[here, :] = jnp.where(causal, linear, soft).astype(BF16)
    near_ref[...] = jnp.dot(
        w_scr[...], with_ones(values, level >= 0), preferred_element_type=F32
    )


def mix_kernel_of_level(*refs):
    near_refs, fq_refs, (past_ref, step_ref, wk_ref) = refs[:2], refs[2:4], refs[4:7]
    first_ref, refs = refs[7], refs[8:]
    out_refs, (fk_scr, state_scr, out_scr) = refs[:-3], refs[-3:]
    rows, dh = near_refs[0].shape[0], near_refs[0].shape[1] // 2
    feats = fq_refs[0].shape[1]
    heads = past_ref.shape[0] // feats
    half = rows // heads
    place, level = spot()
    side = lax.axis_index("head")
    u = lax.div(place, 2)

    write_key_features(first_ref[:, :dh], wk_ref, fk_scr)
    state = past_ref[...] + jnp.dot(
        fk_scr[...], with_ones(first_ref[:, dh:], level >= 3), preferred_element_type=F32
    )
    state_scr[0] = state.astype(BF16)
    state_scr[1] = (state + step_ref[...]).astype(BF16)
    part = out_refs[0].shape[0]
    for other in (1, 0):
        for h in range(heads):
            here = slice(h * half, (h + 1) * half)
            far = jnp.dot(
                fq_refs[other][here, :],
                state_scr[u ^ other, h * feats : (h + 1) * feats, :],
                preferred_element_type=F32,
            )
            both = near_refs[other][here, :] + far
            out_scr[aligned(u ^ other, half), h * dh : (h + 1) * dh] = (
                both[:, :dh] * pl.reciprocal(both[:, dh:], approx=True)
            ).astype(BF16)
    for n, ref in enumerate(out_refs):
        dr, dy = slot_of(n, lax.rem(place, 2))
        ref[...] = out_scr[aligned((place ^ dr) * 2 + (side ^ dy), part), :]


def whole_spec(space=pltpu.VMEM):
    return pl.BlockSpec(memory_space=space)


def call(kernel, ins, outs, name, scratch=(), limit=4, out_type=BF16, scalars=()):
    return pl.pallas_call(
        kernel,
        in_specs=[whole_spec(pltpu.SMEM) for _ in scalars] + [whole_spec() for _ in ins],
        out_specs=[whole_spec() for _ in outs],
        out_shape=[jax.ShapeDtypeStruct(s, out_type) for s in outs],
        scratch_shapes=list(scratch),
        compiler_params=pltpu.CompilerParams(vmem_limit_bytes=limit * 2**20),
        name=name,
    )(*scalars, *ins)


def by_levels(queries, keys, values, wq, wk, factor):
    tok, width = queries.shape
    local_heads, feat, dh = wq.shape
    heads = local_heads // WAYS
    seq, sides = lax.axis_size("seq"), lax.axis_size("head")
    half = 2 * tok
    rows, states = heads * half, heads * 2 * feat

    def partner(x, dr, dy=0):
        pairs = [
            (i * sides + j, (i // WAYS * WAYS + (i % WAYS ^ dr)) * sides + (j ^ dy))
            for i in range(seq)
            for j in range(sides)
        ]
        return lax.ppermute(x, ("seq", "head"), pairs)

    def levels_back(x, by):
        pairs = [(i, i + by * WAYS) for i in range(seq - by * WAYS)]
        return lax.ppermute(x, "seq", pairs)

    own, away = call(pack_kv_kernel, [keys, values], [(tok, 4 * dh)] * 2, "pack_kv")
    got = partner(away, 2)
    q = list(call(pack_q_kernel, [queries], [(tok, width // WAYS)] * WAYS, "pack_q"))
    (pair,) = call(pair_kernel, [own, got], [(half, 2 * dh)], "pair_kv")
    *q, pair = lax.optimization_barrier((*q, pair))
    pair = partner(pair, 1)
    q[1], q[2], q[3] = partner(q[1], 1), partner(q[2], 2), partner(q[3], 3)
    (kv,) = call(stack_kernel, [own, got, pair], [(2 * half, 2 * dh)], "stack_kv")
    last = levels_back(kv, 1)
    wq, wk, kv, q[1] = lax.optimization_barrier((wq, wk, kv, q[1]))
    before, first = levels_back(kv, 2), levels_back(kv, 3)

    at = lax.rem(lax.axis_index("seq"), WAYS) * heads
    wk = lax.dynamic_slice_in_dim(wk, at, heads)
    (wq,) = call(
        weights_kernel,
        [lax.dynamic_slice_in_dim(wq, at, heads)],
        [(heads, dh, 2 * feat)],
        "weights",
    )
    def query_features(a, b):
        return call(
            query_features_kernel,
            [a, b, wq],
            [(rows, dh), (rows, 2 * feat)],
            "query_features",
            [pltpu.VMEM((rows, 2 * feat), BF16)],
            12,
        )

    def near(other, q_rows, fq, fk):
        return call(
            lambda *refs: near_kernel(other, *refs),
            [q_rows, fq, last, kv, fk],
            [(rows, 2 * dh)],
            "near",
            [pltpu.VMEM((3 * half, 2 * dh), BF16), pltpu.VMEM((rows, 2 * half), BF16)],
            16,
            F32,
            [factor],
        )[0]

    q_own, fq_own = query_features(q[0], q[1])
    (fk_near,) = call(
        near_features_kernel, [last, kv, wk], [(states, 3 * half)], "near_features", limit=16
    )
    near_own = near(0, q_own, fq_own, fk_near)
    q[2], q[3], near_own = lax.optimization_barrier((q[2], q[3], near_own))
    q_other, fq_other = query_features(q[2], q[3])
    near_other = near(1, q_other, fq_other, fk_near)
    before, near_other = lax.optimization_barrier((before, near_other))
    past, step = call(
        past_kernel,
        [last, before, fk_near, wk],
        [(states, 2 * dh)] * 2,
        "past",
        [pltpu.VMEM((states, 3 * half), BF16)],
        16,
        F32,
    )
    first, near_other, past = lax.optimization_barrier((first, near_other, past))
    part = tok // sides
    outs = call(
        mix_kernel_of_level,
        [near_own, near_other, fq_own, fq_other, past, step, wk, first],
        [(part, heads * dh)] * (WAYS * sides),
        "mix_level",
        [
            pltpu.VMEM((states, 2 * half), BF16),
            pltpu.VMEM((2, states, 2 * dh), BF16),
            pltpu.VMEM((2 * half, heads * dh), BF16),
        ],
        24,
    )

    def sent(x, slot):
        pairs = []
        for i in range(seq):
            dr, dy = slot[i % 2]
            to = i // WAYS * WAYS + (i % WAYS ^ dr)
            pairs += [(i * sides + j, to * sides + (j ^ dy)) for j in range(sides)]
        return lax.ppermute(x, ("seq", "head"), pairs)

    outs = [outs[0]] + [sent(x, slot) for x, slot in zip(outs[1:], SLOTS[1:])]
    return pl.pallas_call(
        join_kernel,
        in_specs=[whole_spec()] * (WAYS * sides),
        out_specs=whole_spec(pltpu.HBM),
        out_shape=jax.ShapeDtypeStruct((part, sides * WAYS * heads * dh), BF16),
        scratch_shapes=[pltpu.SemaphoreType.DMA((WAYS * sides,))],
        compiler_params=pltpu.CompilerParams(vmem_limit_bytes=4 * 2**20),
        name="join",
    )(*outs)


def by_blocks(queries, keys, values, wq, wk, ratio):
    group = wq.shape[0] // (keys.shape[1] // DH)
    place = lax.axis_index("seq").astype(jnp.int32).reshape(1)
    kv = lax.all_gather(jnp.concatenate([keys, values], axis=1), "seq", tiled=True)
    out = mix(place, queries, kv, wq, wk, ratio, group)
    return lax.all_to_all(out, "head", split_axis=0, concat_axis=1, tiled=True)


def local(queries, keys, values, q_feature, k_feature, window_factor):
    tok = queries.shape[0]
    seq, sides = lax.axis_size("seq"), lax.axis_size("head")
    wq, wk = jnp.swapaxes(q_feature, 1, 2), jnp.swapaxes(k_feature, 1, 2)
    if keys.shape[1] == WAYS * DH and seq == 4 * WAYS and sides == 2 and tok == WINDOW:
        return by_levels(queries, keys, values, wq, wk, window_factor)
    ratio = window_factor / (1.0 - window_factor)
    return by_blocks(queries, keys, values, wq, wk, ratio)


def solution(mesh):
    return jax.shard_map(
        local,
        mesh=mesh,
        in_specs=(
            P("seq", "head"),
            P("seq", "head"),
            P("seq", "head"),
            P("head", None, None),
            P("head", None, None),
            P("head"),
        ),
        out_specs=P(("seq", "head"), None),
        check_vma=False,
    )
```

```python
import math

import jax
import jax.numpy as jnp
from jax import lax
from jax.experimental import pallas as pl
from jax.experimental.pallas import tpu as pltpu
from jax.sharding import PartitionSpec as P

DH = 128
WINDOW = 64
F32 = jnp.float32
BF16 = jnp.bfloat16


def dot_t(a, b):
    return lax.dot_general(a, b, (((1,), (1,)), ((), ())), preferred_element_type=F32)


def features_t(logits):
    top = jnp.max(logits, axis=0, keepdims=True)
    low = jnp.min(logits, axis=0, keepdims=True)
    up = jnp.exp(logits - top)
    down = jnp.exp(low - logits)
    up = up * (1.0 / jnp.sum(up, axis=0, keepdims=True))
    down = down * (1.0 / jnp.sum(down, axis=0, keepdims=True))
    return jnp.concatenate([up.astype(BF16), down.astype(BF16)], axis=0)


def mix_kernel(
    place_ref, q_ref, k_ref, v_ref, wq_ref, wk_ref, ratio_ref, out_ref, fk_scr, state_scr
):
    tok = q_ref.shape[0]
    heads, feat, dh = wq_ref.shape
    seen = fk_scr.shape[1]
    place = place_ref[0]
    first_head = pl.program_id(0) * heads

    weights = wk_ref[...].reshape(heads * feat, dh)
    for start in range(0, seen, 256):
        size = min(256, seen - start)
        logits = dot_t(weights, k_ref[start : start + size, :])
        for h in range(heads):
            fk_scr[h * 2 * feat : (h + 1) * 2 * feat, start : start + size] = features_t(
                logits[h * feat : (h + 1) * feat]
            )
    row = lax.broadcasted_iota(jnp.int32, (seen, dh), 0)
    kept = row < (place - 1) * tok
    v_seen = jnp.where(kept, v_ref[:seen, :].astype(F32), 0.0).astype(BF16)
    ones_seen = jnp.where(kept, 1.0, 0.0).astype(BF16)
    v_seen = jnp.concatenate([v_seen, ones_seen], axis=1)
    state_scr[...] = jnp.dot(fk_scr[...], v_seen, preferred_element_type=F32).astype(BF16)

    before = pl.multiple_of(jnp.maximum(place - 1, 0) * tok, tok)
    own = pl.multiple_of(place * tok, tok)
    k_ext = jnp.concatenate([k_ref[pl.ds(before, tok), :], k_ref[pl.ds(own, tok), :]], axis=0)
    v_ext = jnp.concatenate([v_ref[pl.ds(before, tok), :], v_ref[pl.ds(own, tok), :]], axis=0)
    v_ext = jnp.concatenate([v_ext, jnp.ones_like(v_ext)], axis=1)
    row = lax.broadcasted_iota(jnp.int32, (tok, 2 * tok), 0)
    col = lax.broadcasted_iota(jnp.int32, (tok, 2 * tok), 1)
    valid = (col >= tok) | (place > 0)
    inside = (col > row) & (col <= row + WINDOW) & valid
    causal = (col <= row) & valid
    lane = lax.broadcasted_iota(jnp.int32, (tok, 2 * feat), 1)
    left = lane < feat
    side_r = lax.broadcasted_iota(jnp.int32, (2 * feat, 2 * feat), 0) < feat
    side_c = lax.broadcasted_iota(jnp.int32, (2 * feat, 2 * feat), 1) < feat
    halves = jnp.where(side_r == side_c, 1.0, 0.0).astype(BF16)

    for h in range(heads):
        q = q_ref[:, h * dh : (h + 1) * dh]
        wq = wq_ref[h]
        logits = dot_t(q, jnp.concatenate([wq, -wq], axis=0))
        top_l = jnp.max(jnp.where(left, logits, -jnp.inf), axis=1, keepdims=True)
        top_r = jnp.max(jnp.where(left, -jnp.inf, logits), axis=1, keepdims=True)
        expd = jnp.exp(logits - jnp.where(left, top_l, top_r)).astype(BF16)
        total = jnp.dot(expd, halves, preferred_element_type=F32)
        fq = (expd.astype(F32) / total).astype(BF16)
        fk = features_t(dot_t(wk_ref[h], k_ext))
        linear = jnp.dot(fq, fk, preferred_element_type=F32)
        scores = dot_t(q, k_ext) * (1.0 / math.sqrt(dh))
        masked = jnp.where(inside, scores, -jnp.inf)
        top = jnp.max(masked, axis=1, keepdims=True)
        soft = jnp.exp(masked - top) * ratio_ref[first_head + h]
        weight = jnp.where(causal, linear, soft).astype(BF16)
        both = jnp.dot(weight, v_ext, preferred_element_type=F32) + jnp.dot(
            fq, state_scr[h * 2 * feat : (h + 1) * 2 * feat, :], preferred_element_type=F32
        )
        out_ref[:, h * dh : (h + 1) * dh] = (both[:, :dh] / both[:, dh:]).astype(BF16)


def mix(place, queries, kv, wq, wk, ratio, group):
    tok = queries.shape[0]
    local_heads, feat, dh = wq.shape
    groups = local_heads // group
    tokens = kv.shape[0]
    seen = tokens - 2 * tok
    return pl.pallas_call(
        mix_kernel,
        grid_spec=pltpu.PrefetchScalarGridSpec(
            num_scalar_prefetch=1,
            grid=(groups,),
            in_specs=[
                pl.BlockSpec((tok, group * dh), lambda g, p: (0, g)),
                pl.BlockSpec((tokens, dh), lambda g, p: (0, g)),
                pl.BlockSpec((tokens, dh), lambda g, p: (0, groups + g)),
                pl.BlockSpec((group, feat, dh), lambda g, p: (g, 0, 0)),
                pl.BlockSpec((group, feat, dh), lambda g, p: (g, 0, 0)),
                pl.BlockSpec(memory_space=pltpu.SMEM),
            ],
            out_specs=pl.BlockSpec((tok, group * dh), lambda g, p: (0, g)),
            scratch_shapes=[
                pltpu.VMEM((group * 2 * feat, seen), BF16),
                pltpu.VMEM((group * 2 * feat, 2 * dh), BF16),
            ],
        ),
        out_shape=jax.ShapeDtypeStruct(queries.shape, BF16),
        compiler_params=pltpu.CompilerParams(vmem_limit_bytes=48 * 2**20),
        cost_estimate=pl.CostEstimate(
            flops=2 * local_heads * tokens * 3 * feat * 2 * dh,
            bytes_accessed=8 * 2**20,
            transcendentals=local_heads * tokens * 2 * feat,
        ),
    )(place, queries, kv, kv, wq, wk, ratio)


WAYS = 4


SLOTS = (
    ((0, 0), (0, 0)),
    ((2, 1), (2, 1)),
    ((2, 0), (0, 1)),
    ((0, 1), (2, 0)),
    ((3, 1), (3, 1)),
    ((3, 0), (1, 1)),
    ((1, 1), (3, 0)),
    ((1, 0), (1, 0)),
)


def slot_of(n, odd):
    return [jnp.where(odd == 1, b, a) if a != b else a for a, b in zip(*SLOTS[n])]


def spot():
    at = lax.axis_index("seq")
    return lax.rem(at, WAYS), lax.div(at, WAYS)


def aligned(at, step):
    return pl.ds(pl.multiple_of(at * step, step), step)


def with_ones(values, kept):
    here = jnp.where(kept, 1.0, 0.0).astype(BF16)
    return jnp.concatenate([values, jnp.full(values.shape, here)], axis=1)


def pack_kv_kernel(k_ref, v_ref, own_ref, away_ref):
    place = spot()[0]
    for d in range(WAYS):
        ref, at = (own_ref, away_ref)[d // 2], d % 2 * 2 * DH
        ref[:, at : at + DH] = k_ref[:, aligned(place ^ d, DH)]
        ref[:, at + DH : at + 2 * DH] = v_ref[:, aligned(place ^ d, DH)]


def pair_kernel(own_ref, got_ref, out_ref):
    tok = own_ref.shape[0]
    out_ref[:tok, :] = own_ref[:, 2 * DH :]
    out_ref[tok:, :] = got_ref[:, 2 * DH :]


def stack_kernel(own_ref, got_ref, pair_ref, out_ref):
    tok = own_ref.shape[0]
    place = spot()[0]
    out_ref[aligned(place, tok), :] = own_ref[:, : 2 * DH]
    out_ref[aligned(place ^ 2, tok), :] = got_ref[:, : 2 * DH]
    out_ref[aligned(place ^ 1, tok), :] = pair_ref[:tok, :]
    out_ref[aligned(place ^ 3, tok), :] = pair_ref[tok:, :]


def pack_q_kernel(q_ref, *out_refs):
    place = spot()[0]
    for d, out in enumerate(out_refs):
        out[...] = q_ref[:, aligned(place ^ d, out.shape[1])]


def weights_kernel(wq_ref, both_ref):
    for h in range(wq_ref.shape[0]):
        wq = wq_ref[h].T
        both_ref[h] = jnp.concatenate([wq, -wq], axis=1)


def join_kernel(slots, *refs):
    got, out_ref, sems = refs[: len(slots)], *refs[-2:]
    width = got[0].shape[1]
    place, side = spot()[0], lax.axis_index("head")
    copies = []
    for n, ref in zip(slots, got):
        dr, dy = slot_of(n, lax.rem(place, 2) ^ (SLOTS[n][0][0] & 1))
        at = aligned((side ^ dy) * WAYS + (place ^ dr), width)
        copies.append(pltpu.make_async_copy(ref, out_ref.at[:, at], sems.at[len(copies)]))
    for copy in copies:
        copy.start()
    for copy in copies:
        copy.wait()


def write_key_features(keys, wk_ref, fk_ref):
    heads, feat, dh = wk_ref.shape
    logits = dot_t(wk_ref[...].reshape(heads * feat, dh), keys)
    for h in range(heads):
        part = logits[h * feat : (h + 1) * feat]
        top = jnp.max(part, axis=0, keepdims=True)
        low = jnp.min(part, axis=0, keepdims=True)
        for n, shifted in enumerate((part - top, low - part)):
            row = (2 * h + n) * feat
            expd = jnp.exp(shifted.astype(BF16))
            total = expd[: feat // 4]
            for q in range(1, 4):
                total = total + expd[q * feat // 4 : (q + 1) * feat // 4]
            total = jnp.sum(total.astype(F32), axis=0, keepdims=True)
            fk_ref[row : row + feat, :] = expd * pl.reciprocal(total).astype(BF16)


def near_features_kernel(last_ref, own_ref, wk_ref, fk_ref, past_ref, step_ref):
    level = spot()[1]
    half = last_ref.shape[0] // 2
    keys = jnp.concatenate([last_ref[:, :DH], own_ref[:, :DH]], axis=0)
    write_key_features(keys, wk_ref, fk_ref)
    for at, ref in ((0, past_ref), (half, step_ref)):
        ref[...] = jnp.dot(
            fk_ref[:, at : at + half],
            with_ones(last_ref[at : at + half, DH:], level >= 1),
            preferred_element_type=F32,
        )


def past_kernel(before_ref, wk_ref, sum_ref, past_ref, fk_scr):
    write_key_features(before_ref[:, :DH], wk_ref, fk_scr)
    past_ref[...] = sum_ref[...] + jnp.dot(
        fk_scr[...],
        with_ones(before_ref[:, DH:], spot()[1] >= 2),
        preferred_element_type=F32,
    )


def query_features_kernel(factor_ref, a_ref, b_ref, w_ref, q_out, fq_out, logit_scr, exp_scr):
    tok = a_ref.shape[0]
    heads, dh, both = w_ref.shape
    half = 2 * tok
    place = spot()[0]
    for d, ref in enumerate((a_ref, b_ref)):
        row = pl.multiple_of(lax.rem(place ^ d, 2) * tok, tok)
        for h in range(heads):
            q_out[pl.ds(h * half + row, tok), :] = ref[:, h * dh : (h + 1) * dh]
    rows_of = [slice(h * half, (h + 1) * half) for h in range(heads)]
    largest = jnp.zeros((half, both), F32)
    for h, rows in enumerate(rows_of):
        logits = jnp.dot(q_out[rows, :], w_ref[h], preferred_element_type=F32)
        logit_scr[rows, :] = logits
        largest = jnp.maximum(largest, logits)
    small = jnp.max(largest) <= 60.0

    @pl.when(small)
    def _():
        exp_scr[...] = jnp.exp(logit_scr[...]).astype(BF16)

    @pl.when(jnp.logical_not(small))
    def _():
        left = lax.broadcasted_iota(jnp.int32, (half, both), 1) < both // 2
        for rows in rows_of:
            logits = logit_scr[rows, :]
            top_l = jnp.max(jnp.where(left, logits, -jnp.inf), axis=1, keepdims=True)
            top_r = jnp.max(jnp.where(left, -jnp.inf, logits), axis=1, keepdims=True)
            exp_scr[rows, :] = jnp.exp(logits - jnp.where(left, top_l, top_r)).astype(BF16)

    side_r = lax.broadcasted_iota(jnp.int32, (both, both), 0) < both // 2
    side_c = lax.broadcasted_iota(jnp.int32, (both, both), 1) < both // 2
    halves = jnp.where(side_r == side_c, 1.0, 0.0).astype(BF16)
    total = jnp.dot(exp_scr[...], halves, preferred_element_type=F32)
    for h, rows in enumerate(rows_of):
        factor = jnp.full((1, both), factor_ref[place * heads + h])
        scale = pl.reciprocal(total[rows], approx=True) * ((1.0 - factor) / factor)
        fq_out[rows, :] = (exp_scr[rows, :].astype(F32) * scale).astype(BF16)


def near_kernel(other, q_ref, fq_ref, last_ref, own_ref, fk_ref, near_ref, kv_scr, w_scr):
    half, dh = last_ref.shape[0] // 2, q_ref.shape[1]
    heads = q_ref.shape[0] // half
    feats = fq_ref.shape[1]
    place, level = spot()
    u = lax.div(place, 2) ^ other
    kv_scr[:half, :] = last_ref[half:, :]
    kv_scr[half:, :] = own_ref[...]
    at = pl.ds(pl.multiple_of(u * half, half), 2 * half)
    keys, values = kv_scr[at, :dh], kv_scr[at, dh:]
    fk_at = pl.ds(pl.multiple_of((u + 1) * half, half), 2 * half)
    known = (level > 0) | (u > 0)
    cut = half - WINDOW
    row = lax.broadcasted_iota(jnp.int32, (WINDOW, 2 * half), 0)
    col = lax.broadcasted_iota(jnp.int32, (WINDOW, 2 * half), 1)
    inside = (col > row + cut) & (col <= row + half) & ((col >= half) | known)
    causal = (col <= row + cut)[:, :half]
    row, col = row[:, :half], col[:, :half]
    inside_low = (col > row) & (col <= row + WINDOW)
    causal_low = col <= row
    scores = dot_t(q_ref[...], keys)
    scale = math.log2(math.e) / math.sqrt(dh)

    def window(part, kept):
        masked = jnp.where(kept, part, -jnp.inf)
        top = jnp.max(masked, axis=1, keepdims=True)
        return jnp.exp2(((masked - top) * scale).astype(BF16))

    for h in range(heads):
        here = slice(h * half, (h + 1) * half)
        up, low = slice(h * half, h * half + cut), slice(h * half + cut, (h + 1) * half)
        linear = jnp.dot(
            fq_ref[here, :],
            fk_ref[h * feats : (h + 1) * feats, fk_at],
            preferred_element_type=F32,
        )
        soft = window(scores[up], inside)
        w_scr[up, :half] = soft[:, :half] + jnp.where(causal, linear[:cut, :half], 0.0).astype(BF16)
        w_scr[up, half:] = soft[:, half:]
        soft = window(scores[low, half:], inside_low)
        w_scr[low, :half] = linear[cut:, :half].astype(BF16)
        w_scr[low, half:] = soft + jnp.where(causal_low, linear[cut:, half:], 0.0).astype(BF16)
    values = jnp.concatenate(
        [with_ones(values[:half], known), with_ones(values[half:], level >= 0)], axis=0
    )
    near_ref[...] = jnp.dot(w_scr[...], values, preferred_element_type=F32)


def mix_kernel_of_level(*refs):
    near_refs, fq_refs, (past_ref, step_ref, wk_ref) = refs[:2], refs[2:4], refs[4:7]
    first_ref, refs = refs[7], refs[8:]
    out_refs, (fk_scr, state_scr, out_scr) = refs[:-3], refs[-3:]
    rows, dh = near_refs[0].shape[0], near_refs[0].shape[1] // 2
    feats = fq_refs[0].shape[1]
    heads = past_ref.shape[0] // feats
    half = rows // heads
    place, level = spot()
    side = lax.axis_index("head")
    u = lax.div(place, 2)

    write_key_features(first_ref[:, :dh], wk_ref, fk_scr)
    state = past_ref[...] + jnp.dot(
        fk_scr[...], with_ones(first_ref[:, dh:], level >= 3), preferred_element_type=F32
    )
    state_scr[0] = state.astype(BF16)
    state_scr[1] = (state + step_ref[...]).astype(BF16)
    part = out_refs[0].shape[0]
    for other in (1, 0):
        for h in range(heads):
            here = slice(h * half, (h + 1) * half)
            far = jnp.dot(
                fq_refs[other][here, :],
                state_scr[u ^ other, h * feats : (h + 1) * feats, :],
                preferred_element_type=F32,
            )
            both = near_refs[other][here, :] + far
            out_scr[aligned(u ^ other, half), h * dh : (h + 1) * dh] = (
                both[:, :dh] * pl.reciprocal(both[:, dh:], approx=True)
            ).astype(BF16)
    for n, ref in enumerate(out_refs):
        dr, dy = slot_of(n, lax.rem(place, 2))
        ref[...] = out_scr[aligned((place ^ dr) * 2 + (side ^ dy), part), :]


def whole_spec(space=pltpu.VMEM):
    return pl.BlockSpec(memory_space=space)


def call(kernel, ins, outs, name, scratch=(), limit=4, out_type=BF16, scalars=()):
    return pl.pallas_call(
        kernel,
        in_specs=[whole_spec(pltpu.SMEM) for _ in scalars] + [whole_spec() for _ in ins],
        out_specs=[whole_spec() for _ in outs],
        out_shape=[
            jax.ShapeDtypeStruct(s, out_type[n] if isinstance(out_type, list) else out_type)
            for n, s in enumerate(outs)
        ],
        scratch_shapes=list(scratch),
        compiler_params=pltpu.CompilerParams(vmem_limit_bytes=limit * 2**20),
        name=name,
    )(*scalars, *ins)


def by_levels(queries, keys, values, wq, wk, factor):
    tok, width = queries.shape
    local_heads, feat, dh = wq.shape
    heads = local_heads // WAYS
    seq, sides = lax.axis_size("seq"), lax.axis_size("head")
    half = 2 * tok
    rows, states = heads * half, heads * 2 * feat

    def partner(x, dr, dy=0):
        pairs = [
            (i * sides + j, (i // WAYS * WAYS + (i % WAYS ^ dr)) * sides + (j ^ dy))
            for i in range(seq)
            for j in range(sides)
        ]
        return lax.ppermute(x, ("seq", "head"), pairs)

    def levels_back(x, by):
        pairs = [(i, i + by * WAYS) for i in range(seq - by * WAYS)]
        return lax.ppermute(x, "seq", pairs)

    own, away = call(pack_kv_kernel, [keys, values], [(tok, 4 * dh)] * 2, "pack_kv")
    got = partner(away, 2)
    q = list(call(pack_q_kernel, [queries], [(tok, width // WAYS)] * WAYS, "pack_q"))
    (pair,) = call(pair_kernel, [own, got], [(half, 2 * dh)], "pair_kv")
    *q, pair = lax.optimization_barrier((*q, pair))
    pair = partner(pair, 1)
    q[1], q[2], q[3] = partner(q[1], 1), partner(q[2], 2), partner(q[3], 3)
    (kv,) = call(stack_kernel, [own, got, pair], [(2 * half, 2 * dh)], "stack_kv")
    last = levels_back(kv, 1)
    wq, wk, kv, q[1] = lax.optimization_barrier((wq, wk, kv, q[1]))
    before = levels_back(kv, 2)

    at = lax.rem(lax.axis_index("seq"), WAYS) * heads
    wk = lax.dynamic_slice_in_dim(wk, at, heads)
    (wq,) = call(
        weights_kernel,
        [lax.dynamic_slice_in_dim(wq, at, heads)],
        [(heads, dh, 2 * feat)],
        "weights",
    )
    def query_features(a, b):
        return call(
            query_features_kernel,
            [a, b, wq],
            [(rows, dh), (rows, 2 * feat)],
            "query_features",
            [pltpu.VMEM((rows, 2 * feat), F32), pltpu.VMEM((rows, 2 * feat), BF16)],
            12,
            scalars=[factor],
        )

    def near(other, q_rows, fq, fk):
        return call(
            lambda *refs: near_kernel(other, *refs),
            [q_rows, fq, last, kv, fk],
            [(rows, 2 * dh)],
            "near",
            [pltpu.VMEM((3 * half, 2 * dh), BF16), pltpu.VMEM((rows, 2 * half), BF16)],
            16,
            F32,
        )[0]

    q_own, fq_own = query_features(q[0], q[1])
    far_kv, last, wk, fq_own = lax.optimization_barrier((kv, last, wk, fq_own))
    first = levels_back(far_kv, 3)
    fk_near, past, step = call(
        near_features_kernel,
        [last, kv, wk],
        [(states, 4 * half), (states, 2 * dh), (states, 2 * dh)],
        "near_features",
        limit=20,
        out_type=[BF16, F32, F32],
    )
    near_own = near(0, q_own, fq_own, fk_near)
    q[2], q[3], near_own = lax.optimization_barrier((q[2], q[3], near_own))
    q_other, fq_other = query_features(q[2], q[3])
    near_other = near(1, q_other, fq_other, fk_near)
    before, near_other = lax.optimization_barrier((before, near_other))
    (past,) = call(
        past_kernel,
        [before, wk, past],
        [(states, 2 * dh)],
        "past",
        [pltpu.VMEM((states, 2 * half), BF16)],
        16,
        F32,
    )
    first, near_other, past = lax.optimization_barrier((first, near_other, past))
    part = tok // sides
    outs = call(
        mix_kernel_of_level,
        [near_own, near_other, fq_own, fq_other, past, step, wk, first],
        [(part, heads * dh)] * (WAYS * sides),
        "mix_level",
        [
            pltpu.VMEM((states, 2 * half), BF16),
            pltpu.VMEM((2, states, 2 * dh), BF16),
            pltpu.VMEM((2 * half, heads * dh), BF16),
        ],
        24,
    )

    def sent(x, slot):
        pairs = []
        for i in range(seq):
            dr, dy = slot[i % 2]
            to = i // WAYS * WAYS + (i % WAYS ^ dr)
            pairs += [(i * sides + j, to * sides + (j ^ dy)) for j in range(sides)]
        return lax.ppermute(x, ("seq", "head"), pairs)

    outs = [outs[0]] + [sent(x, slot) for x, slot in zip(outs[1:], SLOTS[1:])]

    def joined(slots, into):
        return pl.pallas_call(
            lambda *refs: join_kernel(slots, *refs),
            in_specs=[whole_spec()] * len(slots) + [whole_spec(pltpu.HBM)] * len(into),
            out_specs=whole_spec(pltpu.HBM),
            out_shape=jax.ShapeDtypeStruct((part, sides * WAYS * heads * dh), BF16),
            input_output_aliases={len(slots): 0} if into else {},
            scratch_shapes=[pltpu.SemaphoreType.DMA((len(slots),))],
            compiler_params=pltpu.CompilerParams(vmem_limit_bytes=4 * 2**20),
            name="join",
        )(*[outs[n] for n in slots], *into)

    return joined((6, 7), [joined(range(6), [])])


def by_blocks(queries, keys, values, wq, wk, ratio):
    group = wq.shape[0] // (keys.shape[1] // DH)
    place = lax.axis_index("seq").astype(jnp.int32).reshape(1)
    kv = lax.all_gather(jnp.concatenate([keys, values], axis=1), "seq", tiled=True)
    out = mix(place, queries, kv, wq, wk, ratio, group)
    return lax.all_to_all(out, "head", split_axis=0, concat_axis=1, tiled=True)


def local(queries, keys, values, q_feature, k_feature, window_factor):
    tok = queries.shape[0]
    seq, sides = lax.axis_size("seq"), lax.axis_size("head")
    wq, wk = jnp.swapaxes(q_feature, 1, 2), jnp.swapaxes(k_feature, 1, 2)
    if keys.shape[1] == WAYS * DH and seq == 4 * WAYS and sides == 2 and tok == WINDOW:
        return by_levels(queries, keys, values, wq, wk, window_factor)
    ratio = window_factor / (1.0 - window_factor)
    return by_blocks(queries, keys, values, wq, wk, ratio)


def solution(mesh):
    return jax.shard_map(
        local,
        mesh=mesh,
        in_specs=(
            P("seq", "head"),
            P("seq", "head"),
            P("seq", "head"),
            P("head", None, None),
            P("head", None, None),
            P("head"),
        ),
        out_specs=P(("seq", "head"), None),
        check_vma=False,
    )
```

```python
import math

import jax
import jax.numpy as jnp
from jax import lax
from jax.experimental import pallas as pl
from jax.experimental.pallas import tpu as pltpu
from jax.sharding import PartitionSpec as P

DH = 128
WINDOW = 64
F32 = jnp.float32
BF16 = jnp.bfloat16


def dot_t(a, b):
    return lax.dot_general(a, b, (((1,), (1,)), ((), ())), preferred_element_type=F32)


def features_t(logits):
    top = jnp.max(logits, axis=0, keepdims=True)
    low = jnp.min(logits, axis=0, keepdims=True)
    up = jnp.exp(logits - top)
    down = jnp.exp(low - logits)
    up = up * (1.0 / jnp.sum(up, axis=0, keepdims=True))
    down = down * (1.0 / jnp.sum(down, axis=0, keepdims=True))
    return jnp.concatenate([up.astype(BF16), down.astype(BF16)], axis=0)


def mix_kernel(
    place_ref, q_ref, k_ref, v_ref, wq_ref, wk_ref, ratio_ref, out_ref, fk_scr, state_scr
):
    tok = q_ref.shape[0]
    heads, feat, dh = wq_ref.shape
    seen = fk_scr.shape[1]
    place = place_ref[0]
    first_head = pl.program_id(0) * heads

    weights = wk_ref[...].reshape(heads * feat, dh)
    for start in range(0, seen, 256):
        size = min(256, seen - start)
        logits = dot_t(weights, k_ref[start : start + size, :])
        for h in range(heads):
            fk_scr[h * 2 * feat : (h + 1) * 2 * feat, start : start + size] = features_t(
                logits[h * feat : (h + 1) * feat]
            )
    row = lax.broadcasted_iota(jnp.int32, (seen, dh), 0)
    kept = row < (place - 1) * tok
    v_seen = jnp.where(kept, v_ref[:seen, :].astype(F32), 0.0).astype(BF16)
    ones_seen = jnp.where(kept, 1.0, 0.0).astype(BF16)
    v_seen = jnp.concatenate([v_seen, ones_seen], axis=1)
    state_scr[...] = jnp.dot(fk_scr[...], v_seen, preferred_element_type=F32).astype(BF16)

    before = pl.multiple_of(jnp.maximum(place - 1, 0) * tok, tok)
    own = pl.multiple_of(place * tok, tok)
    k_ext = jnp.concatenate([k_ref[pl.ds(before, tok), :], k_ref[pl.ds(own, tok), :]], axis=0)
    v_ext = jnp.concatenate([v_ref[pl.ds(before, tok), :], v_ref[pl.ds(own, tok), :]], axis=0)
    v_ext = jnp.concatenate([v_ext, jnp.ones_like(v_ext)], axis=1)
    row = lax.broadcasted_iota(jnp.int32, (tok, 2 * tok), 0)
    col = lax.broadcasted_iota(jnp.int32, (tok, 2 * tok), 1)
    valid = (col >= tok) | (place > 0)
    inside = (col > row) & (col <= row + WINDOW) & valid
    causal = (col <= row) & valid
    lane = lax.broadcasted_iota(jnp.int32, (tok, 2 * feat), 1)
    left = lane < feat
    side_r = lax.broadcasted_iota(jnp.int32, (2 * feat, 2 * feat), 0) < feat
    side_c = lax.broadcasted_iota(jnp.int32, (2 * feat, 2 * feat), 1) < feat
    halves = jnp.where(side_r == side_c, 1.0, 0.0).astype(BF16)

    for h in range(heads):
        q = q_ref[:, h * dh : (h + 1) * dh]
        wq = wq_ref[h]
        logits = dot_t(q, jnp.concatenate([wq, -wq], axis=0))
        top_l = jnp.max(jnp.where(left, logits, -jnp.inf), axis=1, keepdims=True)
        top_r = jnp.max(jnp.where(left, -jnp.inf, logits), axis=1, keepdims=True)
        expd = jnp.exp(logits - jnp.where(left, top_l, top_r)).astype(BF16)
        total = jnp.dot(expd, halves, preferred_element_type=F32)
        fq = (expd.astype(F32) / total).astype(BF16)
        fk = features_t(dot_t(wk_ref[h], k_ext))
        linear = jnp.dot(fq, fk, preferred_element_type=F32)
        scores = dot_t(q, k_ext) * (1.0 / math.sqrt(dh))
        masked = jnp.where(inside, scores, -jnp.inf)
        top = jnp.max(masked, axis=1, keepdims=True)
        soft = jnp.exp(masked - top) * ratio_ref[first_head + h]
        weight = jnp.where(causal, linear, soft).astype(BF16)
        both = jnp.dot(weight, v_ext, preferred_element_type=F32) + jnp.dot(
            fq, state_scr[h * 2 * feat : (h + 1) * 2 * feat, :], preferred_element_type=F32
        )
        out_ref[:, h * dh : (h + 1) * dh] = (both[:, :dh] / both[:, dh:]).astype(BF16)


def mix(place, queries, kv, wq, wk, ratio, group):
    tok = queries.shape[0]
    local_heads, feat, dh = wq.shape
    groups = local_heads // group
    tokens = kv.shape[0]
    seen = tokens - 2 * tok
    return pl.pallas_call(
        mix_kernel,
        grid_spec=pltpu.PrefetchScalarGridSpec(
            num_scalar_prefetch=1,
            grid=(groups,),
            in_specs=[
                pl.BlockSpec((tok, group * dh), lambda g, p: (0, g)),
                pl.BlockSpec((tokens, dh), lambda g, p: (0, g)),
                pl.BlockSpec((tokens, dh), lambda g, p: (0, groups + g)),
                pl.BlockSpec((group, feat, dh), lambda g, p: (g, 0, 0)),
                pl.BlockSpec((group, feat, dh), lambda g, p: (g, 0, 0)),
                pl.BlockSpec(memory_space=pltpu.SMEM),
            ],
            out_specs=pl.BlockSpec((tok, group * dh), lambda g, p: (0, g)),
            scratch_shapes=[
                pltpu.VMEM((group * 2 * feat, seen), BF16),
                pltpu.VMEM((group * 2 * feat, 2 * dh), BF16),
            ],
        ),
        out_shape=jax.ShapeDtypeStruct(queries.shape, BF16),
        compiler_params=pltpu.CompilerParams(vmem_limit_bytes=48 * 2**20),
        cost_estimate=pl.CostEstimate(
            flops=2 * local_heads * tokens * 3 * feat * 2 * dh,
            bytes_accessed=8 * 2**20,
            transcendentals=local_heads * tokens * 2 * feat,
        ),
    )(place, queries, kv, kv, wq, wk, ratio)


WAYS = 4


SLOTS = (
    ((0, 0), (0, 0)),
    ((2, 1), (2, 1)),
    ((2, 0), (0, 1)),
    ((0, 1), (2, 0)),
    ((3, 1), (3, 1)),
    ((3, 0), (1, 1)),
    ((1, 1), (3, 0)),
    ((1, 0), (1, 0)),
)


def slot_of(n, odd):
    return [jnp.where(odd == 1, b, a) if a != b else a for a, b in zip(*SLOTS[n])]


def spot():
    at = lax.axis_index("seq")
    return lax.rem(at, WAYS), lax.div(at, WAYS)


def aligned(at, step):
    return pl.ds(pl.multiple_of(at * step, step), step)


def with_ones(values, kept=True):
    here = jnp.where(kept, 1.0, 0.0).astype(BF16)
    return jnp.concatenate([values, jnp.full(values.shape, here)], axis=1)


def pack_kv_kernel(k_ref, v_ref, own_ref, away_ref):
    place = spot()[0]
    for d in range(WAYS):
        ref, at = (own_ref, away_ref)[d // 2], d % 2 * 2 * DH
        ref[:, at : at + DH] = k_ref[:, aligned(place ^ d, DH)]
        ref[:, at + DH : at + 2 * DH] = v_ref[:, aligned(place ^ d, DH)]


def pair_kernel(own_ref, got_ref, out_ref):
    tok = own_ref.shape[0]
    out_ref[:tok, :] = own_ref[:, 2 * DH :]
    out_ref[tok:, :] = got_ref[:, 2 * DH :]


def stack_kernel(own_ref, got_ref, pair_ref, out_ref):
    tok = own_ref.shape[0]
    place = spot()[0]
    out_ref[aligned(place, tok), :] = own_ref[:, : 2 * DH]
    out_ref[aligned(place ^ 2, tok), :] = got_ref[:, : 2 * DH]
    out_ref[aligned(place ^ 1, tok), :] = pair_ref[:tok, :]
    out_ref[aligned(place ^ 3, tok), :] = pair_ref[tok:, :]


def pack_q_kernel(q_ref, *out_refs):
    place = spot()[0]
    for d, out in enumerate(out_refs):
        out[...] = q_ref[:, aligned(place ^ d, out.shape[1])]


def weights_kernel(wq_ref, both_ref):
    for h in range(wq_ref.shape[0]):
        wq = wq_ref[h].T
        both_ref[h] = jnp.concatenate([wq, -wq], axis=1)


def join_kernel(*refs):
    got, out_ref, sems = refs[:-2], *refs[-2:]
    width = got[0].shape[1]
    place, side = spot()[0], lax.axis_index("head")
    copies = []
    for n, ref in enumerate(got):
        dr, dy = slot_of(n, lax.rem(place, 2) ^ (SLOTS[n][0][0] & 1))
        at = aligned((side ^ dy) * WAYS + (place ^ dr), width)
        copies.append(pltpu.make_async_copy(ref, out_ref.at[:, at], sems.at[n]))
    for copy in copies:
        copy.start()
    for copy in copies:
        copy.wait()


def write_key_features(keys, wk_ref, fk_ref):
    heads, feat, dh = wk_ref.shape
    logits = dot_t(wk_ref[...].reshape(heads * feat, dh), keys)
    for h in range(heads):
        part = logits[h * feat : (h + 1) * feat]
        top = jnp.max(part, axis=0, keepdims=True)
        low = jnp.min(part, axis=0, keepdims=True)
        for n, shifted in enumerate((part - top, low - part)):
            row = (2 * h + n) * feat
            expd = jnp.exp(shifted.astype(BF16))
            total = expd[: feat // 4]
            for q in range(1, 4):
                total = total + expd[q * feat // 4 : (q + 1) * feat // 4]
            total = jnp.sum(total.astype(F32), axis=0, keepdims=True)
            fk_ref[row : row + feat, :] = expd * pl.reciprocal(total).astype(BF16)


def own_features_kernel(own_ref, wk_ref, fk_ref):
    write_key_features(own_ref[:, :DH], wk_ref, fk_ref)


def last_features_kernel(last_ref, wk_ref, fk_ref, past_ref, step_ref):
    half = last_ref.shape[0] // 2
    level = spot()[1]

    @pl.when(level == 0)
    def _():
        for ref in (fk_ref, past_ref, step_ref):
            ref[...] = jnp.zeros_like(ref)

    @pl.when(level > 0)
    def _():
        write_key_features(last_ref[:, :DH], wk_ref, fk_ref)
        for at, ref in ((0, past_ref), (half, step_ref)):
            ref[...] = jnp.dot(
                fk_ref[:, at : at + half],
                with_ones(last_ref[at : at + half, DH:]),
                preferred_element_type=F32,
            )


def past_kernel(before_ref, wk_ref, sum_ref, past_ref, fk_scr):
    level = spot()[1]

    @pl.when(level < 2)
    def _():
        past_ref[...] = sum_ref[...]

    @pl.when(level >= 2)
    def _():
        write_key_features(before_ref[:, :DH], wk_ref, fk_scr)
        past_ref[...] = sum_ref[...] + jnp.dot(
            fk_scr[...], with_ones(before_ref[:, DH:]), preferred_element_type=F32
        )


def query_features_kernel(factor_ref, a_ref, b_ref, w_ref, q_out, fq_out, exp_scr):
    tok = a_ref.shape[0]
    heads, dh, both = w_ref.shape
    half = 2 * tok
    place = spot()[0]
    for d, ref in enumerate((a_ref, b_ref)):
        row = pl.multiple_of(lax.rem(place ^ d, 2) * tok, tok)
        for h in range(heads):
            q_out[pl.ds(h * half + row, tok), :] = ref[:, h * dh : (h + 1) * dh]
    rows_of = [slice(h * half, (h + 1) * half) for h in range(heads)]
    left = lax.broadcasted_iota(jnp.int32, (half, both), 1) < both // 2
    for h, rows in enumerate(rows_of):
        logits = jnp.dot(q_out[rows, :], w_ref[h], preferred_element_type=F32)
        top_l = jnp.max(jnp.where(left, logits, -jnp.inf), axis=1, keepdims=True)
        top_r = jnp.max(jnp.where(left, -jnp.inf, logits), axis=1, keepdims=True)
        exp_scr[rows, :] = jnp.exp((logits - jnp.where(left, top_l, top_r)).astype(BF16))
    side_r = lax.broadcasted_iota(jnp.int32, (both, both), 0) < both // 2
    side_c = lax.broadcasted_iota(jnp.int32, (both, both), 1) < both // 2
    halves = jnp.where(side_r == side_c, 1.0, 0.0).astype(BF16)
    total = jnp.dot(exp_scr[...], halves, preferred_element_type=F32)
    for h, rows in enumerate(rows_of):
        factor = jnp.full((1, both), factor_ref[place * heads + h])
        scale = pl.reciprocal(total[rows], approx=True) * ((1.0 - factor) / factor)
        fq_out[rows, :] = (exp_scr[rows, :].astype(F32) * scale).astype(BF16)


def near_kernel(
    other, q_ref, fq_ref, last_ref, own_ref, fk_last_ref, fk_own_ref, near_ref, kv_scr, fk_scr, w_scr
):
    half, dh = last_ref.shape[0] // 2, q_ref.shape[1]
    heads = q_ref.shape[0] // half
    feats = fq_ref.shape[1]
    place, level = spot()
    u = lax.div(place, 2) ^ other
    kv_scr[:half, :] = last_ref[half:, :]
    kv_scr[half:, :] = own_ref[...]
    at = pl.ds(pl.multiple_of(u * half, half), 2 * half)
    keys, values = kv_scr[at, :dh], kv_scr[at, dh:]
    fk_scr[:, half:] = fk_own_ref[:, aligned(u, half)]

    @pl.when(u == 0)
    def _():
        fk_scr[:, :half] = fk_last_ref[:, half:]

    @pl.when(u > 0)
    def _():
        fk_scr[:, :half] = fk_own_ref[:, :half]

    known = (level > 0) | (u > 0)
    cut = half - WINDOW
    row = lax.broadcasted_iota(jnp.int32, (WINDOW, 2 * half), 0)
    col = lax.broadcasted_iota(jnp.int32, (WINDOW, 2 * half), 1)
    inside = (col > row + cut) & (col <= row + half) & ((col >= half) | known)
    causal = (col <= row + cut)[:, :half]
    row, col = row[:, :half], col[:, :half]
    inside_low = (col > row) & (col <= row + WINDOW)
    causal_low = col <= row
    scores = dot_t(q_ref[...], keys)
    scale = math.log2(math.e) / math.sqrt(dh)

    def window(part, kept):
        masked = jnp.where(kept, part, -jnp.inf)
        top = jnp.max(masked, axis=1, keepdims=True)
        return jnp.exp2(((masked - top) * scale).astype(BF16))

    for h in range(heads):
        here = slice(h * half, (h + 1) * half)
        up, low = slice(h * half, h * half + cut), slice(h * half + cut, (h + 1) * half)
        linear = jnp.dot(
            fq_ref[here, :],
            fk_scr[h * feats : (h + 1) * feats, :],
            preferred_element_type=F32,
        )
        soft = window(scores[up], inside)
        w_scr[up, :half] = soft[:, :half] + jnp.where(causal, linear[:cut, :half], 0.0).astype(BF16)
        w_scr[up, half:] = soft[:, half:]
        soft = window(scores[low, half:], inside_low)
        w_scr[low, :half] = linear[cut:, :half].astype(BF16)
        w_scr[low, half:] = soft + jnp.where(causal_low, linear[cut:, half:], 0.0).astype(BF16)
    values = jnp.concatenate(
        [with_ones(values[:half], known), with_ones(values[half:])], axis=0
    )
    near_ref[...] = jnp.dot(w_scr[...], values, preferred_element_type=F32)


def mix_kernel_of_level(*refs):
    near_refs, fq_refs, (past_ref, step_ref, wk_ref) = refs[:2], refs[2:4], refs[4:7]
    first_ref, refs = refs[7], refs[8:]
    out_refs, (fk_scr, state_scr, out_scr) = refs[:-3], refs[-3:]
    rows, dh = near_refs[0].shape[0], near_refs[0].shape[1] // 2
    feats = fq_refs[0].shape[1]
    heads = past_ref.shape[0] // feats
    half = rows // heads
    place, level = spot()
    side = lax.axis_index("head")
    u = lax.div(place, 2)

    @pl.when(level < 3)
    def _():
        state_scr[0] = past_ref[...].astype(BF16)
        state_scr[1] = (past_ref[...] + step_ref[...]).astype(BF16)

    @pl.when(level >= 3)
    def _():
        write_key_features(first_ref[:, :dh], wk_ref, fk_scr)
        state = past_ref[...] + jnp.dot(
            fk_scr[...], with_ones(first_ref[:, dh:]), preferred_element_type=F32
        )
        state_scr[0] = state.astype(BF16)
        state_scr[1] = (state + step_ref[...]).astype(BF16)

    part = out_refs[0].shape[0]
    for other in (1, 0):
        for h in range(heads):
            here = slice(h * half, (h + 1) * half)
            far = jnp.dot(
                fq_refs[other][here, :],
                state_scr[u ^ other, h * feats : (h + 1) * feats, :],
                preferred_element_type=F32,
            )
            both = near_refs[other][here, :] + far
            out_scr[aligned(u ^ other, half), h * dh : (h + 1) * dh] = (
                both[:, :dh] * pl.reciprocal(both[:, dh:], approx=True)
            ).astype(BF16)
    for n, ref in enumerate(out_refs):
        dr, dy = slot_of(n, lax.rem(place, 2))
        ref[...] = out_scr[aligned((place ^ dr) * 2 + (side ^ dy), part), :]


def whole_spec(space=pltpu.VMEM):
    return pl.BlockSpec(memory_space=space)


def call(kernel, ins, outs, name, scratch=(), limit=4, out_type=BF16, scalars=()):
    return pl.pallas_call(
        kernel,
        in_specs=[whole_spec(pltpu.SMEM) for _ in scalars] + [whole_spec() for _ in ins],
        out_specs=[whole_spec() for _ in outs],
        out_shape=[
            jax.ShapeDtypeStruct(s, out_type[n] if isinstance(out_type, list) else out_type)
            for n, s in enumerate(outs)
        ],
        scratch_shapes=list(scratch),
        compiler_params=pltpu.CompilerParams(vmem_limit_bytes=limit * 2**20),
        name=name,
    )(*scalars, *ins)


def by_levels(queries, keys, values, wq, wk, factor):
    tok, width = queries.shape
    local_heads, feat, dh = wq.shape
    heads = local_heads // WAYS
    seq, sides = lax.axis_size("seq"), lax.axis_size("head")
    half = 2 * tok
    rows, states = heads * half, heads * 2 * feat

    def partner(x, dr, dy=0):
        pairs = [
            (i * sides + j, (i // WAYS * WAYS + (i % WAYS ^ dr)) * sides + (j ^ dy))
            for i in range(seq)
            for j in range(sides)
        ]
        return lax.ppermute(x, ("seq", "head"), pairs)

    def levels_back(x, by):
        pairs = [(i, i + by * WAYS) for i in range(seq - by * WAYS)]
        return lax.ppermute(x, "seq", pairs)

    own, away = call(pack_kv_kernel, [keys, values], [(tok, 4 * dh)] * 2, "pack_kv")
    got = partner(away, 2)
    q = list(call(pack_q_kernel, [queries], [(tok, width // WAYS)] * WAYS, "pack_q"))
    (pair,) = call(pair_kernel, [own, got], [(half, 2 * dh)], "pair_kv")
    *q, pair = lax.optimization_barrier((*q, pair))
    pair = partner(pair, 1)
    q[1], q[2], q[3] = partner(q[1], 1), partner(q[2], 2), partner(q[3], 3)
    (kv,) = call(stack_kernel, [own, got, pair], [(2 * half, 2 * dh)], "stack_kv")
    last = levels_back(kv, 1)
    wq, wk, kv, q[1] = lax.optimization_barrier((wq, wk, kv, q[1]))
    before, first = levels_back(kv, 2), levels_back(kv, 3)

    at = lax.rem(lax.axis_index("seq"), WAYS) * heads
    wk = lax.dynamic_slice_in_dim(wk, at, heads)
    (wq,) = call(
        weights_kernel,
        [lax.dynamic_slice_in_dim(wq, at, heads)],
        [(heads, dh, 2 * feat)],
        "weights",
    )
    def query_features(a, b):
        return call(
            query_features_kernel,
            [a, b, wq],
            [(rows, dh), (rows, 2 * feat)],
            "query_features",
            [pltpu.VMEM((rows, 2 * feat), BF16)],
            12,
            scalars=[factor],
        )

    def near(other, q_rows, fq):
        return call(
            lambda *refs: near_kernel(other, *refs),
            [q_rows, fq, last, kv, fk_last, fk_own],
            [(rows, 2 * dh)],
            "near",
            [
                pltpu.VMEM((3 * half, 2 * dh), BF16),
                pltpu.VMEM((states, 2 * half), BF16),
                pltpu.VMEM((rows, 2 * half), BF16),
            ],
            16,
            F32,
        )[0]

    q_own, fq_own = query_features(q[0], q[1])
    (fk_own,) = call(
        own_features_kernel, [kv, wk], [(states, 2 * half)], "own_features", limit=16
    )
    last, fq_own, fk_own = lax.optimization_barrier((last, fq_own, fk_own))
    fk_last, past, step = call(
        last_features_kernel,
        [last, wk],
        [(states, 2 * half), (states, 2 * dh), (states, 2 * dh)],
        "last_features",
        limit=20,
        out_type=[BF16, F32, F32],
    )
    near_own = near(0, q_own, fq_own)
    q[2], q[3], near_own = lax.optimization_barrier((q[2], q[3], near_own))
    q_other, fq_other = query_features(q[2], q[3])
    near_other = near(1, q_other, fq_other)
    before, near_other = lax.optimization_barrier((before, near_other))
    (past,) = call(
        past_kernel,
        [before, wk, past],
        [(states, 2 * dh)],
        "past",
        [pltpu.VMEM((states, 2 * half), BF16)],
        16,
        F32,
    )
    first, near_other, past = lax.optimization_barrier((first, near_other, past))
    part = tok // sides
    outs = call(
        mix_kernel_of_level,
        [near_own, near_other, fq_own, fq_other, past, step, wk, first],
        [(part, heads * dh)] * (WAYS * sides),
        "mix_level",
        [
            pltpu.VMEM((states, 2 * half), BF16),
            pltpu.VMEM((2, states, 2 * dh), BF16),
            pltpu.VMEM((2 * half, heads * dh), BF16),
        ],
        24,
    )

    def sent(x, slot):
        pairs = []
        for i in range(seq):
            dr, dy = slot[i % 2]
            to = i // WAYS * WAYS + (i % WAYS ^ dr)
            pairs += [(i * sides + j, to * sides + (j ^ dy)) for j in range(sides)]
        return lax.ppermute(x, ("seq", "head"), pairs)

    outs = [outs[0]] + [sent(x, slot) for x, slot in zip(outs[1:], SLOTS[1:])]

    return pl.pallas_call(
        join_kernel,
        in_specs=[whole_spec()] * len(outs),
        out_specs=whole_spec(pltpu.HBM),
        out_shape=jax.ShapeDtypeStruct((part, sides * WAYS * heads * dh), BF16),
        scratch_shapes=[pltpu.SemaphoreType.DMA((len(outs),))],
        compiler_params=pltpu.CompilerParams(vmem_limit_bytes=4 * 2**20),
        name="join",
    )(*outs)


def by_blocks(queries, keys, values, wq, wk, ratio):
    group = wq.shape[0] // (keys.shape[1] // DH)
    place = lax.axis_index("seq").astype(jnp.int32).reshape(1)
    kv = lax.all_gather(jnp.concatenate([keys, values], axis=1), "seq", tiled=True)
    out = mix(place, queries, kv, wq, wk, ratio, group)
    return lax.all_to_all(out, "head", split_axis=0, concat_axis=1, tiled=True)


def local(queries, keys, values, q_feature, k_feature, window_factor):
    tok = queries.shape[0]
    seq, sides = lax.axis_size("seq"), lax.axis_size("head")
    wq, wk = jnp.swapaxes(q_feature, 1, 2), jnp.swapaxes(k_feature, 1, 2)
    if keys.shape[1] == WAYS * DH and seq == 4 * WAYS and sides == 2 and tok == WINDOW:
        return by_levels(queries, keys, values, wq, wk, window_factor)
    ratio = window_factor / (1.0 - window_factor)
    return by_blocks(queries, keys, values, wq, wk, ratio)


def solution(mesh):
    return jax.shard_map(
        local,
        mesh=mesh,
        in_specs=(
            P("seq", "head"),
            P("seq", "head"),
            P("seq", "head"),
            P("head", None, None),
            P("head", None, None),
            P("head"),
        ),
        out_specs=P(("seq", "head"), None),
        check_vma=False,
    )
```

```python
import math

import jax
import jax.numpy as jnp
from jax import lax
from jax.experimental import pallas as pl
from jax.experimental.pallas import tpu as pltpu
from jax.sharding import PartitionSpec as P

DH = 128
WINDOW = 64
F32 = jnp.float32
BF16 = jnp.bfloat16


def dot_t(a, b):
    return lax.dot_general(a, b, (((1,), (1,)), ((), ())), preferred_element_type=F32)


def features_t(logits):
    top = jnp.max(logits, axis=0, keepdims=True)
    low = jnp.min(logits, axis=0, keepdims=True)
    up = jnp.exp(logits - top)
    down = jnp.exp(low - logits)
    up = up * (1.0 / jnp.sum(up, axis=0, keepdims=True))
    down = down * (1.0 / jnp.sum(down, axis=0, keepdims=True))
    return jnp.concatenate([up.astype(BF16), down.astype(BF16)], axis=0)


def mix_kernel(
    place_ref, q_ref, k_ref, v_ref, wq_ref, wk_ref, ratio_ref, out_ref, fk_scr, state_scr
):
    tok = q_ref.shape[0]
    heads, feat, dh = wq_ref.shape
    seen = fk_scr.shape[1]
    place = place_ref[0]
    first_head = pl.program_id(0) * heads

    weights = wk_ref[...].reshape(heads * feat, dh)
    for start in range(0, seen, 256):
        size = min(256, seen - start)
        logits = dot_t(weights, k_ref[start : start + size, :])
        for h in range(heads):
            fk_scr[h * 2 * feat : (h + 1) * 2 * feat, start : start + size] = features_t(
                logits[h * feat : (h + 1) * feat]
            )
    row = lax.broadcasted_iota(jnp.int32, (seen, dh), 0)
    kept = row < (place - 1) * tok
    v_seen = jnp.where(kept, v_ref[:seen, :].astype(F32), 0.0).astype(BF16)
    ones_seen = jnp.where(kept, 1.0, 0.0).astype(BF16)
    v_seen = jnp.concatenate([v_seen, ones_seen], axis=1)
    state_scr[...] = jnp.dot(fk_scr[...], v_seen, preferred_element_type=F32).astype(BF16)

    before = pl.multiple_of(jnp.maximum(place - 1, 0) * tok, tok)
    own = pl.multiple_of(place * tok, tok)
    k_ext = jnp.concatenate([k_ref[pl.ds(before, tok), :], k_ref[pl.ds(own, tok), :]], axis=0)
    v_ext = jnp.concatenate([v_ref[pl.ds(before, tok), :], v_ref[pl.ds(own, tok), :]], axis=0)
    v_ext = jnp.concatenate([v_ext, jnp.ones_like(v_ext)], axis=1)
    row = lax.broadcasted_iota(jnp.int32, (tok, 2 * tok), 0)
    col = lax.broadcasted_iota(jnp.int32, (tok, 2 * tok), 1)
    valid = (col >= tok) | (place > 0)
    inside = (col > row) & (col <= row + WINDOW) & valid
    causal = (col <= row) & valid
    lane = lax.broadcasted_iota(jnp.int32, (tok, 2 * feat), 1)
    left = lane < feat
    side_r = lax.broadcasted_iota(jnp.int32, (2 * feat, 2 * feat), 0) < feat
    side_c = lax.broadcasted_iota(jnp.int32, (2 * feat, 2 * feat), 1) < feat
    halves = jnp.where(side_r == side_c, 1.0, 0.0).astype(BF16)

    for h in range(heads):
        q = q_ref[:, h * dh : (h + 1) * dh]
        wq = wq_ref[h]
        logits = dot_t(q, jnp.concatenate([wq, -wq], axis=0))
        top_l = jnp.max(jnp.where(left, logits, -jnp.inf), axis=1, keepdims=True)
        top_r = jnp.max(jnp.where(left, -jnp.inf, logits), axis=1, keepdims=True)
        expd = jnp.exp(logits - jnp.where(left, top_l, top_r)).astype(BF16)
        total = jnp.dot(expd, halves, preferred_element_type=F32)
        fq = (expd.astype(F32) / total).astype(BF16)
        fk = features_t(dot_t(wk_ref[h], k_ext))
        linear = jnp.dot(fq, fk, preferred_element_type=F32)
        scores = dot_t(q, k_ext) * (1.0 / math.sqrt(dh))
        masked = jnp.where(inside, scores, -jnp.inf)
        top = jnp.max(masked, axis=1, keepdims=True)
        soft = jnp.exp(masked - top) * ratio_ref[first_head + h]
        weight = jnp.where(causal, linear, soft).astype(BF16)
        both = jnp.dot(weight, v_ext, preferred_element_type=F32) + jnp.dot(
            fq, state_scr[h * 2 * feat : (h + 1) * 2 * feat, :], preferred_element_type=F32
        )
        out_ref[:, h * dh : (h + 1) * dh] = (both[:, :dh] / both[:, dh:]).astype(BF16)


def mix(place, queries, kv, wq, wk, ratio, group):
    tok = queries.shape[0]
    local_heads, feat, dh = wq.shape
    groups = local_heads // group
    tokens = kv.shape[0]
    seen = tokens - 2 * tok
    return pl.pallas_call(
        mix_kernel,
        grid_spec=pltpu.PrefetchScalarGridSpec(
            num_scalar_prefetch=1,
            grid=(groups,),
            in_specs=[
                pl.BlockSpec((tok, group * dh), lambda g, p: (0, g)),
                pl.BlockSpec((tokens, dh), lambda g, p: (0, g)),
                pl.BlockSpec((tokens, dh), lambda g, p: (0, groups + g)),
                pl.BlockSpec((group, feat, dh), lambda g, p: (g, 0, 0)),
                pl.BlockSpec((group, feat, dh), lambda g, p: (g, 0, 0)),
                pl.BlockSpec(memory_space=pltpu.SMEM),
            ],
            out_specs=pl.BlockSpec((tok, group * dh), lambda g, p: (0, g)),
            scratch_shapes=[
                pltpu.VMEM((group * 2 * feat, seen), BF16),
                pltpu.VMEM((group * 2 * feat, 2 * dh), BF16),
            ],
        ),
        out_shape=jax.ShapeDtypeStruct(queries.shape, BF16),
        compiler_params=pltpu.CompilerParams(vmem_limit_bytes=48 * 2**20),
        cost_estimate=pl.CostEstimate(
            flops=2 * local_heads * tokens * 3 * feat * 2 * dh,
            bytes_accessed=8 * 2**20,
            transcendentals=local_heads * tokens * 2 * feat,
        ),
    )(place, queries, kv, kv, wq, wk, ratio)


WAYS = 4


SLOTS = (
    ((0, 0), (0, 0)),
    ((2, 1), (2, 1)),
    ((2, 0), (0, 1)),
    ((0, 1), (2, 0)),
    ((3, 1), (3, 1)),
    ((3, 0), (1, 1)),
    ((1, 1), (3, 0)),
    ((1, 0), (1, 0)),
)


def slot_of(n, odd):
    return [jnp.where(odd == 1, b, a) if a != b else a for a, b in zip(*SLOTS[n])]


def spot():
    at = lax.axis_index("seq")
    return lax.rem(at, WAYS), lax.div(at, WAYS)


def aligned(at, step):
    return pl.ds(pl.multiple_of(at * step, step), step)


def with_ones(values, kept=True):
    here = jnp.where(kept, 1.0, 0.0).astype(BF16)
    return jnp.concatenate([values, jnp.full(values.shape, here)], axis=1)


def pack_kv_kernel(k_ref, v_ref, own_ref, away_ref):
    place = spot()[0]
    for d in range(WAYS):
        ref, at = (own_ref, away_ref)[d // 2], d % 2 * 2 * DH
        ref[:, at : at + DH] = k_ref[:, aligned(place ^ d, DH)]
        ref[:, at + DH : at + 2 * DH] = v_ref[:, aligned(place ^ d, DH)]


def pair_kernel(own_ref, got_ref, out_ref):
    tok = own_ref.shape[0]
    out_ref[:tok, :] = own_ref[:, 2 * DH :]
    out_ref[tok:, :] = got_ref[:, 2 * DH :]


def stack_kernel(own_ref, got_ref, pair_ref, out_ref):
    tok = own_ref.shape[0]
    place = spot()[0]
    out_ref[aligned(place, tok), :] = own_ref[:, : 2 * DH]
    out_ref[aligned(place ^ 2, tok), :] = got_ref[:, : 2 * DH]
    out_ref[aligned(place ^ 1, tok), :] = pair_ref[:tok, :]
    out_ref[aligned(place ^ 3, tok), :] = pair_ref[tok:, :]


def pack_q_kernel(q_ref, *out_refs):
    place = spot()[0]
    for d, out in enumerate(out_refs):
        out[...] = q_ref[:, aligned(place ^ d, out.shape[1])]


def weights_kernel(wq_ref, factor_ref, both_ref, ratio_ref):
    ratio_ref[...] = (1.0 - factor_ref[...]) / factor_ref[...]
    for h in range(wq_ref.shape[0]):
        wq = wq_ref[h].T
        both_ref[h] = jnp.concatenate([wq, -wq], axis=1)


def join_kernel(*refs):
    got, out_ref, sems = refs[:-2], *refs[-2:]
    width = got[0].shape[1]
    place, side = spot()[0], lax.axis_index("head")
    copies = []
    for n, ref in enumerate(got):
        dr, dy = slot_of(n, lax.rem(place, 2) ^ (SLOTS[n][0][0] & 1))
        at = aligned((side ^ dy) * WAYS + (place ^ dr), width)
        copies.append(pltpu.make_async_copy(ref, out_ref.at[:, at], sems.at[n]))
    for copy in copies:
        copy.start()
    for copy in copies:
        copy.wait()


def write_key_features(keys, wk_ref, fk_ref):
    heads, feat, dh = wk_ref.shape
    logits = dot_t(wk_ref[...].reshape(heads * feat, dh), keys)
    for h in range(heads):
        part = logits[h * feat : (h + 1) * feat]
        top = jnp.max(part, axis=0, keepdims=True)
        low = jnp.min(part, axis=0, keepdims=True)
        for n, shifted in enumerate((part - top, low - part)):
            row = (2 * h + n) * feat
            expd = jnp.exp(shifted.astype(BF16))
            total = expd[: feat // 4]
            for q in range(1, 4):
                total = total + expd[q * feat // 4 : (q + 1) * feat // 4]
            total = jnp.sum(total.astype(F32), axis=0, keepdims=True)
            fk_ref[row : row + feat, :] = expd * pl.reciprocal(total).astype(BF16)


def own_features_kernel(own_ref, wk_ref, fk_ref):
    write_key_features(own_ref[:, :DH], wk_ref, fk_ref.at[:, own_ref.shape[0] :])


def last_features_kernel(last_ref, wk_ref, _, fk_ref, past_ref, step_ref):
    size = last_ref.shape[0]
    half = size // 2
    level = spot()[1]

    @pl.when(level == 0)
    def _():
        fk_ref[:, :size] = jnp.zeros((fk_ref.shape[0], size), BF16)
        for ref in (past_ref, step_ref):
            ref[...] = jnp.zeros_like(ref)

    @pl.when(level > 0)
    def _():
        write_key_features(last_ref[:, :DH], wk_ref, fk_ref.at[:, :size])
        for at, ref in ((0, past_ref), (half, step_ref)):
            ref[...] = jnp.dot(
                fk_ref[:, at : at + half],
                with_ones(last_ref[at : at + half, DH:]),
                preferred_element_type=F32,
            )


def past_kernel(before_ref, wk_ref, sum_ref, past_ref, fk_scr):
    level = spot()[1]

    @pl.when(level < 2)
    def _():
        past_ref[...] = sum_ref[...]

    @pl.when(level >= 2)
    def _():
        write_key_features(before_ref[:, :DH], wk_ref, fk_scr)
        past_ref[...] = sum_ref[...] + jnp.dot(
            fk_scr[...], with_ones(before_ref[:, DH:]), preferred_element_type=F32
        )


def query_features_kernel(ratio_ref, a_ref, b_ref, w_ref, q_out, fq_out, exp_scr):
    tok = a_ref.shape[0]
    heads, dh, both = w_ref.shape
    half = 2 * tok
    place = spot()[0]
    for d, ref in enumerate((a_ref, b_ref)):
        row = pl.multiple_of(lax.rem(place ^ d, 2) * tok, tok)
        for h in range(heads):
            q_out[pl.ds(h * half + row, tok), :] = ref[:, h * dh : (h + 1) * dh]
    rows_of = [slice(h * half, (h + 1) * half) for h in range(heads)]
    left = lax.broadcasted_iota(jnp.int32, (half, both), 1) < both // 2
    for h, rows in enumerate(rows_of):
        logits = jnp.dot(q_out[rows, :], w_ref[h], preferred_element_type=F32)
        top_l = jnp.max(jnp.where(left, logits, -jnp.inf), axis=1, keepdims=True)
        top_r = jnp.max(jnp.where(left, -jnp.inf, logits), axis=1, keepdims=True)
        exp_scr[rows, :] = jnp.exp((logits - jnp.where(left, top_l, top_r)).astype(BF16))
    side_r = lax.broadcasted_iota(jnp.int32, (both, both), 0) < both // 2
    side_c = lax.broadcasted_iota(jnp.int32, (both, both), 1) < both // 2
    halves = jnp.where(side_r == side_c, 1.0, 0.0).astype(BF16)
    total = jnp.dot(exp_scr[...], halves, preferred_element_type=F32)
    for h, rows in enumerate(rows_of):
        scale = pl.reciprocal(total[rows], approx=True) * ratio_ref[place * heads + h]
        fq_out[rows, :] = (exp_scr[rows, :].astype(F32) * scale).astype(BF16)


def near_kernel(other, q_ref, fq_ref, last_ref, own_ref, fk_ref, near_ref, kv_scr, w_scr):
    half, dh = last_ref.shape[0] // 2, q_ref.shape[1]
    heads = q_ref.shape[0] // half
    feats = fq_ref.shape[1]
    place, level = spot()
    u = lax.div(place, 2) ^ other
    kv_scr[:half, :] = last_ref[half:, :]
    kv_scr[half:, :] = own_ref[...]
    at = pl.ds(pl.multiple_of(u * half, half), 2 * half)
    keys, values = kv_scr[at, :dh], kv_scr[at, dh:]
    fk_at = pl.ds(pl.multiple_of((u + 1) * half, half), 2 * half)
    known = (level > 0) | (u > 0)
    cut = half - WINDOW
    row = lax.broadcasted_iota(jnp.int32, (WINDOW, 2 * half), 0)
    col = lax.broadcasted_iota(jnp.int32, (WINDOW, 2 * half), 1)
    inside = (col > row + cut) & (col <= row + half) & ((col >= half) | known)
    causal = (col <= row + cut)[:, :half]
    row, col = row[:, :half], col[:, :half]
    inside_low = (col > row) & (col <= row + WINDOW)
    causal_low = col <= row
    scores = dot_t(q_ref[...], keys)
    scale = math.log2(math.e) / math.sqrt(dh)

    def window(part, kept):
        masked = jnp.where(kept, part, -jnp.inf)
        top = jnp.max(masked, axis=1, keepdims=True)
        return jnp.exp2(((masked - top) * scale).astype(BF16))

    for h in range(heads):
        here = slice(h * half, (h + 1) * half)
        up, low = slice(h * half, h * half + cut), slice(h * half + cut, (h + 1) * half)
        linear = jnp.dot(
            fq_ref[here, :],
            fk_ref[h * feats : (h + 1) * feats, fk_at],
            preferred_element_type=F32,
        )
        soft = window(scores[up], inside)
        w_scr[up, :half] = soft[:, :half] + jnp.where(causal, linear[:cut, :half], 0.0).astype(BF16)
        w_scr[up, half:] = soft[:, half:]
        soft = window(scores[low, half:], inside_low)
        w_scr[low, :half] = linear[cut:, :half].astype(BF16)
        w_scr[low, half:] = soft + jnp.where(causal_low, linear[cut:, half:], 0.0).astype(BF16)
    values = jnp.concatenate(
        [with_ones(values[:half], known), with_ones(values[half:])], axis=0
    )
    near_ref[...] = jnp.dot(w_scr[...], values, preferred_element_type=F32)


def mix_kernel_of_level(*refs):
    near_refs, fq_refs, (past_ref, step_ref, wk_ref) = refs[:2], refs[2:4], refs[4:7]
    first_ref, refs = refs[7], refs[8:]
    out_refs, (fk_scr, state_scr, out_scr) = refs[:-3], refs[-3:]
    rows, dh = near_refs[0].shape[0], near_refs[0].shape[1] // 2
    feats = fq_refs[0].shape[1]
    heads = past_ref.shape[0] // feats
    half = rows // heads
    place, level = spot()
    side = lax.axis_index("head")
    u = lax.div(place, 2)

    @pl.when(level < 3)
    def _():
        state_scr[0] = past_ref[...].astype(BF16)
        state_scr[1] = (past_ref[...] + step_ref[...]).astype(BF16)

    @pl.when(level >= 3)
    def _():
        write_key_features(first_ref[:, :dh], wk_ref, fk_scr)
        state = past_ref[...] + jnp.dot(
            fk_scr[...], with_ones(first_ref[:, dh:]), preferred_element_type=F32
        )
        state_scr[0] = state.astype(BF16)
        state_scr[1] = (state + step_ref[...]).astype(BF16)

    part = out_refs[0].shape[0]
    for other in (1, 0):
        for h in range(heads):
            here = slice(h * half, (h + 1) * half)
            far = jnp.dot(
                fq_refs[other][here, :],
                state_scr[u ^ other, h * feats : (h + 1) * feats, :],
                preferred_element_type=F32,
            )
            both = near_refs[other][here, :] + far
            out_scr[aligned(u ^ other, half), h * dh : (h + 1) * dh] = (
                both[:, :dh] * pl.reciprocal(both[:, dh:], approx=True)
            ).astype(BF16)
    for n, ref in enumerate(out_refs):
        dr, dy = slot_of(n, lax.rem(place, 2))
        ref[...] = out_scr[aligned((place ^ dr) * 2 + (side ^ dy), part), :]


def whole_spec(space=pltpu.VMEM):
    return pl.BlockSpec(memory_space=space)


def call(kernel, ins, outs, name, scratch=(), limit=4, out_type=BF16, scalars=(), aliases={}):
    return pl.pallas_call(
        kernel,
        in_specs=[whole_spec(pltpu.SMEM) for _ in scalars] + [whole_spec() for _ in ins],
        out_specs=[whole_spec() for _ in outs],
        out_shape=[
            jax.ShapeDtypeStruct(s, out_type[n] if isinstance(out_type, list) else out_type)
            for n, s in enumerate(outs)
        ],
        scratch_shapes=list(scratch),
        input_output_aliases=aliases,
        compiler_params=pltpu.CompilerParams(vmem_limit_bytes=limit * 2**20),
        name=name,
    )(*scalars, *ins)


def by_levels(queries, keys, values, wq, wk, factor):
    tok, width = queries.shape
    local_heads, feat, dh = wq.shape
    heads = local_heads // WAYS
    seq, sides = lax.axis_size("seq"), lax.axis_size("head")
    half = 2 * tok
    rows, states = heads * half, heads * 2 * feat

    def partner(x, dr, dy=0):
        pairs = [
            (i * sides + j, (i // WAYS * WAYS + (i % WAYS ^ dr)) * sides + (j ^ dy))
            for i in range(seq)
            for j in range(sides)
        ]
        return lax.ppermute(x, ("seq", "head"), pairs)

    def to_next_level(x, first_level):
        pairs = [(i, i + WAYS) for i in range(first_level * WAYS, seq - WAYS)]
        return lax.ppermute(x, "seq", pairs)

    own, away = call(pack_kv_kernel, [keys, values], [(tok, 4 * dh)] * 2, "pack_kv")
    got = partner(away, 2)
    q = list(call(pack_q_kernel, [queries], [(tok, width // WAYS)] * WAYS, "pack_q"))
    (pair,) = call(pair_kernel, [own, got], [(half, 2 * dh)], "pair_kv")
    *q, pair = lax.optimization_barrier((*q, pair))
    pair = partner(pair, 1)
    q[1], q[2], q[3] = partner(q[1], 1), partner(q[2], 2), partner(q[3], 3)
    (kv,) = call(stack_kernel, [own, got, pair], [(2 * half, 2 * dh)], "stack_kv")
    last = to_next_level(kv, 0)
    wq, wk, kv = lax.optimization_barrier((wq, wk, kv))

    at = lax.rem(lax.axis_index("seq"), WAYS) * heads
    wk = lax.dynamic_slice_in_dim(wk, at, heads)
    wq, ratio = call(
        weights_kernel,
        [lax.dynamic_slice_in_dim(wq, at, heads), factor],
        [(heads, dh, 2 * feat), factor.shape],
        "weights",
        out_type=[BF16, F32],
    )

    def query_features(a, b):
        return call(
            query_features_kernel,
            [a, b, wq],
            [(rows, dh), (rows, 2 * feat)],
            "query_features",
            [pltpu.VMEM((rows, 2 * feat), BF16)],
            12,
            scalars=[ratio],
        )

    def near(other, q_rows, fq):
        return call(
            lambda *refs: near_kernel(other, *refs),
            [q_rows, fq, last, kv, fk],
            [(rows, 2 * dh)],
            "near",
            [
                pltpu.VMEM((3 * half, 2 * dh), BF16),
                pltpu.VMEM((rows, 2 * half), BF16),
            ],
            16,
            F32,
        )[0]

    q_own, fq_own = query_features(q[0], q[1])
    (fk,) = call(own_features_kernel, [kv, wk], [(states, 4 * half)], "own_features", limit=16)
    last, fq_own, fk = lax.optimization_barrier((last, fq_own, fk))
    before = to_next_level(last, 1)
    fk, past, step = call(
        last_features_kernel,
        [last, wk, fk],
        [(states, 4 * half), (states, 2 * dh), (states, 2 * dh)],
        "last_features",
        limit=20,
        out_type=[BF16, F32, F32],
        aliases={2: 0},
    )
    near_own = near(0, q_own, fq_own)
    before, near_own = lax.optimization_barrier((before, near_own))
    first = to_next_level(before, 2)
    (past,) = call(
        past_kernel,
        [before, wk, past],
        [(states, 2 * dh)],
        "past",
        [pltpu.VMEM((states, 2 * half), BF16)],
        16,
        F32,
    )
    q[2], q[3], past = lax.optimization_barrier((q[2], q[3], past))
    q_other, fq_other = query_features(q[2], q[3])
    near_other = near(1, q_other, fq_other)
    first, near_other = lax.optimization_barrier((first, near_other))
    part = tok // sides
    outs = call(
        mix_kernel_of_level,
        [near_own, near_other, fq_own, fq_other, past, step, wk, first],
        [(part, heads * dh)] * (WAYS * sides),
        "mix_level",
        [
            pltpu.VMEM((states, 2 * half), BF16),
            pltpu.VMEM((2, states, 2 * dh), BF16),
            pltpu.VMEM((2 * half, heads * dh), BF16),
        ],
        24,
    )

    def sent(x, slot):
        pairs = []
        for i in range(seq):
            dr, dy = slot[i % 2]
            to = i // WAYS * WAYS + (i % WAYS ^ dr)
            pairs += [(i * sides + j, to * sides + (j ^ dy)) for j in range(sides)]
        return lax.ppermute(x, ("seq", "head"), pairs)

    outs = list(outs)
    for n in range(1, 6):
        outs[n] = sent(outs[n], SLOTS[n])
    for n in (6, 7):
        outs[n], outs[n - 5] = lax.optimization_barrier((outs[n], outs[n - 5]))
        outs[n] = sent(outs[n], SLOTS[n])

    return pl.pallas_call(
        join_kernel,
        in_specs=[whole_spec()] * len(outs),
        out_specs=whole_spec(pltpu.HBM),
        out_shape=jax.ShapeDtypeStruct((part, sides * WAYS * heads * dh), BF16),
        scratch_shapes=[pltpu.SemaphoreType.DMA((len(outs),))],
        compiler_params=pltpu.CompilerParams(vmem_limit_bytes=4 * 2**20),
        name="join",
    )(*outs)


def by_blocks(queries, keys, values, wq, wk, ratio):
    group = wq.shape[0] // (keys.shape[1] // DH)
    place = lax.axis_index("seq").astype(jnp.int32).reshape(1)
    kv = lax.all_gather(jnp.concatenate([keys, values], axis=1), "seq", tiled=True)
    out = mix(place, queries, kv, wq, wk, ratio, group)
    return lax.all_to_all(out, "head", split_axis=0, concat_axis=1, tiled=True)


def local(queries, keys, values, q_feature, k_feature, window_factor):
    tok = queries.shape[0]
    seq, sides = lax.axis_size("seq"), lax.axis_size("head")
    wq, wk = jnp.swapaxes(q_feature, 1, 2), jnp.swapaxes(k_feature, 1, 2)
    if keys.shape[1] == WAYS * DH and seq == 4 * WAYS and sides == 2 and tok == WINDOW:
        return by_levels(queries, keys, values, wq, wk, window_factor)
    ratio = window_factor / (1.0 - window_factor)
    return by_blocks(queries, keys, values, wq, wk, ratio)


def solution(mesh):
    return jax.shard_map(
        local,
        mesh=mesh,
        in_specs=(
            P("seq", "head"),
            P("seq", "head"),
            P("seq", "head"),
            P("head", None, None),
            P("head", None, None),
            P("head"),
        ),
        out_specs=P(("seq", "head"), None),
        check_vma=False,
    )
```

```python
import math

import jax
import jax.numpy as jnp
from jax import lax
from jax.experimental import pallas as pl
from jax.experimental.pallas import tpu as pltpu
from jax.sharding import PartitionSpec as P

DH = 128
WINDOW = 64
F32 = jnp.float32
BF16 = jnp.bfloat16


def dot_t(a, b):
    return lax.dot_general(a, b, (((1,), (1,)), ((), ())), preferred_element_type=F32)


def features_t(logits):
    top = jnp.max(logits, axis=0, keepdims=True)
    low = jnp.min(logits, axis=0, keepdims=True)
    up = jnp.exp(logits - top)
    down = jnp.exp(low - logits)
    up = up * (1.0 / jnp.sum(up, axis=0, keepdims=True))
    down = down * (1.0 / jnp.sum(down, axis=0, keepdims=True))
    return jnp.concatenate([up.astype(BF16), down.astype(BF16)], axis=0)


def mix_kernel(
    place_ref, q_ref, k_ref, v_ref, wq_ref, wk_ref, ratio_ref, out_ref, fk_scr, state_scr
):
    tok = q_ref.shape[0]
    heads, feat, dh = wq_ref.shape
    seen = fk_scr.shape[1]
    place = place_ref[0]
    first_head = pl.program_id(0) * heads

    weights = wk_ref[...].reshape(heads * feat, dh)
    for start in range(0, seen, 256):
        size = min(256, seen - start)
        logits = dot_t(weights, k_ref[start : start + size, :])
        for h in range(heads):
            fk_scr[h * 2 * feat : (h + 1) * 2 * feat, start : start + size] = features_t(
                logits[h * feat : (h + 1) * feat]
            )
    row = lax.broadcasted_iota(jnp.int32, (seen, dh), 0)
    kept = row < (place - 1) * tok
    v_seen = jnp.where(kept, v_ref[:seen, :].astype(F32), 0.0).astype(BF16)
    ones_seen = jnp.where(kept, 1.0, 0.0).astype(BF16)
    v_seen = jnp.concatenate([v_seen, ones_seen], axis=1)
    state_scr[...] = jnp.dot(fk_scr[...], v_seen, preferred_element_type=F32).astype(BF16)

    before = pl.multiple_of(jnp.maximum(place - 1, 0) * tok, tok)
    own = pl.multiple_of(place * tok, tok)
    k_ext = jnp.concatenate([k_ref[pl.ds(before, tok), :], k_ref[pl.ds(own, tok), :]], axis=0)
    v_ext = jnp.concatenate([v_ref[pl.ds(before, tok), :], v_ref[pl.ds(own, tok), :]], axis=0)
    v_ext = jnp.concatenate([v_ext, jnp.ones_like(v_ext)], axis=1)
    row = lax.broadcasted_iota(jnp.int32, (tok, 2 * tok), 0)
    col = lax.broadcasted_iota(jnp.int32, (tok, 2 * tok), 1)
    valid = (col >= tok) | (place > 0)
    inside = (col > row) & (col <= row + WINDOW) & valid
    causal = (col <= row) & valid
    lane = lax.broadcasted_iota(jnp.int32, (tok, 2 * feat), 1)
    left = lane < feat
    side_r = lax.broadcasted_iota(jnp.int32, (2 * feat, 2 * feat), 0) < feat
    side_c = lax.broadcasted_iota(jnp.int32, (2 * feat, 2 * feat), 1) < feat
    halves = jnp.where(side_r == side_c, 1.0, 0.0).astype(BF16)

    for h in range(heads):
        q = q_ref[:, h * dh : (h + 1) * dh]
        wq = wq_ref[h]
        logits = dot_t(q, jnp.concatenate([wq, -wq], axis=0))
        top_l = jnp.max(jnp.where(left, logits, -jnp.inf), axis=1, keepdims=True)
        top_r = jnp.max(jnp.where(left, -jnp.inf, logits), axis=1, keepdims=True)
        expd = jnp.exp(logits - jnp.where(left, top_l, top_r)).astype(BF16)
        total = jnp.dot(expd, halves, preferred_element_type=F32)
        fq = (expd.astype(F32) / total).astype(BF16)
        fk = features_t(dot_t(wk_ref[h], k_ext))
        linear = jnp.dot(fq, fk, preferred_element_type=F32)
        scores = dot_t(q, k_ext) * (1.0 / math.sqrt(dh))
        masked = jnp.where(inside, scores, -jnp.inf)
        top = jnp.max(masked, axis=1, keepdims=True)
        soft = jnp.exp(masked - top) * ratio_ref[first_head + h]
        weight = jnp.where(causal, linear, soft).astype(BF16)
        both = jnp.dot(weight, v_ext, preferred_element_type=F32) + jnp.dot(
            fq, state_scr[h * 2 * feat : (h + 1) * 2 * feat, :], preferred_element_type=F32
        )
        out_ref[:, h * dh : (h + 1) * dh] = (both[:, :dh] / both[:, dh:]).astype(BF16)


def mix(place, queries, kv, wq, wk, ratio, group):
    tok = queries.shape[0]
    local_heads, feat, dh = wq.shape
    groups = local_heads // group
    tokens = kv.shape[0]
    seen = tokens - 2 * tok
    return pl.pallas_call(
        mix_kernel,
        grid_spec=pltpu.PrefetchScalarGridSpec(
            num_scalar_prefetch=1,
            grid=(groups,),
            in_specs=[
                pl.BlockSpec((tok, group * dh), lambda g, p: (0, g)),
                pl.BlockSpec((tokens, dh), lambda g, p: (0, g)),
                pl.BlockSpec((tokens, dh), lambda g, p: (0, groups + g)),
                pl.BlockSpec((group, feat, dh), lambda g, p: (g, 0, 0)),
                pl.BlockSpec((group, feat, dh), lambda g, p: (g, 0, 0)),
                pl.BlockSpec(memory_space=pltpu.SMEM),
            ],
            out_specs=pl.BlockSpec((tok, group * dh), lambda g, p: (0, g)),
            scratch_shapes=[
                pltpu.VMEM((group * 2 * feat, seen), BF16),
                pltpu.VMEM((group * 2 * feat, 2 * dh), BF16),
            ],
        ),
        out_shape=jax.ShapeDtypeStruct(queries.shape, BF16),
        compiler_params=pltpu.CompilerParams(vmem_limit_bytes=48 * 2**20),
        cost_estimate=pl.CostEstimate(
            flops=2 * local_heads * tokens * 3 * feat * 2 * dh,
            bytes_accessed=8 * 2**20,
            transcendentals=local_heads * tokens * 2 * feat,
        ),
    )(place, queries, kv, kv, wq, wk, ratio)


WAYS = 4


SLOTS = (
    ((0, 0), (0, 0)),
    ((2, 1), (2, 1)),
    ((2, 0), (0, 1)),
    ((0, 1), (2, 0)),
    ((3, 1), (3, 1)),
    ((3, 0), (1, 1)),
    ((1, 1), (3, 0)),
    ((1, 0), (1, 0)),
)


def slot_of(n, odd):
    return [jnp.where(odd == 1, b, a) if a != b else a for a, b in zip(*SLOTS[n])]


def spot():
    at = lax.axis_index("seq")
    return lax.rem(at, WAYS), lax.div(at, WAYS)


def aligned(at, step):
    return pl.ds(pl.multiple_of(at * step, step), step)


def with_ones(values, kept=True):
    here = jnp.where(kept, 1.0, 0.0).astype(BF16)
    return jnp.concatenate([values, jnp.full(values.shape, here)], axis=1)


def pack_kv_kernel(k_ref, v_ref, own_ref, away_ref):
    place = spot()[0]
    for d in range(WAYS):
        ref, at = (own_ref, away_ref)[d // 2], d % 2 * 2 * DH
        ref[:, at : at + DH] = k_ref[:, aligned(place ^ d, DH)]
        ref[:, at + DH : at + 2 * DH] = v_ref[:, aligned(place ^ d, DH)]


def pair_kernel(own_ref, got_ref, out_ref):
    tok = own_ref.shape[0]
    out_ref[:tok, :] = own_ref[:, 2 * DH :]
    out_ref[tok:, :] = got_ref[:, 2 * DH :]


def stack_kernel(own_ref, got_ref, pair_ref, out_ref):
    tok = own_ref.shape[0]
    place = spot()[0]
    out_ref[aligned(place, tok), :] = own_ref[:, : 2 * DH]
    out_ref[aligned(place ^ 2, tok), :] = got_ref[:, : 2 * DH]
    out_ref[aligned(place ^ 1, tok), :] = pair_ref[:tok, :]
    out_ref[aligned(place ^ 3, tok), :] = pair_ref[tok:, :]


def pack_q_kernel(q_ref, *out_refs):
    place = spot()[0]
    for d, out in enumerate(out_refs):
        out[...] = q_ref[:, aligned(place ^ d, out.shape[1])]


def weights_kernel(wq_ref, factor_ref, both_ref, ratio_ref):
    heads = both_ref.shape[0]
    shape = (heads, factor_ref.shape[1])
    head = lax.broadcasted_iota(jnp.int32, shape, 0) + spot()[0] * heads
    ratio = jnp.broadcast_to((1.0 - factor_ref[...]) / factor_ref[...], shape)
    ratio = jnp.where(lax.broadcasted_iota(jnp.int32, shape, 1) == head, ratio, 0.0)
    ratio = jnp.sum(ratio, axis=1, keepdims=True)
    ratio_ref[...] = jnp.broadcast_to(ratio, ratio_ref.shape)
    for h in range(heads):
        wq = wq_ref[h].T
        both_ref[h] = jnp.concatenate([wq, -wq], axis=1)


def join_kernel(*refs):
    got, out_ref, sems = refs[:-2], *refs[-2:]
    width = got[0].shape[1]
    place, side = spot()[0], lax.axis_index("head")
    copies = []
    for n, ref in enumerate(got):
        dr, dy = slot_of(n, lax.rem(place, 2) ^ (SLOTS[n][0][0] & 1))
        at = aligned((side ^ dy) * WAYS + (place ^ dr), width)
        copies.append(pltpu.make_async_copy(ref, out_ref.at[:, at], sems.at[n]))
    for copy in copies:
        copy.start()
    for copy in copies:
        copy.wait()


def write_key_features(keys, wk_ref, fk_ref):
    heads, feat, dh = wk_ref.shape
    logits = dot_t(wk_ref[...].reshape(heads * feat, dh), keys)
    for h in range(heads):
        part = logits[h * feat : (h + 1) * feat]
        top = jnp.max(part, axis=0, keepdims=True)
        low = jnp.min(part, axis=0, keepdims=True)
        for n, shifted in enumerate((part - top, low - part)):
            row = (2 * h + n) * feat
            expd = jnp.exp(shifted.astype(BF16))
            total = expd[: feat // 4]
            for q in range(1, 4):
                total = total + expd[q * feat // 4 : (q + 1) * feat // 4]
            total = jnp.sum(total.astype(F32), axis=0, keepdims=True)
            fk_ref[row : row + feat, :] = expd * pl.reciprocal(total).astype(BF16)


def own_features_kernel(own_ref, wk_ref, fk_ref):
    write_key_features(own_ref[:, :DH], wk_ref, fk_ref.at[:, own_ref.shape[0] :])


def last_features_kernel(last_ref, wk_ref, _, fk_ref, past_ref, step_ref):
    size = last_ref.shape[0]
    half = size // 2
    level = spot()[1]

    @pl.when(level == 0)
    def _():
        fk_ref[:, :size] = jnp.zeros((fk_ref.shape[0], size), BF16)
        for ref in (past_ref, step_ref):
            ref[...] = jnp.zeros_like(ref)

    @pl.when(level > 0)
    def _():
        write_key_features(last_ref[:, :DH], wk_ref, fk_ref.at[:, :size])
        for at, ref in ((0, past_ref), (half, step_ref)):
            ref[...] = jnp.dot(
                fk_ref[:, at : at + half],
                with_ones(last_ref[at : at + half, DH:]),
                preferred_element_type=F32,
            )


def past_kernel(before_ref, wk_ref, sum_ref, past_ref, fk_scr):
    level = spot()[1]

    @pl.when(level < 2)
    def _():
        past_ref[...] = sum_ref[...]

    @pl.when(level >= 2)
    def _():
        write_key_features(before_ref[:, :DH], wk_ref, fk_scr)
        past_ref[...] = sum_ref[...] + jnp.dot(
            fk_scr[...], with_ones(before_ref[:, DH:]), preferred_element_type=F32
        )


def query_features_kernel(a_ref, b_ref, w_ref, ratio_ref, q_out, fq_out, exp_scr):
    tok = a_ref.shape[0]
    heads, dh, both = w_ref.shape
    half = 2 * tok
    place = spot()[0]
    for d, ref in enumerate((a_ref, b_ref)):
        row = pl.multiple_of(lax.rem(place ^ d, 2) * tok, tok)
        for h in range(heads):
            q_out[pl.ds(h * half + row, tok), :] = ref[:, h * dh : (h + 1) * dh]
    rows_of = [slice(h * half, (h + 1) * half) for h in range(heads)]
    left = lax.broadcasted_iota(jnp.int32, (half, both), 1) < both // 2
    for h, rows in enumerate(rows_of):
        logits = jnp.dot(q_out[rows, :], w_ref[h], preferred_element_type=F32)
        top_l = jnp.max(jnp.where(left, logits, -jnp.inf), axis=1, keepdims=True)
        top_r = jnp.max(jnp.where(left, -jnp.inf, logits), axis=1, keepdims=True)
        exp_scr[rows, :] = jnp.exp((logits - jnp.where(left, top_l, top_r)).astype(BF16))
    side_r = lax.broadcasted_iota(jnp.int32, (both, both), 0) < both // 2
    side_c = lax.broadcasted_iota(jnp.int32, (both, both), 1) < both // 2
    halves = jnp.where(side_r == side_c, 1.0, 0.0).astype(BF16)
    total = jnp.dot(exp_scr[...], halves, preferred_element_type=F32)
    for h, rows in enumerate(rows_of):
        scale = pl.reciprocal(total[rows], approx=True) * ratio_ref[h : h + 1, :]
        fq_out[rows, :] = (exp_scr[rows, :].astype(F32) * scale).astype(BF16)


def near_kernel(other, q_ref, fq_ref, last_ref, own_ref, fk_ref, near_ref, kv_scr, w_scr):
    half, dh = last_ref.shape[0] // 2, q_ref.shape[1]
    heads = q_ref.shape[0] // half
    feats = fq_ref.shape[1]
    place, level = spot()
    u = lax.div(place, 2) ^ other
    kv_scr[:half, :] = last_ref[half:, :]
    kv_scr[half:, :] = own_ref[...]
    at = pl.ds(pl.multiple_of(u * half, half), 2 * half)
    keys, values = kv_scr[at, :dh], kv_scr[at, dh:]
    fk_at = pl.ds(pl.multiple_of((u + 1) * half, half), 2 * half)
    known = (level > 0) | (u > 0)
    cut = half - WINDOW
    row = lax.broadcasted_iota(jnp.int32, (WINDOW, 2 * half), 0)
    col = lax.broadcasted_iota(jnp.int32, (WINDOW, 2 * half), 1)
    inside = (col > row + cut) & (col <= row + half) & ((col >= half) | known)
    causal = (col <= row + cut)[:, :half]
    row, col = row[:, :half], col[:, :half]
    inside_low = (col > row) & (col <= row + WINDOW)
    causal_low = col <= row
    scores = dot_t(q_ref[...], keys)
    scale = math.log2(math.e) / math.sqrt(dh)

    def window(part, kept):
        masked = jnp.where(kept, part, -jnp.inf)
        top = jnp.max(masked, axis=1, keepdims=True)
        return jnp.exp2(((masked - top) * scale).astype(BF16))

    for h in range(heads):
        here = slice(h * half, (h + 1) * half)
        up, low = slice(h * half, h * half + cut), slice(h * half + cut, (h + 1) * half)
        linear = jnp.dot(
            fq_ref[here, :],
            fk_ref[h * feats : (h + 1) * feats, fk_at],
            preferred_element_type=F32,
        )
        soft = window(scores[up], inside)
        w_scr[up, :half] = soft[:, :half] + jnp.where(causal, linear[:cut, :half], 0.0).astype(BF16)
        w_scr[up, half:] = soft[:, half:]
        soft = window(scores[low, half:], inside_low)
        w_scr[low, :half] = linear[cut:, :half].astype(BF16)
        w_scr[low, half:] = soft + jnp.where(causal_low, linear[cut:, half:], 0.0).astype(BF16)
    values = jnp.concatenate(
        [with_ones(values[:half], known), with_ones(values[half:])], axis=0
    )
    near_ref[...] = jnp.dot(w_scr[...], values, preferred_element_type=F32)


def mix_kernel_of_level(*refs):
    near_refs, fq_refs, (past_ref, step_ref, wk_ref) = refs[:2], refs[2:4], refs[4:7]
    first_ref, refs = refs[7], refs[8:]
    out_refs, (fk_scr, state_scr, out_scr) = refs[:-3], refs[-3:]
    rows, dh = near_refs[0].shape[0], near_refs[0].shape[1] // 2
    feats = fq_refs[0].shape[1]
    heads = past_ref.shape[0] // feats
    half = rows // heads
    place, level = spot()
    side = lax.axis_index("head")
    u = lax.div(place, 2)

    @pl.when(level < 3)
    def _():
        state_scr[0] = past_ref[...].astype(BF16)
        state_scr[1] = (past_ref[...] + step_ref[...]).astype(BF16)

    @pl.when(level >= 3)
    def _():
        write_key_features(first_ref[:, :dh], wk_ref, fk_scr)
        state = past_ref[...] + jnp.dot(
            fk_scr[...], with_ones(first_ref[:, dh:]), preferred_element_type=F32
        )
        state_scr[0] = state.astype(BF16)
        state_scr[1] = (state + step_ref[...]).astype(BF16)

    part = out_refs[0].shape[0]
    for other in (1, 0):
        for h in range(heads):
            here = slice(h * half, (h + 1) * half)
            far = jnp.dot(
                fq_refs[other][here, :],
                state_scr[u ^ other, h * feats : (h + 1) * feats, :],
                preferred_element_type=F32,
            )
            both = near_refs[other][here, :] + far
            out_scr[aligned(u ^ other, half), h * dh : (h + 1) * dh] = (
                both[:, :dh] * pl.reciprocal(both[:, dh:], approx=True)
            ).astype(BF16)
    for n, ref in enumerate(out_refs):
        dr, dy = slot_of(n, lax.rem(place, 2))
        ref[...] = out_scr[aligned((place ^ dr) * 2 + (side ^ dy), part), :]


def whole_spec(space=pltpu.VMEM):
    return pl.BlockSpec(memory_space=space)


def call(kernel, ins, outs, name, scratch=(), limit=4, out_type=BF16, aliases={}):
    return pl.pallas_call(
        kernel,
        in_specs=[whole_spec() for _ in ins],
        out_specs=[whole_spec() for _ in outs],
        out_shape=[
            jax.ShapeDtypeStruct(s, out_type[n] if isinstance(out_type, list) else out_type)
            for n, s in enumerate(outs)
        ],
        scratch_shapes=list(scratch),
        input_output_aliases=aliases,
        compiler_params=pltpu.CompilerParams(vmem_limit_bytes=limit * 2**20),
        name=name,
    )(*ins)


def by_levels(queries, keys, values, wq, wk, factor):
    tok, width = queries.shape
    local_heads, feat, dh = wq.shape
    heads = local_heads // WAYS
    seq, sides = lax.axis_size("seq"), lax.axis_size("head")
    half = 2 * tok
    rows, states = heads * half, heads * 2 * feat

    def partner(x, dr, dy=0):
        pairs = [
            (i * sides + j, (i // WAYS * WAYS + (i % WAYS ^ dr)) * sides + (j ^ dy))
            for i in range(seq)
            for j in range(sides)
        ]
        return lax.ppermute(x, ("seq", "head"), pairs)

    def levels_back(x, by):
        pairs = [(i, i + by * WAYS) for i in range(seq - by * WAYS)]
        return lax.ppermute(x, "seq", pairs)

    own, away = call(pack_kv_kernel, [keys, values], [(tok, 4 * dh)] * 2, "pack_kv")
    got = partner(away, 2)
    q = list(call(pack_q_kernel, [queries], [(tok, width // WAYS)] * WAYS, "pack_q"))
    (pair,) = call(pair_kernel, [own, got], [(half, 2 * dh)], "pair_kv")
    *q, pair = lax.optimization_barrier((*q, pair))
    q[2], q[3] = partner(q[2], 2), partner(q[3], 3)
    pair = partner(pair, 1)
    at = lax.rem(lax.axis_index("seq"), WAYS) * heads
    wk = lax.dynamic_slice_in_dim(wk, at, heads)
    wq = lax.dynamic_slice_in_dim(wq, at, heads)
    pair, q[1], wk, wq = lax.optimization_barrier((pair, q[1], wk, wq))
    q[1] = partner(q[1], 1)
    (kv,) = call(stack_kernel, [own, got, pair], [(2 * half, 2 * dh)], "stack_kv")
    last = levels_back(kv, 1)
    wq, kv, q[1] = lax.optimization_barrier((wq, kv, q[1]))
    before = levels_back(kv, 2)

    (fk,) = call(own_features_kernel, [kv, wk], [(states, 4 * half)], "own_features", limit=16)
    wq, ratio = call(
        weights_kernel,
        [wq, factor.reshape(1, local_heads)],
        [(heads, dh, 2 * feat), (heads, 2 * feat)],
        "weights",
        out_type=[BF16, F32],
    )
    far_kv, fk, wq = lax.optimization_barrier((kv, fk, wq))
    first = levels_back(far_kv, 3)

    def query_features(a, b):
        return call(
            query_features_kernel,
            [a, b, wq, ratio],
            [(rows, dh), (rows, 2 * feat)],
            "query_features",
            [pltpu.VMEM((rows, 2 * feat), BF16)],
            12,
        )

    def near(other, q_rows, fq):
        return call(
            lambda *refs: near_kernel(other, *refs),
            [q_rows, fq, last, kv, fk],
            [(rows, 2 * dh)],
            "near",
            [
                pltpu.VMEM((3 * half, 2 * dh), BF16),
                pltpu.VMEM((rows, 2 * half), BF16),
            ],
            16,
            F32,
        )[0]

    q_own, fq_own = query_features(q[0], q[1])
    last, fq_own, fk = lax.optimization_barrier((last, fq_own, fk))
    fk, past, step = call(
        last_features_kernel,
        [last, wk, fk],
        [(states, 4 * half), (states, 2 * dh), (states, 2 * dh)],
        "last_features",
        limit=20,
        out_type=[BF16, F32, F32],
        aliases={2: 0},
    )
    near_own = near(0, q_own, fq_own)
    q[2], q[3], near_own = lax.optimization_barrier((q[2], q[3], near_own))
    q_other, fq_other = query_features(q[2], q[3])
    near_other = near(1, q_other, fq_other)
    before, near_other = lax.optimization_barrier((before, near_other))
    (past,) = call(
        past_kernel,
        [before, wk, past],
        [(states, 2 * dh)],
        "past",
        [pltpu.VMEM((states, 2 * half), BF16)],
        16,
        F32,
    )
    first, past = lax.optimization_barrier((first, past))
    part = tok // sides
    outs = call(
        mix_kernel_of_level,
        [near_own, near_other, fq_own, fq_other, past, step, wk, first],
        [(part, heads * dh)] * (WAYS * sides),
        "mix_level",
        [
            pltpu.VMEM((states, 2 * half), BF16),
            pltpu.VMEM((2, states, 2 * dh), BF16),
            pltpu.VMEM((2 * half, heads * dh), BF16),
        ],
        24,
    )

    def sent(x, slot):
        pairs = []
        for i in range(seq):
            dr, dy = slot[i % 2]
            to = i // WAYS * WAYS + (i % WAYS ^ dr)
            pairs += [(i * sides + j, to * sides + (j ^ dy)) for j in range(sides)]
        return lax.ppermute(x, ("seq", "head"), pairs)

    outs = list(outs)
    for n in range(1, 6):
        outs[n] = sent(outs[n], SLOTS[n])
    for n in (6, 7):
        outs[n], outs[n - 5] = lax.optimization_barrier((outs[n], outs[n - 5]))
        outs[n] = sent(outs[n], SLOTS[n])

    return pl.pallas_call(
        join_kernel,
        in_specs=[whole_spec()] * len(outs),
        out_specs=whole_spec(pltpu.HBM),
        out_shape=jax.ShapeDtypeStruct((part, sides * WAYS * heads * dh), BF16),
        scratch_shapes=[pltpu.SemaphoreType.DMA((len(outs),))],
        compiler_params=pltpu.CompilerParams(vmem_limit_bytes=4 * 2**20),
        name="join",
    )(*outs)


def by_blocks(queries, keys, values, wq, wk, ratio):
    group = wq.shape[0] // (keys.shape[1] // DH)
    place = lax.axis_index("seq").astype(jnp.int32).reshape(1)
    kv = lax.all_gather(jnp.concatenate([keys, values], axis=1), "seq", tiled=True)
    out = mix(place, queries, kv, wq, wk, ratio, group)
    return lax.all_to_all(out, "head", split_axis=0, concat_axis=1, tiled=True)


def local(queries, keys, values, q_feature, k_feature, window_factor):
    tok = queries.shape[0]
    seq, sides = lax.axis_size("seq"), lax.axis_size("head")
    wq, wk = jnp.swapaxes(q_feature, 1, 2), jnp.swapaxes(k_feature, 1, 2)
    if keys.shape[1] == WAYS * DH and seq == 4 * WAYS and sides == 2 and tok == WINDOW:
        return by_levels(queries, keys, values, wq, wk, window_factor)
    ratio = window_factor / (1.0 - window_factor)
    return by_blocks(queries, keys, values, wq, wk, ratio)


def solution(mesh):
    return jax.shard_map(
        local,
        mesh=mesh,
        in_specs=(
            P("seq", "head"),
            P("seq", "head"),
            P("seq", "head"),
            P("head", None, None),
            P("head", None, None),
            P("head"),
        ),
        out_specs=P(("seq", "head"), None),
        check_vma=False,
    )
```

```python
import math

import jax
import jax.numpy as jnp
from jax import lax
from jax.experimental import pallas as pl
from jax.experimental.pallas import tpu as pltpu
from jax.sharding import PartitionSpec as P

DH = 128
WINDOW = 64
F32 = jnp.float32
BF16 = jnp.bfloat16


def dot_t(a, b):
    return lax.dot_general(a, b, (((1,), (1,)), ((), ())), preferred_element_type=F32)


def features_t(logits):
    top = jnp.max(logits, axis=0, keepdims=True)
    low = jnp.min(logits, axis=0, keepdims=True)
    up = jnp.exp(logits - top)
    down = jnp.exp(low - logits)
    up = up * (1.0 / jnp.sum(up, axis=0, keepdims=True))
    down = down * (1.0 / jnp.sum(down, axis=0, keepdims=True))
    return jnp.concatenate([up.astype(BF16), down.astype(BF16)], axis=0)


def mix_kernel(
    place_ref, q_ref, k_ref, v_ref, wq_ref, wk_ref, ratio_ref, out_ref, fk_scr, state_scr
):
    tok = q_ref.shape[0]
    heads, feat, dh = wq_ref.shape
    seen = fk_scr.shape[1]
    place = place_ref[0]
    first_head = pl.program_id(0) * heads

    weights = wk_ref[...].reshape(heads * feat, dh)
    for start in range(0, seen, 256):
        size = min(256, seen - start)
        logits = dot_t(weights, k_ref[start : start + size, :])
        for h in range(heads):
            fk_scr[h * 2 * feat : (h + 1) * 2 * feat, start : start + size] = features_t(
                logits[h * feat : (h + 1) * feat]
            )
    row = lax.broadcasted_iota(jnp.int32, (seen, dh), 0)
    kept = row < (place - 1) * tok
    v_seen = jnp.where(kept, v_ref[:seen, :].astype(F32), 0.0).astype(BF16)
    ones_seen = jnp.where(kept, 1.0, 0.0).astype(BF16)
    v_seen = jnp.concatenate([v_seen, ones_seen], axis=1)
    state_scr[...] = jnp.dot(fk_scr[...], v_seen, preferred_element_type=F32).astype(BF16)

    before = pl.multiple_of(jnp.maximum(place - 1, 0) * tok, tok)
    own = pl.multiple_of(place * tok, tok)
    k_ext = jnp.concatenate([k_ref[pl.ds(before, tok), :], k_ref[pl.ds(own, tok), :]], axis=0)
    v_ext = jnp.concatenate([v_ref[pl.ds(before, tok), :], v_ref[pl.ds(own, tok), :]], axis=0)
    v_ext = jnp.concatenate([v_ext, jnp.ones_like(v_ext)], axis=1)
    row = lax.broadcasted_iota(jnp.int32, (tok, 2 * tok), 0)
    col = lax.broadcasted_iota(jnp.int32, (tok, 2 * tok), 1)
    valid = (col >= tok) | (place > 0)
    inside = (col > row) & (col <= row + WINDOW) & valid
    causal = (col <= row) & valid
    lane = lax.broadcasted_iota(jnp.int32, (tok, 2 * feat), 1)
    left = lane < feat
    side_r = lax.broadcasted_iota(jnp.int32, (2 * feat, 2 * feat), 0) < feat
    side_c = lax.broadcasted_iota(jnp.int32, (2 * feat, 2 * feat), 1) < feat
    halves = jnp.where(side_r == side_c, 1.0, 0.0).astype(BF16)

    for h in range(heads):
        q = q_ref[:, h * dh : (h + 1) * dh]
        wq = wq_ref[h]
        logits = dot_t(q, jnp.concatenate([wq, -wq], axis=0))
        top_l = jnp.max(jnp.where(left, logits, -jnp.inf), axis=1, keepdims=True)
        top_r = jnp.max(jnp.where(left, -jnp.inf, logits), axis=1, keepdims=True)
        expd = jnp.exp(logits - jnp.where(left, top_l, top_r)).astype(BF16)
        total = jnp.dot(expd, halves, preferred_element_type=F32)
        fq = (expd.astype(F32) / total).astype(BF16)
        fk = features_t(dot_t(wk_ref[h], k_ext))
        linear = jnp.dot(fq, fk, preferred_element_type=F32)
        scores = dot_t(q, k_ext) * (1.0 / math.sqrt(dh))
        masked = jnp.where(inside, scores, -jnp.inf)
        top = jnp.max(masked, axis=1, keepdims=True)
        soft = jnp.exp(masked - top) * ratio_ref[first_head + h]
        weight = jnp.where(causal, linear, soft).astype(BF16)
        both = jnp.dot(weight, v_ext, preferred_element_type=F32) + jnp.dot(
            fq, state_scr[h * 2 * feat : (h + 1) * 2 * feat, :], preferred_element_type=F32
        )
        out_ref[:, h * dh : (h + 1) * dh] = (both[:, :dh] / both[:, dh:]).astype(BF16)


def mix(place, queries, kv, wq, wk, ratio, group):
    tok = queries.shape[0]
    local_heads, feat, dh = wq.shape
    groups = local_heads // group
    tokens = kv.shape[0]
    seen = tokens - 2 * tok
    return pl.pallas_call(
        mix_kernel,
        grid_spec=pltpu.PrefetchScalarGridSpec(
            num_scalar_prefetch=1,
            grid=(groups,),
            in_specs=[
                pl.BlockSpec((tok, group * dh), lambda g, p: (0, g)),
                pl.BlockSpec((tokens, dh), lambda g, p: (0, g)),
                pl.BlockSpec((tokens, dh), lambda g, p: (0, groups + g)),
                pl.BlockSpec((group, feat, dh), lambda g, p: (g, 0, 0)),
                pl.BlockSpec((group, feat, dh), lambda g, p: (g, 0, 0)),
                pl.BlockSpec(memory_space=pltpu.SMEM),
            ],
            out_specs=pl.BlockSpec((tok, group * dh), lambda g, p: (0, g)),
            scratch_shapes=[
                pltpu.VMEM((group * 2 * feat, seen), BF16),
                pltpu.VMEM((group * 2 * feat, 2 * dh), BF16),
            ],
        ),
        out_shape=jax.ShapeDtypeStruct(queries.shape, BF16),
        compiler_params=pltpu.CompilerParams(vmem_limit_bytes=48 * 2**20),
        cost_estimate=pl.CostEstimate(
            flops=2 * local_heads * tokens * 3 * feat * 2 * dh,
            bytes_accessed=8 * 2**20,
            transcendentals=local_heads * tokens * 2 * feat,
        ),
    )(place, queries, kv, kv, wq, wk, ratio)


WAYS = 4


SLOTS = (
    ((0, 0), (0, 0)),
    ((2, 0), (0, 1)),
    ((0, 1), (2, 0)),
    ((3, 0), (1, 1)),
    ((1, 1), (3, 0)),
    ((2, 1), (2, 1)),
    ((3, 1), (3, 1)),
    ((1, 0), (1, 0)),
)


def slot_of(n, odd):
    return [jnp.where(odd == 1, b, a) if a != b else a for a, b in zip(*SLOTS[n])]


def spot():
    at = lax.axis_index("seq")
    return lax.rem(at, WAYS), lax.div(at, WAYS)


def aligned(at, step):
    return pl.ds(pl.multiple_of(at * step, step), step)


def with_ones(values, kept=True):
    here = jnp.where(kept, 1.0, 0.0).astype(BF16)
    return jnp.concatenate([values, jnp.full(values.shape, here)], axis=1)


def pack_kv_kernel(k_ref, v_ref, own_ref, away_ref):
    place = spot()[0]
    for d in range(WAYS):
        ref, at = (own_ref, away_ref)[d // 2], d % 2 * 2 * DH
        ref[:, at : at + DH] = k_ref[:, aligned(place ^ d, DH)]
        ref[:, at + DH : at + 2 * DH] = v_ref[:, aligned(place ^ d, DH)]


def pair_kernel(own_ref, got_ref, out_ref):
    tok = own_ref.shape[0]
    out_ref[:tok, :] = own_ref[:, 2 * DH :]
    out_ref[tok:, :] = got_ref[:, 2 * DH :]


def stack_kernel(own_ref, got_ref, pair_ref, out_ref):
    tok = own_ref.shape[0]
    place = spot()[0]
    out_ref[aligned(place, tok), :] = own_ref[:, : 2 * DH]
    out_ref[aligned(place ^ 2, tok), :] = got_ref[:, : 2 * DH]
    out_ref[aligned(place ^ 1, tok), :] = pair_ref[:tok, :]
    out_ref[aligned(place ^ 3, tok), :] = pair_ref[tok:, :]


def pack_q_kernel(q_ref, *out_refs):
    place = spot()[0]
    for d, out in enumerate(out_refs):
        out[...] = q_ref[:, aligned(place ^ d, out.shape[1])]


def weights_kernel(wq_ref, factor_ref, both_ref, ratio_ref):
    heads = both_ref.shape[0]
    shape = (heads, factor_ref.shape[1])
    head = lax.broadcasted_iota(jnp.int32, shape, 0) + spot()[0] * heads
    ratio = jnp.broadcast_to((1.0 - factor_ref[...]) / factor_ref[...], shape)
    ratio = jnp.where(lax.broadcasted_iota(jnp.int32, shape, 1) == head, ratio, 0.0)
    ratio = jnp.sum(ratio, axis=1, keepdims=True)
    ratio_ref[...] = jnp.broadcast_to(ratio, ratio_ref.shape)
    for h in range(heads):
        wq = wq_ref[h].T
        both_ref[h] = jnp.concatenate([wq, -wq], axis=1)


def join_kernel(*refs):
    got, out_ref, sems = refs[:-2], *refs[-2:]
    width = got[0].shape[1]
    place, side = spot()[0], lax.axis_index("head")
    copies = []
    for n, ref in enumerate(got):
        dr, dy = slot_of(n, lax.rem(place, 2) ^ (SLOTS[n][0][0] & 1))
        at = aligned((side ^ dy) * WAYS + (place ^ dr), width)
        copies.append(pltpu.make_async_copy(ref, out_ref.at[:, at], sems.at[n]))
    for copy in copies:
        copy.start()
    for copy in copies:
        copy.wait()


def write_key_features(keys, wk_ref, fk_ref):
    heads, feat, dh = wk_ref.shape
    logits = dot_t(wk_ref[...].reshape(heads * feat, dh), keys)
    for h in range(heads):
        part = logits[h * feat : (h + 1) * feat]
        top = jnp.max(part, axis=0, keepdims=True)
        low = jnp.min(part, axis=0, keepdims=True)
        for n, shifted in enumerate((part - top, low - part)):
            row = (2 * h + n) * feat
            expd = jnp.exp(shifted.astype(BF16))
            total = expd[: feat // 4]
            for q in range(1, 4):
                total = total + expd[q * feat // 4 : (q + 1) * feat // 4]
            total = jnp.sum(total.astype(F32), axis=0, keepdims=True)
            fk_ref[row : row + feat, :] = expd * pl.reciprocal(total).astype(BF16)


def own_features_kernel(own_ref, wk_ref, fk_ref):
    write_key_features(own_ref[:, :DH], wk_ref, fk_ref.at[:, own_ref.shape[0] :])


def last_features_kernel(last_ref, wk_ref, _, fk_ref, past_ref, step_ref):
    size = last_ref.shape[0]
    half = size // 2
    level = spot()[1]

    @pl.when(level == 0)
    def _():
        fk_ref[:, :size] = jnp.zeros((fk_ref.shape[0], size), BF16)
        for ref in (past_ref, step_ref):
            ref[...] = jnp.zeros_like(ref)

    @pl.when(level > 0)
    def _():
        write_key_features(last_ref[:, :DH], wk_ref, fk_ref.at[:, :size])
        for at, ref in ((0, past_ref), (half, step_ref)):
            ref[...] = jnp.dot(
                fk_ref[:, at : at + half],
                with_ones(last_ref[at : at + half, DH:]),
                preferred_element_type=F32,
            )


def past_kernel(before_ref, wk_ref, sum_ref, past_ref, fk_scr):
    level = spot()[1]

    @pl.when(level < 2)
    def _():
        past_ref[...] = sum_ref[...]

    @pl.when(level >= 2)
    def _():
        write_key_features(before_ref[:, :DH], wk_ref, fk_scr)
        past_ref[...] = sum_ref[...] + jnp.dot(
            fk_scr[...], with_ones(before_ref[:, DH:]), preferred_element_type=F32
        )


def query_features_kernel(a_ref, b_ref, w_ref, ratio_ref, q_out, fq_out, exp_scr):
    tok = a_ref.shape[0]
    heads, dh, both = w_ref.shape
    half = 2 * tok
    place = spot()[0]
    for d, ref in enumerate((a_ref, b_ref)):
        row = pl.multiple_of(lax.rem(place ^ d, 2) * tok, tok)
        for h in range(heads):
            q_out[pl.ds(h * half + row, tok), :] = ref[:, h * dh : (h + 1) * dh]
    rows_of = [slice(h * half, (h + 1) * half) for h in range(heads)]
    left = lax.broadcasted_iota(jnp.int32, (half, both), 1) < both // 2
    for h, rows in enumerate(rows_of):
        logits = jnp.dot(q_out[rows, :], w_ref[h], preferred_element_type=F32)
        top_l = jnp.max(jnp.where(left, logits, -jnp.inf), axis=1, keepdims=True)
        top_r = jnp.max(jnp.where(left, -jnp.inf, logits), axis=1, keepdims=True)
        exp_scr[rows, :] = jnp.exp((logits - jnp.where(left, top_l, top_r)).astype(BF16))
    side_r = lax.broadcasted_iota(jnp.int32, (both, both), 0) < both // 2
    side_c = lax.broadcasted_iota(jnp.int32, (both, both), 1) < both // 2
    halves = jnp.where(side_r == side_c, 1.0, 0.0).astype(BF16)
    total = jnp.dot(exp_scr[...], halves, preferred_element_type=F32)
    for h, rows in enumerate(rows_of):
        scale = pl.reciprocal(total[rows], approx=True) * ratio_ref[h : h + 1, :]
        fq_out[rows, :] = (exp_scr[rows, :].astype(F32) * scale).astype(BF16)


def near_kernel(other, q_ref, fq_ref, last_ref, own_ref, fk_ref, near_ref, kv_scr, w_scr):
    half, dh = last_ref.shape[0] // 2, q_ref.shape[1]
    heads = q_ref.shape[0] // half
    feats = fq_ref.shape[1]
    place, level = spot()
    u = lax.div(place, 2) ^ other
    kv_scr[:half, :] = last_ref[half:, :]
    kv_scr[half:, :] = own_ref[...]
    at = pl.ds(pl.multiple_of(u * half, half), 2 * half)
    keys, values = kv_scr[at, :dh], kv_scr[at, dh:]
    fk_at = pl.ds(pl.multiple_of((u + 1) * half, half), 2 * half)
    known = (level > 0) | (u > 0)
    cut = half - WINDOW
    row = lax.broadcasted_iota(jnp.int32, (WINDOW, 2 * half), 0)
    col = lax.broadcasted_iota(jnp.int32, (WINDOW, 2 * half), 1)
    inside = (col > row + cut) & (col <= row + half) & ((col >= half) | known)
    causal = (col <= row + cut)[:, :half]
    row, col = row[:, :half], col[:, :half]
    inside_low = (col > row) & (col <= row + WINDOW)
    causal_low = col <= row
    scores = dot_t(q_ref[...], keys)
    scale = math.log2(math.e) / math.sqrt(dh)

    def window(part, kept):
        masked = jnp.where(kept, part, -jnp.inf)
        top = jnp.max(masked, axis=1, keepdims=True)
        return jnp.exp2(((masked - top) * scale).astype(BF16))

    for h in range(heads):
        here = slice(h * half, (h + 1) * half)
        up, low = slice(h * half, h * half + cut), slice(h * half + cut, (h + 1) * half)
        linear = jnp.dot(
            fq_ref[here, :],
            fk_ref[h * feats : (h + 1) * feats, fk_at],
            preferred_element_type=F32,
        )
        soft = window(scores[up], inside)
        w_scr[up, :half] = soft[:, :half] + jnp.where(causal, linear[:cut, :half], 0.0).astype(BF16)
        w_scr[up, half:] = soft[:, half:]
        soft = window(scores[low, half:], inside_low)
        w_scr[low, :half] = linear[cut:, :half].astype(BF16)
        w_scr[low, half:] = soft + jnp.where(causal_low, linear[cut:, half:], 0.0).astype(BF16)
    values = jnp.concatenate(
        [with_ones(values[:half], known), with_ones(values[half:])], axis=0
    )
    near_ref[...] = jnp.dot(w_scr[...], values, preferred_element_type=F32)


def mix_kernel_of_level(*refs):
    near_refs, fq_refs, (past_ref, step_ref, wk_ref) = refs[:2], refs[2:4], refs[4:7]
    first_ref, refs = refs[7], refs[8:]
    out_refs, (fk_scr, state_scr, out_scr) = refs[:-3], refs[-3:]
    rows, dh = near_refs[0].shape[0], near_refs[0].shape[1] // 2
    feats = fq_refs[0].shape[1]
    heads = past_ref.shape[0] // feats
    half = rows // heads
    place, level = spot()
    side = lax.axis_index("head")
    u = lax.div(place, 2)

    @pl.when(level < 3)
    def _():
        state_scr[0] = past_ref[...].astype(BF16)
        state_scr[1] = (past_ref[...] + step_ref[...]).astype(BF16)

    @pl.when(level >= 3)
    def _():
        write_key_features(first_ref[:, :dh], wk_ref, fk_scr)
        state = past_ref[...] + jnp.dot(
            fk_scr[...], with_ones(first_ref[:, dh:]), preferred_element_type=F32
        )
        state_scr[0] = state.astype(BF16)
        state_scr[1] = (state + step_ref[...]).astype(BF16)

    part = out_refs[0].shape[0]
    for other in (1, 0):
        for h in range(heads):
            here = slice(h * half, (h + 1) * half)
            far = jnp.dot(
                fq_refs[other][here, :],
                state_scr[u ^ other, h * feats : (h + 1) * feats, :],
                preferred_element_type=F32,
            )
            both = near_refs[other][here, :] + far
            out_scr[aligned(u ^ other, half), h * dh : (h + 1) * dh] = (
                both[:, :dh] * pl.reciprocal(both[:, dh:], approx=True)
            ).astype(BF16)
    for n, ref in enumerate(out_refs):
        dr, dy = slot_of(n, lax.rem(place, 2))
        ref[...] = out_scr[aligned((place ^ dr) * 2 + (side ^ dy), part), :]


def whole_spec(space=pltpu.VMEM):
    return pl.BlockSpec(memory_space=space)


def call(kernel, ins, outs, name, scratch=(), limit=4, out_type=BF16, aliases={}):
    return pl.pallas_call(
        kernel,
        in_specs=[whole_spec() for _ in ins],
        out_specs=[whole_spec() for _ in outs],
        out_shape=[
            jax.ShapeDtypeStruct(s, out_type[n] if isinstance(out_type, list) else out_type)
            for n, s in enumerate(outs)
        ],
        scratch_shapes=list(scratch),
        input_output_aliases=aliases,
        compiler_params=pltpu.CompilerParams(vmem_limit_bytes=limit * 2**20),
        name=name,
    )(*ins)


def by_levels(queries, keys, values, wq, wk, factor):
    tok, width = queries.shape
    local_heads, feat, dh = wq.shape
    heads = local_heads // WAYS
    seq, sides = lax.axis_size("seq"), lax.axis_size("head")
    half = 2 * tok
    rows, states = heads * half, heads * 2 * feat

    def partner(x, dr, dy=0):
        pairs = [
            (i * sides + j, (i // WAYS * WAYS + (i % WAYS ^ dr)) * sides + (j ^ dy))
            for i in range(seq)
            for j in range(sides)
        ]
        return lax.ppermute(x, ("seq", "head"), pairs)

    def levels_back(x, by):
        pairs = [(i, i + by * WAYS) for i in range(seq - by * WAYS)]
        return lax.ppermute(x, "seq", pairs)

    own, away = call(pack_kv_kernel, [keys, values], [(tok, 4 * dh)] * 2, "pack_kv")
    got = partner(away, 2)
    q = list(call(pack_q_kernel, [queries], [(tok, width // WAYS)] * WAYS, "pack_q"))
    (pair,) = call(pair_kernel, [own, got], [(half, 2 * dh)], "pair_kv")
    *q, pair = lax.optimization_barrier((*q, pair))
    pair = partner(pair, 1)
    q[1], q[2], q[3] = partner(q[1], 1), partner(q[2], 2), partner(q[3], 3)
    (kv,) = call(stack_kernel, [own, got, pair], [(2 * half, 2 * dh)], "stack_kv")
    last, before = levels_back(kv, 1), levels_back(kv, 2)
    wq, wk, kv, q[1] = lax.optimization_barrier((wq, wk, kv, q[1]))
    at = lax.rem(lax.axis_index("seq"), WAYS) * heads
    wq, wk = [lax.dynamic_slice_in_dim(w, at, heads) for w in (wq, wk)]
    wq, wk = lax.optimization_barrier((wq, wk))
    (fk,) = call(own_features_kernel, [kv, wk], [(states, 4 * half)], "own_features", limit=16)
    wq, ratio = call(
        weights_kernel,
        [wq, factor.reshape(1, local_heads)],
        [(heads, dh, 2 * feat), (heads, 2 * feat)],
        "weights",
        out_type=[BF16, F32],
    )
    far_kv, fk, wq = lax.optimization_barrier((kv, fk, wq))
    first = levels_back(far_kv, 3)

    def query_features(a, b):
        return call(
            query_features_kernel,
            [a, b, wq, ratio],
            [(rows, dh), (rows, 2 * feat)],
            "query_features",
            [pltpu.VMEM((rows, 2 * feat), BF16)],
            12,
        )

    def near(other, q_rows, fq):
        return call(
            lambda *refs: near_kernel(other, *refs),
            [q_rows, fq, last, kv, fk],
            [(rows, 2 * dh)],
            "near",
            [
                pltpu.VMEM((3 * half, 2 * dh), BF16),
                pltpu.VMEM((rows, 2 * half), BF16),
            ],
            16,
            F32,
        )[0]

    q_own, fq_own = query_features(q[0], q[1])
    last, fq_own, fk = lax.optimization_barrier((last, fq_own, fk))
    fk, past, step = call(
        last_features_kernel,
        [last, wk, fk],
        [(states, 4 * half), (states, 2 * dh), (states, 2 * dh)],
        "last_features",
        limit=20,
        out_type=[BF16, F32, F32],
        aliases={2: 0},
    )
    near_own = near(0, q_own, fq_own)
    q[2], q[3], near_own = lax.optimization_barrier((q[2], q[3], near_own))
    q_other, fq_other = query_features(q[2], q[3])
    near_other = near(1, q_other, fq_other)
    before, near_other = lax.optimization_barrier((before, near_other))
    (past,) = call(
        past_kernel,
        [before, wk, past],
        [(states, 2 * dh)],
        "past",
        [pltpu.VMEM((states, 2 * half), BF16)],
        16,
        F32,
    )
    first, past = lax.optimization_barrier((first, past))
    part = tok // sides
    outs = call(
        mix_kernel_of_level,
        [near_own, near_other, fq_own, fq_other, past, step, wk, first],
        [(part, heads * dh)] * (WAYS * sides),
        "mix_level",
        [
            pltpu.VMEM((states, 2 * half), BF16),
            pltpu.VMEM((2, states, 2 * dh), BF16),
            pltpu.VMEM((2 * half, heads * dh), BF16),
        ],
        24,
    )

    def sent(x, slot):
        pairs = []
        for i in range(seq):
            dr, dy = slot[i % 2]
            to = i // WAYS * WAYS + (i % WAYS ^ dr)
            pairs += [(i * sides + j, to * sides + (j ^ dy)) for j in range(sides)]
        return lax.ppermute(x, ("seq", "head"), pairs)

    outs = list(outs)
    for n in range(1, 6):
        outs[n] = sent(outs[n], SLOTS[n])
    for n, ahead in ((6, 2), (7, 1)):
        outs[n], outs[ahead] = lax.optimization_barrier((outs[n], outs[ahead]))
        outs[n] = sent(outs[n], SLOTS[n])

    return pl.pallas_call(
        join_kernel,
        in_specs=[whole_spec()] * len(outs),
        out_specs=whole_spec(pltpu.HBM),
        out_shape=jax.ShapeDtypeStruct((part, sides * WAYS * heads * dh), BF16),
        scratch_shapes=[pltpu.SemaphoreType.DMA((len(outs),))],
        compiler_params=pltpu.CompilerParams(vmem_limit_bytes=4 * 2**20),
        name="join",
    )(*outs)


def by_blocks(queries, keys, values, wq, wk, ratio):
    group = wq.shape[0] // (keys.shape[1] // DH)
    place = lax.axis_index("seq").astype(jnp.int32).reshape(1)
    kv = lax.all_gather(jnp.concatenate([keys, values], axis=1), "seq", tiled=True)
    out = mix(place, queries, kv, wq, wk, ratio, group)
    return lax.all_to_all(out, "head", split_axis=0, concat_axis=1, tiled=True)


def local(queries, keys, values, q_feature, k_feature, window_factor):
    tok = queries.shape[0]
    seq, sides = lax.axis_size("seq"), lax.axis_size("head")
    wq, wk = jnp.swapaxes(q_feature, 1, 2), jnp.swapaxes(k_feature, 1, 2)
    if keys.shape[1] == WAYS * DH and seq == 4 * WAYS and sides == 2 and tok == WINDOW:
        return by_levels(queries, keys, values, wq, wk, window_factor)
    ratio = window_factor / (1.0 - window_factor)
    return by_blocks(queries, keys, values, wq, wk, ratio)


def solution(mesh):
    return jax.shard_map(
        local,
        mesh=mesh,
        in_specs=(
            P("seq", "head"),
            P("seq", "head"),
            P("seq", "head"),
            P("head", None, None),
            P("head", None, None),
            P("head"),
        ),
        out_specs=P(("seq", "head"), None),
        check_vma=False,
    )
```

```python
import math

import jax
import jax.numpy as jnp
from jax import lax
from jax.experimental import pallas as pl
from jax.experimental.pallas import tpu as pltpu
from jax.sharding import PartitionSpec as P

DH = 128
WINDOW = 64
F32 = jnp.float32
BF16 = jnp.bfloat16


def dot_t(a, b):
    return lax.dot_general(a, b, (((1,), (1,)), ((), ())), preferred_element_type=F32)


def features_t(logits):
    top = jnp.max(logits, axis=0, keepdims=True)
    low = jnp.min(logits, axis=0, keepdims=True)
    up = jnp.exp(logits - top)
    down = jnp.exp(low - logits)
    up = up * (1.0 / jnp.sum(up, axis=0, keepdims=True))
    down = down * (1.0 / jnp.sum(down, axis=0, keepdims=True))
    return jnp.concatenate([up.astype(BF16), down.astype(BF16)], axis=0)


def mix_kernel(
    place_ref, q_ref, k_ref, v_ref, wq_ref, wk_ref, ratio_ref, out_ref, fk_scr, state_scr
):
    tok = q_ref.shape[0]
    heads, feat, dh = wq_ref.shape
    seen = fk_scr.shape[1]
    place = place_ref[0]
    first_head = pl.program_id(0) * heads

    weights = wk_ref[...].reshape(heads * feat, dh)
    for start in range(0, seen, 256):
        size = min(256, seen - start)
        logits = dot_t(weights, k_ref[start : start + size, :])
        for h in range(heads):
            fk_scr[h * 2 * feat : (h + 1) * 2 * feat, start : start + size] = features_t(
                logits[h * feat : (h + 1) * feat]
            )
    row = lax.broadcasted_iota(jnp.int32, (seen, dh), 0)
    kept = row < (place - 1) * tok
    v_seen = jnp.where(kept, v_ref[:seen, :].astype(F32), 0.0).astype(BF16)
    ones_seen = jnp.where(kept, 1.0, 0.0).astype(BF16)
    v_seen = jnp.concatenate([v_seen, ones_seen], axis=1)
    state_scr[...] = jnp.dot(fk_scr[...], v_seen, preferred_element_type=F32).astype(BF16)

    before = pl.multiple_of(jnp.maximum(place - 1, 0) * tok, tok)
    own = pl.multiple_of(place * tok, tok)
    k_ext = jnp.concatenate([k_ref[pl.ds(before, tok), :], k_ref[pl.ds(own, tok), :]], axis=0)
    v_ext = jnp.concatenate([v_ref[pl.ds(before, tok), :], v_ref[pl.ds(own, tok), :]], axis=0)
    v_ext = jnp.concatenate([v_ext, jnp.ones_like(v_ext)], axis=1)
    row = lax.broadcasted_iota(jnp.int32, (tok, 2 * tok), 0)
    col = lax.broadcasted_iota(jnp.int32, (tok, 2 * tok), 1)
    valid = (col >= tok) | (place > 0)
    inside = (col > row) & (col <= row + WINDOW) & valid
    causal = (col <= row) & valid
    lane = lax.broadcasted_iota(jnp.int32, (tok, 2 * feat), 1)
    left = lane < feat
    side_r = lax.broadcasted_iota(jnp.int32, (2 * feat, 2 * feat), 0) < feat
    side_c = lax.broadcasted_iota(jnp.int32, (2 * feat, 2 * feat), 1) < feat
    halves = jnp.where(side_r == side_c, 1.0, 0.0).astype(BF16)

    for h in range(heads):
        q = q_ref[:, h * dh : (h + 1) * dh]
        wq = wq_ref[h]
        logits = dot_t(q, jnp.concatenate([wq, -wq], axis=0))
        top_l = jnp.max(jnp.where(left, logits, -jnp.inf), axis=1, keepdims=True)
        top_r = jnp.max(jnp.where(left, -jnp.inf, logits), axis=1, keepdims=True)
        expd = jnp.exp(logits - jnp.where(left, top_l, top_r)).astype(BF16)
        total = jnp.dot(expd, halves, preferred_element_type=F32)
        fq = (expd.astype(F32) / total).astype(BF16)
        fk = features_t(dot_t(wk_ref[h], k_ext))
        linear = jnp.dot(fq, fk, preferred_element_type=F32)
        scores = dot_t(q, k_ext) * (1.0 / math.sqrt(dh))
        masked = jnp.where(inside, scores, -jnp.inf)
        top = jnp.max(masked, axis=1, keepdims=True)
        soft = jnp.exp(masked - top) * ratio_ref[first_head + h]
        weight = jnp.where(causal, linear, soft).astype(BF16)
        both = jnp.dot(weight, v_ext, preferred_element_type=F32) + jnp.dot(
            fq, state_scr[h * 2 * feat : (h + 1) * 2 * feat, :], preferred_element_type=F32
        )
        out_ref[:, h * dh : (h + 1) * dh] = (both[:, :dh] / both[:, dh:]).astype(BF16)


def mix(place, queries, kv, wq, wk, ratio, group):
    tok = queries.shape[0]
    local_heads, feat, dh = wq.shape
    groups = local_heads // group
    tokens = kv.shape[0]
    seen = tokens - 2 * tok
    return pl.pallas_call(
        mix_kernel,
        grid_spec=pltpu.PrefetchScalarGridSpec(
            num_scalar_prefetch=1,
            grid=(groups,),
            in_specs=[
                pl.BlockSpec((tok, group * dh), lambda g, p: (0, g)),
                pl.BlockSpec((tokens, dh), lambda g, p: (0, g)),
                pl.BlockSpec((tokens, dh), lambda g, p: (0, groups + g)),
                pl.BlockSpec((group, feat, dh), lambda g, p: (g, 0, 0)),
                pl.BlockSpec((group, feat, dh), lambda g, p: (g, 0, 0)),
                pl.BlockSpec(memory_space=pltpu.SMEM),
            ],
            out_specs=pl.BlockSpec((tok, group * dh), lambda g, p: (0, g)),
            scratch_shapes=[
                pltpu.VMEM((group * 2 * feat, seen), BF16),
                pltpu.VMEM((group * 2 * feat, 2 * dh), BF16),
            ],
        ),
        out_shape=jax.ShapeDtypeStruct(queries.shape, BF16),
        compiler_params=pltpu.CompilerParams(vmem_limit_bytes=48 * 2**20),
        cost_estimate=pl.CostEstimate(
            flops=2 * local_heads * tokens * 3 * feat * 2 * dh,
            bytes_accessed=8 * 2**20,
            transcendentals=local_heads * tokens * 2 * feat,
        ),
    )(place, queries, kv, kv, wq, wk, ratio)


WAYS = 4


SLOTS = (
    ((0, 0), (0, 0)),
    ((2, 0), (0, 1)),
    ((0, 1), (2, 0)),
    ((3, 0), (1, 1)),
    ((1, 1), (3, 0)),
    ((2, 1), (2, 1)),
    ((3, 1), (3, 1)),
    ((1, 0), (1, 0)),
)


def slot_of(n, odd):
    return [jnp.where(odd == 1, b, a) if a != b else a for a, b in zip(*SLOTS[n])]


def spot():
    at = lax.axis_index("seq")
    return lax.rem(at, WAYS), lax.div(at, WAYS)


def aligned(at, step):
    return pl.ds(pl.multiple_of(at * step, step), step)


def with_ones(values, kept=True):
    here = jnp.where(kept, 1.0, 0.0).astype(BF16)
    return jnp.concatenate([values, jnp.full(values.shape, here)], axis=1)


def pack_kv_kernel(k_ref, v_ref, k_away_ref, v_away_ref, own_ref, away_ref):
    odd = lax.rem(spot()[0], 2)
    for k, v, ref in ((k_ref, v_ref, own_ref), (k_away_ref, v_away_ref, away_ref)):
        for d in range(2):
            at = aligned(odd ^ d, DH)
            ref[:, 2 * d * DH : (2 * d + 1) * DH] = k[:, at]
            ref[:, (2 * d + 1) * DH : (2 * d + 2) * DH] = v[:, at]


def pair_kernel(own_ref, got_ref, out_ref):
    tok = own_ref.shape[0]
    out_ref[:tok, :] = own_ref[:, 2 * DH :]
    out_ref[tok:, :] = got_ref[:, 2 * DH :]


def stack_kernel(own_ref, got_ref, pair_ref, out_ref):
    tok = own_ref.shape[0]
    place = spot()[0]
    out_ref[aligned(place, tok), :] = own_ref[:, : 2 * DH]
    out_ref[aligned(place ^ 2, tok), :] = got_ref[:, : 2 * DH]
    out_ref[aligned(place ^ 1, tok), :] = pair_ref[:tok, :]
    out_ref[aligned(place ^ 3, tok), :] = pair_ref[tok:, :]


def pack_q_kernel(q_ref, *out_refs):
    place = spot()[0]
    for d, out in enumerate(out_refs):
        out[...] = q_ref[:, aligned(place ^ d, out.shape[1])]


def weights_kernel(wq_ref, factor_ref, both_ref, ratio_ref):
    heads = both_ref.shape[0]
    shape = (heads, factor_ref.shape[1])
    head = lax.broadcasted_iota(jnp.int32, shape, 0) + spot()[0] * heads
    ratio = jnp.broadcast_to((1.0 - factor_ref[...]) / factor_ref[...], shape)
    ratio = jnp.where(lax.broadcasted_iota(jnp.int32, shape, 1) == head, ratio, 0.0)
    ratio = jnp.sum(ratio, axis=1, keepdims=True)
    ratio_ref[...] = jnp.broadcast_to(ratio, ratio_ref.shape)
    for h in range(heads):
        wq = wq_ref[h].T
        both_ref[h] = jnp.concatenate([wq, -wq], axis=1)


def join_kernel(slots, *refs):
    got, out_ref, sems = refs[: len(slots)], *refs[-2:]
    width = got[0].shape[1]
    place, side = spot()[0], lax.axis_index("head")
    copies = []
    for n, ref in zip(slots, got):
        dr, dy = slot_of(n, lax.rem(place, 2) ^ (SLOTS[n][0][0] & 1))
        at = aligned((side ^ dy) * WAYS + (place ^ dr), width)
        copies.append(pltpu.make_async_copy(ref, out_ref.at[:, at], sems.at[len(copies)]))
    for copy in copies:
        copy.start()
    for copy in copies:
        copy.wait()


def write_key_features(keys, wk_ref, fk_ref):
    heads, feat, dh = wk_ref.shape
    logits = dot_t(wk_ref[...].reshape(heads * feat, dh), keys)
    for h in range(heads):
        part = logits[h * feat : (h + 1) * feat]
        top = jnp.max(part, axis=0, keepdims=True)
        low = jnp.min(part, axis=0, keepdims=True)
        for n, shifted in enumerate((part - top, low - part)):
            row = (2 * h + n) * feat
            expd = jnp.exp(shifted.astype(BF16))
            total = expd[: feat // 4]
            for q in range(1, 4):
                total = total + expd[q * feat // 4 : (q + 1) * feat // 4]
            total = jnp.sum(total.astype(F32), axis=0, keepdims=True)
            fk_ref[row : row + feat, :] = expd * pl.reciprocal(total).astype(BF16)


def own_features_kernel(own_ref, wk_ref, fk_ref):
    write_key_features(own_ref[:, :DH], wk_ref, fk_ref.at[:, own_ref.shape[0] :])


def last_features_kernel(last_ref, wk_ref, _, fk_ref, past_ref, step_ref):
    size = last_ref.shape[0]
    half = size // 2
    level = spot()[1]

    @pl.when(level == 0)
    def _():
        fk_ref[:, :size] = jnp.zeros((fk_ref.shape[0], size), BF16)
        for ref in (past_ref, step_ref):
            ref[...] = jnp.zeros_like(ref)

    @pl.when(level > 0)
    def _():
        write_key_features(last_ref[:, :DH], wk_ref, fk_ref.at[:, :size])
        for at, ref in ((0, past_ref), (half, step_ref)):
            ref[...] = jnp.dot(
                fk_ref[:, at : at + half],
                with_ones(last_ref[at : at + half, DH:]),
                preferred_element_type=F32,
            )


def past_kernel(before_ref, wk_ref, sum_ref, past_ref, fk_scr):
    level = spot()[1]

    @pl.when(level < 2)
    def _():
        past_ref[...] = sum_ref[...]

    @pl.when(level >= 2)
    def _():
        write_key_features(before_ref[:, :DH], wk_ref, fk_scr)
        past_ref[...] = sum_ref[...] + jnp.dot(
            fk_scr[...], with_ones(before_ref[:, DH:]), preferred_element_type=F32
        )


def query_features_kernel(a_ref, b_ref, w_ref, ratio_ref, q_out, fq_out, exp_scr):
    tok = a_ref.shape[0]
    heads, dh, both = w_ref.shape
    half = 2 * tok
    place = spot()[0]
    for d, ref in enumerate((a_ref, b_ref)):
        row = pl.multiple_of(lax.rem(place ^ d, 2) * tok, tok)
        for h in range(heads):
            q_out[pl.ds(h * half + row, tok), :] = ref[:, h * dh : (h + 1) * dh]
    rows_of = [slice(h * half, (h + 1) * half) for h in range(heads)]
    left = lax.broadcasted_iota(jnp.int32, (half, both), 1) < both // 2
    for h, rows in enumerate(rows_of):
        logits = jnp.dot(q_out[rows, :], w_ref[h], preferred_element_type=F32)
        top_l = jnp.max(jnp.where(left, logits, -jnp.inf), axis=1, keepdims=True)
        top_r = jnp.max(jnp.where(left, -jnp.inf, logits), axis=1, keepdims=True)
        exp_scr[rows, :] = jnp.exp((logits - jnp.where(left, top_l, top_r)).astype(BF16))
    side_r = lax.broadcasted_iota(jnp.int32, (both, both), 0) < both // 2
    side_c = lax.broadcasted_iota(jnp.int32, (both, both), 1) < both // 2
    halves = jnp.where(side_r == side_c, 1.0, 0.0).astype(BF16)
    total = jnp.dot(exp_scr[...], halves, preferred_element_type=F32)
    for h, rows in enumerate(rows_of):
        scale = pl.reciprocal(total[rows], approx=True) * ratio_ref[h : h + 1, :]
        fq_out[rows, :] = (exp_scr[rows, :].astype(F32) * scale).astype(BF16)


def near_kernel(other, q_ref, fq_ref, last_ref, own_ref, fk_ref, near_ref, kv_scr, w_scr):
    half, dh = last_ref.shape[0] // 2, q_ref.shape[1]
    heads = q_ref.shape[0] // half
    feats = fq_ref.shape[1]
    place, level = spot()
    u = lax.div(place, 2) ^ other
    kv_scr[:half, :] = last_ref[half:, :]
    kv_scr[half:, :] = own_ref[...]
    at = pl.ds(pl.multiple_of(u * half, half), 2 * half)
    keys, values = kv_scr[at, :dh], kv_scr[at, dh:]
    fk_at = pl.ds(pl.multiple_of((u + 1) * half, half), 2 * half)
    known = (level > 0) | (u > 0)
    cut = half - WINDOW
    row = lax.broadcasted_iota(jnp.int32, (WINDOW, 2 * half), 0)
    col = lax.broadcasted_iota(jnp.int32, (WINDOW, 2 * half), 1)
    inside = (col > row + cut) & (col <= row + half) & ((col >= half) | known)
    causal = (col <= row + cut)[:, :half]
    row, col = row[:, :half], col[:, :half]
    inside_low = (col > row) & (col <= row + WINDOW)
    causal_low = col <= row
    scores = dot_t(q_ref[...], keys)
    scale = math.log2(math.e) / math.sqrt(dh)

    def window(part, kept):
        masked = jnp.where(kept, part, -jnp.inf)
        top = jnp.max(masked, axis=1, keepdims=True)
        return jnp.exp2(((masked - top) * scale).astype(BF16))

    for h in range(heads):
        here = slice(h * half, (h + 1) * half)
        up, low = slice(h * half, h * half + cut), slice(h * half + cut, (h + 1) * half)
        linear = jnp.dot(
            fq_ref[here, :],
            fk_ref[h * feats : (h + 1) * feats, fk_at],
            preferred_element_type=F32,
        )
        soft = window(scores[up], inside)
        w_scr[up, :half] = soft[:, :half] + jnp.where(causal, linear[:cut, :half], 0.0).astype(BF16)
        w_scr[up, half:] = soft[:, half:]
        soft = window(scores[low, half:], inside_low)
        w_scr[low, :half] = linear[cut:, :half].astype(BF16)
        w_scr[low, half:] = soft + jnp.where(causal_low, linear[cut:, half:], 0.0).astype(BF16)
    values = jnp.concatenate(
        [with_ones(values[:half], known), with_ones(values[half:])], axis=0
    )
    near_ref[...] = jnp.dot(w_scr[...], values, preferred_element_type=F32)


def mix_kernel_of_level(*refs):
    near_refs, fq_refs, (past_ref, step_ref, wk_ref) = refs[:2], refs[2:4], refs[4:7]
    first_ref, refs = refs[7], refs[8:]
    out_refs, (fk_scr, state_scr, out_scr) = refs[:-3], refs[-3:]
    rows, dh = near_refs[0].shape[0], near_refs[0].shape[1] // 2
    feats = fq_refs[0].shape[1]
    heads = past_ref.shape[0] // feats
    half = rows // heads
    place, level = spot()
    side = lax.axis_index("head")
    u = lax.div(place, 2)

    @pl.when(level < 3)
    def _():
        state_scr[0] = past_ref[...].astype(BF16)
        state_scr[1] = (past_ref[...] + step_ref[...]).astype(BF16)

    @pl.when(level >= 3)
    def _():
        write_key_features(first_ref[:, :dh], wk_ref, fk_scr)
        state = past_ref[...] + jnp.dot(
            fk_scr[...], with_ones(first_ref[:, dh:]), preferred_element_type=F32
        )
        state_scr[0] = state.astype(BF16)
        state_scr[1] = (state + step_ref[...]).astype(BF16)

    part = out_refs[0].shape[0]
    for other in (1, 0):
        for h in range(heads):
            here = slice(h * half, (h + 1) * half)
            far = jnp.dot(
                fq_refs[other][here, :],
                state_scr[u ^ other, h * feats : (h + 1) * feats, :],
                preferred_element_type=F32,
            )
            both = near_refs[other][here, :] + far
            out_scr[aligned(u ^ other, half), h * dh : (h + 1) * dh] = (
                both[:, :dh] * pl.reciprocal(both[:, dh:], approx=True)
            ).astype(BF16)
    for n, ref in enumerate(out_refs):
        dr, dy = slot_of(n, lax.rem(place, 2))
        ref[...] = out_scr[aligned((place ^ dr) * 2 + (side ^ dy), part), :]


def whole_spec(space=pltpu.VMEM):
    return pl.BlockSpec(memory_space=space)


def call(kernel, ins, outs, name, scratch=(), limit=4, out_type=BF16, aliases={}):
    return pl.pallas_call(
        kernel,
        in_specs=[whole_spec() for _ in ins],
        out_specs=[whole_spec() for _ in outs],
        out_shape=[
            jax.ShapeDtypeStruct(s, out_type[n] if isinstance(out_type, list) else out_type)
            for n, s in enumerate(outs)
        ],
        scratch_shapes=list(scratch),
        input_output_aliases=aliases,
        compiler_params=pltpu.CompilerParams(vmem_limit_bytes=limit * 2**20),
        name=name,
    )(*ins)


def by_levels(queries, keys, values, wq, wk, factor):
    tok, width = queries.shape
    local_heads, feat, dh = wq.shape
    heads = local_heads // WAYS
    seq, sides = lax.axis_size("seq"), lax.axis_size("head")
    half = 2 * tok
    rows, states = heads * half, heads * 2 * feat

    def partner(x, dr, dy=0):
        pairs = [
            (i * sides + j, (i // WAYS * WAYS + (i % WAYS ^ dr)) * sides + (j ^ dy))
            for i in range(seq)
            for j in range(sides)
        ]
        return lax.ppermute(x, ("seq", "head"), pairs)

    def levels_back(x, by):
        pairs = [(i, i + by * WAYS) for i in range(seq - by * WAYS)]
        return lax.ppermute(x, "seq", pairs)

    place = lax.rem(lax.axis_index("seq"), WAYS)
    ours = place // 2 * 2 * dh
    cuts = [
        lax.dynamic_slice_in_dim(x, at, 2 * dh, 1)
        for at in (ours, 2 * dh - ours)
        for x in (keys, values)
    ]
    own, away = call(pack_kv_kernel, cuts, [(tok, 4 * dh)] * 2, "pack_kv")
    got = partner(away, 2)
    q = list(call(pack_q_kernel, [queries], [(tok, width // WAYS)] * WAYS, "pack_q"))
    (pair,) = call(pair_kernel, [own, got], [(half, 2 * dh)], "pair_kv")
    *q, pair = lax.optimization_barrier((*q, pair))
    pair = partner(pair, 1)
    q[1], q[2], q[3] = partner(q[1], 1), partner(q[2], 2), partner(q[3], 3)
    (kv,) = call(stack_kernel, [own, got, pair], [(2 * half, 2 * dh)], "stack_kv")
    last, before = levels_back(kv, 1), levels_back(kv, 2)
    wq, wk, kv, q[1] = lax.optimization_barrier((wq, wk, kv, q[1]))
    wq, wk = [lax.dynamic_slice_in_dim(w, place * heads, heads) for w in (wq, wk)]
    wq, wk = lax.optimization_barrier((wq, wk))
    (fk,) = call(own_features_kernel, [kv, wk], [(states, 4 * half)], "own_features", limit=16)
    wq, ratio = call(
        weights_kernel,
        [wq, factor.reshape(1, local_heads)],
        [(heads, dh, 2 * feat), (heads, 2 * feat)],
        "weights",
        out_type=[BF16, F32],
    )
    far_kv, fk, wq = lax.optimization_barrier((kv, fk, wq))
    first = levels_back(far_kv, 3)

    def query_features(a, b):
        return call(
            query_features_kernel,
            [a, b, wq, ratio],
            [(rows, dh), (rows, 2 * feat)],
            "query_features",
            [pltpu.VMEM((rows, 2 * feat), BF16)],
            12,
        )

    def near(other, q_rows, fq):
        return call(
            lambda *refs: near_kernel(other, *refs),
            [q_rows, fq, last, kv, fk],
            [(rows, 2 * dh)],
            "near",
            [
                pltpu.VMEM((3 * half, 2 * dh), BF16),
                pltpu.VMEM((rows, 2 * half), BF16),
            ],
            16,
            F32,
        )[0]

    q_own, fq_own = query_features(q[0], q[1])
    last, fq_own, fk = lax.optimization_barrier((last, fq_own, fk))
    fk, past, step = call(
        last_features_kernel,
        [last, wk, fk],
        [(states, 4 * half), (states, 2 * dh), (states, 2 * dh)],
        "last_features",
        limit=20,
        out_type=[BF16, F32, F32],
        aliases={2: 0},
    )
    near_own = near(0, q_own, fq_own)
    q[2], q[3], near_own = lax.optimization_barrier((q[2], q[3], near_own))
    q_other, fq_other = query_features(q[2], q[3])
    near_other = near(1, q_other, fq_other)
    before, near_other = lax.optimization_barrier((before, near_other))
    (past,) = call(
        past_kernel,
        [before, wk, past],
        [(states, 2 * dh)],
        "past",
        [pltpu.VMEM((states, 2 * half), BF16)],
        16,
        F32,
    )
    first, past = lax.optimization_barrier((first, past))
    part = tok // sides
    outs = call(
        mix_kernel_of_level,
        [near_own, near_other, fq_own, fq_other, past, step, wk, first],
        [(part, heads * dh)] * (WAYS * sides),
        "mix_level",
        [
            pltpu.VMEM((states, 2 * half), BF16),
            pltpu.VMEM((2, states, 2 * dh), BF16),
            pltpu.VMEM((2 * half, heads * dh), BF16),
        ],
        24,
    )

    def sent(x, slot):
        pairs = []
        for i in range(seq):
            dr, dy = slot[i % 2]
            to = i // WAYS * WAYS + (i % WAYS ^ dr)
            pairs += [(i * sides + j, to * sides + (j ^ dy)) for j in range(sides)]
        return lax.ppermute(x, ("seq", "head"), pairs)

    outs = list(outs)
    for n in range(1, 6):
        outs[n] = sent(outs[n], SLOTS[n])
    for n, ahead in ((6, 2), (7, 1)):
        outs[n], outs[ahead] = lax.optimization_barrier((outs[n], outs[ahead]))
        outs[n] = sent(outs[n], SLOTS[n])

    def joined(slots, into):
        return pl.pallas_call(
            lambda *refs: join_kernel(slots, *refs),
            in_specs=[whole_spec()] * len(slots) + [whole_spec(pltpu.HBM)] * len(into),
            out_specs=whole_spec(pltpu.HBM),
            out_shape=jax.ShapeDtypeStruct((part, sides * WAYS * heads * dh), BF16),
            input_output_aliases={len(slots): 0} if into else {},
            scratch_shapes=[pltpu.SemaphoreType.DMA((len(slots),))],
            compiler_params=pltpu.CompilerParams(vmem_limit_bytes=4 * 2**20),
            name="join",
        )(*[outs[n] for n in slots], *into)

    return joined((5, 6, 7), [joined((0, 1, 2, 3, 4), [])])


def by_blocks(queries, keys, values, wq, wk, ratio):
    group = wq.shape[0] // (keys.shape[1] // DH)
    place = lax.axis_index("seq").astype(jnp.int32).reshape(1)
    kv = lax.all_gather(jnp.concatenate([keys, values], axis=1), "seq", tiled=True)
    out = mix(place, queries, kv, wq, wk, ratio, group)
    return lax.all_to_all(out, "head", split_axis=0, concat_axis=1, tiled=True)


def local(queries, keys, values, q_feature, k_feature, window_factor):
    tok = queries.shape[0]
    seq, sides = lax.axis_size("seq"), lax.axis_size("head")
    wq, wk = jnp.swapaxes(q_feature, 1, 2), jnp.swapaxes(k_feature, 1, 2)
    if keys.shape[1] == WAYS * DH and seq == 4 * WAYS and sides == 2 and tok == WINDOW:
        return by_levels(queries, keys, values, wq, wk, window_factor)
    ratio = window_factor / (1.0 - window_factor)
    return by_blocks(queries, keys, values, wq, wk, ratio)


def solution(mesh):
    return jax.shard_map(
        local,
        mesh=mesh,
        in_specs=(
            P("seq", "head"),
            P("seq", "head"),
            P("seq", "head"),
            P("head", None, None),
            P("head", None, None),
            P("head"),
        ),
        out_specs=P(("seq", "head"), None),
        check_vma=False,
    )
```

```python
import math

import jax
import jax.numpy as jnp
from jax import lax
from jax.experimental import pallas as pl
from jax.experimental.pallas import tpu as pltpu
from jax.sharding import PartitionSpec as P

DH = 128
WINDOW = 64
F32 = jnp.float32
BF16 = jnp.bfloat16


def dot_t(a, b):
    return lax.dot_general(a, b, (((1,), (1,)), ((), ())), preferred_element_type=F32)


def features_t(logits):
    top = jnp.max(logits, axis=0, keepdims=True)
    low = jnp.min(logits, axis=0, keepdims=True)
    up = jnp.exp(logits - top)
    down = jnp.exp(low - logits)
    up = up * (1.0 / jnp.sum(up, axis=0, keepdims=True))
    down = down * (1.0 / jnp.sum(down, axis=0, keepdims=True))
    return jnp.concatenate([up.astype(BF16), down.astype(BF16)], axis=0)


def mix_kernel(
    place_ref, q_ref, k_ref, v_ref, wq_ref, wk_ref, ratio_ref, out_ref, fk_scr, state_scr
):
    tok = q_ref.shape[0]
    heads, feat, dh = wq_ref.shape
    seen = fk_scr.shape[1]
    place = place_ref[0]
    first_head = pl.program_id(0) * heads

    weights = wk_ref[...].reshape(heads * feat, dh)
    for start in range(0, seen, 256):
        size = min(256, seen - start)
        logits = dot_t(weights, k_ref[start : start + size, :])
        for h in range(heads):
            fk_scr[h * 2 * feat : (h + 1) * 2 * feat, start : start + size] = features_t(
                logits[h * feat : (h + 1) * feat]
            )
    row = lax.broadcasted_iota(jnp.int32, (seen, dh), 0)
    kept = row < (place - 1) * tok
    v_seen = jnp.where(kept, v_ref[:seen, :].astype(F32), 0.0).astype(BF16)
    ones_seen = jnp.where(kept, 1.0, 0.0).astype(BF16)
    v_seen = jnp.concatenate([v_seen, ones_seen], axis=1)
    state_scr[...] = jnp.dot(fk_scr[...], v_seen, preferred_element_type=F32).astype(BF16)

    before = pl.multiple_of(jnp.maximum(place - 1, 0) * tok, tok)
    own = pl.multiple_of(place * tok, tok)
    k_ext = jnp.concatenate([k_ref[pl.ds(before, tok), :], k_ref[pl.ds(own, tok), :]], axis=0)
    v_ext = jnp.concatenate([v_ref[pl.ds(before, tok), :], v_ref[pl.ds(own, tok), :]], axis=0)
    v_ext = jnp.concatenate([v_ext, jnp.ones_like(v_ext)], axis=1)
    row = lax.broadcasted_iota(jnp.int32, (tok, 2 * tok), 0)
    col = lax.broadcasted_iota(jnp.int32, (tok, 2 * tok), 1)
    valid = (col >= tok) | (place > 0)
    inside = (col > row) & (col <= row + WINDOW) & valid
    causal = (col <= row) & valid
    lane = lax.broadcasted_iota(jnp.int32, (tok, 2 * feat), 1)
    left = lane < feat
    side_r = lax.broadcasted_iota(jnp.int32, (2 * feat, 2 * feat), 0) < feat
    side_c = lax.broadcasted_iota(jnp.int32, (2 * feat, 2 * feat), 1) < feat
    halves = jnp.where(side_r == side_c, 1.0, 0.0).astype(BF16)

    for h in range(heads):
        q = q_ref[:, h * dh : (h + 1) * dh]
        wq = wq_ref[h]
        logits = dot_t(q, jnp.concatenate([wq, -wq], axis=0))
        top_l = jnp.max(jnp.where(left, logits, -jnp.inf), axis=1, keepdims=True)
        top_r = jnp.max(jnp.where(left, -jnp.inf, logits), axis=1, keepdims=True)
        expd = jnp.exp(logits - jnp.where(left, top_l, top_r)).astype(BF16)
        total = jnp.dot(expd, halves, preferred_element_type=F32)
        fq = (expd.astype(F32) / total).astype(BF16)
        fk = features_t(dot_t(wk_ref[h], k_ext))
        linear = jnp.dot(fq, fk, preferred_element_type=F32)
        scores = dot_t(q, k_ext) * (1.0 / math.sqrt(dh))
        masked = jnp.where(inside, scores, -jnp.inf)
        top = jnp.max(masked, axis=1, keepdims=True)
        soft = jnp.exp(masked - top) * ratio_ref[first_head + h]
        weight = jnp.where(causal, linear, soft).astype(BF16)
        both = jnp.dot(weight, v_ext, preferred_element_type=F32) + jnp.dot(
            fq, state_scr[h * 2 * feat : (h + 1) * 2 * feat, :], preferred_element_type=F32
        )
        out_ref[:, h * dh : (h + 1) * dh] = (both[:, :dh] / both[:, dh:]).astype(BF16)


def mix(place, queries, kv, wq, wk, ratio, group):
    tok = queries.shape[0]
    local_heads, feat, dh = wq.shape
    groups = local_heads // group
    tokens = kv.shape[0]
    seen = tokens - 2 * tok
    return pl.pallas_call(
        mix_kernel,
        grid_spec=pltpu.PrefetchScalarGridSpec(
            num_scalar_prefetch=1,
            grid=(groups,),
            in_specs=[
                pl.BlockSpec((tok, group * dh), lambda g, p: (0, g)),
                pl.BlockSpec((tokens, dh), lambda g, p: (0, g)),
                pl.BlockSpec((tokens, dh), lambda g, p: (0, groups + g)),
                pl.BlockSpec((group, feat, dh), lambda g, p: (g, 0, 0)),
                pl.BlockSpec((group, feat, dh), lambda g, p: (g, 0, 0)),
                pl.BlockSpec(memory_space=pltpu.SMEM),
            ],
            out_specs=pl.BlockSpec((tok, group * dh), lambda g, p: (0, g)),
            scratch_shapes=[
                pltpu.VMEM((group * 2 * feat, seen), BF16),
                pltpu.VMEM((group * 2 * feat, 2 * dh), BF16),
            ],
        ),
        out_shape=jax.ShapeDtypeStruct(queries.shape, BF16),
        compiler_params=pltpu.CompilerParams(vmem_limit_bytes=48 * 2**20),
        cost_estimate=pl.CostEstimate(
            flops=2 * local_heads * tokens * 3 * feat * 2 * dh,
            bytes_accessed=8 * 2**20,
            transcendentals=local_heads * tokens * 2 * feat,
        ),
    )(place, queries, kv, kv, wq, wk, ratio)


WAYS = 4


SLOTS = (
    ((0, 0), (0, 0)),
    ((2, 0), (0, 1)),
    ((0, 1), (2, 0)),
    ((3, 0), (1, 1)),
    ((1, 1), (3, 0)),
    ((2, 1), (2, 1)),
    ((3, 1), (3, 1)),
    ((1, 0), (1, 0)),
)


def slot_of(n, odd):
    return [jnp.where(odd == 1, b, a) if a != b else a for a, b in zip(*SLOTS[n])]


def spot():
    at = lax.axis_index("seq")
    return lax.rem(at, WAYS), lax.div(at, WAYS)


def aligned(at, step):
    return pl.ds(pl.multiple_of(at * step, step), step)


def with_ones(values, kept=True):
    here = jnp.where(kept, 1.0, 0.0).astype(BF16)
    return jnp.concatenate([values, jnp.full(values.shape, here)], axis=1)


def pack_kv_kernel(k_ref, v_ref, k_away_ref, v_away_ref, own_ref, away_ref):
    odd = lax.rem(spot()[0], 2)
    for k, v, ref in ((k_ref, v_ref, own_ref), (k_away_ref, v_away_ref, away_ref)):
        for d in range(2):
            at = aligned(odd ^ d, DH)
            ref[:, 2 * d * DH : (2 * d + 1) * DH] = k[:, at]
            ref[:, (2 * d + 1) * DH : (2 * d + 2) * DH] = v[:, at]


def pair_kernel(own_ref, got_ref, out_ref):
    tok = own_ref.shape[0]
    out_ref[:tok, :] = own_ref[:, 2 * DH :]
    out_ref[tok:, :] = got_ref[:, 2 * DH :]


def stack_kernel(own_ref, got_ref, pair_ref, out_ref):
    tok = own_ref.shape[0]
    place = spot()[0]
    out_ref[aligned(place, tok), :] = own_ref[:, : 2 * DH]
    out_ref[aligned(place ^ 2, tok), :] = got_ref[:, : 2 * DH]
    out_ref[aligned(place ^ 1, tok), :] = pair_ref[:tok, :]
    out_ref[aligned(place ^ 3, tok), :] = pair_ref[tok:, :]


def pack_q_kernel(q_ref, *out_refs):
    place = spot()[0]
    for d, out in enumerate(out_refs):
        out[...] = q_ref[:, aligned(place ^ d, out.shape[1])]


def weights_kernel(wq_ref, factor_ref, both_ref, ratio_ref):
    heads = both_ref.shape[0]
    shape = (heads, factor_ref.shape[1])
    head = lax.broadcasted_iota(jnp.int32, shape, 0) + spot()[0] * heads
    ratio = jnp.broadcast_to((1.0 - factor_ref[...]) / factor_ref[...], shape)
    ratio = jnp.where(lax.broadcasted_iota(jnp.int32, shape, 1) == head, ratio, 0.0)
    ratio = jnp.sum(ratio, axis=1, keepdims=True)
    ratio_ref[...] = jnp.broadcast_to(ratio, ratio_ref.shape)
    for h in range(heads):
        wq = wq_ref[h].T
        both_ref[h] = jnp.concatenate([wq, -wq], axis=1)


def join_kernel(slots, *refs):
    got, out_ref, sems = refs[: len(slots)], *refs[-2:]
    width = got[0].shape[1]
    place, side = spot()[0], lax.axis_index("head")
    copies = []
    for n, ref in zip(slots, got):
        dr, dy = slot_of(n, lax.rem(place, 2) ^ (SLOTS[n][0][0] & 1))
        at = aligned((side ^ dy) * WAYS + (place ^ dr), width)
        copies.append(pltpu.make_async_copy(ref, out_ref.at[:, at], sems.at[len(copies)]))
    for copy in copies:
        copy.start()
    for copy in copies:
        copy.wait()


def write_key_features(keys, wk_ref, fk_ref):
    heads, feat, dh = wk_ref.shape
    logits = dot_t(wk_ref[...].reshape(heads * feat, dh), keys)
    for h in range(heads):
        part = logits[h * feat : (h + 1) * feat]
        top = jnp.max(part, axis=0, keepdims=True)
        low = jnp.min(part, axis=0, keepdims=True)
        for n, shifted in enumerate((part - top, low - part)):
            row = (2 * h + n) * feat
            expd = jnp.exp(shifted.astype(BF16))
            total = expd[: feat // 4]
            for q in range(1, 4):
                total = total + expd[q * feat // 4 : (q + 1) * feat // 4]
            total = jnp.sum(total.astype(F32), axis=0, keepdims=True)
            fk_ref[row : row + feat, :] = expd * pl.reciprocal(total).astype(BF16)


def own_features_kernel(own_ref, wk_ref, fk_ref):
    write_key_features(own_ref[:, :DH], wk_ref, fk_ref.at[:, own_ref.shape[0] :])


def last_features_kernel(last_ref, wk_ref, _, fk_ref, past_ref, step_ref):
    size = last_ref.shape[0]
    half = size // 2
    level = spot()[1]

    @pl.when(level == 0)
    def _():
        fk_ref[:, :size] = jnp.zeros((fk_ref.shape[0], size), BF16)
        for ref in (past_ref, step_ref):
            ref[...] = jnp.zeros_like(ref)

    @pl.when(level > 0)
    def _():
        write_key_features(last_ref[:, :DH], wk_ref, fk_ref.at[:, :size])
        for at, ref in ((0, past_ref), (half, step_ref)):
            ref[...] = jnp.dot(
                fk_ref[:, at : at + half],
                with_ones(last_ref[at : at + half, DH:]),
                preferred_element_type=F32,
            )


def past_kernel(before_ref, wk_ref, sum_ref, past_ref, fk_scr):
    level = spot()[1]

    @pl.when(level < 2)
    def _():
        past_ref[...] = sum_ref[...]

    @pl.when(level >= 2)
    def _():
        write_key_features(before_ref[:, :DH], wk_ref, fk_scr)
        past_ref[...] = sum_ref[...] + jnp.dot(
            fk_scr[...], with_ones(before_ref[:, DH:]), preferred_element_type=F32
        )


def query_features_kernel(a_ref, b_ref, w_ref, ratio_ref, q_out, fq_out, exp_scr):
    tok = a_ref.shape[0]
    heads, dh, both = w_ref.shape
    half = 2 * tok
    place = spot()[0]
    for d, ref in enumerate((a_ref, b_ref)):
        row = pl.multiple_of(lax.rem(place ^ d, 2) * tok, tok)
        for h in range(heads):
            q_out[pl.ds(h * half + row, tok), :] = ref[:, h * dh : (h + 1) * dh]
    rows_of = [slice(h * half, (h + 1) * half) for h in range(heads)]
    left = lax.broadcasted_iota(jnp.int32, (half, both), 1) < both // 2
    for h, rows in enumerate(rows_of):
        logits = jnp.dot(q_out[rows, :], w_ref[h], preferred_element_type=F32)
        top_l = jnp.max(jnp.where(left, logits, -jnp.inf), axis=1, keepdims=True)
        top_r = jnp.max(jnp.where(left, -jnp.inf, logits), axis=1, keepdims=True)
        exp_scr[rows, :] = jnp.exp((logits - jnp.where(left, top_l, top_r)).astype(BF16))
    side_r = lax.broadcasted_iota(jnp.int32, (both, both), 0) < both // 2
    side_c = lax.broadcasted_iota(jnp.int32, (both, both), 1) < both // 2
    halves = jnp.where(side_r == side_c, 1.0, 0.0).astype(BF16)
    total = jnp.dot(exp_scr[...], halves, preferred_element_type=F32)
    for h, rows in enumerate(rows_of):
        scale = pl.reciprocal(total[rows], approx=True) * ratio_ref[h : h + 1, :]
        fq_out[rows, :] = (exp_scr[rows, :].astype(F32) * scale).astype(BF16)


def near_kernel(other, q_ref, fq_ref, last_ref, own_ref, fk_ref, near_ref, kv_scr, w_scr):
    half, dh = last_ref.shape[0] // 2, q_ref.shape[1]
    heads = q_ref.shape[0] // half
    feats = fq_ref.shape[1]
    place, level = spot()
    u = lax.div(place, 2) ^ other
    kv_scr[:half, :] = last_ref[half:, :]
    kv_scr[half:, :] = own_ref[...]
    at = pl.ds(pl.multiple_of(u * half, half), 2 * half)
    keys, values = kv_scr[at, :dh], kv_scr[at, dh:]
    fk_at = pl.ds(pl.multiple_of((u + 1) * half, half), 2 * half)
    known = (level > 0) | (u > 0)
    cut = half - WINDOW
    row = lax.broadcasted_iota(jnp.int32, (WINDOW, 2 * half), 0)
    col = lax.broadcasted_iota(jnp.int32, (WINDOW, 2 * half), 1)
    inside = (col > row + cut) & (col <= row + half) & ((col >= half) | known)
    causal = (col <= row + cut)[:, :half]
    row, col = row[:, :half], col[:, :half]
    inside_low = (col > row) & (col <= row + WINDOW)
    causal_low = col <= row
    scores = dot_t(q_ref[...], keys)
    scale = math.log2(math.e) / math.sqrt(dh)

    def window(part, kept):
        masked = jnp.where(kept, part, -jnp.inf)
        top = jnp.max(masked, axis=1, keepdims=True)
        return jnp.exp2(((masked - top) * scale).astype(BF16))

    for h in range(heads):
        here = slice(h * half, (h + 1) * half)
        up, low = slice(h * half, h * half + cut), slice(h * half + cut, (h + 1) * half)
        linear = jnp.dot(
            fq_ref[here, :],
            fk_ref[h * feats : (h + 1) * feats, fk_at],
            preferred_element_type=F32,
        )
        soft = window(scores[up], inside)
        w_scr[up, :half] = soft[:, :half] + jnp.where(causal, linear[:cut, :half], 0.0).astype(BF16)
        w_scr[up, half:] = soft[:, half:]
        soft = window(scores[low, half:], inside_low)
        w_scr[low, :half] = linear[cut:, :half].astype(BF16)
        w_scr[low, half:] = soft + jnp.where(causal_low, linear[cut:, half:], 0.0).astype(BF16)
    values = jnp.concatenate(
        [with_ones(values[:half], known), with_ones(values[half:])], axis=0
    )
    near_ref[...] = jnp.dot(w_scr[...], values, preferred_element_type=F32)


def mix_kernel_of_level(*refs):
    near_refs, fq_refs, (past_ref, step_ref, wk_ref) = refs[:2], refs[2:4], refs[4:7]
    first_ref, refs = refs[7], refs[8:]
    out_refs, (fk_scr, state_scr, out_scr) = refs[:-3], refs[-3:]
    rows, dh = near_refs[0].shape[0], near_refs[0].shape[1] // 2
    feats = fq_refs[0].shape[1]
    heads = past_ref.shape[0] // feats
    half = rows // heads
    place, level = spot()
    side = lax.axis_index("head")
    u = lax.div(place, 2)

    @pl.when(level < 3)
    def _():
        state_scr[0] = past_ref[...].astype(BF16)
        state_scr[1] = (past_ref[...] + step_ref[...]).astype(BF16)

    @pl.when(level >= 3)
    def _():
        write_key_features(first_ref[:, :dh], wk_ref, fk_scr)
        state = past_ref[...] + jnp.dot(
            fk_scr[...], with_ones(first_ref[:, dh:]), preferred_element_type=F32
        )
        state_scr[0] = state.astype(BF16)
        state_scr[1] = (state + step_ref[...]).astype(BF16)

    part = out_refs[0].shape[0]
    for other in (1, 0):
        for h in range(heads):
            here = slice(h * half, (h + 1) * half)
            far = jnp.dot(
                fq_refs[other][here, :],
                state_scr[u ^ other, h * feats : (h + 1) * feats, :],
                preferred_element_type=F32,
            )
            both = near_refs[other][here, :] + far
            out_scr[aligned(u ^ other, half), h * dh : (h + 1) * dh] = (
                both[:, :dh] * pl.reciprocal(both[:, dh:], approx=True)
            ).astype(BF16)
    for n, ref in enumerate(out_refs):
        dr, dy = slot_of(n, lax.rem(place, 2))
        ref[...] = out_scr[aligned((place ^ dr) * 2 + (side ^ dy), part), :]


def whole_spec(space=pltpu.VMEM):
    return pl.BlockSpec(memory_space=space)


def call(kernel, ins, outs, name, scratch=(), limit=4, out_type=BF16, aliases={}):
    return pl.pallas_call(
        kernel,
        in_specs=[whole_spec() for _ in ins],
        out_specs=[whole_spec() for _ in outs],
        out_shape=[
            jax.ShapeDtypeStruct(s, out_type[n] if isinstance(out_type, list) else out_type)
            for n, s in enumerate(outs)
        ],
        scratch_shapes=list(scratch),
        input_output_aliases=aliases,
        cost_estimate=pl.CostEstimate(flops=10**10, bytes_accessed=10**8, transcendentals=0),
        compiler_params=pltpu.CompilerParams(vmem_limit_bytes=limit * 2**20),
        name=name,
    )(*ins)


def by_levels(queries, keys, values, wq, wk, factor):
    tok, width = queries.shape
    local_heads, feat, dh = wq.shape
    heads = local_heads // WAYS
    seq, sides = lax.axis_size("seq"), lax.axis_size("head")
    half = 2 * tok
    rows, states = heads * half, heads * 2 * feat

    def partner(x, dr, dy=0):
        pairs = [
            (i * sides + j, (i // WAYS * WAYS + (i % WAYS ^ dr)) * sides + (j ^ dy))
            for i in range(seq)
            for j in range(sides)
        ]
        return lax.ppermute(x, ("seq", "head"), pairs)

    def levels_back(x, by):
        pairs = [(i, i + by * WAYS) for i in range(seq - by * WAYS)]
        return lax.ppermute(x, "seq", pairs)

    place = lax.rem(lax.axis_index("seq"), WAYS)
    ours = place // 2 * 2 * dh
    cuts = [
        lax.dynamic_slice_in_dim(x, at, 2 * dh, 1)
        for at in (ours, 2 * dh - ours)
        for x in (keys, values)
    ]
    own, away = call(pack_kv_kernel, cuts, [(tok, 4 * dh)] * 2, "pack_kv")
    got = partner(away, 2)
    queries, away = lax.optimization_barrier((queries, away))
    q = list(call(pack_q_kernel, [queries], [(tok, width // WAYS)] * WAYS, "pack_q"))
    q[2], q[3] = partner(q[2], 2), partner(q[3], 3)
    (pair,) = call(pair_kernel, [own, got], [(half, 2 * dh)], "pair_kv")
    pair, q[1], wq, wk = lax.optimization_barrier((pair, q[1], wq, wk))
    pair, q[1] = partner(pair, 1), partner(q[1], 1)
    wq, wk = [lax.dynamic_slice_in_dim(w, place * heads, heads) for w in (wq, wk)]
    pair, wq, wk = lax.optimization_barrier((pair, wq, wk))
    (kv,) = call(stack_kernel, [own, got, pair], [(2 * half, 2 * dh)], "stack_kv")
    last, before = levels_back(kv, 1), levels_back(kv, 2)
    wq, kv, q[1] = lax.optimization_barrier((wq, kv, q[1]))
    (fk,) = call(own_features_kernel, [kv, wk], [(states, 4 * half)], "own_features", limit=16)
    wq, ratio = call(
        weights_kernel,
        [wq, factor.reshape(1, local_heads)],
        [(heads, dh, 2 * feat), (heads, 2 * feat)],
        "weights",
        out_type=[BF16, F32],
    )
    far_kv, fk, wq = lax.optimization_barrier((kv, fk, wq))
    first = levels_back(far_kv, 3)

    def query_features(a, b):
        return call(
            query_features_kernel,
            [a, b, wq, ratio],
            [(rows, dh), (rows, 2 * feat)],
            "query_features",
            [pltpu.VMEM((rows, 2 * feat), BF16)],
            12,
        )

    def near(other, q_rows, fq):
        return call(
            lambda *refs: near_kernel(other, *refs),
            [q_rows, fq, last, kv, fk],
            [(rows, 2 * dh)],
            "near",
            [
                pltpu.VMEM((3 * half, 2 * dh), BF16),
                pltpu.VMEM((rows, 2 * half), BF16),
            ],
            16,
            F32,
        )[0]

    q_own, fq_own = query_features(q[0], q[1])
    last, fq_own, fk = lax.optimization_barrier((last, fq_own, fk))
    fk, past, step = call(
        last_features_kernel,
        [last, wk, fk],
        [(states, 4 * half), (states, 2 * dh), (states, 2 * dh)],
        "last_features",
        limit=20,
        out_type=[BF16, F32, F32],
        aliases={2: 0},
    )
    near_own = near(0, q_own, fq_own)
    q[2], q[3], near_own = lax.optimization_barrier((q[2], q[3], near_own))
    q_other, fq_other = query_features(q[2], q[3])
    near_other = near(1, q_other, fq_other)
    before, near_other = lax.optimization_barrier((before, near_other))
    (past,) = call(
        past_kernel,
        [before, wk, past],
        [(states, 2 * dh)],
        "past",
        [pltpu.VMEM((states, 2 * half), BF16)],
        16,
        F32,
    )
    first, past = lax.optimization_barrier((first, past))
    part = tok // sides
    outs = call(
        mix_kernel_of_level,
        [near_own, near_other, fq_own, fq_other, past, step, wk, first],
        [(part, heads * dh)] * (WAYS * sides),
        "mix_level",
        [
            pltpu.VMEM((states, 2 * half), BF16),
            pltpu.VMEM((2, states, 2 * dh), BF16),
            pltpu.VMEM((2 * half, heads * dh), BF16),
        ],
        24,
    )

    def sent(x, slot):
        pairs = []
        for i in range(seq):
            dr, dy = slot[i % 2]
            to = i // WAYS * WAYS + (i % WAYS ^ dr)
            pairs += [(i * sides + j, to * sides + (j ^ dy)) for j in range(sides)]
        return lax.ppermute(x, ("seq", "head"), pairs)

    outs = list(outs)
    for n in range(1, 6):
        outs[n] = sent(outs[n], SLOTS[n])
    for n, ahead in ((6, 2), (7, 1)):
        outs[n], outs[ahead] = lax.optimization_barrier((outs[n], outs[ahead]))
        outs[n] = sent(outs[n], SLOTS[n])

    def joined(slots, into):
        return pl.pallas_call(
            lambda *refs: join_kernel(slots, *refs),
            in_specs=[whole_spec()] * len(slots) + [whole_spec(pltpu.HBM)] * len(into),
            out_specs=whole_spec(pltpu.HBM),
            out_shape=jax.ShapeDtypeStruct((part, sides * WAYS * heads * dh), BF16),
            input_output_aliases={len(slots): 0} if into else {},
            scratch_shapes=[pltpu.SemaphoreType.DMA((len(slots),))],
            compiler_params=pltpu.CompilerParams(vmem_limit_bytes=4 * 2**20),
            name="join",
        )(*[outs[n] for n in slots], *into)

    return joined((4, 5, 6, 7), [joined((0, 1, 2, 3), [])])


def by_blocks(queries, keys, values, wq, wk, ratio):
    group = wq.shape[0] // (keys.shape[1] // DH)
    place = lax.axis_index("seq").astype(jnp.int32).reshape(1)
    kv = lax.all_gather(jnp.concatenate([keys, values], axis=1), "seq", tiled=True)
    out = mix(place, queries, kv, wq, wk, ratio, group)
    return lax.all_to_all(out, "head", split_axis=0, concat_axis=1, tiled=True)


def local(queries, keys, values, q_feature, k_feature, window_factor):
    tok = queries.shape[0]
    seq, sides = lax.axis_size("seq"), lax.axis_size("head")
    wq, wk = jnp.swapaxes(q_feature, 1, 2), jnp.swapaxes(k_feature, 1, 2)
    if keys.shape[1] == WAYS * DH and seq == 4 * WAYS and sides == 2 and tok == WINDOW:
        return by_levels(queries, keys, values, wq, wk, window_factor)
    ratio = window_factor / (1.0 - window_factor)
    return by_blocks(queries, keys, values, wq, wk, ratio)


def solution(mesh):
    return jax.shard_map(
        local,
        mesh=mesh,
        in_specs=(
            P("seq", "head"),
            P("seq", "head"),
            P("seq", "head"),
            P("head", None, None),
            P("head", None, None),
            P("head"),
        ),
        out_specs=P(("seq", "head"), None),
        check_vma=False,
    )
```

```python
import math

import jax
import jax.numpy as jnp
from jax import lax
from jax.experimental import pallas as pl
from jax.experimental.pallas import tpu as pltpu
from jax.sharding import PartitionSpec as P

DH = 128
WINDOW = 64
F32 = jnp.float32
BF16 = jnp.bfloat16


def dot_t(a, b):
    return lax.dot_general(a, b, (((1,), (1,)), ((), ())), preferred_element_type=F32)


def features_t(logits):
    top = jnp.max(logits, axis=0, keepdims=True)
    low = jnp.min(logits, axis=0, keepdims=True)
    up = jnp.exp(logits - top)
    down = jnp.exp(low - logits)
    up = up * (1.0 / jnp.sum(up, axis=0, keepdims=True))
    down = down * (1.0 / jnp.sum(down, axis=0, keepdims=True))
    return jnp.concatenate([up.astype(BF16), down.astype(BF16)], axis=0)


def mix_kernel(
    place_ref, q_ref, k_ref, v_ref, wq_ref, wk_ref, ratio_ref, out_ref, fk_scr, state_scr
):
    tok = q_ref.shape[0]
    heads, feat, dh = wq_ref.shape
    seen = fk_scr.shape[1]
    place = place_ref[0]
    first_head = pl.program_id(0) * heads

    weights = wk_ref[...].reshape(heads * feat, dh)
    for start in range(0, seen, 256):
        size = min(256, seen - start)
        logits = dot_t(weights, k_ref[start : start + size, :])
        for h in range(heads):
            fk_scr[h * 2 * feat : (h + 1) * 2 * feat, start : start + size] = features_t(
                logits[h * feat : (h + 1) * feat]
            )
    row = lax.broadcasted_iota(jnp.int32, (seen, dh), 0)
    kept = row < (place - 1) * tok
    v_seen = jnp.where(kept, v_ref[:seen, :].astype(F32), 0.0).astype(BF16)
    ones_seen = jnp.where(kept, 1.0, 0.0).astype(BF16)
    v_seen = jnp.concatenate([v_seen, ones_seen], axis=1)
    state_scr[...] = jnp.dot(fk_scr[...], v_seen, preferred_element_type=F32).astype(BF16)

    before = pl.multiple_of(jnp.maximum(place - 1, 0) * tok, tok)
    own = pl.multiple_of(place * tok, tok)
    k_ext = jnp.concatenate([k_ref[pl.ds(before, tok), :], k_ref[pl.ds(own, tok), :]], axis=0)
    v_ext = jnp.concatenate([v_ref[pl.ds(before, tok), :], v_ref[pl.ds(own, tok), :]], axis=0)
    v_ext = jnp.concatenate([v_ext, jnp.ones_like(v_ext)], axis=1)
    row = lax.broadcasted_iota(jnp.int32, (tok, 2 * tok), 0)
    col = lax.broadcasted_iota(jnp.int32, (tok, 2 * tok), 1)
    valid = (col >= tok) | (place > 0)
    inside = (col > row) & (col <= row + WINDOW) & valid
    causal = (col <= row) & valid
    lane = lax.broadcasted_iota(jnp.int32, (tok, 2 * feat), 1)
    left = lane < feat
    side_r = lax.broadcasted_iota(jnp.int32, (2 * feat, 2 * feat), 0) < feat
    side_c = lax.broadcasted_iota(jnp.int32, (2 * feat, 2 * feat), 1) < feat
    halves = jnp.where(side_r == side_c, 1.0, 0.0).astype(BF16)

    for h in range(heads):
        q = q_ref[:, h * dh : (h + 1) * dh]
        wq = wq_ref[h]
        logits = dot_t(q, jnp.concatenate([wq, -wq], axis=0))
        top_l = jnp.max(jnp.where(left, logits, -jnp.inf), axis=1, keepdims=True)
        top_r = jnp.max(jnp.where(left, -jnp.inf, logits), axis=1, keepdims=True)
        expd = jnp.exp(logits - jnp.where(left, top_l, top_r)).astype(BF16)
        total = jnp.dot(expd, halves, preferred_element_type=F32)
        fq = (expd.astype(F32) / total).astype(BF16)
        fk = features_t(dot_t(wk_ref[h], k_ext))
        linear = jnp.dot(fq, fk, preferred_element_type=F32)
        scores = dot_t(q, k_ext) * (1.0 / math.sqrt(dh))
        masked = jnp.where(inside, scores, -jnp.inf)
        top = jnp.max(masked, axis=1, keepdims=True)
        soft = jnp.exp(masked - top) * ratio_ref[first_head + h]
        weight = jnp.where(causal, linear, soft).astype(BF16)
        both = jnp.dot(weight, v_ext, preferred_element_type=F32) + jnp.dot(
            fq, state_scr[h * 2 * feat : (h + 1) * 2 * feat, :], preferred_element_type=F32
        )
        out_ref[:, h * dh : (h + 1) * dh] = (both[:, :dh] / both[:, dh:]).astype(BF16)


def mix(place, queries, kv, wq, wk, ratio, group):
    tok = queries.shape[0]
    local_heads, feat, dh = wq.shape
    groups = local_heads // group
    tokens = kv.shape[0]
    seen = tokens - 2 * tok
    return pl.pallas_call(
        mix_kernel,
        grid_spec=pltpu.PrefetchScalarGridSpec(
            num_scalar_prefetch=1,
            grid=(groups,),
            in_specs=[
                pl.BlockSpec((tok, group * dh), lambda g, p: (0, g)),
                pl.BlockSpec((tokens, dh), lambda g, p: (0, g)),
                pl.BlockSpec((tokens, dh), lambda g, p: (0, groups + g)),
                pl.BlockSpec((group, feat, dh), lambda g, p: (g, 0, 0)),
                pl.BlockSpec((group, feat, dh), lambda g, p: (g, 0, 0)),
                pl.BlockSpec(memory_space=pltpu.SMEM),
            ],
            out_specs=pl.BlockSpec((tok, group * dh), lambda g, p: (0, g)),
            scratch_shapes=[
                pltpu.VMEM((group * 2 * feat, seen), BF16),
                pltpu.VMEM((group * 2 * feat, 2 * dh), BF16),
            ],
        ),
        out_shape=jax.ShapeDtypeStruct(queries.shape, BF16),
        compiler_params=pltpu.CompilerParams(vmem_limit_bytes=48 * 2**20),
        cost_estimate=pl.CostEstimate(
            flops=2 * local_heads * tokens * 3 * feat * 2 * dh,
            bytes_accessed=8 * 2**20,
            transcendentals=local_heads * tokens * 2 * feat,
        ),
    )(place, queries, kv, kv, wq, wk, ratio)


WAYS = 4

EARLY = pl.CostEstimate(flops=10**10, bytes_accessed=10**8, transcendentals=0)
EARLY_KERNELS = ("pack_kv", "pack_q", "pair_kv", "stack_kv")


SLOTS = (
    ((0, 0), (0, 0)),
    ((2, 0), (0, 1)),
    ((0, 1), (2, 0)),
    ((3, 0), (1, 1)),
    ((1, 1), (3, 0)),
    ((2, 1), (2, 1)),
    ((3, 1), (3, 1)),
    ((1, 0), (1, 0)),
)


def slot_of(n, odd):
    return [jnp.where(odd == 1, b, a) if a != b else a for a, b in zip(*SLOTS[n])]


def spot():
    at = lax.axis_index("seq")
    return lax.rem(at, WAYS), lax.div(at, WAYS)


def aligned(at, step):
    return pl.ds(pl.multiple_of(at * step, step), step)


def with_ones(values, kept=True):
    here = jnp.where(kept, 1.0, 0.0).astype(BF16)
    return jnp.concatenate([values, jnp.full(values.shape, here)], axis=1)


def pack_kv_kernel(k_ref, v_ref, k_away_ref, v_away_ref, own_ref, away_ref):
    odd = lax.rem(spot()[0], 2)
    for k, v, ref in ((k_ref, v_ref, own_ref), (k_away_ref, v_away_ref, away_ref)):
        for d in range(2):
            at = aligned(odd ^ d, DH)
            ref[:, 2 * d * DH : (2 * d + 1) * DH] = k[:, at]
            ref[:, (2 * d + 1) * DH : (2 * d + 2) * DH] = v[:, at]


def pair_kernel(own_ref, got_ref, out_ref):
    tok = own_ref.shape[0]
    out_ref[:tok, :] = own_ref[:, 2 * DH :]
    out_ref[tok:, :] = got_ref[:, 2 * DH :]


def stack_kernel(own_ref, got_ref, pair_ref, out_ref):
    tok = own_ref.shape[0]
    place = spot()[0]
    out_ref[aligned(place, tok), :] = own_ref[:, : 2 * DH]
    out_ref[aligned(place ^ 2, tok), :] = got_ref[:, : 2 * DH]
    out_ref[aligned(place ^ 1, tok), :] = pair_ref[:tok, :]
    out_ref[aligned(place ^ 3, tok), :] = pair_ref[tok:, :]


def pack_q_kernel(q_ref, *out_refs):
    place = spot()[0]
    for d, out in enumerate(out_refs):
        out[...] = q_ref[:, aligned(place ^ d, out.shape[1])]


def weights_kernel(wq_ref, factor_ref, both_ref, ratio_ref):
    heads = both_ref.shape[0]
    shape = (heads, factor_ref.shape[1])
    head = lax.broadcasted_iota(jnp.int32, shape, 0) + spot()[0] * heads
    ratio = jnp.broadcast_to((1.0 - factor_ref[...]) / factor_ref[...], shape)
    ratio = jnp.where(lax.broadcasted_iota(jnp.int32, shape, 1) == head, ratio, 0.0)
    ratio = jnp.sum(ratio, axis=1, keepdims=True)
    ratio_ref[...] = jnp.broadcast_to(ratio, ratio_ref.shape)
    for h in range(heads):
        wq = wq_ref[h].T
        both_ref[h] = jnp.concatenate([wq, -wq], axis=1)


def join_kernel(slots, *refs):
    got, out_ref, sems = refs[: len(slots)], *refs[-2:]
    width = got[0].shape[1]
    place, side = spot()[0], lax.axis_index("head")
    copies = []
    for n, ref in zip(slots, got):
        dr, dy = slot_of(n, lax.rem(place, 2) ^ (SLOTS[n][0][0] & 1))
        at = aligned((side ^ dy) * WAYS + (place ^ dr), width)
        copies.append(pltpu.make_async_copy(ref, out_ref.at[:, at], sems.at[len(copies)]))
    for copy in copies:
        copy.start()
    for copy in copies:
        copy.wait()


def write_key_features(keys, wk_ref, fk_ref):
    heads, feat, dh = wk_ref.shape
    logits = dot_t(wk_ref[...].reshape(heads * feat, dh), keys)
    for h in range(heads):
        part = logits[h * feat : (h + 1) * feat]
        top = jnp.max(part, axis=0, keepdims=True)
        low = jnp.min(part, axis=0, keepdims=True)
        for n, shifted in enumerate((part - top, low - part)):
            row = (2 * h + n) * feat
            expd = jnp.exp(shifted.astype(BF16))
            total = expd[: feat // 4]
            for q in range(1, 4):
                total = total + expd[q * feat // 4 : (q + 1) * feat // 4]
            total = jnp.sum(total.astype(F32), axis=0, keepdims=True)
            fk_ref[row : row + feat, :] = expd * pl.reciprocal(total).astype(BF16)


def own_features_kernel(own_ref, wk_ref, fk_ref):
    write_key_features(own_ref[:, :DH], wk_ref, fk_ref.at[:, own_ref.shape[0] :])


def last_features_kernel(last_ref, wk_ref, _, fk_ref, past_ref, step_ref):
    size = last_ref.shape[0]
    half = size // 2
    level = spot()[1]

    @pl.when(level == 0)
    def _():
        fk_ref[:, :size] = jnp.zeros((fk_ref.shape[0], size), BF16)
        for ref in (past_ref, step_ref):
            ref[...] = jnp.zeros_like(ref)

    @pl.when(level > 0)
    def _():
        write_key_features(last_ref[:, :DH], wk_ref, fk_ref.at[:, :size])
        for at, ref in ((0, past_ref), (half, step_ref)):
            ref[...] = jnp.dot(
                fk_ref[:, at : at + half],
                with_ones(last_ref[at : at + half, DH:]),
                preferred_element_type=F32,
            )


def past_kernel(before_ref, wk_ref, sum_ref, past_ref, fk_scr):
    level = spot()[1]

    @pl.when(level < 2)
    def _():
        past_ref[...] = sum_ref[...]

    @pl.when(level >= 2)
    def _():
        write_key_features(before_ref[:, :DH], wk_ref, fk_scr)
        past_ref[...] = sum_ref[...] + jnp.dot(
            fk_scr[...], with_ones(before_ref[:, DH:]), preferred_element_type=F32
        )


def query_features_kernel(a_ref, b_ref, w_ref, ratio_ref, q_out, fq_out, exp_scr):
    tok = a_ref.shape[0]
    heads, dh, both = w_ref.shape
    half = 2 * tok
    place = spot()[0]
    for d, ref in enumerate((a_ref, b_ref)):
        row = pl.multiple_of(lax.rem(place ^ d, 2) * tok, tok)
        for h in range(heads):
            q_out[pl.ds(h * half + row, tok), :] = ref[:, h * dh : (h + 1) * dh]
    rows_of = [slice(h * half, (h + 1) * half) for h in range(heads)]
    left = lax.broadcasted_iota(jnp.int32, (half, both), 1) < both // 2
    for h, rows in enumerate(rows_of):
        logits = jnp.dot(q_out[rows, :], w_ref[h], preferred_element_type=F32)
        top_l = jnp.max(jnp.where(left, logits, -jnp.inf), axis=1, keepdims=True)
        top_r = jnp.max(jnp.where(left, -jnp.inf, logits), axis=1, keepdims=True)
        exp_scr[rows, :] = jnp.exp((logits - jnp.where(left, top_l, top_r)).astype(BF16))
    side_r = lax.broadcasted_iota(jnp.int32, (both, both), 0) < both // 2
    side_c = lax.broadcasted_iota(jnp.int32, (both, both), 1) < both // 2
    halves = jnp.where(side_r == side_c, 1.0, 0.0).astype(BF16)
    total = jnp.dot(exp_scr[...], halves, preferred_element_type=F32)
    for h, rows in enumerate(rows_of):
        scale = pl.reciprocal(total[rows], approx=True) * ratio_ref[h : h + 1, :]
        fq_out[rows, :] = (exp_scr[rows, :].astype(F32) * scale).astype(BF16)


def near_kernel(other, q_ref, fq_ref, last_ref, own_ref, fk_ref, near_ref, kv_scr, w_scr):
    half, dh = last_ref.shape[0] // 2, q_ref.shape[1]
    heads = q_ref.shape[0] // half
    feats = fq_ref.shape[1]
    place, level = spot()
    u = lax.div(place, 2) ^ other
    kv_scr[:half, :] = last_ref[half:, :]
    kv_scr[half:, :] = own_ref[...]
    at = pl.ds(pl.multiple_of(u * half, half), 2 * half)
    keys, values = kv_scr[at, :dh], kv_scr[at, dh:]
    fk_at = pl.ds(pl.multiple_of((u + 1) * half, half), 2 * half)
    known = (level > 0) | (u > 0)
    cut = half - WINDOW
    row = lax.broadcasted_iota(jnp.int32, (WINDOW, 2 * half), 0)
    col = lax.broadcasted_iota(jnp.int32, (WINDOW, 2 * half), 1)
    inside = (col > row + cut) & (col <= row + half) & ((col >= half) | known)
    causal = (col <= row + cut)[:, :half]
    row, col = row[:, :half], col[:, :half]
    inside_low = (col > row) & (col <= row + WINDOW)
    causal_low = col <= row
    scores = dot_t(q_ref[...], keys)
    scale = math.log2(math.e) / math.sqrt(dh)

    def window(part, kept):
        masked = jnp.where(kept, part, -jnp.inf)
        top = jnp.max(masked, axis=1, keepdims=True)
        return jnp.exp2(((masked - top) * scale).astype(BF16))

    for h in range(heads):
        here = slice(h * half, (h + 1) * half)
        up, low = slice(h * half, h * half + cut), slice(h * half + cut, (h + 1) * half)
        linear = jnp.dot(
            fq_ref[here, :],
            fk_ref[h * feats : (h + 1) * feats, fk_at],
            preferred_element_type=F32,
        )
        soft = window(scores[up], inside)
        w_scr[up, :half] = soft[:, :half] + jnp.where(causal, linear[:cut, :half], 0.0).astype(BF16)
        w_scr[up, half:] = soft[:, half:]
        soft = window(scores[low, half:], inside_low)
        w_scr[low, :half] = linear[cut:, :half].astype(BF16)
        w_scr[low, half:] = soft + jnp.where(causal_low, linear[cut:, half:], 0.0).astype(BF16)
    values = jnp.concatenate(
        [with_ones(values[:half], known), with_ones(values[half:])], axis=0
    )
    near_ref[...] = jnp.dot(w_scr[...], values, preferred_element_type=F32)


def mix_kernel_of_level(*refs):
    near_refs, fq_refs, (past_ref, step_ref, wk_ref) = refs[:2], refs[2:4], refs[4:7]
    first_ref, refs = refs[7], refs[8:]
    out_refs, (fk_scr, state_scr, out_scr) = refs[:-3], refs[-3:]
    rows, dh = near_refs[0].shape[0], near_refs[0].shape[1] // 2
    feats = fq_refs[0].shape[1]
    heads = past_ref.shape[0] // feats
    half = rows // heads
    place, level = spot()
    side = lax.axis_index("head")
    u = lax.div(place, 2)

    @pl.when(level < 3)
    def _():
        state_scr[0] = past_ref[...].astype(BF16)
        state_scr[1] = (past_ref[...] + step_ref[...]).astype(BF16)

    @pl.when(level >= 3)
    def _():
        write_key_features(first_ref[:, :dh], wk_ref, fk_scr)
        state = past_ref[...] + jnp.dot(
            fk_scr[...], with_ones(first_ref[:, dh:]), preferred_element_type=F32
        )
        state_scr[0] = state.astype(BF16)
        state_scr[1] = (state + step_ref[...]).astype(BF16)

    part = out_refs[0].shape[0]
    for other in (1, 0):
        for h in range(heads):
            here = slice(h * half, (h + 1) * half)
            far = jnp.dot(
                fq_refs[other][here, :],
                state_scr[u ^ other, h * feats : (h + 1) * feats, :],
                preferred_element_type=F32,
            )
            both = near_refs[other][here, :] + far
            out_scr[aligned(u ^ other, half), h * dh : (h + 1) * dh] = (
                both[:, :dh] * pl.reciprocal(both[:, dh:], approx=True)
            ).astype(BF16)
    for n, ref in enumerate(out_refs):
        dr, dy = slot_of(n, lax.rem(place, 2))
        ref[...] = out_scr[aligned((place ^ dr) * 2 + (side ^ dy), part), :]


def whole_spec(space=pltpu.VMEM):
    return pl.BlockSpec(memory_space=space)


def call(kernel, ins, outs, name, scratch=(), limit=4, out_type=BF16, aliases={}):
    return pl.pallas_call(
        kernel,
        in_specs=[whole_spec() for _ in ins],
        out_specs=[whole_spec() for _ in outs],
        out_shape=[
            jax.ShapeDtypeStruct(s, out_type[n] if isinstance(out_type, list) else out_type)
            for n, s in enumerate(outs)
        ],
        scratch_shapes=list(scratch),
        input_output_aliases=aliases,
        cost_estimate=EARLY if name in EARLY_KERNELS else None,
        compiler_params=pltpu.CompilerParams(vmem_limit_bytes=limit * 2**20),
        name=name,
    )(*ins)


def by_levels(queries, keys, values, wq, wk, factor):
    tok, width = queries.shape
    local_heads, feat, dh = wq.shape
    heads = local_heads // WAYS
    seq, sides = lax.axis_size("seq"), lax.axis_size("head")
    half = 2 * tok
    rows, states = heads * half, heads * 2 * feat

    def partner(x, dr, dy=0):
        pairs = [
            (i * sides + j, (i // WAYS * WAYS + (i % WAYS ^ dr)) * sides + (j ^ dy))
            for i in range(seq)
            for j in range(sides)
        ]
        return lax.ppermute(x, ("seq", "head"), pairs)

    def levels_back(x, by):
        pairs = [(i, i + by * WAYS) for i in range(seq - by * WAYS)]
        return lax.ppermute(x, "seq", pairs)

    place = lax.rem(lax.axis_index("seq"), WAYS)
    ours = place // 2 * 2 * dh
    cuts = [
        lax.dynamic_slice_in_dim(x, at, 2 * dh, 1)
        for at in (ours, 2 * dh - ours)
        for x in (keys, values)
    ]
    own, away = call(pack_kv_kernel, cuts, [(tok, 4 * dh)] * 2, "pack_kv")
    got = partner(away, 2)
    queries, away = lax.optimization_barrier((queries, away))
    q = list(call(pack_q_kernel, [queries], [(tok, width // WAYS)] * WAYS, "pack_q"))
    q[2], q[3] = partner(q[2], 2), partner(q[3], 3)
    (pair,) = call(pair_kernel, [own, got], [(half, 2 * dh)], "pair_kv")
    pair, q[1], wq, wk = lax.optimization_barrier((pair, q[1], wq, wk))
    pair, q[1] = partner(pair, 1), partner(q[1], 1)
    wq, wk = [lax.dynamic_slice_in_dim(w, place * heads, heads) for w in (wq, wk)]
    pair, wq, wk = lax.optimization_barrier((pair, wq, wk))
    (kv,) = call(stack_kernel, [own, got, pair], [(2 * half, 2 * dh)], "stack_kv")
    last, before = levels_back(kv, 1), levels_back(kv, 2)
    wq, kv, q[1] = lax.optimization_barrier((wq, kv, q[1]))
    (fk,) = call(own_features_kernel, [kv, wk], [(states, 4 * half)], "own_features", limit=16)
    wq, ratio = call(
        weights_kernel,
        [wq, factor.reshape(1, local_heads)],
        [(heads, dh, 2 * feat), (heads, 2 * feat)],
        "weights",
        out_type=[BF16, F32],
    )
    far_kv, fk, wq = lax.optimization_barrier((kv, fk, wq))
    first = levels_back(far_kv, 3)

    def query_features(a, b):
        return call(
            query_features_kernel,
            [a, b, wq, ratio],
            [(rows, dh), (rows, 2 * feat)],
            "query_features",
            [pltpu.VMEM((rows, 2 * feat), BF16)],
            12,
        )

    def near(other, q_rows, fq):
        return call(
            lambda *refs: near_kernel(other, *refs),
            [q_rows, fq, last, kv, fk],
            [(rows, 2 * dh)],
            "near",
            [
                pltpu.VMEM((3 * half, 2 * dh), BF16),
                pltpu.VMEM((rows, 2 * half), BF16),
            ],
            16,
            F32,
        )[0]

    q_own, fq_own = query_features(q[0], q[1])
    last, fq_own, fk = lax.optimization_barrier((last, fq_own, fk))
    fk, past, step = call(
        last_features_kernel,
        [last, wk, fk],
        [(states, 4 * half), (states, 2 * dh), (states, 2 * dh)],
        "last_features",
        limit=20,
        out_type=[BF16, F32, F32],
        aliases={2: 0},
    )
    near_own = near(0, q_own, fq_own)
    q[2], q[3], near_own = lax.optimization_barrier((q[2], q[3], near_own))
    q_other, fq_other = query_features(q[2], q[3])
    near_other = near(1, q_other, fq_other)
    before, near_other = lax.optimization_barrier((before, near_other))
    (past,) = call(
        past_kernel,
        [before, wk, past],
        [(states, 2 * dh)],
        "past",
        [pltpu.VMEM((states, 2 * half), BF16)],
        16,
        F32,
    )
    first, past = lax.optimization_barrier((first, past))
    part = tok // sides
    outs = call(
        mix_kernel_of_level,
        [near_own, near_other, fq_own, fq_other, past, step, wk, first],
        [(part, heads * dh)] * (WAYS * sides),
        "mix_level",
        [
            pltpu.VMEM((states, 2 * half), BF16),
            pltpu.VMEM((2, states, 2 * dh), BF16),
            pltpu.VMEM((2 * half, heads * dh), BF16),
        ],
        24,
    )

    def sent(x, slot):
        pairs = []
        for i in range(seq):
            dr, dy = slot[i % 2]
            to = i // WAYS * WAYS + (i % WAYS ^ dr)
            pairs += [(i * sides + j, to * sides + (j ^ dy)) for j in range(sides)]
        return lax.ppermute(x, ("seq", "head"), pairs)

    outs = list(outs)
    for n in range(1, 6):
        outs[n] = sent(outs[n], SLOTS[n])
    for n, ahead in ((6, 2), (7, 1)):
        outs[n], outs[ahead] = lax.optimization_barrier((outs[n], outs[ahead]))
        outs[n] = sent(outs[n], SLOTS[n])

    def joined(slots, into):
        return pl.pallas_call(
            lambda *refs: join_kernel(slots, *refs),
            in_specs=[whole_spec()] * len(slots) + [whole_spec(pltpu.HBM)] * len(into),
            out_specs=whole_spec(pltpu.HBM),
            out_shape=jax.ShapeDtypeStruct((part, sides * WAYS * heads * dh), BF16),
            input_output_aliases={len(slots): 0} if into else {},
            scratch_shapes=[pltpu.SemaphoreType.DMA((len(slots),))],
            compiler_params=pltpu.CompilerParams(vmem_limit_bytes=4 * 2**20),
            name="join",
        )(*[outs[n] for n in slots], *into)

    return joined((4, 5, 6, 7), [joined((0, 1, 2, 3), [])])


def by_blocks(queries, keys, values, wq, wk, ratio):
    group = wq.shape[0] // (keys.shape[1] // DH)
    place = lax.axis_index("seq").astype(jnp.int32).reshape(1)
    kv = lax.all_gather(jnp.concatenate([keys, values], axis=1), "seq", tiled=True)
    out = mix(place, queries, kv, wq, wk, ratio, group)
    return lax.all_to_all(out, "head", split_axis=0, concat_axis=1, tiled=True)


def local(queries, keys, values, q_feature, k_feature, window_factor):
    tok = queries.shape[0]
    seq, sides = lax.axis_size("seq"), lax.axis_size("head")
    wq, wk = jnp.swapaxes(q_feature, 1, 2), jnp.swapaxes(k_feature, 1, 2)
    if keys.shape[1] == WAYS * DH and seq == 4 * WAYS and sides == 2 and tok == WINDOW:
        return by_levels(queries, keys, values, wq, wk, window_factor)
    ratio = window_factor / (1.0 - window_factor)
    return by_blocks(queries, keys, values, wq, wk, ratio)


def solution(mesh):
    return jax.shard_map(
        local,
        mesh=mesh,
        in_specs=(
            P("seq", "head"),
            P("seq", "head"),
            P("seq", "head"),
            P("head", None, None),
            P("head", None, None),
            P("head"),
        ),
        out_specs=P(("seq", "head"), None),
        check_vma=False,
    )
```

```python
import math

import jax
import jax.numpy as jnp
from jax import lax
from jax.experimental import pallas as pl
from jax.experimental.pallas import tpu as pltpu
from jax.sharding import PartitionSpec as P

DH = 128
WINDOW = 64
F32 = jnp.float32
BF16 = jnp.bfloat16


def dot_t(a, b):
    return lax.dot_general(a, b, (((1,), (1,)), ((), ())), preferred_element_type=F32)


def features_t(logits):
    top = jnp.max(logits, axis=0, keepdims=True)
    low = jnp.min(logits, axis=0, keepdims=True)
    up = jnp.exp(logits - top)
    down = jnp.exp(low - logits)
    up = up * (1.0 / jnp.sum(up, axis=0, keepdims=True))
    down = down * (1.0 / jnp.sum(down, axis=0, keepdims=True))
    return jnp.concatenate([up.astype(BF16), down.astype(BF16)], axis=0)


def mix_kernel(
    place_ref, q_ref, k_ref, v_ref, wq_ref, wk_ref, ratio_ref, out_ref, fk_scr, state_scr
):
    tok = q_ref.shape[0]
    heads, feat, dh = wq_ref.shape
    seen = fk_scr.shape[1]
    place = place_ref[0]
    first_head = pl.program_id(0) * heads

    weights = wk_ref[...].reshape(heads * feat, dh)
    for start in range(0, seen, 256):
        size = min(256, seen - start)
        logits = dot_t(weights, k_ref[start : start + size, :])
        for h in range(heads):
            fk_scr[h * 2 * feat : (h + 1) * 2 * feat, start : start + size] = features_t(
                logits[h * feat : (h + 1) * feat]
            )
    row = lax.broadcasted_iota(jnp.int32, (seen, dh), 0)
    kept = row < (place - 1) * tok
    v_seen = jnp.where(kept, v_ref[:seen, :].astype(F32), 0.0).astype(BF16)
    ones_seen = jnp.where(kept, 1.0, 0.0).astype(BF16)
    v_seen = jnp.concatenate([v_seen, ones_seen], axis=1)
    state_scr[...] = jnp.dot(fk_scr[...], v_seen, preferred_element_type=F32).astype(BF16)

    before = pl.multiple_of(jnp.maximum(place - 1, 0) * tok, tok)
    own = pl.multiple_of(place * tok, tok)
    k_ext = jnp.concatenate([k_ref[pl.ds(before, tok), :], k_ref[pl.ds(own, tok), :]], axis=0)
    v_ext = jnp.concatenate([v_ref[pl.ds(before, tok), :], v_ref[pl.ds(own, tok), :]], axis=0)
    v_ext = jnp.concatenate([v_ext, jnp.ones_like(v_ext)], axis=1)
    row = lax.broadcasted_iota(jnp.int32, (tok, 2 * tok), 0)
    col = lax.broadcasted_iota(jnp.int32, (tok, 2 * tok), 1)
    valid = (col >= tok) | (place > 0)
    inside = (col > row) & (col <= row + WINDOW) & valid
    causal = (col <= row) & valid
    lane = lax.broadcasted_iota(jnp.int32, (tok, 2 * feat), 1)
    left = lane < feat
    side_r = lax.broadcasted_iota(jnp.int32, (2 * feat, 2 * feat), 0) < feat
    side_c = lax.broadcasted_iota(jnp.int32, (2 * feat, 2 * feat), 1) < feat
    halves = jnp.where(side_r == side_c, 1.0, 0.0).astype(BF16)

    for h in range(heads):
        q = q_ref[:, h * dh : (h + 1) * dh]
        wq = wq_ref[h]
        logits = dot_t(q, jnp.concatenate([wq, -wq], axis=0))
        top_l = jnp.max(jnp.where(left, logits, -jnp.inf), axis=1, keepdims=True)
        top_r = jnp.max(jnp.where(left, -jnp.inf, logits), axis=1, keepdims=True)
        expd = jnp.exp(logits - jnp.where(left, top_l, top_r)).astype(BF16)
        total = jnp.dot(expd, halves, preferred_element_type=F32)
        fq = (expd.astype(F32) / total).astype(BF16)
        fk = features_t(dot_t(wk_ref[h], k_ext))
        linear = jnp.dot(fq, fk, preferred_element_type=F32)
        scores = dot_t(q, k_ext) * (1.0 / math.sqrt(dh))
        masked = jnp.where(inside, scores, -jnp.inf)
        top = jnp.max(masked, axis=1, keepdims=True)
        soft = jnp.exp(masked - top) * ratio_ref[first_head + h]
        weight = jnp.where(causal, linear, soft).astype(BF16)
        both = jnp.dot(weight, v_ext, preferred_element_type=F32) + jnp.dot(
            fq, state_scr[h * 2 * feat : (h + 1) * 2 * feat, :], preferred_element_type=F32
        )
        out_ref[:, h * dh : (h + 1) * dh] = (both[:, :dh] / both[:, dh:]).astype(BF16)


def mix(place, queries, kv, wq, wk, ratio, group):
    tok = queries.shape[0]
    local_heads, feat, dh = wq.shape
    groups = local_heads // group
    tokens = kv.shape[0]
    seen = tokens - 2 * tok
    return pl.pallas_call(
        mix_kernel,
        grid_spec=pltpu.PrefetchScalarGridSpec(
            num_scalar_prefetch=1,
            grid=(groups,),
            in_specs=[
                pl.BlockSpec((tok, group * dh), lambda g, p: (0, g)),
                pl.BlockSpec((tokens, dh), lambda g, p: (0, g)),
                pl.BlockSpec((tokens, dh), lambda g, p: (0, groups + g)),
                pl.BlockSpec((group, feat, dh), lambda g, p: (g, 0, 0)),
                pl.BlockSpec((group, feat, dh), lambda g, p: (g, 0, 0)),
                pl.BlockSpec(memory_space=pltpu.SMEM),
            ],
            out_specs=pl.BlockSpec((tok, group * dh), lambda g, p: (0, g)),
            scratch_shapes=[
                pltpu.VMEM((group * 2 * feat, seen), BF16),
                pltpu.VMEM((group * 2 * feat, 2 * dh), BF16),
            ],
        ),
        out_shape=jax.ShapeDtypeStruct(queries.shape, BF16),
        compiler_params=pltpu.CompilerParams(vmem_limit_bytes=48 * 2**20),
        cost_estimate=pl.CostEstimate(
            flops=2 * local_heads * tokens * 3 * feat * 2 * dh,
            bytes_accessed=8 * 2**20,
            transcendentals=local_heads * tokens * 2 * feat,
        ),
    )(place, queries, kv, kv, wq, wk, ratio)


WAYS = 4

EARLY = pl.CostEstimate(flops=10**10, bytes_accessed=10**8, transcendentals=0)
EARLY_KERNELS = ("pack_kv", "pack_q", "pair_kv", "stack_kv")


SLOTS = (
    ((0, 0), (0, 0)),
    ((2, 0), (0, 1)),
    ((0, 1), (2, 0)),
    ((1, 0), (1, 0)),
    ((2, 1), (2, 1)),
    ((3, 0), (1, 1)),
    ((3, 1), (3, 1)),
    ((1, 1), (3, 0)),
)


def slot_of(n, odd):
    return [jnp.where(odd == 1, b, a) if a != b else a for a, b in zip(*SLOTS[n])]


def spot():
    at = lax.axis_index("seq")
    return lax.rem(at, WAYS), lax.div(at, WAYS)


def aligned(at, step):
    return pl.ds(pl.multiple_of(at * step, step), step)


def with_ones(values, kept=True):
    here = jnp.where(kept, 1.0, 0.0).astype(BF16)
    return jnp.concatenate([values, jnp.full(values.shape, here)], axis=1)


def pack_kv_kernel(k_ref, v_ref, k_away_ref, v_away_ref, own_ref, away_ref):
    odd = lax.rem(spot()[0], 2)
    for k, v, ref in ((k_ref, v_ref, own_ref), (k_away_ref, v_away_ref, away_ref)):
        for d in range(2):
            at = aligned(odd ^ d, DH)
            ref[:, 2 * d * DH : (2 * d + 1) * DH] = k[:, at]
            ref[:, (2 * d + 1) * DH : (2 * d + 2) * DH] = v[:, at]


def pair_kernel(own_ref, got_ref, out_ref):
    tok = own_ref.shape[0]
    out_ref[:tok, :] = own_ref[:, 2 * DH :]
    out_ref[tok:, :] = got_ref[:, 2 * DH :]


def stack_kernel(own_ref, got_ref, pair_ref, out_ref):
    tok = own_ref.shape[0]
    place = spot()[0]
    out_ref[aligned(place, tok), :] = own_ref[:, : 2 * DH]
    out_ref[aligned(place ^ 2, tok), :] = got_ref[:, : 2 * DH]
    out_ref[aligned(place ^ 1, tok), :] = pair_ref[:tok, :]
    out_ref[aligned(place ^ 3, tok), :] = pair_ref[tok:, :]


def pack_q_kernel(q_ref, *out_refs):
    place = spot()[0]
    for d, out in enumerate(out_refs):
        out[...] = q_ref[:, aligned(place ^ d, out.shape[1])]


def weights_kernel(wq_ref, factor_ref, both_ref, ratio_ref):
    heads = both_ref.shape[0]
    shape = (heads, factor_ref.shape[1])
    head = lax.broadcasted_iota(jnp.int32, shape, 0) + spot()[0] * heads
    ratio = jnp.broadcast_to((1.0 - factor_ref[...]) / factor_ref[...], shape)
    ratio = jnp.where(lax.broadcasted_iota(jnp.int32, shape, 1) == head, ratio, 0.0)
    ratio = jnp.sum(ratio, axis=1, keepdims=True)
    ratio_ref[...] = jnp.broadcast_to(ratio, ratio_ref.shape)
    for h in range(heads):
        wq = wq_ref[h].T
        both_ref[h] = jnp.concatenate([wq, -wq], axis=1)


def join_kernel(slots, *refs):
    got, out_ref, sems = refs[: len(slots)], *refs[-2:]
    width = got[0].shape[1]
    place, side = spot()[0], lax.axis_index("head")
    copies = []
    for n, ref in zip(slots, got):
        dr, dy = slot_of(n, lax.rem(place, 2) ^ (SLOTS[n][0][0] & 1))
        at = aligned((side ^ dy) * WAYS + (place ^ dr), width)
        copies.append(pltpu.make_async_copy(ref, out_ref.at[:, at], sems.at[len(copies)]))
    for copy in copies:
        copy.start()
    for copy in copies:
        copy.wait()


def write_key_features(keys, wk_ref, fk_ref):
    heads, feat, dh = wk_ref.shape
    logits = dot_t(wk_ref[...].reshape(heads * feat, dh), keys)
    for h in range(heads):
        part = logits[h * feat : (h + 1) * feat]
        top = jnp.max(part, axis=0, keepdims=True)
        low = jnp.min(part, axis=0, keepdims=True)
        for n, shifted in enumerate((part - top, low - part)):
            row = (2 * h + n) * feat
            expd = jnp.exp(shifted.astype(BF16))
            total = expd[: feat // 4]
            for q in range(1, 4):
                total = total + expd[q * feat // 4 : (q + 1) * feat // 4]
            total = jnp.sum(total.astype(F32), axis=0, keepdims=True)
            fk_ref[row : row + feat, :] = expd * pl.reciprocal(total).astype(BF16)


def own_features_kernel(own_ref, wk_ref, fk_ref):
    write_key_features(own_ref[:, :DH], wk_ref, fk_ref.at[:, own_ref.shape[0] :])


def last_features_kernel(last_ref, wk_ref, _, fk_ref, past_ref, step_ref):
    size = last_ref.shape[0]
    half = size // 2
    level = spot()[1]

    @pl.when(level == 0)
    def _():
        fk_ref[:, :size] = jnp.zeros((fk_ref.shape[0], size), BF16)
        for ref in (past_ref, step_ref):
            ref[...] = jnp.zeros_like(ref)

    @pl.when(level > 0)
    def _():
        write_key_features(last_ref[:, :DH], wk_ref, fk_ref.at[:, :size])
        for at, ref in ((0, past_ref), (half, step_ref)):
            ref[...] = jnp.dot(
                fk_ref[:, at : at + half],
                with_ones(last_ref[at : at + half, DH:]),
                preferred_element_type=F32,
            )


def past_kernel(before_ref, wk_ref, sum_ref, past_ref, fk_scr):
    level = spot()[1]

    @pl.when(level < 2)
    def _():
        past_ref[...] = sum_ref[...]

    @pl.when(level >= 2)
    def _():
        write_key_features(before_ref[:, :DH], wk_ref, fk_scr)
        past_ref[...] = sum_ref[...] + jnp.dot(
            fk_scr[...], with_ones(before_ref[:, DH:]), preferred_element_type=F32
        )


def query_features_kernel(a_ref, b_ref, w_ref, ratio_ref, q_out, fq_out, exp_scr):
    tok = a_ref.shape[0]
    heads, dh, both = w_ref.shape
    half = 2 * tok
    place = spot()[0]
    for d, ref in enumerate((a_ref, b_ref)):
        row = pl.multiple_of(lax.rem(place ^ d, 2) * tok, tok)
        for h in range(heads):
            q_out[pl.ds(h * half + row, tok), :] = ref[:, h * dh : (h + 1) * dh]
    rows_of = [slice(h * half, (h + 1) * half) for h in range(heads)]
    left = lax.broadcasted_iota(jnp.int32, (half, both), 1) < both // 2
    for h, rows in enumerate(rows_of):
        logits = jnp.dot(q_out[rows, :], w_ref[h], preferred_element_type=F32)
        top_l = jnp.max(jnp.where(left, logits, -jnp.inf), axis=1, keepdims=True)
        top_r = jnp.max(jnp.where(left, -jnp.inf, logits), axis=1, keepdims=True)
        exp_scr[rows, :] = jnp.exp((logits - jnp.where(left, top_l, top_r)).astype(BF16))
    side_r = lax.broadcasted_iota(jnp.int32, (both, both), 0) < both // 2
    side_c = lax.broadcasted_iota(jnp.int32, (both, both), 1) < both // 2
    halves = jnp.where(side_r == side_c, 1.0, 0.0).astype(BF16)
    total = jnp.dot(exp_scr[...], halves, preferred_element_type=F32)
    for h, rows in enumerate(rows_of):
        scale = pl.reciprocal(total[rows], approx=True) * ratio_ref[h : h + 1, :]
        fq_out[rows, :] = (exp_scr[rows, :].astype(F32) * scale).astype(BF16)


def near_kernel(other, q_ref, fq_ref, last_ref, own_ref, fk_ref, near_ref, kv_scr, w_scr):
    half, dh = last_ref.shape[0] // 2, q_ref.shape[1]
    heads = q_ref.shape[0] // half
    feats = fq_ref.shape[1]
    place, level = spot()
    u = lax.div(place, 2) ^ other
    kv_scr[:half, :] = last_ref[half:, :]
    kv_scr[half:, :] = own_ref[...]
    at = pl.ds(pl.multiple_of(u * half, half), 2 * half)
    keys, values = kv_scr[at, :dh], kv_scr[at, dh:]
    fk_at = pl.ds(pl.multiple_of((u + 1) * half, half), 2 * half)
    known = (level > 0) | (u > 0)
    cut = half - WINDOW
    row = lax.broadcasted_iota(jnp.int32, (WINDOW, 2 * half), 0)
    col = lax.broadcasted_iota(jnp.int32, (WINDOW, 2 * half), 1)
    inside = (col > row + cut) & (col <= row + half) & ((col >= half) | known)
    causal = (col <= row + cut)[:, :half]
    row, col = row[:, :half], col[:, :half]
    inside_low = (col > row) & (col <= row + WINDOW)
    causal_low = col <= row
    scores = dot_t(q_ref[...], keys)
    scale = math.log2(math.e) / math.sqrt(dh)

    def window(part, kept):
        masked = jnp.where(kept, part, -jnp.inf)
        top = jnp.max(masked, axis=1, keepdims=True)
        return jnp.exp2(((masked - top) * scale).astype(BF16))

    for h in range(heads):
        here = slice(h * half, (h + 1) * half)
        up, low = slice(h * half, h * half + cut), slice(h * half + cut, (h + 1) * half)
        linear = jnp.dot(
            fq_ref[here, :],
            fk_ref[h * feats : (h + 1) * feats, fk_at],
            preferred_element_type=F32,
        )
        soft = window(scores[up], inside)
        w_scr[up, :half] = soft[:, :half] + jnp.where(causal, linear[:cut, :half], 0.0).astype(BF16)
        w_scr[up, half:] = soft[:, half:]
        soft = window(scores[low, half:], inside_low)
        w_scr[low, :half] = linear[cut:, :half].astype(BF16)
        w_scr[low, half:] = soft + jnp.where(causal_low, linear[cut:, half:], 0.0).astype(BF16)
    values = jnp.concatenate(
        [with_ones(values[:half], known), with_ones(values[half:])], axis=0
    )
    near_ref[...] = jnp.dot(w_scr[...], values, preferred_element_type=F32)


def mix_kernel_of_level(*refs):
    near_refs, fq_refs, (past_ref, step_ref, wk_ref) = refs[:2], refs[2:4], refs[4:7]
    first_ref, refs = refs[7], refs[8:]
    out_refs, (fk_scr, state_scr, out_scr) = refs[:-3], refs[-3:]
    rows, dh = near_refs[0].shape[0], near_refs[0].shape[1] // 2
    feats = fq_refs[0].shape[1]
    heads = past_ref.shape[0] // feats
    half = rows // heads
    place, level = spot()
    side = lax.axis_index("head")
    u = lax.div(place, 2)

    @pl.when(level < 3)
    def _():
        state_scr[0] = past_ref[...].astype(BF16)
        state_scr[1] = (past_ref[...] + step_ref[...]).astype(BF16)

    @pl.when(level >= 3)
    def _():
        write_key_features(first_ref[:, :dh], wk_ref, fk_scr)
        state = past_ref[...] + jnp.dot(
            fk_scr[...], with_ones(first_ref[:, dh:]), preferred_element_type=F32
        )
        state_scr[0] = state.astype(BF16)
        state_scr[1] = (state + step_ref[...]).astype(BF16)

    part = out_refs[0].shape[0]
    for other in (1, 0):
        for h in range(heads):
            here = slice(h * half, (h + 1) * half)
            far = jnp.dot(
                fq_refs[other][here, :],
                state_scr[u ^ other, h * feats : (h + 1) * feats, :],
                preferred_element_type=F32,
            )
            both = near_refs[other][here, :] + far
            out_scr[aligned(u ^ other, half), h * dh : (h + 1) * dh] = (
                both[:, :dh] * pl.reciprocal(both[:, dh:], approx=True)
            ).astype(BF16)
    for n, ref in enumerate(out_refs):
        dr, dy = slot_of(n, lax.rem(place, 2))
        ref[...] = out_scr[aligned((place ^ dr) * 2 + (side ^ dy), part), :]


def whole_spec(space=pltpu.VMEM):
    return pl.BlockSpec(memory_space=space)


def call(kernel, ins, outs, name, scratch=(), limit=4, out_type=BF16, aliases={}):
    return pl.pallas_call(
        kernel,
        in_specs=[whole_spec() for _ in ins],
        out_specs=[whole_spec() for _ in outs],
        out_shape=[
            jax.ShapeDtypeStruct(s, out_type[n] if isinstance(out_type, list) else out_type)
            for n, s in enumerate(outs)
        ],
        scratch_shapes=list(scratch),
        input_output_aliases=aliases,
        cost_estimate=EARLY if name in EARLY_KERNELS else None,
        compiler_params=pltpu.CompilerParams(vmem_limit_bytes=limit * 2**20),
        name=name,
    )(*ins)


def by_levels(queries, keys, values, wq, wk, factor):
    tok, width = queries.shape
    local_heads, feat, dh = wq.shape
    heads = local_heads // WAYS
    seq, sides = lax.axis_size("seq"), lax.axis_size("head")
    half = 2 * tok
    rows, states = heads * half, heads * 2 * feat

    def partner(x, dr, dy=0):
        pairs = [
            (i * sides + j, (i // WAYS * WAYS + (i % WAYS ^ dr)) * sides + (j ^ dy))
            for i in range(seq)
            for j in range(sides)
        ]
        return lax.ppermute(x, ("seq", "head"), pairs)

    def levels_back(x, by):
        pairs = [(i, i + by * WAYS) for i in range(seq - by * WAYS)]
        return lax.ppermute(x, "seq", pairs)

    place = lax.rem(lax.axis_index("seq"), WAYS)
    ours = place // 2 * 2 * dh
    cuts = [
        lax.dynamic_slice_in_dim(x, at, 2 * dh, 1)
        for at in (ours, 2 * dh - ours)
        for x in (keys, values)
    ]
    own, away = call(pack_kv_kernel, cuts, [(tok, 4 * dh)] * 2, "pack_kv")
    got = partner(away, 2)
    queries, away = lax.optimization_barrier((queries, away))
    q = list(call(pack_q_kernel, [queries], [(tok, width // WAYS)] * WAYS, "pack_q"))
    q[2], q[3] = partner(q[2], 2), partner(q[3], 3)
    (pair,) = call(pair_kernel, [own, got], [(half, 2 * dh)], "pair_kv")
    pair, q[1], wq, wk = lax.optimization_barrier((pair, q[1], wq, wk))
    pair, q[1] = partner(pair, 1), partner(q[1], 1)
    wq, wk = [lax.dynamic_slice_in_dim(w, place * heads, heads) for w in (wq, wk)]
    pair, wq, wk = lax.optimization_barrier((pair, wq, wk))
    (kv,) = call(stack_kernel, [own, got, pair], [(2 * half, 2 * dh)], "stack_kv")
    last, before = levels_back(kv, 1), levels_back(kv, 2)
    wq, kv, q[1] = lax.optimization_barrier((wq, kv, q[1]))
    (fk,) = call(own_features_kernel, [kv, wk], [(states, 4 * half)], "own_features", limit=16)
    wq, ratio = call(
        weights_kernel,
        [wq, factor.reshape(1, local_heads)],
        [(heads, dh, 2 * feat), (heads, 2 * feat)],
        "weights",
        out_type=[BF16, F32],
    )

    def query_features(a, b):
        return call(
            query_features_kernel,
            [a, b, wq, ratio],
            [(rows, dh), (rows, 2 * feat)],
            "query_features",
            [pltpu.VMEM((rows, 2 * feat), BF16)],
            12,
        )

    def near(other, q_rows, fq):
        return call(
            lambda *refs: near_kernel(other, *refs),
            [q_rows, fq, last, kv, fk],
            [(rows, 2 * dh)],
            "near",
            [
                pltpu.VMEM((3 * half, 2 * dh), BF16),
                pltpu.VMEM((rows, 2 * half), BF16),
            ],
            16,
            F32,
        )[0]

    q_own, fq_own = query_features(q[0], q[1])
    far_kv, fk, fq_own = lax.optimization_barrier((kv, fk, fq_own))
    first = levels_back(far_kv, 3)
    last, fq_own, fk = lax.optimization_barrier((last, fq_own, fk))
    fk, past, step = call(
        last_features_kernel,
        [last, wk, fk],
        [(states, 4 * half), (states, 2 * dh), (states, 2 * dh)],
        "last_features",
        limit=20,
        out_type=[BF16, F32, F32],
        aliases={2: 0},
    )
    near_own = near(0, q_own, fq_own)
    q[2], q[3], near_own = lax.optimization_barrier((q[2], q[3], near_own))
    q_other, fq_other = query_features(q[2], q[3])
    near_other = near(1, q_other, fq_other)
    before, near_other = lax.optimization_barrier((before, near_other))
    (past,) = call(
        past_kernel,
        [before, wk, past],
        [(states, 2 * dh)],
        "past",
        [pltpu.VMEM((states, 2 * half), BF16)],
        16,
        F32,
    )
    first, past = lax.optimization_barrier((first, past))
    part = tok // sides
    outs = call(
        mix_kernel_of_level,
        [near_own, near_other, fq_own, fq_other, past, step, wk, first],
        [(part, heads * dh)] * (WAYS * sides),
        "mix_level",
        [
            pltpu.VMEM((states, 2 * half), BF16),
            pltpu.VMEM((2, states, 2 * dh), BF16),
            pltpu.VMEM((2 * half, heads * dh), BF16),
        ],
        24,
    )

    def sent(x, slot):
        pairs = []
        for i in range(seq):
            dr, dy = slot[i % 2]
            to = i // WAYS * WAYS + (i % WAYS ^ dr)
            pairs += [(i * sides + j, to * sides + (j ^ dy)) for j in range(sides)]
        return lax.ppermute(x, ("seq", "head"), pairs)

    outs = list(outs)
    for n in range(1, 6):
        outs[n] = sent(outs[n], SLOTS[n])
    outs[6], outs[7], outs[3] = lax.optimization_barrier((outs[6], outs[7], outs[3]))
    outs[6], outs[7] = sent(outs[6], SLOTS[6]), sent(outs[7], SLOTS[7])

    def joined(slots, into):
        return pl.pallas_call(
            lambda *refs: join_kernel(slots, *refs),
            in_specs=[whole_spec()] * len(slots) + [whole_spec(pltpu.HBM)] * len(into),
            out_specs=whole_spec(pltpu.HBM),
            out_shape=jax.ShapeDtypeStruct((part, sides * WAYS * heads * dh), BF16),
            input_output_aliases={len(slots): 0} if into else {},
            scratch_shapes=[pltpu.SemaphoreType.DMA((len(slots),))],
            compiler_params=pltpu.CompilerParams(vmem_limit_bytes=4 * 2**20),
            name="join",
        )(*[outs[n] for n in slots], *into)

    return joined((4, 5, 6, 7), [joined((0, 1, 2, 3), [])])


def by_blocks(queries, keys, values, wq, wk, ratio):
    group = wq.shape[0] // (keys.shape[1] // DH)
    place = lax.axis_index("seq").astype(jnp.int32).reshape(1)
    kv = lax.all_gather(jnp.concatenate([keys, values], axis=1), "seq", tiled=True)
    out = mix(place, queries, kv, wq, wk, ratio, group)
    return lax.all_to_all(out, "head", split_axis=0, concat_axis=1, tiled=True)


def local(queries, keys, values, q_feature, k_feature, window_factor):
    tok = queries.shape[0]
    seq, sides = lax.axis_size("seq"), lax.axis_size("head")
    wq, wk = jnp.swapaxes(q_feature, 1, 2), jnp.swapaxes(k_feature, 1, 2)
    if keys.shape[1] == WAYS * DH and seq == 4 * WAYS and sides == 2 and tok == WINDOW:
        return by_levels(queries, keys, values, wq, wk, window_factor)
    ratio = window_factor / (1.0 - window_factor)
    return by_blocks(queries, keys, values, wq, wk, ratio)


def solution(mesh):
    return jax.shard_map(
        local,
        mesh=mesh,
        in_specs=(
            P("seq", "head"),
            P("seq", "head"),
            P("seq", "head"),
            P("head", None, None),
            P("head", None, None),
            P("head"),
        ),
        out_specs=P(("seq", "head"), None),
        check_vma=False,
    )
```

```python
import math

import jax
import jax.numpy as jnp
from jax import lax
from jax.experimental import pallas as pl
from jax.experimental.pallas import tpu as pltpu
from jax.sharding import PartitionSpec as P

DH = 128
WINDOW = 64
F32 = jnp.float32
BF16 = jnp.bfloat16


def dot_t(a, b):
    return lax.dot_general(a, b, (((1,), (1,)), ((), ())), preferred_element_type=F32)


def features_t(logits):
    top = jnp.max(logits, axis=0, keepdims=True)
    low = jnp.min(logits, axis=0, keepdims=True)
    up = jnp.exp(logits - top)
    down = jnp.exp(low - logits)
    up = up * (1.0 / jnp.sum(up, axis=0, keepdims=True))
    down = down * (1.0 / jnp.sum(down, axis=0, keepdims=True))
    return jnp.concatenate([up.astype(BF16), down.astype(BF16)], axis=0)


def mix_kernel(
    place_ref, q_ref, k_ref, v_ref, wq_ref, wk_ref, ratio_ref, out_ref, fk_scr, state_scr
):
    tok = q_ref.shape[0]
    heads, feat, dh = wq_ref.shape
    seen = fk_scr.shape[1]
    place = place_ref[0]
    first_head = pl.program_id(0) * heads

    weights = wk_ref[...].reshape(heads * feat, dh)
    for start in range(0, seen, 256):
        size = min(256, seen - start)
        logits = dot_t(weights, k_ref[start : start + size, :])
        for h in range(heads):
            fk_scr[h * 2 * feat : (h + 1) * 2 * feat, start : start + size] = features_t(
                logits[h * feat : (h + 1) * feat]
            )
    row = lax.broadcasted_iota(jnp.int32, (seen, dh), 0)
    kept = row < (place - 1) * tok
    v_seen = jnp.where(kept, v_ref[:seen, :].astype(F32), 0.0).astype(BF16)
    ones_seen = jnp.where(kept, 1.0, 0.0).astype(BF16)
    v_seen = jnp.concatenate([v_seen, ones_seen], axis=1)
    state_scr[...] = jnp.dot(fk_scr[...], v_seen, preferred_element_type=F32).astype(BF16)

    before = pl.multiple_of(jnp.maximum(place - 1, 0) * tok, tok)
    own = pl.multiple_of(place * tok, tok)
    k_ext = jnp.concatenate([k_ref[pl.ds(before, tok), :], k_ref[pl.ds(own, tok), :]], axis=0)
    v_ext = jnp.concatenate([v_ref[pl.ds(before, tok), :], v_ref[pl.ds(own, tok), :]], axis=0)
    v_ext = jnp.concatenate([v_ext, jnp.ones_like(v_ext)], axis=1)
    row = lax.broadcasted_iota(jnp.int32, (tok, 2 * tok), 0)
    col = lax.broadcasted_iota(jnp.int32, (tok, 2 * tok), 1)
    valid = (col >= tok) | (place > 0)
    inside = (col > row) & (col <= row + WINDOW) & valid
    causal = (col <= row) & valid
    lane = lax.broadcasted_iota(jnp.int32, (tok, 2 * feat), 1)
    left = lane < feat
    side_r = lax.broadcasted_iota(jnp.int32, (2 * feat, 2 * feat), 0) < feat
    side_c = lax.broadcasted_iota(jnp.int32, (2 * feat, 2 * feat), 1) < feat
    halves = jnp.where(side_r == side_c, 1.0, 0.0).astype(BF16)

    for h in range(heads):
        q = q_ref[:, h * dh : (h + 1) * dh]
        wq = wq_ref[h]
        logits = dot_t(q, jnp.concatenate([wq, -wq], axis=0))
        top_l = jnp.max(jnp.where(left, logits, -jnp.inf), axis=1, keepdims=True)
        top_r = jnp.max(jnp.where(left, -jnp.inf, logits), axis=1, keepdims=True)
        expd = jnp.exp(logits - jnp.where(left, top_l, top_r)).astype(BF16)
        total = jnp.dot(expd, halves, preferred_element_type=F32)
        fq = (expd.astype(F32) / total).astype(BF16)
        fk = features_t(dot_t(wk_ref[h], k_ext))
        linear = jnp.dot(fq, fk, preferred_element_type=F32)
        scores = dot_t(q, k_ext) * (1.0 / math.sqrt(dh))
        masked = jnp.where(inside, scores, -jnp.inf)
        top = jnp.max(masked, axis=1, keepdims=True)
        soft = jnp.exp(masked - top) * ratio_ref[first_head + h]
        weight = jnp.where(causal, linear, soft).astype(BF16)
        both = jnp.dot(weight, v_ext, preferred_element_type=F32) + jnp.dot(
            fq, state_scr[h * 2 * feat : (h + 1) * 2 * feat, :], preferred_element_type=F32
        )
        out_ref[:, h * dh : (h + 1) * dh] = (both[:, :dh] / both[:, dh:]).astype(BF16)


def mix(place, queries, kv, wq, wk, ratio, group):
    tok = queries.shape[0]
    local_heads, feat, dh = wq.shape
    groups = local_heads // group
    tokens = kv.shape[0]
    seen = tokens - 2 * tok
    return pl.pallas_call(
        mix_kernel,
        grid_spec=pltpu.PrefetchScalarGridSpec(
            num_scalar_prefetch=1,
            grid=(groups,),
            in_specs=[
                pl.BlockSpec((tok, group * dh), lambda g, p: (0, g)),
                pl.BlockSpec((tokens, dh), lambda g, p: (0, g)),
                pl.BlockSpec((tokens, dh), lambda g, p: (0, groups + g)),
                pl.BlockSpec((group, feat, dh), lambda g, p: (g, 0, 0)),
                pl.BlockSpec((group, feat, dh), lambda g, p: (g, 0, 0)),
                pl.BlockSpec(memory_space=pltpu.SMEM),
            ],
            out_specs=pl.BlockSpec((tok, group * dh), lambda g, p: (0, g)),
            scratch_shapes=[
                pltpu.VMEM((group * 2 * feat, seen), BF16),
                pltpu.VMEM((group * 2 * feat, 2 * dh), BF16),
            ],
        ),
        out_shape=jax.ShapeDtypeStruct(queries.shape, BF16),
        compiler_params=pltpu.CompilerParams(vmem_limit_bytes=48 * 2**20),
        cost_estimate=pl.CostEstimate(
            flops=2 * local_heads * tokens * 3 * feat * 2 * dh,
            bytes_accessed=8 * 2**20,
            transcendentals=local_heads * tokens * 2 * feat,
        ),
    )(place, queries, kv, kv, wq, wk, ratio)


WAYS = 4

EARLY = pl.CostEstimate(flops=10**10, bytes_accessed=10**8, transcendentals=0)
EARLY_KERNELS = ("pack_kv", "pack_q", "pair_kv", "stack_kv")


SLOTS = (
    ((0, 0), (0, 0)),
    ((2, 0), (0, 1)),
    ((0, 1), (2, 0)),
    ((1, 0), (1, 0)),
    ((2, 1), (2, 1)),
    ((3, 0), (1, 1)),
    ((3, 1), (3, 1)),
    ((1, 1), (3, 0)),
)


def slot_of(n, odd):
    return [jnp.where(odd == 1, b, a) if a != b else a for a, b in zip(*SLOTS[n])]


def spot():
    at = lax.axis_index("seq")
    return lax.rem(at, WAYS), lax.div(at, WAYS)


def aligned(at, step):
    return pl.ds(pl.multiple_of(at * step, step), step)


def with_ones(values, kept=True):
    here = jnp.where(kept, 1.0, 0.0).astype(BF16)
    return jnp.concatenate([values, jnp.full(values.shape, here)], axis=1)


def pack_kv_kernel(k_ref, v_ref, k_away_ref, v_away_ref, own_ref, away_ref):
    odd = lax.rem(spot()[0], 2)
    for k, v, ref in ((k_ref, v_ref, own_ref), (k_away_ref, v_away_ref, away_ref)):
        for d in range(2):
            at = aligned(odd ^ d, DH)
            ref[:, 2 * d * DH : (2 * d + 1) * DH] = k[:, at]
            ref[:, (2 * d + 1) * DH : (2 * d + 2) * DH] = v[:, at]


def pair_kernel(own_ref, got_ref, out_ref):
    tok = own_ref.shape[0]
    out_ref[:tok, :] = own_ref[:, 2 * DH :]
    out_ref[tok:, :] = got_ref[:, 2 * DH :]


def stack_kernel(own_ref, got_ref, pair_ref, out_ref):
    tok = own_ref.shape[0]
    place = spot()[0]
    out_ref[aligned(place, tok), :] = own_ref[:, : 2 * DH]
    out_ref[aligned(place ^ 2, tok), :] = got_ref[:, : 2 * DH]
    out_ref[aligned(place ^ 1, tok), :] = pair_ref[:tok, :]
    out_ref[aligned(place ^ 3, tok), :] = pair_ref[tok:, :]


def pack_q_kernel(q_ref, *out_refs):
    place = spot()[0]
    for d, out in enumerate(out_refs):
        out[...] = q_ref[:, aligned(place ^ d, out.shape[1])]


def weights_kernel(wq_ref, factor_ref, both_ref, ratio_ref):
    heads = both_ref.shape[0]
    shape = (heads, factor_ref.shape[1])
    head = lax.broadcasted_iota(jnp.int32, shape, 0) + spot()[0] * heads
    ratio = jnp.broadcast_to((1.0 - factor_ref[...]) / factor_ref[...], shape)
    ratio = jnp.where(lax.broadcasted_iota(jnp.int32, shape, 1) == head, ratio, 0.0)
    ratio = jnp.sum(ratio, axis=1, keepdims=True)
    ratio_ref[...] = jnp.broadcast_to(ratio, ratio_ref.shape)
    for h in range(heads):
        wq = wq_ref[h].T
        both_ref[h] = jnp.concatenate([wq, -wq], axis=1)


def join_kernel(slots, *refs):
    got, out_ref, sems = refs[: len(slots)], *refs[-2:]
    width = got[0].shape[1]
    place, side = spot()[0], lax.axis_index("head")
    copies = []
    for n, ref in zip(slots, got):
        dr, dy = slot_of(n, lax.rem(place, 2) ^ (SLOTS[n][0][0] & 1))
        at = aligned((side ^ dy) * WAYS + (place ^ dr), width)
        copies.append(pltpu.make_async_copy(ref, out_ref.at[:, at], sems.at[len(copies)]))
    for copy in copies:
        copy.start()
    for copy in copies:
        copy.wait()


def write_key_features(keys, wk_ref, fk_ref):
    heads, feat, dh = wk_ref.shape
    logits = dot_t(wk_ref[...].reshape(heads * feat, dh), keys)
    for h in range(heads):
        part = logits[h * feat : (h + 1) * feat]
        top = jnp.max(part, axis=0, keepdims=True)
        low = jnp.min(part, axis=0, keepdims=True)
        for n, shifted in enumerate((part - top, low - part)):
            row = (2 * h + n) * feat
            expd = jnp.exp(shifted.astype(BF16))
            total = expd[: feat // 4]
            for q in range(1, 4):
                total = total + expd[q * feat // 4 : (q + 1) * feat // 4]
            total = jnp.sum(total.astype(F32), axis=0, keepdims=True)
            fk_ref[row : row + feat, :] = expd * pl.reciprocal(total).astype(BF16)


def own_features_kernel(own_ref, wk_ref, fk_ref):
    write_key_features(own_ref[:, :DH], wk_ref, fk_ref.at[:, own_ref.shape[0] :])


def last_features_kernel(last_ref, wk_ref, _, fk_ref, past_ref, step_ref):
    size = last_ref.shape[0]
    half = size // 2
    level = spot()[1]

    @pl.when(level == 0)
    def _():
        fk_ref[:, :size] = jnp.zeros((fk_ref.shape[0], size), BF16)
        for ref in (past_ref, step_ref):
            ref[...] = jnp.zeros_like(ref)

    @pl.when(level > 0)
    def _():
        write_key_features(last_ref[:, :DH], wk_ref, fk_ref.at[:, :size])
        for at, ref in ((0, past_ref), (half, step_ref)):
            ref[...] = jnp.dot(
                fk_ref[:, at : at + half],
                with_ones(last_ref[at : at + half, DH:]),
                preferred_element_type=F32,
            )


def past_kernel(first_ref, wk_ref, sum_ref, past_ref, fk_scr):
    level = spot()[1]

    @pl.when(level < 3)
    def _():
        past_ref[...] = sum_ref[...]

    @pl.when(level >= 3)
    def _():
        write_key_features(first_ref[:, :DH], wk_ref, fk_scr)
        past_ref[...] = sum_ref[...] + jnp.dot(
            fk_scr[...], with_ones(first_ref[:, DH:]), preferred_element_type=F32
        )


def query_features_kernel(a_ref, b_ref, w_ref, ratio_ref, q_out, fq_out, exp_scr):
    tok = a_ref.shape[0]
    heads, dh, both = w_ref.shape
    half = 2 * tok
    place = spot()[0]
    for d, ref in enumerate((a_ref, b_ref)):
        row = pl.multiple_of(lax.rem(place ^ d, 2) * tok, tok)
        for h in range(heads):
            q_out[pl.ds(h * half + row, tok), :] = ref[:, h * dh : (h + 1) * dh]
    rows_of = [slice(h * half, (h + 1) * half) for h in range(heads)]
    left = lax.broadcasted_iota(jnp.int32, (half, both), 1) < both // 2
    for h, rows in enumerate(rows_of):
        logits = jnp.dot(q_out[rows, :], w_ref[h], preferred_element_type=F32)
        top_l = jnp.max(jnp.where(left, logits, -jnp.inf), axis=1, keepdims=True)
        top_r = jnp.max(jnp.where(left, -jnp.inf, logits), axis=1, keepdims=True)
        exp_scr[rows, :] = jnp.exp((logits - jnp.where(left, top_l, top_r)).astype(BF16))
    side_r = lax.broadcasted_iota(jnp.int32, (both, both), 0) < both // 2
    side_c = lax.broadcasted_iota(jnp.int32, (both, both), 1) < both // 2
    halves = jnp.where(side_r == side_c, 1.0, 0.0).astype(BF16)
    total = jnp.dot(exp_scr[...], halves, preferred_element_type=F32)
    for h, rows in enumerate(rows_of):
        scale = pl.reciprocal(total[rows], approx=True) * ratio_ref[h : h + 1, :]
        fq_out[rows, :] = (exp_scr[rows, :].astype(F32) * scale).astype(BF16)


def near_kernel(other, q_ref, fq_ref, last_ref, own_ref, fk_ref, near_ref, kv_scr, w_scr):
    half, dh = last_ref.shape[0] // 2, q_ref.shape[1]
    heads = q_ref.shape[0] // half
    feats = fq_ref.shape[1]
    place, level = spot()
    u = lax.div(place, 2) ^ other
    kv_scr[:half, :] = last_ref[half:, :]
    kv_scr[half:, :] = own_ref[...]
    at = pl.ds(pl.multiple_of(u * half, half), 2 * half)
    keys, values = kv_scr[at, :dh], kv_scr[at, dh:]
    fk_at = pl.ds(pl.multiple_of((u + 1) * half, half), 2 * half)
    known = (level > 0) | (u > 0)
    cut = half - WINDOW
    row = lax.broadcasted_iota(jnp.int32, (WINDOW, 2 * half), 0)
    col = lax.broadcasted_iota(jnp.int32, (WINDOW, 2 * half), 1)
    inside = (col > row + cut) & (col <= row + half) & ((col >= half) | known)
    causal = (col <= row + cut)[:, :half]
    row, col = row[:, :half], col[:, :half]
    inside_low = (col > row) & (col <= row + WINDOW)
    causal_low = col <= row
    scores = dot_t(q_ref[...], keys)
    scale = math.log2(math.e) / math.sqrt(dh)

    def window(part, kept):
        masked = jnp.where(kept, part, -jnp.inf)
        top = jnp.max(masked, axis=1, keepdims=True)
        return jnp.exp2(((masked - top) * scale).astype(BF16))

    for h in range(heads):
        here = slice(h * half, (h + 1) * half)
        up, low = slice(h * half, h * half + cut), slice(h * half + cut, (h + 1) * half)
        linear = jnp.dot(
            fq_ref[here, :],
            fk_ref[h * feats : (h + 1) * feats, fk_at],
            preferred_element_type=F32,
        )
        soft = window(scores[up], inside)
        w_scr[up, :half] = soft[:, :half] + jnp.where(causal, linear[:cut, :half], 0.0).astype(BF16)
        w_scr[up, half:] = soft[:, half:]
        soft = window(scores[low, half:], inside_low)
        w_scr[low, :half] = linear[cut:, :half].astype(BF16)
        w_scr[low, half:] = soft + jnp.where(causal_low, linear[cut:, half:], 0.0).astype(BF16)
    values = jnp.concatenate(
        [with_ones(values[:half], known), with_ones(values[half:])], axis=0
    )
    near_ref[...] = jnp.dot(w_scr[...], values, preferred_element_type=F32)


def mix_kernel_of_level(*refs):
    near_refs, fq_refs, (past_ref, step_ref, wk_ref) = refs[:2], refs[2:4], refs[4:7]
    before_ref, refs = refs[7], refs[8:]
    out_refs, (fk_scr, state_scr, out_scr) = refs[:-3], refs[-3:]
    rows, dh = near_refs[0].shape[0], near_refs[0].shape[1] // 2
    feats = fq_refs[0].shape[1]
    heads = past_ref.shape[0] // feats
    half = rows // heads
    place, level = spot()
    side = lax.axis_index("head")
    u = lax.div(place, 2)

    @pl.when(level < 2)
    def _():
        state_scr[0] = past_ref[...].astype(BF16)
        state_scr[1] = (past_ref[...] + step_ref[...]).astype(BF16)

    @pl.when(level >= 2)
    def _():
        write_key_features(before_ref[:, :dh], wk_ref, fk_scr)
        state = past_ref[...] + jnp.dot(
            fk_scr[...], with_ones(before_ref[:, dh:]), preferred_element_type=F32
        )
        state_scr[0] = state.astype(BF16)
        state_scr[1] = (state + step_ref[...]).astype(BF16)

    part = out_refs[0].shape[0]
    for other in (1, 0):
        for h in range(heads):
            here = slice(h * half, (h + 1) * half)
            far = jnp.dot(
                fq_refs[other][here, :],
                state_scr[u ^ other, h * feats : (h + 1) * feats, :],
                preferred_element_type=F32,
            )
            both = near_refs[other][here, :] + far
            out_scr[aligned(u ^ other, half), h * dh : (h + 1) * dh] = (
                both[:, :dh] * pl.reciprocal(both[:, dh:], approx=True)
            ).astype(BF16)
    for n, ref in enumerate(out_refs):
        dr, dy = slot_of(n, lax.rem(place, 2))
        ref[...] = out_scr[aligned((place ^ dr) * 2 + (side ^ dy), part), :]


def whole_spec(space=pltpu.VMEM):
    return pl.BlockSpec(memory_space=space)


def call(kernel, ins, outs, name, scratch=(), limit=4, out_type=BF16, aliases={}):
    return pl.pallas_call(
        kernel,
        in_specs=[whole_spec() for _ in ins],
        out_specs=[whole_spec() for _ in outs],
        out_shape=[
            jax.ShapeDtypeStruct(s, out_type[n] if isinstance(out_type, list) else out_type)
            for n, s in enumerate(outs)
        ],
        scratch_shapes=list(scratch),
        input_output_aliases=aliases,
        cost_estimate=EARLY if name in EARLY_KERNELS else None,
        compiler_params=pltpu.CompilerParams(vmem_limit_bytes=limit * 2**20),
        name=name,
    )(*ins)


def by_levels(queries, keys, values, wq, wk, factor):
    tok, width = queries.shape
    local_heads, feat, dh = wq.shape
    heads = local_heads // WAYS
    seq, sides = lax.axis_size("seq"), lax.axis_size("head")
    half = 2 * tok
    rows, states = heads * half, heads * 2 * feat

    def partner(x, dr, dy=0):
        pairs = [
            (i * sides + j, (i // WAYS * WAYS + (i % WAYS ^ dr)) * sides + (j ^ dy))
            for i in range(seq)
            for j in range(sides)
        ]
        return lax.ppermute(x, ("seq", "head"), pairs)

    def levels_back(x, by):
        pairs = [(i, i + by * WAYS) for i in range(seq - by * WAYS)]
        return lax.ppermute(x, "seq", pairs)

    place = lax.rem(lax.axis_index("seq"), WAYS)
    ours = place // 2 * 2 * dh
    cuts = [
        lax.dynamic_slice_in_dim(x, at, 2 * dh, 1)
        for at in (ours, 2 * dh - ours)
        for x in (keys, values)
    ]
    own, away = call(pack_kv_kernel, cuts, [(tok, 4 * dh)] * 2, "pack_kv")
    got = partner(away, 2)
    queries, away = lax.optimization_barrier((queries, away))
    q = list(call(pack_q_kernel, [queries], [(tok, width // WAYS)] * WAYS, "pack_q"))
    q[2], q[3] = partner(q[2], 2), partner(q[3], 3)
    (pair,) = call(pair_kernel, [own, got], [(half, 2 * dh)], "pair_kv")
    pair, q[1], wq, wk = lax.optimization_barrier((pair, q[1], wq, wk))
    pair, q[1] = partner(pair, 1), partner(q[1], 1)
    wq, wk = [lax.dynamic_slice_in_dim(w, place * heads, heads) for w in (wq, wk)]
    pair, wq, wk = lax.optimization_barrier((pair, wq, wk))
    (kv,) = call(stack_kernel, [own, got, pair], [(2 * half, 2 * dh)], "stack_kv")
    last, first = levels_back(kv, 1), levels_back(kv, 3)
    wq, kv, q[1] = lax.optimization_barrier((wq, kv, q[1]))
    before = levels_back(kv, 2)
    (fk,) = call(own_features_kernel, [kv, wk], [(states, 4 * half)], "own_features", limit=16)
    wq, ratio = call(
        weights_kernel,
        [wq, factor.reshape(1, local_heads)],
        [(heads, dh, 2 * feat), (heads, 2 * feat)],
        "weights",
        out_type=[BF16, F32],
    )

    def query_features(a, b):
        return call(
            query_features_kernel,
            [a, b, wq, ratio],
            [(rows, dh), (rows, 2 * feat)],
            "query_features",
            [pltpu.VMEM((rows, 2 * feat), BF16)],
            12,
        )

    def near(other, q_rows, fq):
        return call(
            lambda *refs: near_kernel(other, *refs),
            [q_rows, fq, last, kv, fk],
            [(rows, 2 * dh)],
            "near",
            [
                pltpu.VMEM((3 * half, 2 * dh), BF16),
                pltpu.VMEM((rows, 2 * half), BF16),
            ],
            16,
            F32,
        )[0]

    q_own, fq_own = query_features(q[0], q[1])
    last, fq_own, fk = lax.optimization_barrier((last, fq_own, fk))
    fk, past, step = call(
        last_features_kernel,
        [last, wk, fk],
        [(states, 4 * half), (states, 2 * dh), (states, 2 * dh)],
        "last_features",
        limit=20,
        out_type=[BF16, F32, F32],
        aliases={2: 0},
    )
    near_own = near(0, q_own, fq_own)
    q[2], q[3], near_own = lax.optimization_barrier((q[2], q[3], near_own))
    q_other, fq_other = query_features(q[2], q[3])
    near_other = near(1, q_other, fq_other)
    first, near_other = lax.optimization_barrier((first, near_other))
    (past,) = call(
        past_kernel,
        [first, wk, past],
        [(states, 2 * dh)],
        "past",
        [pltpu.VMEM((states, 2 * half), BF16)],
        16,
        F32,
    )
    before, past = lax.optimization_barrier((before, past))
    part = tok // sides
    outs = call(
        mix_kernel_of_level,
        [near_own, near_other, fq_own, fq_other, past, step, wk, before],
        [(part, heads * dh)] * (WAYS * sides),
        "mix_level",
        [
            pltpu.VMEM((states, 2 * half), BF16),
            pltpu.VMEM((2, states, 2 * dh), BF16),
            pltpu.VMEM((2 * half, heads * dh), BF16),
        ],
        24,
    )

    def sent(x, slot):
        pairs = []
        for i in range(seq):
            dr, dy = slot[i % 2]
            to = i // WAYS * WAYS + (i % WAYS ^ dr)
            pairs += [(i * sides + j, to * sides + (j ^ dy)) for j in range(sides)]
        return lax.ppermute(x, ("seq", "head"), pairs)

    outs = list(outs)
    for n in range(1, 6):
        outs[n] = sent(outs[n], SLOTS[n])
    outs[6], outs[7], outs[3] = lax.optimization_barrier((outs[6], outs[7], outs[3]))
    outs[6], outs[7] = sent(outs[6], SLOTS[6]), sent(outs[7], SLOTS[7])

    def joined(slots, into):
        return pl.pallas_call(
            lambda *refs: join_kernel(slots, *refs),
            in_specs=[whole_spec()] * len(slots) + [whole_spec(pltpu.HBM)] * len(into),
            out_specs=whole_spec(pltpu.HBM),
            out_shape=jax.ShapeDtypeStruct((part, sides * WAYS * heads * dh), BF16),
            input_output_aliases={len(slots): 0} if into else {},
            scratch_shapes=[pltpu.SemaphoreType.DMA((len(slots),))],
            compiler_params=pltpu.CompilerParams(vmem_limit_bytes=4 * 2**20),
            name="join",
        )(*[outs[n] for n in slots], *into)

    return joined((4, 5, 6, 7), [joined((0, 1, 2, 3), [])])


def by_blocks(queries, keys, values, wq, wk, ratio):
    group = wq.shape[0] // (keys.shape[1] // DH)
    place = lax.axis_index("seq").astype(jnp.int32).reshape(1)
    kv = lax.all_gather(jnp.concatenate([keys, values], axis=1), "seq", tiled=True)
    out = mix(place, queries, kv, wq, wk, ratio, group)
    return lax.all_to_all(out, "head", split_axis=0, concat_axis=1, tiled=True)


def local(queries, keys, values, q_feature, k_feature, window_factor):
    tok = queries.shape[0]
    seq, sides = lax.axis_size("seq"), lax.axis_size("head")
    wq, wk = jnp.swapaxes(q_feature, 1, 2), jnp.swapaxes(k_feature, 1, 2)
    if keys.shape[1] == WAYS * DH and seq == 4 * WAYS and sides == 2 and tok == WINDOW:
        return by_levels(queries, keys, values, wq, wk, window_factor)
    ratio = window_factor / (1.0 - window_factor)
    return by_blocks(queries, keys, values, wq, wk, ratio)


def solution(mesh):
    return jax.shard_map(
        local,
        mesh=mesh,
        in_specs=(
            P("seq", "head"),
            P("seq", "head"),
            P("seq", "head"),
            P("head", None, None),
            P("head", None, None),
            P("head"),
        ),
        out_specs=P(("seq", "head"), None),
        check_vma=False,
    )
```

```python
import math

import jax
import jax.numpy as jnp
from jax import lax
from jax.experimental import pallas as pl
from jax.experimental.pallas import tpu as pltpu
from jax.sharding import PartitionSpec as P

DH = 128
WINDOW = 64
F32 = jnp.float32
BF16 = jnp.bfloat16


def dot_t(a, b):
    return lax.dot_general(a, b, (((1,), (1,)), ((), ())), preferred_element_type=F32)


def features_t(logits):
    top = jnp.max(logits, axis=0, keepdims=True)
    low = jnp.min(logits, axis=0, keepdims=True)
    up = jnp.exp(logits - top)
    down = jnp.exp(low - logits)
    up = up * (1.0 / jnp.sum(up, axis=0, keepdims=True))
    down = down * (1.0 / jnp.sum(down, axis=0, keepdims=True))
    return jnp.concatenate([up.astype(BF16), down.astype(BF16)], axis=0)


def mix_kernel(
    place_ref, q_ref, k_ref, v_ref, wq_ref, wk_ref, ratio_ref, out_ref, fk_scr, state_scr
):
    tok = q_ref.shape[0]
    heads, feat, dh = wq_ref.shape
    seen = fk_scr.shape[1]
    place = place_ref[0]
    first_head = pl.program_id(0) * heads

    weights = wk_ref[...].reshape(heads * feat, dh)
    for start in range(0, seen, 256):
        size = min(256, seen - start)
        logits = dot_t(weights, k_ref[start : start + size, :])
        for h in range(heads):
            fk_scr[h * 2 * feat : (h + 1) * 2 * feat, start : start + size] = features_t(
                logits[h * feat : (h + 1) * feat]
            )
    row = lax.broadcasted_iota(jnp.int32, (seen, dh), 0)
    kept = row < (place - 1) * tok
    v_seen = jnp.where(kept, v_ref[:seen, :].astype(F32), 0.0).astype(BF16)
    ones_seen = jnp.where(kept, 1.0, 0.0).astype(BF16)
    v_seen = jnp.concatenate([v_seen, ones_seen], axis=1)
    state_scr[...] = jnp.dot(fk_scr[...], v_seen, preferred_element_type=F32).astype(BF16)

    before = pl.multiple_of(jnp.maximum(place - 1, 0) * tok, tok)
    own = pl.multiple_of(place * tok, tok)
    k_ext = jnp.concatenate([k_ref[pl.ds(before, tok), :], k_ref[pl.ds(own, tok), :]], axis=0)
    v_ext = jnp.concatenate([v_ref[pl.ds(before, tok), :], v_ref[pl.ds(own, tok), :]], axis=0)
    v_ext = jnp.concatenate([v_ext, jnp.ones_like(v_ext)], axis=1)
    row = lax.broadcasted_iota(jnp.int32, (tok, 2 * tok), 0)
    col = lax.broadcasted_iota(jnp.int32, (tok, 2 * tok), 1)
    valid = (col >= tok) | (place > 0)
    inside = (col > row) & (col <= row + WINDOW) & valid
    causal = (col <= row) & valid
    lane = lax.broadcasted_iota(jnp.int32, (tok, 2 * feat), 1)
    left = lane < feat
    side_r = lax.broadcasted_iota(jnp.int32, (2 * feat, 2 * feat), 0) < feat
    side_c = lax.broadcasted_iota(jnp.int32, (2 * feat, 2 * feat), 1) < feat
    halves = jnp.where(side_r == side_c, 1.0, 0.0).astype(BF16)

    for h in range(heads):
        q = q_ref[:, h * dh : (h + 1) * dh]
        wq = wq_ref[h]
        logits = dot_t(q, jnp.concatenate([wq, -wq], axis=0))
        top_l = jnp.max(jnp.where(left, logits, -jnp.inf), axis=1, keepdims=True)
        top_r = jnp.max(jnp.where(left, -jnp.inf, logits), axis=1, keepdims=True)
        expd = jnp.exp(logits - jnp.where(left, top_l, top_r)).astype(BF16)
        total = jnp.dot(expd, halves, preferred_element_type=F32)
        fq = (expd.astype(F32) / total).astype(BF16)
        fk = features_t(dot_t(wk_ref[h], k_ext))
        linear = jnp.dot(fq, fk, preferred_element_type=F32)
        scores = dot_t(q, k_ext) * (1.0 / math.sqrt(dh))
        masked = jnp.where(inside, scores, -jnp.inf)
        top = jnp.max(masked, axis=1, keepdims=True)
        soft = jnp.exp(masked - top) * ratio_ref[first_head + h]
        weight = jnp.where(causal, linear, soft).astype(BF16)
        both = jnp.dot(weight, v_ext, preferred_element_type=F32) + jnp.dot(
            fq, state_scr[h * 2 * feat : (h + 1) * 2 * feat, :], preferred_element_type=F32
        )
        out_ref[:, h * dh : (h + 1) * dh] = (both[:, :dh] / both[:, dh:]).astype(BF16)


def mix(place, queries, kv, wq, wk, ratio, group):
    tok = queries.shape[0]
    local_heads, feat, dh = wq.shape
    groups = local_heads // group
    tokens = kv.shape[0]
    seen = tokens - 2 * tok
    return pl.pallas_call(
        mix_kernel,
        grid_spec=pltpu.PrefetchScalarGridSpec(
            num_scalar_prefetch=1,
            grid=(groups,),
            in_specs=[
                pl.BlockSpec((tok, group * dh), lambda g, p: (0, g)),
                pl.BlockSpec((tokens, dh), lambda g, p: (0, g)),
                pl.BlockSpec((tokens, dh), lambda g, p: (0, groups + g)),
                pl.BlockSpec((group, feat, dh), lambda g, p: (g, 0, 0)),
                pl.BlockSpec((group, feat, dh), lambda g, p: (g, 0, 0)),
                pl.BlockSpec(memory_space=pltpu.SMEM),
            ],
            out_specs=pl.BlockSpec((tok, group * dh), lambda g, p: (0, g)),
            scratch_shapes=[
                pltpu.VMEM((group * 2 * feat, seen), BF16),
                pltpu.VMEM((group * 2 * feat, 2 * dh), BF16),
            ],
        ),
        out_shape=jax.ShapeDtypeStruct(queries.shape, BF16),
        compiler_params=pltpu.CompilerParams(vmem_limit_bytes=48 * 2**20),
        cost_estimate=pl.CostEstimate(
            flops=2 * local_heads * tokens * 3 * feat * 2 * dh,
            bytes_accessed=8 * 2**20,
            transcendentals=local_heads * tokens * 2 * feat,
        ),
    )(place, queries, kv, kv, wq, wk, ratio)


WAYS = 4

EARLY = pl.CostEstimate(flops=10**10, bytes_accessed=10**8, transcendentals=0)
EARLY_KERNELS = ("pack_kv", "pack_q", "pair_kv", "stack_kv")


SLOTS = (
    ((0, 0), (0, 0)),
    ((2, 0), (0, 1)),
    ((0, 1), (2, 0)),
    ((1, 0), (1, 0)),
    ((2, 1), (2, 1)),
    ((3, 0), (1, 1)),
    ((3, 1), (3, 1)),
    ((1, 1), (3, 0)),
)


def slot_of(n, odd):
    return [jnp.where(odd == 1, b, a) if a != b else a for a, b in zip(*SLOTS[n])]


def spot():
    at = lax.axis_index("seq")
    return lax.rem(at, WAYS), lax.div(at, WAYS)


def aligned(at, step):
    return pl.ds(pl.multiple_of(at * step, step), step)


def with_ones(values, kept=True):
    here = jnp.where(kept, 1.0, 0.0).astype(BF16)
    return jnp.concatenate([values, jnp.full(values.shape, here)], axis=1)


def pack_kv_kernel(k_ref, v_ref, k_away_ref, v_away_ref, own_ref, away_ref):
    odd = lax.rem(spot()[0], 2)
    for k, v, ref in ((k_ref, v_ref, own_ref), (k_away_ref, v_away_ref, away_ref)):
        for d in range(2):
            at = aligned(odd ^ d, DH)
            ref[:, 2 * d * DH : (2 * d + 1) * DH] = k[:, at]
            ref[:, (2 * d + 1) * DH : (2 * d + 2) * DH] = v[:, at]


def pair_kernel(own_ref, got_ref, out_ref):
    tok = own_ref.shape[0]
    out_ref[:tok, :] = own_ref[:, 2 * DH :]
    out_ref[tok:, :] = got_ref[:, 2 * DH :]


def stack_kernel(own_ref, got_ref, pair_ref, out_ref):
    tok = own_ref.shape[0]
    place = spot()[0]
    out_ref[aligned(place, tok), :] = own_ref[:, : 2 * DH]
    out_ref[aligned(place ^ 2, tok), :] = got_ref[:, : 2 * DH]
    out_ref[aligned(place ^ 1, tok), :] = pair_ref[:tok, :]
    out_ref[aligned(place ^ 3, tok), :] = pair_ref[tok:, :]


def pack_q_kernel(q_ref, *out_refs):
    place = spot()[0]
    for d, out in enumerate(out_refs):
        out[...] = q_ref[:, aligned(place ^ d, out.shape[1])]


def weights_kernel(wq_ref, factor_ref, both_ref, ratio_ref):
    heads = both_ref.shape[0]
    shape = (heads, factor_ref.shape[1])
    head = lax.broadcasted_iota(jnp.int32, shape, 0) + spot()[0] * heads
    ratio = jnp.broadcast_to((1.0 - factor_ref[...]) / factor_ref[...], shape)
    ratio = jnp.where(lax.broadcasted_iota(jnp.int32, shape, 1) == head, ratio, 0.0)
    ratio = jnp.sum(ratio, axis=1, keepdims=True)
    ratio_ref[...] = jnp.broadcast_to(ratio, ratio_ref.shape)
    for h in range(heads):
        wq = wq_ref[h].T
        both_ref[h] = jnp.concatenate([wq, -wq], axis=1)


def join_kernel(slots, *refs):
    got, out_ref, sems = refs[: len(slots)], *refs[-2:]
    width = got[0].shape[1]
    place, side = spot()[0], lax.axis_index("head")
    copies = []
    for n, ref in zip(slots, got):
        dr, dy = slot_of(n, lax.rem(place, 2) ^ (SLOTS[n][0][0] & 1))
        at = aligned((side ^ dy) * WAYS + (place ^ dr), width)
        copies.append(pltpu.make_async_copy(ref, out_ref.at[:, at], sems.at[len(copies)]))
    for copy in copies:
        copy.start()
    for copy in copies:
        copy.wait()


def write_key_features(keys, wk_ref, fk_ref):
    heads, feat, dh = wk_ref.shape
    logits = dot_t(wk_ref[...].reshape(heads * feat, dh), keys)
    for h in range(heads):
        part = logits[h * feat : (h + 1) * feat]
        top = jnp.max(part, axis=0, keepdims=True)
        low = jnp.min(part, axis=0, keepdims=True)
        for n, shifted in enumerate((part - top, low - part)):
            row = (2 * h + n) * feat
            expd = jnp.exp(shifted.astype(BF16))
            total = expd[: feat // 4]
            for q in range(1, 4):
                total = total + expd[q * feat // 4 : (q + 1) * feat // 4]
            total = jnp.sum(total.astype(F32), axis=0, keepdims=True)
            fk_ref[row : row + feat, :] = expd * pl.reciprocal(total).astype(BF16)


def own_features_kernel(own_ref, wk_ref, fk_ref):
    write_key_features(own_ref[:, :DH], wk_ref, fk_ref.at[:, own_ref.shape[0] :])


def last_features_kernel(last_ref, wk_ref, _, fk_ref, past_ref, step_ref):
    size = last_ref.shape[0]
    half = size // 2
    level = spot()[1]

    @pl.when(level == 0)
    def _():
        fk_ref[:, :size] = jnp.zeros((fk_ref.shape[0], size), BF16)
        for ref in (past_ref, step_ref):
            ref[...] = jnp.zeros_like(ref)

    @pl.when(level > 0)
    def _():
        write_key_features(last_ref[:, :DH], wk_ref, fk_ref.at[:, :size])
        for at, ref in ((0, past_ref), (half, step_ref)):
            ref[...] = jnp.dot(
                fk_ref[:, at : at + half],
                with_ones(last_ref[at : at + half, DH:]),
                preferred_element_type=F32,
            )


def past_kernel(first_ref, wk_ref, sum_ref, past_ref, fk_scr):
    level = spot()[1]

    @pl.when(level < 3)
    def _():
        past_ref[...] = sum_ref[...]

    @pl.when(level >= 3)
    def _():
        write_key_features(first_ref[:, :DH], wk_ref, fk_scr)
        past_ref[...] = sum_ref[...] + jnp.dot(
            fk_scr[...], with_ones(first_ref[:, DH:]), preferred_element_type=F32
        )


def query_features_kernel(a_ref, b_ref, w_ref, ratio_ref, q_out, fq_out, exp_scr):
    tok = a_ref.shape[0]
    heads, dh, both = w_ref.shape
    half = 2 * tok
    place = spot()[0]
    for d, ref in enumerate((a_ref, b_ref)):
        row = pl.multiple_of(lax.rem(place ^ d, 2) * tok, tok)
        for h in range(heads):
            q_out[pl.ds(h * half + row, tok), :] = ref[:, h * dh : (h + 1) * dh]
    rows_of = [slice(h * half, (h + 1) * half) for h in range(heads)]
    left = lax.broadcasted_iota(jnp.int32, (half, both), 1) < both // 2
    for h, rows in enumerate(rows_of):
        logits = jnp.dot(q_out[rows, :], w_ref[h], preferred_element_type=F32)
        top_l = jnp.max(jnp.where(left, logits, -jnp.inf), axis=1, keepdims=True)
        top_r = jnp.max(jnp.where(left, -jnp.inf, logits), axis=1, keepdims=True)
        exp_scr[rows, :] = jnp.exp((logits - jnp.where(left, top_l, top_r)).astype(BF16))
    side_r = lax.broadcasted_iota(jnp.int32, (both, both), 0) < both // 2
    side_c = lax.broadcasted_iota(jnp.int32, (both, both), 1) < both // 2
    halves = jnp.where(side_r == side_c, 1.0, 0.0).astype(BF16)
    total = jnp.dot(exp_scr[...], halves, preferred_element_type=F32)
    for h, rows in enumerate(rows_of):
        scale = pl.reciprocal(total[rows], approx=True) * ratio_ref[h : h + 1, :]
        fq_out[rows, :] = (exp_scr[rows, :].astype(F32) * scale).astype(BF16)


def near_kernel(other, q_ref, fq_ref, last_ref, own_ref, fk_ref, near_ref, kv_scr, w_scr):
    half, dh = last_ref.shape[0] // 2, q_ref.shape[1]
    heads = q_ref.shape[0] // half
    feats = fq_ref.shape[1]
    place, level = spot()
    u = lax.div(place, 2) ^ other
    kv_scr[:half, :] = last_ref[half:, :]
    kv_scr[half:, :] = own_ref[...]
    at = pl.ds(pl.multiple_of(u * half, half), 2 * half)
    keys, values = kv_scr[at, :dh], kv_scr[at, dh:]
    fk_at = pl.ds(pl.multiple_of((u + 1) * half, half), 2 * half)
    known = (level > 0) | (u > 0)
    cut = half - WINDOW
    row = lax.broadcasted_iota(jnp.int32, (WINDOW, 2 * half), 0)
    col = lax.broadcasted_iota(jnp.int32, (WINDOW, 2 * half), 1)
    inside = (col > row + cut) & (col <= row + half) & ((col >= half) | known)
    causal = (col <= row + cut)[:, :half]
    row, col = row[:, :half], col[:, :half]
    inside_low = (col > row) & (col <= row + WINDOW)
    causal_low = col <= row
    scores = dot_t(q_ref[...], keys)
    scale = math.log2(math.e) / math.sqrt(dh)

    def window(part, kept):
        masked = jnp.where(kept, part, -jnp.inf)
        top = jnp.max(masked, axis=1, keepdims=True)
        return jnp.exp2(((masked - top) * scale).astype(BF16))

    for h in range(heads):
        here = slice(h * half, (h + 1) * half)
        up, low = slice(h * half, h * half + cut), slice(h * half + cut, (h + 1) * half)
        linear = jnp.dot(
            fq_ref[here, :],
            fk_ref[h * feats : (h + 1) * feats, fk_at],
            preferred_element_type=F32,
        )
        soft = window(scores[up], inside)
        w_scr[up, :half] = soft[:, :half] + jnp.where(causal, linear[:cut, :half], 0.0).astype(BF16)
        w_scr[up, half:] = soft[:, half:]
        soft = window(scores[low, half:], inside_low)
        w_scr[low, :half] = linear[cut:, :half].astype(BF16)
        w_scr[low, half:] = soft + jnp.where(causal_low, linear[cut:, half:], 0.0).astype(BF16)
    values = jnp.concatenate(
        [with_ones(values[:half], known), with_ones(values[half:])], axis=0
    )
    near_ref[...] = jnp.dot(w_scr[...], values, preferred_element_type=F32)


def mix_kernel_of_level(*refs):
    near_refs, fq_refs, (past_ref, step_ref, wk_ref) = refs[:2], refs[2:4], refs[4:7]
    before_ref, second_ref, refs = refs[7], refs[8], refs[9:]
    out_refs, (kv_scr, fk_scr, state_scr, out_scr) = refs[:-4], refs[-4:]
    rows, dh = near_refs[0].shape[0], near_refs[0].shape[1] // 2
    feats = fq_refs[0].shape[1]
    heads = past_ref.shape[0] // feats
    half = rows // heads
    place, level = spot()
    side = lax.axis_index("head")
    u = lax.div(place, 2)

    @pl.when(level < 2)
    def _():
        state_scr[0] = past_ref[...].astype(BF16)
        state_scr[1] = (past_ref[...] + step_ref[...]).astype(BF16)

    @pl.when(level == 2)
    def _():
        kv_scr[...] = before_ref[...]

    @pl.when(level == 3)
    def _():
        kv_scr[...] = second_ref[...]

    @pl.when(level >= 2)
    def _():
        write_key_features(kv_scr[:, :dh], wk_ref, fk_scr)
        state = past_ref[...] + jnp.dot(
            fk_scr[...], with_ones(kv_scr[:, dh:]), preferred_element_type=F32
        )
        state_scr[0] = state.astype(BF16)
        state_scr[1] = (state + step_ref[...]).astype(BF16)

    part = out_refs[0].shape[0]
    for other in (1, 0):
        for h in range(heads):
            here = slice(h * half, (h + 1) * half)
            far = jnp.dot(
                fq_refs[other][here, :],
                state_scr[u ^ other, h * feats : (h + 1) * feats, :],
                preferred_element_type=F32,
            )
            both = near_refs[other][here, :] + far
            out_scr[aligned(u ^ other, half), h * dh : (h + 1) * dh] = (
                both[:, :dh] * pl.reciprocal(both[:, dh:], approx=True)
            ).astype(BF16)
    for n, ref in enumerate(out_refs):
        dr, dy = slot_of(n, lax.rem(place, 2))
        ref[...] = out_scr[aligned((place ^ dr) * 2 + (side ^ dy), part), :]


def whole_spec(space=pltpu.VMEM):
    return pl.BlockSpec(memory_space=space)


def call(kernel, ins, outs, name, scratch=(), limit=4, out_type=BF16, aliases={}):
    return pl.pallas_call(
        kernel,
        in_specs=[whole_spec() for _ in ins],
        out_specs=[whole_spec() for _ in outs],
        out_shape=[
            jax.ShapeDtypeStruct(s, out_type[n] if isinstance(out_type, list) else out_type)
            for n, s in enumerate(outs)
        ],
        scratch_shapes=list(scratch),
        input_output_aliases=aliases,
        cost_estimate=EARLY if name in EARLY_KERNELS else None,
        compiler_params=pltpu.CompilerParams(vmem_limit_bytes=limit * 2**20),
        name=name,
    )(*ins)


def by_levels(queries, keys, values, wq, wk, factor):
    tok, width = queries.shape
    local_heads, feat, dh = wq.shape
    heads = local_heads // WAYS
    seq, sides = lax.axis_size("seq"), lax.axis_size("head")
    half = 2 * tok
    rows, states = heads * half, heads * 2 * feat

    def partner(x, dr, dy=0):
        pairs = [
            (i * sides + j, (i // WAYS * WAYS + (i % WAYS ^ dr)) * sides + (j ^ dy))
            for i in range(seq)
            for j in range(sides)
        ]
        return lax.ppermute(x, ("seq", "head"), pairs)

    def levels_on(x, by, senders):
        pairs = [(i, i + by * WAYS) for i in range(seq) if i // WAYS in senders]
        return lax.ppermute(x, "seq", pairs)

    place = lax.rem(lax.axis_index("seq"), WAYS)
    ours = place // 2 * 2 * dh
    cuts = [
        lax.dynamic_slice_in_dim(x, at, 2 * dh, 1)
        for at in (ours, 2 * dh - ours)
        for x in (keys, values)
    ]
    own, away = call(pack_kv_kernel, cuts, [(tok, 4 * dh)] * 2, "pack_kv")
    got = partner(away, 2)
    queries, away = lax.optimization_barrier((queries, away))
    q = list(call(pack_q_kernel, [queries], [(tok, width // WAYS)] * WAYS, "pack_q"))
    q[2], q[3] = partner(q[2], 2), partner(q[3], 3)
    (pair,) = call(pair_kernel, [own, got], [(half, 2 * dh)], "pair_kv")
    pair, q[1], wq, wk = lax.optimization_barrier((pair, q[1], wq, wk))
    pair, q[1] = partner(pair, 1), partner(q[1], 1)
    wq, wk = [lax.dynamic_slice_in_dim(w, place * heads, heads) for w in (wq, wk)]
    pair, wq, wk = lax.optimization_barrier((pair, wq, wk))
    (kv,) = call(stack_kernel, [own, got, pair], [(2 * half, 2 * dh)], "stack_kv")
    last, second = levels_on(kv, 1, (0, 1, 2)), levels_on(kv, 2, (1,))
    wq, kv, q[1] = lax.optimization_barrier((wq, kv, q[1]))
    first = levels_on(kv, 3, (0,))
    (fk,) = call(own_features_kernel, [kv, wk], [(states, 4 * half)], "own_features", limit=16)
    wq, ratio = call(
        weights_kernel,
        [wq, factor.reshape(1, local_heads)],
        [(heads, dh, 2 * feat), (heads, 2 * feat)],
        "weights",
        out_type=[BF16, F32],
    )

    def query_features(a, b):
        return call(
            query_features_kernel,
            [a, b, wq, ratio],
            [(rows, dh), (rows, 2 * feat)],
            "query_features",
            [pltpu.VMEM((rows, 2 * feat), BF16)],
            12,
        )

    def near(other, q_rows, fq):
        return call(
            lambda *refs: near_kernel(other, *refs),
            [q_rows, fq, last, kv, fk],
            [(rows, 2 * dh)],
            "near",
            [
                pltpu.VMEM((3 * half, 2 * dh), BF16),
                pltpu.VMEM((rows, 2 * half), BF16),
            ],
            16,
            F32,
        )[0]

    q_own, fq_own = query_features(q[0], q[1])
    far_kv, fk, fq_own = lax.optimization_barrier((kv, fk, fq_own))
    before = levels_on(far_kv, 2, (0,))
    last, fq_own, fk = lax.optimization_barrier((last, fq_own, fk))
    fk, past, step = call(
        last_features_kernel,
        [last, wk, fk],
        [(states, 4 * half), (states, 2 * dh), (states, 2 * dh)],
        "last_features",
        limit=20,
        out_type=[BF16, F32, F32],
        aliases={2: 0},
    )
    near_own = near(0, q_own, fq_own)
    q[2], q[3], near_own = lax.optimization_barrier((q[2], q[3], near_own))
    q_other, fq_other = query_features(q[2], q[3])
    near_other = near(1, q_other, fq_other)
    first, near_other = lax.optimization_barrier((first, near_other))
    (past,) = call(
        past_kernel,
        [first, wk, past],
        [(states, 2 * dh)],
        "past",
        [pltpu.VMEM((states, 2 * half), BF16)],
        16,
        F32,
    )
    before, second, past = lax.optimization_barrier((before, second, past))
    part = tok // sides
    outs = call(
        mix_kernel_of_level,
        [near_own, near_other, fq_own, fq_other, past, step, wk, before, second],
        [(part, heads * dh)] * (WAYS * sides),
        "mix_level",
        [
            pltpu.VMEM((2 * half, 2 * dh), BF16),
            pltpu.VMEM((states, 2 * half), BF16),
            pltpu.VMEM((2, states, 2 * dh), BF16),
            pltpu.VMEM((2 * half, heads * dh), BF16),
        ],
        24,
    )

    def sent(x, slot):
        pairs = []
        for i in range(seq):
            dr, dy = slot[i % 2]
            to = i // WAYS * WAYS + (i % WAYS ^ dr)
            pairs += [(i * sides + j, to * sides + (j ^ dy)) for j in range(sides)]
        return lax.ppermute(x, ("seq", "head"), pairs)

    outs = list(outs)
    for n in range(1, 6):
        outs[n] = sent(outs[n], SLOTS[n])
    outs[6], outs[7], outs[3] = lax.optimization_barrier((outs[6], outs[7], outs[3]))
    outs[6], outs[7] = sent(outs[6], SLOTS[6]), sent(outs[7], SLOTS[7])

    def joined(slots, into):
        return pl.pallas_call(
            lambda *refs: join_kernel(slots, *refs),
            in_specs=[whole_spec()] * len(slots) + [whole_spec(pltpu.HBM)] * len(into),
            out_specs=whole_spec(pltpu.HBM),
            out_shape=jax.ShapeDtypeStruct((part, sides * WAYS * heads * dh), BF16),
            input_output_aliases={len(slots): 0} if into else {},
            scratch_shapes=[pltpu.SemaphoreType.DMA((len(slots),))],
            compiler_params=pltpu.CompilerParams(vmem_limit_bytes=4 * 2**20),
            name="join",
        )(*[outs[n] for n in slots], *into)

    return joined((4, 5, 6, 7), [joined((0, 1, 2, 3), [])])


def by_blocks(queries, keys, values, wq, wk, ratio):
    group = wq.shape[0] // (keys.shape[1] // DH)
    place = lax.axis_index("seq").astype(jnp.int32).reshape(1)
    kv = lax.all_gather(jnp.concatenate([keys, values], axis=1), "seq", tiled=True)
    out = mix(place, queries, kv, wq, wk, ratio, group)
    return lax.all_to_all(out, "head", split_axis=0, concat_axis=1, tiled=True)


def local(queries, keys, values, q_feature, k_feature, window_factor):
    tok = queries.shape[0]
    seq, sides = lax.axis_size("seq"), lax.axis_size("head")
    wq, wk = jnp.swapaxes(q_feature, 1, 2), jnp.swapaxes(k_feature, 1, 2)
    if keys.shape[1] == WAYS * DH and seq == 4 * WAYS and sides == 2 and tok == WINDOW:
        return by_levels(queries, keys, values, wq, wk, window_factor)
    ratio = window_factor / (1.0 - window_factor)
    return by_blocks(queries, keys, values, wq, wk, ratio)


def solution(mesh):
    return jax.shard_map(
        local,
        mesh=mesh,
        in_specs=(
            P("seq", "head"),
            P("seq", "head"),
            P("seq", "head"),
            P("head", None, None),
            P("head", None, None),
            P("head"),
        ),
        out_specs=P(("seq", "head"), None),
        check_vma=False,
    )
```

```python
import math

import jax
import jax.numpy as jnp
from jax import lax
from jax.experimental import pallas as pl
from jax.experimental.pallas import tpu as pltpu
from jax.sharding import PartitionSpec as P

DH = 128
WINDOW = 64
F32 = jnp.float32
BF16 = jnp.bfloat16


def dot_t(a, b):
    return lax.dot_general(a, b, (((1,), (1,)), ((), ())), preferred_element_type=F32)


def features_t(logits):
    top = jnp.max(logits, axis=0, keepdims=True)
    low = jnp.min(logits, axis=0, keepdims=True)
    up = jnp.exp(logits - top)
    down = jnp.exp(low - logits)
    up = up * (1.0 / jnp.sum(up, axis=0, keepdims=True))
    down = down * (1.0 / jnp.sum(down, axis=0, keepdims=True))
    return jnp.concatenate([up.astype(BF16), down.astype(BF16)], axis=0)


def mix_kernel(
    place_ref, q_ref, k_ref, v_ref, wq_ref, wk_ref, ratio_ref, out_ref, fk_scr, state_scr
):
    tok = q_ref.shape[0]
    heads, feat, dh = wq_ref.shape
    seen = fk_scr.shape[1]
    place = place_ref[0]
    first_head = pl.program_id(0) * heads

    weights = wk_ref[...].reshape(heads * feat, dh)
    for start in range(0, seen, 256):
        size = min(256, seen - start)
        logits = dot_t(weights, k_ref[start : start + size, :])
        for h in range(heads):
            fk_scr[h * 2 * feat : (h + 1) * 2 * feat, start : start + size] = features_t(
                logits[h * feat : (h + 1) * feat]
            )
    row = lax.broadcasted_iota(jnp.int32, (seen, dh), 0)
    kept = row < (place - 1) * tok
    v_seen = jnp.where(kept, v_ref[:seen, :].astype(F32), 0.0).astype(BF16)
    ones_seen = jnp.where(kept, 1.0, 0.0).astype(BF16)
    v_seen = jnp.concatenate([v_seen, ones_seen], axis=1)
    state_scr[...] = jnp.dot(fk_scr[...], v_seen, preferred_element_type=F32).astype(BF16)

    before = pl.multiple_of(jnp.maximum(place - 1, 0) * tok, tok)
    own = pl.multiple_of(place * tok, tok)
    k_ext = jnp.concatenate([k_ref[pl.ds(before, tok), :], k_ref[pl.ds(own, tok), :]], axis=0)
    v_ext = jnp.concatenate([v_ref[pl.ds(before, tok), :], v_ref[pl.ds(own, tok), :]], axis=0)
    v_ext = jnp.concatenate([v_ext, jnp.ones_like(v_ext)], axis=1)
    row = lax.broadcasted_iota(jnp.int32, (tok, 2 * tok), 0)
    col = lax.broadcasted_iota(jnp.int32, (tok, 2 * tok), 1)
    valid = (col >= tok) | (place > 0)
    inside = (col > row) & (col <= row + WINDOW) & valid
    causal = (col <= row) & valid
    lane = lax.broadcasted_iota(jnp.int32, (tok, 2 * feat), 1)
    left = lane < feat
    side_r = lax.broadcasted_iota(jnp.int32, (2 * feat, 2 * feat), 0) < feat
    side_c = lax.broadcasted_iota(jnp.int32, (2 * feat, 2 * feat), 1) < feat
    halves = jnp.where(side_r == side_c, 1.0, 0.0).astype(BF16)

    for h in range(heads):
        q = q_ref[:, h * dh : (h + 1) * dh]
        wq = wq_ref[h]
        logits = dot_t(q, jnp.concatenate([wq, -wq], axis=0))
        top_l = jnp.max(jnp.where(left, logits, -jnp.inf), axis=1, keepdims=True)
        top_r = jnp.max(jnp.where(left, -jnp.inf, logits), axis=1, keepdims=True)
        expd = jnp.exp(logits - jnp.where(left, top_l, top_r)).astype(BF16)
        total = jnp.dot(expd, halves, preferred_element_type=F32)
        fq = (expd.astype(F32) / total).astype(BF16)
        fk = features_t(dot_t(wk_ref[h], k_ext))
        linear = jnp.dot(fq, fk, preferred_element_type=F32)
        scores = dot_t(q, k_ext) * (1.0 / math.sqrt(dh))
        masked = jnp.where(inside, scores, -jnp.inf)
        top = jnp.max(masked, axis=1, keepdims=True)
        soft = jnp.exp(masked - top) * ratio_ref[first_head + h]
        weight = jnp.where(causal, linear, soft).astype(BF16)
        both = jnp.dot(weight, v_ext, preferred_element_type=F32) + jnp.dot(
            fq, state_scr[h * 2 * feat : (h + 1) * 2 * feat, :], preferred_element_type=F32
        )
        out_ref[:, h * dh : (h + 1) * dh] = (both[:, :dh] / both[:, dh:]).astype(BF16)


def mix(place, queries, kv, wq, wk, ratio, group):
    tok = queries.shape[0]
    local_heads, feat, dh = wq.shape
    groups = local_heads // group
    tokens = kv.shape[0]
    seen = tokens - 2 * tok
    return pl.pallas_call(
        mix_kernel,
        grid_spec=pltpu.PrefetchScalarGridSpec(
            num_scalar_prefetch=1,
            grid=(groups,),
            in_specs=[
                pl.BlockSpec((tok, group * dh), lambda g, p: (0, g)),
                pl.BlockSpec((tokens, dh), lambda g, p: (0, g)),
                pl.BlockSpec((tokens, dh), lambda g, p: (0, groups + g)),
                pl.BlockSpec((group, feat, dh), lambda g, p: (g, 0, 0)),
                pl.BlockSpec((group, feat, dh), lambda g, p: (g, 0, 0)),
                pl.BlockSpec(memory_space=pltpu.SMEM),
            ],
            out_specs=pl.BlockSpec((tok, group * dh), lambda g, p: (0, g)),
            scratch_shapes=[
                pltpu.VMEM((group * 2 * feat, seen), BF16),
                pltpu.VMEM((group * 2 * feat, 2 * dh), BF16),
            ],
        ),
        out_shape=jax.ShapeDtypeStruct(queries.shape, BF16),
        compiler_params=pltpu.CompilerParams(vmem_limit_bytes=48 * 2**20),
        cost_estimate=pl.CostEstimate(
            flops=2 * local_heads * tokens * 3 * feat * 2 * dh,
            bytes_accessed=8 * 2**20,
            transcendentals=local_heads * tokens * 2 * feat,
        ),
    )(place, queries, kv, kv, wq, wk, ratio)


WAYS = 4

EARLY = pl.CostEstimate(flops=10**10, bytes_accessed=10**8, transcendentals=0)
EARLY_KERNELS = ("pack_kv", "pack_q", "pair_kv", "stack_kv")


SLOTS = (
    ((0, 0), (0, 0)),
    ((2, 0), (0, 1)),
    ((0, 1), (2, 0)),
    ((1, 0), (1, 0)),
    ((2, 1), (2, 1)),
    ((3, 0), (1, 1)),
    ((3, 1), (3, 1)),
    ((1, 1), (3, 0)),
)


def slot_of(n, odd):
    return [jnp.where(odd == 1, b, a) if a != b else a for a, b in zip(*SLOTS[n])]


def spot():
    at = lax.axis_index("seq")
    return lax.rem(at, WAYS), lax.div(at, WAYS)


def aligned(at, step):
    return pl.ds(pl.multiple_of(at * step, step), step)


def with_ones(values, kept=True):
    here = jnp.where(kept, 1.0, 0.0).astype(BF16)
    return jnp.concatenate([values, jnp.full(values.shape, here)], axis=1)


def pack_kv_kernel(k_ref, v_ref, k_away_ref, v_away_ref, own_ref, away_ref):
    odd = lax.rem(spot()[0], 2)
    for k, v, ref in ((k_ref, v_ref, own_ref), (k_away_ref, v_away_ref, away_ref)):
        for d in range(2):
            at = aligned(odd ^ d, DH)
            ref[:, 2 * d * DH : (2 * d + 1) * DH] = k[:, at]
            ref[:, (2 * d + 1) * DH : (2 * d + 2) * DH] = v[:, at]


def pair_kernel(own_ref, got_ref, out_ref):
    tok = own_ref.shape[0]
    out_ref[:tok, :] = own_ref[:, 2 * DH :]
    out_ref[tok:, :] = got_ref[:, 2 * DH :]


def stack_kernel(own_ref, got_ref, pair_ref, out_ref):
    tok = own_ref.shape[0]
    place = spot()[0]
    out_ref[aligned(place, tok), :] = own_ref[:, : 2 * DH]
    out_ref[aligned(place ^ 2, tok), :] = got_ref[:, : 2 * DH]
    out_ref[aligned(place ^ 1, tok), :] = pair_ref[:tok, :]
    out_ref[aligned(place ^ 3, tok), :] = pair_ref[tok:, :]


def pack_q_kernel(q_ref, *out_refs):
    place = spot()[0]
    for d, out in enumerate(out_refs):
        out[...] = q_ref[:, aligned(place ^ d, out.shape[1])]


def join_kernel(slots, *refs):
    got, out_ref, sems = refs[: len(slots)], *refs[-2:]
    width = got[0].shape[1]
    place, side = spot()[0], lax.axis_index("head")
    copies = []
    for n, ref in zip(slots, got):
        dr, dy = slot_of(n, lax.rem(place, 2) ^ (SLOTS[n][0][0] & 1))
        at = aligned((side ^ dy) * WAYS + (place ^ dr), width)
        copies.append(pltpu.make_async_copy(ref, out_ref.at[:, at], sems.at[len(copies)]))
    for copy in copies:
        copy.start()
    for copy in copies:
        copy.wait()


def write_key_features(keys, wk_ref, fk_ref):
    heads, feat, dh = wk_ref.shape
    logits = dot_t(wk_ref[...].reshape(heads * feat, dh), keys)
    for h in range(heads):
        part = logits[h * feat : (h + 1) * feat]
        top = jnp.max(part, axis=0, keepdims=True)
        low = jnp.min(part, axis=0, keepdims=True)
        for n, shifted in enumerate((part - top, low - part)):
            row = (2 * h + n) * feat
            expd = jnp.exp(shifted.astype(BF16))
            total = expd[: feat // 4]
            for q in range(1, 4):
                total = total + expd[q * feat // 4 : (q + 1) * feat // 4]
            total = jnp.sum(total.astype(F32), axis=0, keepdims=True)
            fk_ref[row : row + feat, :] = expd * pl.reciprocal(total).astype(BF16)


def prepare_kernel(here, kv_ref, wk_ref, wq_ref, factor_ref, *refs):
    fk_ref, both_ref, ratio_ref = refs[-3:]
    place, level = spot()

    @pl.when(here(level))
    def _():
        write_key_features(kv_ref[:, :DH], wk_ref, fk_ref.at[:, kv_ref.shape[0] :])
        heads = both_ref.shape[0]
        shape = (heads, factor_ref.shape[1])
        head = lax.broadcasted_iota(jnp.int32, shape, 0) + place * heads
        ratio = jnp.broadcast_to((1.0 - factor_ref[...]) / factor_ref[...], shape)
        ratio = jnp.where(lax.broadcasted_iota(jnp.int32, shape, 1) == head, ratio, 0.0)
        ratio = jnp.sum(ratio, axis=1, keepdims=True)
        ratio_ref[...] = jnp.broadcast_to(ratio, ratio_ref.shape)
        for h in range(heads):
            wq = wq_ref[h].T
            both_ref[h] = jnp.concatenate([wq, -wq], axis=1)


def last_features_kernel(last_ref, wk_ref, _, fk_ref, past_ref, step_ref):
    size = last_ref.shape[0]
    half = size // 2
    level = spot()[1]

    @pl.when(level == 0)
    def _():
        fk_ref[:, :size] = jnp.zeros((fk_ref.shape[0], size), BF16)
        for ref in (past_ref, step_ref):
            ref[...] = jnp.zeros_like(ref)

    @pl.when(level > 0)
    def _():
        write_key_features(last_ref[:, :DH], wk_ref, fk_ref.at[:, :size])
        for at, ref in ((0, past_ref), (half, step_ref)):
            ref[...] = jnp.dot(
                fk_ref[:, at : at + half],
                with_ones(last_ref[at : at + half, DH:]),
                preferred_element_type=F32,
            )


def past_kernel(first_ref, wk_ref, sum_ref, past_ref, fk_scr):
    level = spot()[1]

    @pl.when(level < 3)
    def _():
        past_ref[...] = sum_ref[...]

    @pl.when(level >= 3)
    def _():
        write_key_features(first_ref[:, :DH], wk_ref, fk_scr)
        past_ref[...] = sum_ref[...] + jnp.dot(
            fk_scr[...], with_ones(first_ref[:, DH:]), preferred_element_type=F32
        )


def query_features_kernel(a_ref, b_ref, w_ref, ratio_ref, q_out, fq_out, exp_scr):
    tok = a_ref.shape[0]
    heads, dh, both = w_ref.shape
    half = 2 * tok
    place = spot()[0]
    for d, ref in enumerate((a_ref, b_ref)):
        row = pl.multiple_of(lax.rem(place ^ d, 2) * tok, tok)
        for h in range(heads):
            q_out[pl.ds(h * half + row, tok), :] = ref[:, h * dh : (h + 1) * dh]
    rows_of = [slice(h * half, (h + 1) * half) for h in range(heads)]
    left = lax.broadcasted_iota(jnp.int32, (half, both), 1) < both // 2
    for h, rows in enumerate(rows_of):
        logits = jnp.dot(q_out[rows, :], w_ref[h], preferred_element_type=F32)
        top_l = jnp.max(jnp.where(left, logits, -jnp.inf), axis=1, keepdims=True)
        top_r = jnp.max(jnp.where(left, -jnp.inf, logits), axis=1, keepdims=True)
        exp_scr[rows, :] = jnp.exp((logits - jnp.where(left, top_l, top_r)).astype(BF16))
    side_r = lax.broadcasted_iota(jnp.int32, (both, both), 0) < both // 2
    side_c = lax.broadcasted_iota(jnp.int32, (both, both), 1) < both // 2
    halves = jnp.where(side_r == side_c, 1.0, 0.0).astype(BF16)
    total = jnp.dot(exp_scr[...], halves, preferred_element_type=F32)
    for h, rows in enumerate(rows_of):
        scale = pl.reciprocal(total[rows], approx=True) * ratio_ref[h : h + 1, :]
        fq_out[rows, :] = (exp_scr[rows, :].astype(F32) * scale).astype(BF16)


def near_kernel(other, q_ref, fq_ref, last_ref, own_ref, fk_ref, near_ref, kv_scr, w_scr):
    half, dh = last_ref.shape[0] // 2, q_ref.shape[1]
    heads = q_ref.shape[0] // half
    feats = fq_ref.shape[1]
    place, level = spot()
    u = lax.div(place, 2) ^ other
    kv_scr[:half, :] = last_ref[half:, :]
    kv_scr[half:, :] = own_ref[...]
    at = pl.ds(pl.multiple_of(u * half, half), 2 * half)
    keys, values = kv_scr[at, :dh], kv_scr[at, dh:]
    fk_at = pl.ds(pl.multiple_of((u + 1) * half, half), 2 * half)
    known = (level > 0) | (u > 0)
    cut = half - WINDOW
    row = lax.broadcasted_iota(jnp.int32, (WINDOW, 2 * half), 0)
    col = lax.broadcasted_iota(jnp.int32, (WINDOW, 2 * half), 1)
    inside = (col > row + cut) & (col <= row + half) & ((col >= half) | known)
    causal = (col <= row + cut)[:, :half]
    row, col = row[:, :half], col[:, :half]
    inside_low = (col > row) & (col <= row + WINDOW)
    causal_low = col <= row
    scores = dot_t(q_ref[...], keys)
    scale = math.log2(math.e) / math.sqrt(dh)

    def window(part, kept):
        masked = jnp.where(kept, part, -jnp.inf)
        top = jnp.max(masked, axis=1, keepdims=True)
        return jnp.exp2(((masked - top) * scale).astype(BF16))

    for h in range(heads):
        here = slice(h * half, (h + 1) * half)
        up, low = slice(h * half, h * half + cut), slice(h * half + cut, (h + 1) * half)
        linear = jnp.dot(
            fq_ref[here, :],
            fk_ref[h * feats : (h + 1) * feats, fk_at],
            preferred_element_type=F32,
        )
        soft = window(scores[up], inside)
        w_scr[up, :half] = soft[:, :half] + jnp.where(causal, linear[:cut, :half], 0.0).astype(BF16)
        w_scr[up, half:] = soft[:, half:]
        soft = window(scores[low, half:], inside_low)
        w_scr[low, :half] = linear[cut:, :half].astype(BF16)
        w_scr[low, half:] = soft + jnp.where(causal_low, linear[cut:, half:], 0.0).astype(BF16)
    values = jnp.concatenate(
        [with_ones(values[:half], known), with_ones(values[half:])], axis=0
    )
    near_ref[...] = jnp.dot(w_scr[...], values, preferred_element_type=F32)


def mix_kernel_of_level(*refs):
    near_refs, fq_refs, (past_ref, step_ref, wk_ref) = refs[:2], refs[2:4], refs[4:7]
    before_ref, second_ref, refs = refs[7], refs[8], refs[9:]
    out_refs, (kv_scr, fk_scr, state_scr, out_scr) = refs[:-4], refs[-4:]
    rows, dh = near_refs[0].shape[0], near_refs[0].shape[1] // 2
    feats = fq_refs[0].shape[1]
    heads = past_ref.shape[0] // feats
    half = rows // heads
    place, level = spot()
    side = lax.axis_index("head")
    u = lax.div(place, 2)

    @pl.when(level < 2)
    def _():
        state_scr[0] = past_ref[...].astype(BF16)
        state_scr[1] = (past_ref[...] + step_ref[...]).astype(BF16)

    @pl.when(level == 2)
    def _():
        kv_scr[...] = before_ref[...]

    @pl.when(level == 3)
    def _():
        kv_scr[...] = second_ref[...]

    @pl.when(level >= 2)
    def _():
        write_key_features(kv_scr[:, :dh], wk_ref, fk_scr)
        state = past_ref[...] + jnp.dot(
            fk_scr[...], with_ones(kv_scr[:, dh:]), preferred_element_type=F32
        )
        state_scr[0] = state.astype(BF16)
        state_scr[1] = (state + step_ref[...]).astype(BF16)

    part = out_refs[0].shape[0]
    for other in (1, 0):
        for h in range(heads):
            here = slice(h * half, (h + 1) * half)
            far = jnp.dot(
                fq_refs[other][here, :],
                state_scr[u ^ other, h * feats : (h + 1) * feats, :],
                preferred_element_type=F32,
            )
            both = near_refs[other][here, :] + far
            out_scr[aligned(u ^ other, half), h * dh : (h + 1) * dh] = (
                both[:, :dh] * pl.reciprocal(both[:, dh:], approx=True)
            ).astype(BF16)
    for n, ref in enumerate(out_refs):
        dr, dy = slot_of(n, lax.rem(place, 2))
        ref[...] = out_scr[aligned((place ^ dr) * 2 + (side ^ dy), part), :]


def whole_spec(space=pltpu.VMEM):
    return pl.BlockSpec(memory_space=space)


def call(kernel, ins, outs, name, scratch=(), limit=4, out_type=BF16, aliases={}):
    return pl.pallas_call(
        kernel,
        in_specs=[whole_spec() for _ in ins],
        out_specs=[whole_spec() for _ in outs],
        out_shape=[
            jax.ShapeDtypeStruct(s, out_type[n] if isinstance(out_type, list) else out_type)
            for n, s in enumerate(outs)
        ],
        scratch_shapes=list(scratch),
        input_output_aliases=aliases,
        cost_estimate=EARLY if name in EARLY_KERNELS else None,
        compiler_params=pltpu.CompilerParams(vmem_limit_bytes=limit * 2**20),
        name=name,
    )(*ins)


def by_levels(queries, keys, values, wq, wk, factor):
    tok, width = queries.shape
    local_heads, feat, dh = wq.shape
    heads = local_heads // WAYS
    seq, sides = lax.axis_size("seq"), lax.axis_size("head")
    half = 2 * tok
    rows, states = heads * half, heads * 2 * feat

    def partner(x, dr, dy=0):
        pairs = [
            (i * sides + j, (i // WAYS * WAYS + (i % WAYS ^ dr)) * sides + (j ^ dy))
            for i in range(seq)
            for j in range(sides)
        ]
        return lax.ppermute(x, ("seq", "head"), pairs)

    def levels_on(x, by, senders):
        pairs = [(i, i + by * WAYS) for i in range(seq) if i // WAYS in senders]
        return lax.ppermute(x, "seq", pairs)

    place = lax.rem(lax.axis_index("seq"), WAYS)
    ours = place // 2 * 2 * dh
    cuts = [
        lax.dynamic_slice_in_dim(x, at, 2 * dh, 1)
        for at in (ours, 2 * dh - ours)
        for x in (keys, values)
    ]
    own, away = call(pack_kv_kernel, cuts, [(tok, 4 * dh)] * 2, "pack_kv")
    got = partner(away, 2)
    queries, away = lax.optimization_barrier((queries, away))
    q = list(call(pack_q_kernel, [queries], [(tok, width // WAYS)] * WAYS, "pack_q"))
    q[2], q[3] = partner(q[2], 2), partner(q[3], 3)
    (pair,) = call(pair_kernel, [own, got], [(half, 2 * dh)], "pair_kv")
    pair, q[1], wq, wk = lax.optimization_barrier((pair, q[1], wq, wk))
    pair, q[1] = partner(pair, 1), partner(q[1], 1)
    wq, wk = [lax.dynamic_slice_in_dim(w, place * heads, heads) for w in (wq, wk)]
    pair, wq, wk = lax.optimization_barrier((pair, wq, wk))
    (kv,) = call(stack_kernel, [own, got, pair], [(2 * half, 2 * dh)], "stack_kv")
    def prepared(here, into, name):
        return call(
            lambda *refs: prepare_kernel(here, *refs),
            [kv, wk, wq, factor.reshape(1, local_heads), *into],
            [(states, 4 * half), (heads, dh, 2 * feat), (heads, 2 * feat)],
            name,
            limit=16,
            out_type=[BF16, BF16, F32],
            aliases={4 + n: n for n in range(len(into))},
        )

    ready = prepared(lambda level: level == 0, [], "prepare_first")
    kv, *ready = lax.optimization_barrier((kv, *ready))
    last, first = levels_on(kv, 1, (0, 1, 2)), levels_on(kv, 3, (0,))
    second = levels_on(kv, 2, (1,))
    kv, q[1], *ready = lax.optimization_barrier((kv, q[1], *ready))
    fk, wq, ratio = prepared(lambda level: level > 0, ready, "prepare")

    def query_features(a, b):
        return call(
            query_features_kernel,
            [a, b, wq, ratio],
            [(rows, dh), (rows, 2 * feat)],
            "query_features",
            [pltpu.VMEM((rows, 2 * feat), BF16)],
            12,
        )

    def near(other, q_rows, fq):
        return call(
            lambda *refs: near_kernel(other, *refs),
            [q_rows, fq, last, kv, fk],
            [(rows, 2 * dh)],
            "near",
            [
                pltpu.VMEM((3 * half, 2 * dh), BF16),
                pltpu.VMEM((rows, 2 * half), BF16),
            ],
            16,
            F32,
        )[0]

    q_own, fq_own = query_features(q[0], q[1])
    far_kv, fk, fq_own = lax.optimization_barrier((kv, fk, fq_own))
    before = levels_on(far_kv, 2, (0,))
    last, fq_own, fk = lax.optimization_barrier((last, fq_own, fk))
    fk, past, step = call(
        last_features_kernel,
        [last, wk, fk],
        [(states, 4 * half), (states, 2 * dh), (states, 2 * dh)],
        "last_features",
        limit=20,
        out_type=[BF16, F32, F32],
        aliases={2: 0},
    )
    near_own = near(0, q_own, fq_own)
    q[2], q[3], near_own = lax.optimization_barrier((q[2], q[3], near_own))
    q_other, fq_other = query_features(q[2], q[3])
    near_other = near(1, q_other, fq_other)
    first, near_other = lax.optimization_barrier((first, near_other))
    (past,) = call(
        past_kernel,
        [first, wk, past],
        [(states, 2 * dh)],
        "past",
        [pltpu.VMEM((states, 2 * half), BF16)],
        16,
        F32,
    )
    before, second, past = lax.optimization_barrier((before, second, past))
    part = tok // sides
    outs = call(
        mix_kernel_of_level,
        [near_own, near_other, fq_own, fq_other, past, step, wk, before, second],
        [(part, heads * dh)] * (WAYS * sides),
        "mix_level",
        [
            pltpu.VMEM((2 * half, 2 * dh), BF16),
            pltpu.VMEM((states, 2 * half), BF16),
            pltpu.VMEM((2, states, 2 * dh), BF16),
            pltpu.VMEM((2 * half, heads * dh), BF16),
        ],
        24,
    )

    def sent(x, slot):
        pairs = []
        for i in range(seq):
            dr, dy = slot[i % 2]
            to = i // WAYS * WAYS + (i % WAYS ^ dr)
            pairs += [(i * sides + j, to * sides + (j ^ dy)) for j in range(sides)]
        return lax.ppermute(x, ("seq", "head"), pairs)

    outs = list(outs)
    for n in range(1, 6):
        outs[n] = sent(outs[n], SLOTS[n])
    outs[6], outs[7], outs[3] = lax.optimization_barrier((outs[6], outs[7], outs[3]))
    outs[6], outs[7] = sent(outs[6], SLOTS[6]), sent(outs[7], SLOTS[7])

    def joined(slots, into):
        return pl.pallas_call(
            lambda *refs: join_kernel(slots, *refs),
            in_specs=[whole_spec()] * len(slots) + [whole_spec(pltpu.HBM)] * len(into),
            out_specs=whole_spec(pltpu.HBM),
            out_shape=jax.ShapeDtypeStruct((part, sides * WAYS * heads * dh), BF16),
            input_output_aliases={len(slots): 0} if into else {},
            scratch_shapes=[pltpu.SemaphoreType.DMA((len(slots),))],
            compiler_params=pltpu.CompilerParams(vmem_limit_bytes=4 * 2**20),
            name="join",
        )(*[outs[n] for n in slots], *into)

    return joined((4, 5, 6, 7), [joined((0, 1, 2, 3), [])])


def by_blocks(queries, keys, values, wq, wk, ratio):
    group = wq.shape[0] // (keys.shape[1] // DH)
    place = lax.axis_index("seq").astype(jnp.int32).reshape(1)
    kv = lax.all_gather(jnp.concatenate([keys, values], axis=1), "seq", tiled=True)
    out = mix(place, queries, kv, wq, wk, ratio, group)
    return lax.all_to_all(out, "head", split_axis=0, concat_axis=1, tiled=True)


def local(queries, keys, values, q_feature, k_feature, window_factor):
    tok = queries.shape[0]
    seq, sides = lax.axis_size("seq"), lax.axis_size("head")
    wq, wk = jnp.swapaxes(q_feature, 1, 2), jnp.swapaxes(k_feature, 1, 2)
    if keys.shape[1] == WAYS * DH and seq == 4 * WAYS and sides == 2 and tok == WINDOW:
        return by_levels(queries, keys, values, wq, wk, window_factor)
    ratio = window_factor / (1.0 - window_factor)
    return by_blocks(queries, keys, values, wq, wk, ratio)


def solution(mesh):
    return jax.shard_map(
        local,
        mesh=mesh,
        in_specs=(
            P("seq", "head"),
            P("seq", "head"),
            P("seq", "head"),
            P("head", None, None),
            P("head", None, None),
            P("head"),
        ),
        out_specs=P(("seq", "head"), None),
        check_vma=False,
    )
```

```python
import math

import jax
import jax.numpy as jnp
from jax import lax
from jax.experimental import pallas as pl
from jax.experimental.pallas import tpu as pltpu
from jax.sharding import PartitionSpec as P

DH = 128
WINDOW = 64
F32 = jnp.float32
BF16 = jnp.bfloat16


def dot_t(a, b):
    return lax.dot_general(a, b, (((1,), (1,)), ((), ())), preferred_element_type=F32)


def features_t(logits):
    top = jnp.max(logits, axis=0, keepdims=True)
    low = jnp.min(logits, axis=0, keepdims=True)
    up = jnp.exp(logits - top)
    down = jnp.exp(low - logits)
    up = up * (1.0 / jnp.sum(up, axis=0, keepdims=True))
    down = down * (1.0 / jnp.sum(down, axis=0, keepdims=True))
    return jnp.concatenate([up.astype(BF16), down.astype(BF16)], axis=0)


def mix_kernel(
    place_ref, q_ref, k_ref, v_ref, wq_ref, wk_ref, ratio_ref, out_ref, fk_scr, state_scr
):
    tok = q_ref.shape[0]
    heads, feat, dh = wq_ref.shape
    seen = fk_scr.shape[1]
    place = place_ref[0]
    first_head = pl.program_id(0) * heads

    weights = wk_ref[...].reshape(heads * feat, dh)
    for start in range(0, seen, 256):
        size = min(256, seen - start)
        logits = dot_t(weights, k_ref[start : start + size, :])
        for h in range(heads):
            fk_scr[h * 2 * feat : (h + 1) * 2 * feat, start : start + size] = features_t(
                logits[h * feat : (h + 1) * feat]
            )
    row = lax.broadcasted_iota(jnp.int32, (seen, dh), 0)
    kept = row < (place - 1) * tok
    v_seen = jnp.where(kept, v_ref[:seen, :].astype(F32), 0.0).astype(BF16)
    ones_seen = jnp.where(kept, 1.0, 0.0).astype(BF16)
    v_seen = jnp.concatenate([v_seen, ones_seen], axis=1)
    state_scr[...] = jnp.dot(fk_scr[...], v_seen, preferred_element_type=F32).astype(BF16)

    before = pl.multiple_of(jnp.maximum(place - 1, 0) * tok, tok)
    own = pl.multiple_of(place * tok, tok)
    k_ext = jnp.concatenate([k_ref[pl.ds(before, tok), :], k_ref[pl.ds(own, tok), :]], axis=0)
    v_ext = jnp.concatenate([v_ref[pl.ds(before, tok), :], v_ref[pl.ds(own, tok), :]], axis=0)
    v_ext = jnp.concatenate([v_ext, jnp.ones_like(v_ext)], axis=1)
    row = lax.broadcasted_iota(jnp.int32, (tok, 2 * tok), 0)
    col = lax.broadcasted_iota(jnp.int32, (tok, 2 * tok), 1)
    valid = (col >= tok) | (place > 0)
    inside = (col > row) & (col <= row + WINDOW) & valid
    causal = (col <= row) & valid
    lane = lax.broadcasted_iota(jnp.int32, (tok, 2 * feat), 1)
    left = lane < feat
    side_r = lax.broadcasted_iota(jnp.int32, (2 * feat, 2 * feat), 0) < feat
    side_c = lax.broadcasted_iota(jnp.int32, (2 * feat, 2 * feat), 1) < feat
    halves = jnp.where(side_r == side_c, 1.0, 0.0).astype(BF16)

    for h in range(heads):
        q = q_ref[:, h * dh : (h + 1) * dh]
        wq = wq_ref[h]
        logits = dot_t(q, jnp.concatenate([wq, -wq], axis=0))
        top_l = jnp.max(jnp.where(left, logits, -jnp.inf), axis=1, keepdims=True)
        top_r = jnp.max(jnp.where(left, -jnp.inf, logits), axis=1, keepdims=True)
        expd = jnp.exp(logits - jnp.where(left, top_l, top_r)).astype(BF16)
        total = jnp.dot(expd, halves, preferred_element_type=F32)
        fq = (expd.astype(F32) / total).astype(BF16)
        fk = features_t(dot_t(wk_ref[h], k_ext))
        linear = jnp.dot(fq, fk, preferred_element_type=F32)
        scores = dot_t(q, k_ext) * (1.0 / math.sqrt(dh))
        masked = jnp.where(inside, scores, -jnp.inf)
        top = jnp.max(masked, axis=1, keepdims=True)
        soft = jnp.exp(masked - top) * ratio_ref[first_head + h]
        weight = jnp.where(causal, linear, soft).astype(BF16)
        both = jnp.dot(weight, v_ext, preferred_element_type=F32) + jnp.dot(
            fq, state_scr[h * 2 * feat : (h + 1) * 2 * feat, :], preferred_element_type=F32
        )
        out_ref[:, h * dh : (h + 1) * dh] = (both[:, :dh] / both[:, dh:]).astype(BF16)


def mix(place, queries, kv, wq, wk, ratio, group):
    tok = queries.shape[0]
    local_heads, feat, dh = wq.shape
    groups = local_heads // group
    tokens = kv.shape[0]
    seen = tokens - 2 * tok
    return pl.pallas_call(
        mix_kernel,
        grid_spec=pltpu.PrefetchScalarGridSpec(
            num_scalar_prefetch=1,
            grid=(groups,),
            in_specs=[
                pl.BlockSpec((tok, group * dh), lambda g, p: (0, g)),
                pl.BlockSpec((tokens, dh), lambda g, p: (0, g)),
                pl.BlockSpec((tokens, dh), lambda g, p: (0, groups + g)),
                pl.BlockSpec((group, feat, dh), lambda g, p: (g, 0, 0)),
                pl.BlockSpec((group, feat, dh), lambda g, p: (g, 0, 0)),
                pl.BlockSpec(memory_space=pltpu.SMEM),
            ],
            out_specs=pl.BlockSpec((tok, group * dh), lambda g, p: (0, g)),
            scratch_shapes=[
                pltpu.VMEM((group * 2 * feat, seen), BF16),
                pltpu.VMEM((group * 2 * feat, 2 * dh), BF16),
            ],
        ),
        out_shape=jax.ShapeDtypeStruct(queries.shape, BF16),
        compiler_params=pltpu.CompilerParams(vmem_limit_bytes=48 * 2**20),
        cost_estimate=pl.CostEstimate(
            flops=2 * local_heads * tokens * 3 * feat * 2 * dh,
            bytes_accessed=8 * 2**20,
            transcendentals=local_heads * tokens * 2 * feat,
        ),
    )(place, queries, kv, kv, wq, wk, ratio)


WAYS = 4

EARLY = pl.CostEstimate(flops=10**10, bytes_accessed=10**8, transcendentals=0)
EARLY_KERNELS = ("pack_kv", "pack_q", "pair_kv", "stack_kv")


SLOTS = (
    ((0, 0), (0, 0)),
    ((2, 0), (0, 1)),
    ((0, 1), (2, 0)),
    ((1, 0), (1, 0)),
    ((2, 1), (2, 1)),
    ((3, 0), (1, 1)),
    ((3, 1), (3, 1)),
    ((1, 1), (3, 0)),
)


def slot_of(n, odd):
    return [jnp.where(odd == 1, b, a) if a != b else a for a, b in zip(*SLOTS[n])]


def spot():
    at = lax.axis_index("seq")
    return lax.rem(at, WAYS), lax.div(at, WAYS)


def aligned(at, step):
    return pl.ds(pl.multiple_of(at * step, step), step)


def with_ones(values, kept=True):
    here = jnp.where(kept, 1.0, 0.0).astype(BF16)
    return jnp.concatenate([values, jnp.full(values.shape, here)], axis=1)


def pack_kv_kernel(k_ref, v_ref, k_away_ref, v_away_ref, own_ref, away_ref):
    odd = lax.rem(spot()[0], 2)
    for k, v, ref in ((k_ref, v_ref, own_ref), (k_away_ref, v_away_ref, away_ref)):
        for d in range(2):
            at = aligned(odd ^ d, DH)
            ref[:, 2 * d * DH : (2 * d + 1) * DH] = k[:, at]
            ref[:, (2 * d + 1) * DH : (2 * d + 2) * DH] = v[:, at]


def pair_kernel(own_ref, got_ref, out_ref):
    tok = own_ref.shape[0]
    out_ref[:tok, :] = own_ref[:, 2 * DH :]
    out_ref[tok:, :] = got_ref[:, 2 * DH :]


def stack_kernel(own_ref, got_ref, pair_ref, out_ref):
    tok = own_ref.shape[0]
    place = spot()[0]
    out_ref[aligned(place, tok), :] = own_ref[:, : 2 * DH]
    out_ref[aligned(place ^ 2, tok), :] = got_ref[:, : 2 * DH]
    out_ref[aligned(place ^ 1, tok), :] = pair_ref[:tok, :]
    out_ref[aligned(place ^ 3, tok), :] = pair_ref[tok:, :]


def pack_q_kernel(q_ref, *out_refs):
    place = spot()[0]
    for d, out in enumerate(out_refs):
        out[...] = q_ref[:, aligned(place ^ d, out.shape[1])]


def weights_kernel(wq_ref, factor_ref, both_ref, ratio_ref):
    heads = both_ref.shape[0]
    shape = (heads, factor_ref.shape[1])
    head = lax.broadcasted_iota(jnp.int32, shape, 0) + spot()[0] * heads
    ratio = jnp.broadcast_to((1.0 - factor_ref[...]) / factor_ref[...], shape)
    ratio = jnp.where(lax.broadcasted_iota(jnp.int32, shape, 1) == head, ratio, 0.0)
    ratio = jnp.sum(ratio, axis=1, keepdims=True)
    ratio_ref[...] = jnp.broadcast_to(ratio, ratio_ref.shape)
    for h in range(heads):
        wq = wq_ref[h].T
        both_ref[h] = jnp.concatenate([wq, -wq], axis=1)


def join_kernel(slots, *refs):
    got, out_ref, sems = refs[: len(slots)], *refs[-2:]
    width = got[0].shape[1]
    place, side = spot()[0], lax.axis_index("head")
    copies = []
    for n, ref in zip(slots, got):
        dr, dy = slot_of(n, lax.rem(place, 2) ^ (SLOTS[n][0][0] & 1))
        at = aligned((side ^ dy) * WAYS + (place ^ dr), width)
        copies.append(pltpu.make_async_copy(ref, out_ref.at[:, at], sems.at[len(copies)]))
    for copy in copies:
        copy.start()
    for copy in copies:
        copy.wait()


def write_key_features(keys, wk_ref, fk_ref):
    heads, feat, dh = wk_ref.shape
    logits = dot_t(wk_ref[...].reshape(heads * feat, dh), keys)
    for h in range(heads):
        for at in range(0, keys.shape[0], 128):
            part = logits[h * feat : (h + 1) * feat, at : at + 128]
            top = jnp.max(part, axis=0, keepdims=True)
            low = jnp.min(part, axis=0, keepdims=True)
            for n, shifted in enumerate((part - top, low - part)):
                row = (2 * h + n) * feat
                expd = jnp.exp(shifted.astype(BF16))
                total = expd[: feat // 4]
                for q in range(1, 4):
                    total = total + expd[q * feat // 4 : (q + 1) * feat // 4]
                total = jnp.sum(total.astype(F32), axis=0, keepdims=True)
                fk_ref[row : row + feat, at : at + 128] = expd * pl.reciprocal(total).astype(BF16)


def own_features_kernel(own_ref, wk_ref, fk_ref):
    write_key_features(own_ref[:, :DH], wk_ref, fk_ref.at[:, own_ref.shape[0] :])


def last_features_kernel(last_ref, wk_ref, _, fk_ref, past_ref, step_ref):
    size = last_ref.shape[0]
    half = size // 2
    level = spot()[1]

    @pl.when(level == 0)
    def _():
        fk_ref[:, :size] = jnp.zeros((fk_ref.shape[0], size), BF16)
        for ref in (past_ref, step_ref):
            ref[...] = jnp.zeros_like(ref)

    @pl.when(level > 0)
    def _():
        write_key_features(last_ref[:, :DH], wk_ref, fk_ref.at[:, :size])
        for at, ref in ((0, past_ref), (half, step_ref)):
            ref[...] = jnp.dot(
                fk_ref[:, at : at + half],
                with_ones(last_ref[at : at + half, DH:]),
                preferred_element_type=F32,
            )


def past_kernel(first_ref, wk_ref, sum_ref, past_ref, fk_scr):
    level = spot()[1]

    @pl.when(level < 3)
    def _():
        past_ref[...] = sum_ref[...]

    @pl.when(level >= 3)
    def _():
        write_key_features(first_ref[:, :DH], wk_ref, fk_scr)
        past_ref[...] = sum_ref[...] + jnp.dot(
            fk_scr[...], with_ones(first_ref[:, DH:]), preferred_element_type=F32
        )


def query_features_kernel(a_ref, b_ref, w_ref, ratio_ref, q_out, fq_out, exp_scr):
    tok = a_ref.shape[0]
    heads, dh, both = w_ref.shape
    half = 2 * tok
    place = spot()[0]
    for d, ref in enumerate((a_ref, b_ref)):
        row = pl.multiple_of(lax.rem(place ^ d, 2) * tok, tok)
        for h in range(heads):
            q_out[pl.ds(h * half + row, tok), :] = ref[:, h * dh : (h + 1) * dh]
    rows_of = [slice(h * half, (h + 1) * half) for h in range(heads)]
    left = lax.broadcasted_iota(jnp.int32, (half, both), 1) < both // 2
    for h, rows in enumerate(rows_of):
        logits = jnp.dot(q_out[rows, :], w_ref[h], preferred_element_type=F32)
        top_l = jnp.max(jnp.where(left, logits, -jnp.inf), axis=1, keepdims=True)
        top_r = jnp.max(jnp.where(left, -jnp.inf, logits), axis=1, keepdims=True)
        exp_scr[rows, :] = jnp.exp((logits - jnp.where(left, top_l, top_r)).astype(BF16))
    side_r = lax.broadcasted_iota(jnp.int32, (both, both), 0) < both // 2
    side_c = lax.broadcasted_iota(jnp.int32, (both, both), 1) < both // 2
    halves = jnp.where(side_r == side_c, 1.0, 0.0).astype(BF16)
    total = jnp.dot(exp_scr[...], halves, preferred_element_type=F32)
    for h, rows in enumerate(rows_of):
        scale = pl.reciprocal(total[rows], approx=True) * ratio_ref[h : h + 1, :]
        fq_out[rows, :] = (exp_scr[rows, :].astype(F32) * scale).astype(BF16)


def near_kernel(other, q_ref, fq_ref, last_ref, own_ref, fk_ref, near_ref, kv_scr, w_scr):
    half, dh = last_ref.shape[0] // 2, q_ref.shape[1]
    heads = q_ref.shape[0] // half
    feats = fq_ref.shape[1]
    place, level = spot()
    u = lax.div(place, 2) ^ other
    kv_scr[:half, :] = last_ref[half:, :]
    kv_scr[half:, :] = own_ref[...]
    at = pl.ds(pl.multiple_of(u * half, half), 2 * half)
    keys, values = kv_scr[at, :dh], kv_scr[at, dh:]
    fk_at = pl.ds(pl.multiple_of((u + 1) * half, half), 2 * half)
    known = (level > 0) | (u > 0)
    cut = half - WINDOW
    row = lax.broadcasted_iota(jnp.int32, (WINDOW, 2 * half), 0)
    col = lax.broadcasted_iota(jnp.int32, (WINDOW, 2 * half), 1)
    inside = (col > row + cut) & (col <= row + half) & ((col >= half) | known)
    causal = (col <= row + cut)[:, :half]
    row, col = row[:, :half], col[:, :half]
    inside_low = (col > row) & (col <= row + WINDOW)
    causal_low = col <= row
    scores = dot_t(q_ref[...], keys)
    scale = math.log2(math.e) / math.sqrt(dh)

    def window(part, kept):
        masked = jnp.where(kept, part, -jnp.inf)
        top = jnp.max(masked, axis=1, keepdims=True)
        return jnp.exp2(((masked - top) * scale).astype(BF16))

    for h in range(heads):
        here = slice(h * half, (h + 1) * half)
        up, low = slice(h * half, h * half + cut), slice(h * half + cut, (h + 1) * half)
        linear = jnp.dot(
            fq_ref[here, :],
            fk_ref[h * feats : (h + 1) * feats, fk_at],
            preferred_element_type=F32,
        )
        soft = window(scores[up], inside)
        w_scr[up, :half] = soft[:, :half] + jnp.where(causal, linear[:cut, :half], 0.0).astype(BF16)
        w_scr[up, half:] = soft[:, half:]
        soft = window(scores[low, half:], inside_low)
        w_scr[low, :half] = linear[cut:, :half].astype(BF16)
        w_scr[low, half:] = soft + jnp.where(causal_low, linear[cut:, half:], 0.0).astype(BF16)
    values = jnp.concatenate(
        [with_ones(values[:half], known), with_ones(values[half:])], axis=0
    )
    near_ref[...] = jnp.dot(w_scr[...], values, preferred_element_type=F32)


def mix_kernel_of_level(*refs):
    near_refs, fq_refs, (past_ref, step_ref, wk_ref) = refs[:2], refs[2:4], refs[4:7]
    before_ref, refs = refs[7], refs[8:]
    out_refs, (fk_scr, state_scr, out_scr) = refs[:-3], refs[-3:]
    rows, dh = near_refs[0].shape[0], near_refs[0].shape[1] // 2
    feats = fq_refs[0].shape[1]
    heads = past_ref.shape[0] // feats
    half = rows // heads
    place, level = spot()
    side = lax.axis_index("head")
    u = lax.div(place, 2)

    @pl.when(level < 2)
    def _():
        state_scr[0] = past_ref[...].astype(BF16)
        state_scr[1] = (past_ref[...] + step_ref[...]).astype(BF16)

    @pl.when(level >= 2)
    def _():
        write_key_features(before_ref[:, :dh], wk_ref, fk_scr)
        state = past_ref[...] + jnp.dot(
            fk_scr[...], with_ones(before_ref[:, dh:]), preferred_element_type=F32
        )
        state_scr[0] = state.astype(BF16)
        state_scr[1] = (state + step_ref[...]).astype(BF16)

    part = out_refs[0].shape[0]
    for other in (1, 0):
        for h in range(heads):
            here = slice(h * half, (h + 1) * half)
            far = jnp.dot(
                fq_refs[other][here, :],
                state_scr[u ^ other, h * feats : (h + 1) * feats, :],
                preferred_element_type=F32,
            )
            both = near_refs[other][here, :] + far
            out_scr[aligned(u ^ other, half), h * dh : (h + 1) * dh] = (
                both[:, :dh] * pl.reciprocal(both[:, dh:], approx=True)
            ).astype(BF16)
    for n, ref in enumerate(out_refs):
        dr, dy = slot_of(n, lax.rem(place, 2))
        ref[...] = out_scr[aligned((place ^ dr) * 2 + (side ^ dy), part), :]


def whole_spec(space=pltpu.VMEM):
    return pl.BlockSpec(memory_space=space)


def call(kernel, ins, outs, name, scratch=(), limit=4, out_type=BF16, aliases={}):
    return pl.pallas_call(
        kernel,
        in_specs=[whole_spec() for _ in ins],
        out_specs=[whole_spec() for _ in outs],
        out_shape=[
            jax.ShapeDtypeStruct(s, out_type[n] if isinstance(out_type, list) else out_type)
            for n, s in enumerate(outs)
        ],
        scratch_shapes=list(scratch),
        input_output_aliases=aliases,
        cost_estimate=EARLY if name in EARLY_KERNELS else None,
        compiler_params=pltpu.CompilerParams(vmem_limit_bytes=limit * 2**20),
        name=name,
    )(*ins)


def by_levels(queries, keys, values, wq, wk, factor):
    tok, width = queries.shape
    local_heads, feat, dh = wq.shape
    heads = local_heads // WAYS
    seq, sides = lax.axis_size("seq"), lax.axis_size("head")
    half = 2 * tok
    rows, states = heads * half, heads * 2 * feat

    def partner(x, dr, dy=0):
        pairs = [
            (i * sides + j, (i // WAYS * WAYS + (i % WAYS ^ dr)) * sides + (j ^ dy))
            for i in range(seq)
            for j in range(sides)
        ]
        return lax.ppermute(x, ("seq", "head"), pairs)

    def levels_back(x, by):
        pairs = [(i, i + by * WAYS) for i in range(seq - by * WAYS)]
        return lax.ppermute(x, "seq", pairs)

    place = lax.rem(lax.axis_index("seq"), WAYS)
    ours = place // 2 * 2 * dh
    cuts = [
        lax.dynamic_slice_in_dim(x, at, 2 * dh, 1)
        for at in (ours, 2 * dh - ours)
        for x in (keys, values)
    ]
    own, away = call(pack_kv_kernel, cuts, [(tok, 4 * dh)] * 2, "pack_kv")
    got = partner(away, 2)
    queries, away = lax.optimization_barrier((queries, away))
    q = list(call(pack_q_kernel, [queries], [(tok, width // WAYS)] * WAYS, "pack_q"))
    q[2], q[3] = partner(q[2], 2), partner(q[3], 3)
    (pair,) = call(pair_kernel, [own, got], [(half, 2 * dh)], "pair_kv")
    pair, q[1], wq, wk = lax.optimization_barrier((pair, q[1], wq, wk))
    pair, q[1] = partner(pair, 1), partner(q[1], 1)
    wq, wk = [lax.dynamic_slice_in_dim(w, place * heads, heads) for w in (wq, wk)]
    pair, wq, wk = lax.optimization_barrier((pair, wq, wk))
    (kv,) = call(stack_kernel, [own, got, pair], [(2 * half, 2 * dh)], "stack_kv")
    last, first = levels_back(kv, 1), levels_back(kv, 3)
    wq, kv, q[1] = lax.optimization_barrier((wq, kv, q[1]))
    before = levels_back(kv, 2)
    (fk,) = call(own_features_kernel, [kv, wk], [(states, 4 * half)], "own_features", limit=16)
    wq, ratio = call(
        weights_kernel,
        [wq, factor.reshape(1, local_heads)],
        [(heads, dh, 2 * feat), (heads, 2 * feat)],
        "weights",
        out_type=[BF16, F32],
    )

    def query_features(a, b):
        return call(
            query_features_kernel,
            [a, b, wq, ratio],
            [(rows, dh), (rows, 2 * feat)],
            "query_features",
            [pltpu.VMEM((rows, 2 * feat), BF16)],
            12,
        )

    def near(other, q_rows, fq):
        return call(
            lambda *refs: near_kernel(other, *refs),
            [q_rows, fq, last, kv, fk],
            [(rows, 2 * dh)],
            "near",
            [
                pltpu.VMEM((3 * half, 2 * dh), BF16),
                pltpu.VMEM((rows, 2 * half), BF16),
            ],
            16,
            F32,
        )[0]

    q_own, fq_own = query_features(q[0], q[1])
    last, fq_own, fk = lax.optimization_barrier((last, fq_own, fk))
    fk, past, step = call(
        last_features_kernel,
        [last, wk, fk],
        [(states, 4 * half), (states, 2 * dh), (states, 2 * dh)],
        "last_features",
        limit=20,
        out_type=[BF16, F32, F32],
        aliases={2: 0},
    )
    near_own = near(0, q_own, fq_own)
    q[2], q[3], near_own = lax.optimization_barrier((q[2], q[3], near_own))
    q_other, fq_other = query_features(q[2], q[3])
    near_other = near(1, q_other, fq_other)
    first, near_other = lax.optimization_barrier((first, near_other))
    (past,) = call(
        past_kernel,
        [first, wk, past],
        [(states, 2 * dh)],
        "past",
        [pltpu.VMEM((states, 2 * half), BF16)],
        16,
        F32,
    )
    before, past = lax.optimization_barrier((before, past))
    part = tok // sides
    outs = call(
        mix_kernel_of_level,
        [near_own, near_other, fq_own, fq_other, past, step, wk, before],
        [(part, heads * dh)] * (WAYS * sides),
        "mix_level",
        [
            pltpu.VMEM((states, 2 * half), BF16),
            pltpu.VMEM((2, states, 2 * dh), BF16),
            pltpu.VMEM((2 * half, heads * dh), BF16),
        ],
        24,
    )

    def sent(x, slot):
        pairs = []
        for i in range(seq):
            dr, dy = slot[i % 2]
            to = i // WAYS * WAYS + (i % WAYS ^ dr)
            pairs += [(i * sides + j, to * sides + (j ^ dy)) for j in range(sides)]
        return lax.ppermute(x, ("seq", "head"), pairs)

    outs = list(outs)
    for n in range(1, 6):
        outs[n] = sent(outs[n], SLOTS[n])
    outs[6], outs[7], outs[3] = lax.optimization_barrier((outs[6], outs[7], outs[3]))
    outs[6], outs[7] = sent(outs[6], SLOTS[6]), sent(outs[7], SLOTS[7])

    def joined(slots, into):
        return pl.pallas_call(
            lambda *refs: join_kernel(slots, *refs),
            in_specs=[whole_spec()] * len(slots) + [whole_spec(pltpu.HBM)] * len(into),
            out_specs=whole_spec(pltpu.HBM),
            out_shape=jax.ShapeDtypeStruct((part, sides * WAYS * heads * dh), BF16),
            input_output_aliases={len(slots): 0} if into else {},
            scratch_shapes=[pltpu.SemaphoreType.DMA((len(slots),))],
            compiler_params=pltpu.CompilerParams(vmem_limit_bytes=4 * 2**20),
            name="join",
        )(*[outs[n] for n in slots], *into)

    return joined((4, 5, 6, 7), [joined((0, 1, 2, 3), [])])


def by_blocks(queries, keys, values, wq, wk, ratio):
    group = wq.shape[0] // (keys.shape[1] // DH)
    place = lax.axis_index("seq").astype(jnp.int32).reshape(1)
    kv = lax.all_gather(jnp.concatenate([keys, values], axis=1), "seq", tiled=True)
    out = mix(place, queries, kv, wq, wk, ratio, group)
    return lax.all_to_all(out, "head", split_axis=0, concat_axis=1, tiled=True)


def local(queries, keys, values, q_feature, k_feature, window_factor):
    tok = queries.shape[0]
    seq, sides = lax.axis_size("seq"), lax.axis_size("head")
    wq, wk = jnp.swapaxes(q_feature, 1, 2), jnp.swapaxes(k_feature, 1, 2)
    if keys.shape[1] == WAYS * DH and seq == 4 * WAYS and sides == 2 and tok == WINDOW:
        return by_levels(queries, keys, values, wq, wk, window_factor)
    ratio = window_factor / (1.0 - window_factor)
    return by_blocks(queries, keys, values, wq, wk, ratio)


def solution(mesh):
    return jax.shard_map(
        local,
        mesh=mesh,
        in_specs=(
            P("seq", "head"),
            P("seq", "head"),
            P("seq", "head"),
            P("head", None, None),
            P("head", None, None),
            P("head"),
        ),
        out_specs=P(("seq", "head"), None),
        check_vma=False,
    )
```

```python
import math

import jax
import jax.numpy as jnp
from jax import lax
from jax.experimental import pallas as pl
from jax.experimental.pallas import tpu as pltpu
from jax.sharding import PartitionSpec as P

DH = 128
WINDOW = 64
F32 = jnp.float32
BF16 = jnp.bfloat16


def dot_t(a, b):
    return lax.dot_general(a, b, (((1,), (1,)), ((), ())), preferred_element_type=F32)


def features_t(logits):
    top = jnp.max(logits, axis=0, keepdims=True)
    low = jnp.min(logits, axis=0, keepdims=True)
    up = jnp.exp(logits - top)
    down = jnp.exp(low - logits)
    up = up * (1.0 / jnp.sum(up, axis=0, keepdims=True))
    down = down * (1.0 / jnp.sum(down, axis=0, keepdims=True))
    return jnp.concatenate([up.astype(BF16), down.astype(BF16)], axis=0)


def mix_kernel(
    place_ref, q_ref, k_ref, v_ref, wq_ref, wk_ref, ratio_ref, out_ref, fk_scr, state_scr
):
    tok = q_ref.shape[0]
    heads, feat, dh = wq_ref.shape
    seen = fk_scr.shape[1]
    place = place_ref[0]
    first_head = pl.program_id(0) * heads

    weights = wk_ref[...].reshape(heads * feat, dh)
    for start in range(0, seen, 256):
        size = min(256, seen - start)
        logits = dot_t(weights, k_ref[start : start + size, :])
        for h in range(heads):
            fk_scr[h * 2 * feat : (h + 1) * 2 * feat, start : start + size] = features_t(
                logits[h * feat : (h + 1) * feat]
            )
    row = lax.broadcasted_iota(jnp.int32, (seen, dh), 0)
    kept = row < (place - 1) * tok
    v_seen = jnp.where(kept, v_ref[:seen, :].astype(F32), 0.0).astype(BF16)
    ones_seen = jnp.where(kept, 1.0, 0.0).astype(BF16)
    v_seen = jnp.concatenate([v_seen, ones_seen], axis=1)
    state_scr[...] = jnp.dot(fk_scr[...], v_seen, preferred_element_type=F32).astype(BF16)

    before = pl.multiple_of(jnp.maximum(place - 1, 0) * tok, tok)
    own = pl.multiple_of(place * tok, tok)
    k_ext = jnp.concatenate([k_ref[pl.ds(before, tok), :], k_ref[pl.ds(own, tok), :]], axis=0)
    v_ext = jnp.concatenate([v_ref[pl.ds(before, tok), :], v_ref[pl.ds(own, tok), :]], axis=0)
    v_ext = jnp.concatenate([v_ext, jnp.ones_like(v_ext)], axis=1)
    row = lax.broadcasted_iota(jnp.int32, (tok, 2 * tok), 0)
    col = lax.broadcasted_iota(jnp.int32, (tok, 2 * tok), 1)
    valid = (col >= tok) | (place > 0)
    inside = (col > row) & (col <= row + WINDOW) & valid
    causal = (col <= row) & valid
    lane = lax.broadcasted_iota(jnp.int32, (tok, 2 * feat), 1)
    left = lane < feat
    side_r = lax.broadcasted_iota(jnp.int32, (2 * feat, 2 * feat), 0) < feat
    side_c = lax.broadcasted_iota(jnp.int32, (2 * feat, 2 * feat), 1) < feat
    halves = jnp.where(side_r == side_c, 1.0, 0.0).astype(BF16)

    for h in range(heads):
        q = q_ref[:, h * dh : (h + 1) * dh]
        wq = wq_ref[h]
        logits = dot_t(q, jnp.concatenate([wq, -wq], axis=0))
        top_l = jnp.max(jnp.where(left, logits, -jnp.inf), axis=1, keepdims=True)
        top_r = jnp.max(jnp.where(left, -jnp.inf, logits), axis=1, keepdims=True)
        expd = jnp.exp(logits - jnp.where(left, top_l, top_r)).astype(BF16)
        total = jnp.dot(expd, halves, preferred_element_type=F32)
        fq = (expd.astype(F32) / total).astype(BF16)
        fk = features_t(dot_t(wk_ref[h], k_ext))
        linear = jnp.dot(fq, fk, preferred_element_type=F32)
        scores = dot_t(q, k_ext) * (1.0 / math.sqrt(dh))
        masked = jnp.where(inside, scores, -jnp.inf)
        top = jnp.max(masked, axis=1, keepdims=True)
        soft = jnp.exp(masked - top) * ratio_ref[first_head + h]
        weight = jnp.where(causal, linear, soft).astype(BF16)
        both = jnp.dot(weight, v_ext, preferred_element_type=F32) + jnp.dot(
            fq, state_scr[h * 2 * feat : (h + 1) * 2 * feat, :], preferred_element_type=F32
        )
        out_ref[:, h * dh : (h + 1) * dh] = (both[:, :dh] / both[:, dh:]).astype(BF16)


def mix(place, queries, kv, wq, wk, ratio, group):
    tok = queries.shape[0]
    local_heads, feat, dh = wq.shape
    groups = local_heads // group
    tokens = kv.shape[0]
    seen = tokens - 2 * tok
    return pl.pallas_call(
        mix_kernel,
        grid_spec=pltpu.PrefetchScalarGridSpec(
            num_scalar_prefetch=1,
            grid=(groups,),
            in_specs=[
                pl.BlockSpec((tok, group * dh), lambda g, p: (0, g)),
                pl.BlockSpec((tokens, dh), lambda g, p: (0, g)),
                pl.BlockSpec((tokens, dh), lambda g, p: (0, groups + g)),
                pl.BlockSpec((group, feat, dh), lambda g, p: (g, 0, 0)),
                pl.BlockSpec((group, feat, dh), lambda g, p: (g, 0, 0)),
                pl.BlockSpec(memory_space=pltpu.SMEM),
            ],
            out_specs=pl.BlockSpec((tok, group * dh), lambda g, p: (0, g)),
            scratch_shapes=[
                pltpu.VMEM((group * 2 * feat, seen), BF16),
                pltpu.VMEM((group * 2 * feat, 2 * dh), BF16),
            ],
        ),
        out_shape=jax.ShapeDtypeStruct(queries.shape, BF16),
        compiler_params=pltpu.CompilerParams(vmem_limit_bytes=48 * 2**20),
        cost_estimate=pl.CostEstimate(
            flops=2 * local_heads * tokens * 3 * feat * 2 * dh,
            bytes_accessed=8 * 2**20,
            transcendentals=local_heads * tokens * 2 * feat,
        ),
    )(place, queries, kv, kv, wq, wk, ratio)


WAYS = 4

EARLY = pl.CostEstimate(flops=10**10, bytes_accessed=10**8, transcendentals=0)
EARLY_KERNELS = ("pack_kv", "pack_q", "pair_kv", "stack_kv")


SLOTS = (
    ((0, 0), (0, 0)),
    ((2, 0), (0, 1)),
    ((0, 1), (2, 0)),
    ((1, 0), (1, 0)),
    ((2, 1), (2, 1)),
    ((3, 0), (1, 1)),
    ((3, 1), (3, 1)),
    ((1, 1), (3, 0)),
)


def slot_of(n, odd):
    return [jnp.where(odd == 1, b, a) if a != b else a for a, b in zip(*SLOTS[n])]


def spot():
    at = lax.axis_index("seq")
    return lax.rem(at, WAYS), lax.div(at, WAYS)


def aligned(at, step):
    return pl.ds(pl.multiple_of(at * step, step), step)


def with_ones(values, kept=True):
    here = jnp.where(kept, 1.0, 0.0).astype(BF16)
    return jnp.concatenate([values, jnp.full(values.shape, here)], axis=1)


def pack_kv_kernel(k_ref, v_ref, k_away_ref, v_away_ref, own_ref, away_ref):
    odd = lax.rem(spot()[0], 2)
    for k, v, ref in ((k_ref, v_ref, own_ref), (k_away_ref, v_away_ref, away_ref)):
        for d in range(2):
            at = aligned(odd ^ d, DH)
            ref[:, 2 * d * DH : (2 * d + 1) * DH] = k[:, at]
            ref[:, (2 * d + 1) * DH : (2 * d + 2) * DH] = v[:, at]


def pair_kernel(own_ref, got_ref, out_ref):
    tok = own_ref.shape[0]
    out_ref[:tok, :] = own_ref[:, 2 * DH :]
    out_ref[tok:, :] = got_ref[:, 2 * DH :]


def stack_kernel(own_ref, got_ref, pair_ref, out_ref):
    tok = own_ref.shape[0]
    place = spot()[0]
    out_ref[aligned(place, tok), :] = own_ref[:, : 2 * DH]
    out_ref[aligned(place ^ 2, tok), :] = got_ref[:, : 2 * DH]
    out_ref[aligned(place ^ 1, tok), :] = pair_ref[:tok, :]
    out_ref[aligned(place ^ 3, tok), :] = pair_ref[tok:, :]


def pack_q_kernel(q_ref, *out_refs):
    place = spot()[0]
    for d, out in enumerate(out_refs):
        out[...] = q_ref[:, aligned(place ^ d, out.shape[1])]


def weights_kernel(wq_ref, factor_ref, both_ref, ratio_ref):
    heads = both_ref.shape[0]
    shape = (heads, factor_ref.shape[1])
    head = lax.broadcasted_iota(jnp.int32, shape, 0) + spot()[0] * heads
    ratio = jnp.broadcast_to((1.0 - factor_ref[...]) / factor_ref[...], shape)
    ratio = jnp.where(lax.broadcasted_iota(jnp.int32, shape, 1) == head, ratio, 0.0)
    ratio = jnp.sum(ratio, axis=1, keepdims=True)
    ratio_ref[...] = jnp.broadcast_to(ratio, ratio_ref.shape)
    for h in range(heads):
        wq = wq_ref[h].T
        both_ref[h] = jnp.concatenate([wq, -wq], axis=1)


def join_kernel(slots, *refs):
    got, out_ref, sems = refs[: len(slots)], *refs[-2:]
    width = got[0].shape[1]
    place, side = spot()[0], lax.axis_index("head")
    copies = []
    for n, ref in zip(slots, got):
        dr, dy = slot_of(n, lax.rem(place, 2) ^ (SLOTS[n][0][0] & 1))
        at = aligned((side ^ dy) * WAYS + (place ^ dr), width)
        copies.append(pltpu.make_async_copy(ref, out_ref.at[:, at], sems.at[len(copies)]))
    for copy in copies:
        copy.start()
    for copy in copies:
        copy.wait()


def write_key_features(keys, wk_ref, fk_ref):
    heads, feat, dh = wk_ref.shape
    logits = dot_t(wk_ref[...].reshape(heads * feat, dh), keys)
    for h in range(heads):
        part = logits[h * feat : (h + 1) * feat]
        top = jnp.max(part, axis=0, keepdims=True)
        low = jnp.min(part, axis=0, keepdims=True)
        for n, shifted in enumerate((part - top, low - part)):
            row = (2 * h + n) * feat
            expd = jnp.exp(shifted.astype(BF16))
            total = expd[: feat // 4]
            for q in range(1, 4):
                total = total + expd[q * feat // 4 : (q + 1) * feat // 4]
            total = jnp.sum(total.astype(F32), axis=0, keepdims=True)
            fk_ref[row : row + feat, :] = expd * pl.reciprocal(total).astype(BF16)


def own_features_kernel(own_ref, wk_ref, fk_ref):
    write_key_features(own_ref[:, :DH], wk_ref, fk_ref.at[:, own_ref.shape[0] :])


def last_features_kernel(
    one_ref, two_ref, three_ref, wk_ref, far_ref, _, fk_ref, past_ref, step_ref, last_ref
):
    size = last_ref.shape[0]
    half = size // 2
    level = spot()[1]
    for n, ref in enumerate((one_ref, two_ref, three_ref)):

        @pl.when(level == n + 1)
        def _():
            last_ref[...] = ref[...]

    @pl.when(level == 0)
    def _():
        last_ref[...] = jnp.zeros_like(last_ref)
        fk_ref[:, :size] = jnp.zeros((fk_ref.shape[0], size), BF16)
        for ref in (past_ref, step_ref):
            ref[...] = jnp.zeros_like(ref)

    @pl.when(level > 0)
    def _():
        write_key_features(last_ref[:, :DH], wk_ref, fk_ref.at[:, :size])
        states = [
            jnp.dot(
                fk_ref[:, at : at + half],
                with_ones(last_ref[at : at + half, DH:]),
                preferred_element_type=F32,
            )
            for at in (0, half)
        ]
        past_ref[...] = far_ref[...] + states[0]
        step_ref[...] = states[1]


def far_kernel(one_ref, two_ref, wk_ref, far_ref, fk_scr):
    level = spot()[1]
    size = one_ref.shape[0]

    @pl.when(level < 3)
    def _():
        far_ref[...] = jnp.zeros_like(far_ref)

    @pl.when(level == 3)
    def _():
        keys = jnp.concatenate([one_ref[:, :DH], two_ref[:, :DH]], axis=0)
        write_key_features(keys, wk_ref, fk_scr)
        values = jnp.concatenate([one_ref[:, DH:], two_ref[:, DH:]], axis=0)
        far_ref[...] = jnp.dot(fk_scr[...], with_ones(values), preferred_element_type=F32)


def query_features_kernel(a_ref, b_ref, w_ref, ratio_ref, q_out, fq_out, exp_scr):
    tok = a_ref.shape[0]
    heads, dh, both = w_ref.shape
    half = 2 * tok
    place = spot()[0]
    for d, ref in enumerate((a_ref, b_ref)):
        row = pl.multiple_of(lax.rem(place ^ d, 2) * tok, tok)
        for h in range(heads):
            q_out[pl.ds(h * half + row, tok), :] = ref[:, h * dh : (h + 1) * dh]
    rows_of = [slice(h * half, (h + 1) * half) for h in range(heads)]
    left = lax.broadcasted_iota(jnp.int32, (half, both), 1) < both // 2
    for h, rows in enumerate(rows_of):
        logits = jnp.dot(q_out[rows, :], w_ref[h], preferred_element_type=F32)
        top_l = jnp.max(jnp.where(left, logits, -jnp.inf), axis=1, keepdims=True)
        top_r = jnp.max(jnp.where(left, -jnp.inf, logits), axis=1, keepdims=True)
        exp_scr[rows, :] = jnp.exp((logits - jnp.where(left, top_l, top_r)).astype(BF16))
    side_r = lax.broadcasted_iota(jnp.int32, (both, both), 0) < both // 2
    side_c = lax.broadcasted_iota(jnp.int32, (both, both), 1) < both // 2
    halves = jnp.where(side_r == side_c, 1.0, 0.0).astype(BF16)
    total = jnp.dot(exp_scr[...], halves, preferred_element_type=F32)
    for h, rows in enumerate(rows_of):
        scale = pl.reciprocal(total[rows], approx=True) * ratio_ref[h : h + 1, :]
        fq_out[rows, :] = (exp_scr[rows, :].astype(F32) * scale).astype(BF16)


def near_kernel(other, q_ref, fq_ref, last_ref, own_ref, fk_ref, near_ref, kv_scr, w_scr):
    half, dh = last_ref.shape[0] // 2, q_ref.shape[1]
    heads = q_ref.shape[0] // half
    feats = fq_ref.shape[1]
    place, level = spot()
    u = lax.div(place, 2) ^ other
    kv_scr[:half, :] = last_ref[half:, :]
    kv_scr[half:, :] = own_ref[...]
    at = pl.ds(pl.multiple_of(u * half, half), 2 * half)
    keys, values = kv_scr[at, :dh], kv_scr[at, dh:]
    fk_at = pl.ds(pl.multiple_of((u + 1) * half, half), 2 * half)
    known = (level > 0) | (u > 0)
    cut = half - WINDOW
    row = lax.broadcasted_iota(jnp.int32, (WINDOW, 2 * half), 0)
    col = lax.broadcasted_iota(jnp.int32, (WINDOW, 2 * half), 1)
    inside = (col > row + cut) & (col <= row + half) & ((col >= half) | known)
    causal = (col <= row + cut)[:, :half]
    row, col = row[:, :half], col[:, :half]
    inside_low = (col > row) & (col <= row + WINDOW)
    causal_low = col <= row
    scores = dot_t(q_ref[...], keys)
    scale = math.log2(math.e) / math.sqrt(dh)

    def window(part, kept):
        masked = jnp.where(kept, part, -jnp.inf)
        top = jnp.max(masked, axis=1, keepdims=True)
        return jnp.exp2(((masked - top) * scale).astype(BF16))

    for h in range(heads):
        here = slice(h * half, (h + 1) * half)
        up, low = slice(h * half, h * half + cut), slice(h * half + cut, (h + 1) * half)
        linear = jnp.dot(
            fq_ref[here, :],
            fk_ref[h * feats : (h + 1) * feats, fk_at],
            preferred_element_type=F32,
        )
        soft = window(scores[up], inside)
        w_scr[up, :half] = soft[:, :half] + jnp.where(causal, linear[:cut, :half], 0.0).astype(BF16)
        w_scr[up, half:] = soft[:, half:]
        soft = window(scores[low, half:], inside_low)
        w_scr[low, :half] = linear[cut:, :half].astype(BF16)
        w_scr[low, half:] = soft + jnp.where(causal_low, linear[cut:, half:], 0.0).astype(BF16)
    values = jnp.concatenate(
        [with_ones(values[:half], known), with_ones(values[half:])], axis=0
    )
    near_ref[...] = jnp.dot(w_scr[...], values, preferred_element_type=F32)


def mix_kernel_of_level(*refs):
    near_refs, fq_refs, (past_ref, step_ref, wk_ref) = refs[:2], refs[2:4], refs[4:7]
    before_ref, refs = refs[7], refs[8:]
    out_refs, (fk_scr, state_scr, out_scr) = refs[:-3], refs[-3:]
    rows, dh = near_refs[0].shape[0], near_refs[0].shape[1] // 2
    feats = fq_refs[0].shape[1]
    heads = past_ref.shape[0] // feats
    half = rows // heads
    place, level = spot()
    side = lax.axis_index("head")
    u = lax.div(place, 2)

    @pl.when(level != 2)
    def _():
        state_scr[0] = past_ref[...].astype(BF16)
        state_scr[1] = (past_ref[...] + step_ref[...]).astype(BF16)

    @pl.when(level == 2)
    def _():
        write_key_features(before_ref[:, :dh], wk_ref, fk_scr)
        state = past_ref[...] + jnp.dot(
            fk_scr[...], with_ones(before_ref[:, dh:]), preferred_element_type=F32
        )
        state_scr[0] = state.astype(BF16)
        state_scr[1] = (state + step_ref[...]).astype(BF16)

    part = out_refs[0].shape[0]
    for other in (1, 0):
        for h in range(heads):
            here = slice(h * half, (h + 1) * half)
            far = jnp.dot(
                fq_refs[other][here, :],
                state_scr[u ^ other, h * feats : (h + 1) * feats, :],
                preferred_element_type=F32,
            )
            both = near_refs[other][here, :] + far
            out_scr[aligned(u ^ other, half), h * dh : (h + 1) * dh] = (
                both[:, :dh] * pl.reciprocal(both[:, dh:], approx=True)
            ).astype(BF16)
    for n, ref in enumerate(out_refs):
        dr, dy = slot_of(n, lax.rem(place, 2))
        ref[...] = out_scr[aligned((place ^ dr) * 2 + (side ^ dy), part), :]


def whole_spec(space=pltpu.VMEM):
    return pl.BlockSpec(memory_space=space)


def call(kernel, ins, outs, name, scratch=(), limit=4, out_type=BF16, aliases={}):
    return pl.pallas_call(
        kernel,
        in_specs=[whole_spec() for _ in ins],
        out_specs=[whole_spec() for _ in outs],
        out_shape=[
            jax.ShapeDtypeStruct(s, out_type[n] if isinstance(out_type, list) else out_type)
            for n, s in enumerate(outs)
        ],
        scratch_shapes=list(scratch),
        input_output_aliases=aliases,
        cost_estimate=EARLY if name in EARLY_KERNELS else None,
        compiler_params=pltpu.CompilerParams(vmem_limit_bytes=limit * 2**20),
        name=name,
    )(*ins)


def by_levels(queries, keys, values, wq, wk, factor):
    tok, width = queries.shape
    local_heads, feat, dh = wq.shape
    heads = local_heads // WAYS
    seq, sides = lax.axis_size("seq"), lax.axis_size("head")
    half = 2 * tok
    rows, states = heads * half, heads * 2 * feat

    def partner(x, dr, dy=0):
        pairs = [
            (i * sides + j, (i // WAYS * WAYS + (i % WAYS ^ dr)) * sides + (j ^ dy))
            for i in range(seq)
            for j in range(sides)
        ]
        return lax.ppermute(x, ("seq", "head"), pairs)

    def along(x, *moves):
        pairs = [(a * WAYS + r, b * WAYS + r) for a, b in moves for r in range(WAYS)]
        return lax.ppermute(x, "seq", pairs)

    place = lax.rem(lax.axis_index("seq"), WAYS)
    ours = place // 2 * 2 * dh
    cuts = [
        lax.dynamic_slice_in_dim(x, at, 2 * dh, 1)
        for at in (ours, 2 * dh - ours)
        for x in (keys, values)
    ]
    own, away = call(pack_kv_kernel, cuts, [(tok, 4 * dh)] * 2, "pack_kv")
    got = partner(away, 2)
    queries, away = lax.optimization_barrier((queries, away))
    q = list(call(pack_q_kernel, [queries], [(tok, width // WAYS)] * WAYS, "pack_q"))
    q[2], q[3] = partner(q[2], 2), partner(q[3], 3)
    (pair,) = call(pair_kernel, [own, got], [(half, 2 * dh)], "pair_kv")
    pair, q[1], wq, wk = lax.optimization_barrier((pair, q[1], wq, wk))
    pair, q[1] = partner(pair, 1), partner(q[1], 1)
    wq, wk = [lax.dynamic_slice_in_dim(w, place * heads, heads) for w in (wq, wk)]
    pair, wq, wk = lax.optimization_barrier((pair, wq, wk))
    (kv,) = call(stack_kernel, [own, got, pair], [(2 * half, 2 * dh)], "stack_kv")
    one = along(kv, (0, 1), (1, 3))
    wq, kv, q[1] = lax.optimization_barrier((wq, kv, q[1]))
    two = along(kv, (0, 3), (1, 2))
    three = along(kv, (2, 3), (0, 2))
    (fk,) = call(own_features_kernel, [kv, wk], [(states, 4 * half)], "own_features", limit=16)
    wq, ratio = call(
        weights_kernel,
        [wq, factor.reshape(1, local_heads)],
        [(heads, dh, 2 * feat), (heads, 2 * feat)],
        "weights",
        out_type=[BF16, F32],
    )

    def query_features(a, b):
        return call(
            query_features_kernel,
            [a, b, wq, ratio],
            [(rows, dh), (rows, 2 * feat)],
            "query_features",
            [pltpu.VMEM((rows, 2 * feat), BF16)],
            12,
        )

    def near(other, q_rows, fq):
        return call(
            lambda *refs: near_kernel(other, *refs),
            [q_rows, fq, last, kv, fk],
            [(rows, 2 * dh)],
            "near",
            [
                pltpu.VMEM((3 * half, 2 * dh), BF16),
                pltpu.VMEM((rows, 2 * half), BF16),
            ],
            16,
            F32,
        )[0]

    q_own, fq_own = query_features(q[0], q[1])
    one, two, fq_own, fk = lax.optimization_barrier((one, two, fq_own, fk))
    (far,) = call(
        far_kernel,
        [one, two, wk],
        [(states, 2 * dh)],
        "far",
        [pltpu.VMEM((states, 4 * half), BF16)],
        20,
        F32,
    )
    q[2], q[3], far = lax.optimization_barrier((q[2], q[3], far))
    q_other, fq_other = query_features(q[2], q[3])
    three, fq_other = lax.optimization_barrier((three, fq_other))
    fk, past, step, last = call(
        last_features_kernel,
        [one, two, three, wk, far, fk],
        [(states, 4 * half), (states, 2 * dh), (states, 2 * dh), kv.shape],
        "last_features",
        limit=24,
        out_type=[BF16, F32, F32, BF16],
        aliases={5: 0},
    )
    near_own = near(0, q_own, fq_own)
    near_other = near(1, q_other, fq_other)
    part = tok // sides
    outs = call(
        mix_kernel_of_level,
        [near_own, near_other, fq_own, fq_other, past, step, wk, three],
        [(part, heads * dh)] * (WAYS * sides),
        "mix_level",
        [
            pltpu.VMEM((states, 2 * half), BF16),
            pltpu.VMEM((2, states, 2 * dh), BF16),
            pltpu.VMEM((2 * half, heads * dh), BF16),
        ],
        24,
    )

    def sent(x, slot):
        pairs = []
        for i in range(seq):
            dr, dy = slot[i % 2]
            to = i // WAYS * WAYS + (i % WAYS ^ dr)
            pairs += [(i * sides + j, to * sides + (j ^ dy)) for j in range(sides)]
        return lax.ppermute(x, ("seq", "head"), pairs)

    outs = list(outs)
    for n in range(1, 6):
        outs[n] = sent(outs[n], SLOTS[n])
    outs[6], outs[7], outs[3] = lax.optimization_barrier((outs[6], outs[7], outs[3]))
    outs[6], outs[7] = sent(outs[6], SLOTS[6]), sent(outs[7], SLOTS[7])

    def joined(slots, into):
        return pl.pallas_call(
            lambda *refs: join_kernel(slots, *refs),
            in_specs=[whole_spec()] * len(slots) + [whole_spec(pltpu.HBM)] * len(into),
            out_specs=whole_spec(pltpu.HBM),
            out_shape=jax.ShapeDtypeStruct((part, sides * WAYS * heads * dh), BF16),
            input_output_aliases={len(slots): 0} if into else {},
            scratch_shapes=[pltpu.SemaphoreType.DMA((len(slots),))],
            compiler_params=pltpu.CompilerParams(vmem_limit_bytes=4 * 2**20),
            name="join",
        )(*[outs[n] for n in slots], *into)

    return joined((4, 5, 6, 7), [joined((0, 1, 2, 3), [])])


def by_blocks(queries, keys, values, wq, wk, ratio):
    group = wq.shape[0] // (keys.shape[1] // DH)
    place = lax.axis_index("seq").astype(jnp.int32).reshape(1)
    kv = lax.all_gather(jnp.concatenate([keys, values], axis=1), "seq", tiled=True)
    out = mix(place, queries, kv, wq, wk, ratio, group)
    return lax.all_to_all(out, "head", split_axis=0, concat_axis=1, tiled=True)


def local(queries, keys, values, q_feature, k_feature, window_factor):
    tok = queries.shape[0]
    seq, sides = lax.axis_size("seq"), lax.axis_size("head")
    wq, wk = jnp.swapaxes(q_feature, 1, 2), jnp.swapaxes(k_feature, 1, 2)
    if keys.shape[1] == WAYS * DH and seq == 4 * WAYS and sides == 2 and tok == WINDOW:
        return by_levels(queries, keys, values, wq, wk, window_factor)
    ratio = window_factor / (1.0 - window_factor)
    return by_blocks(queries, keys, values, wq, wk, ratio)


def solution(mesh):
    return jax.shard_map(
        local,
        mesh=mesh,
        in_specs=(
            P("seq", "head"),
            P("seq", "head"),
            P("seq", "head"),
            P("head", None, None),
            P("head", None, None),
            P("head"),
        ),
        out_specs=P(("seq", "head"), None),
        check_vma=False,
    )
```

```python
import math

import jax
import jax.numpy as jnp
from jax import lax
from jax.experimental import pallas as pl
from jax.experimental.pallas import tpu as pltpu
from jax.sharding import PartitionSpec as P

DH = 128
WINDOW = 64
F32 = jnp.float32
BF16 = jnp.bfloat16


def dot_t(a, b):
    return lax.dot_general(a, b, (((1,), (1,)), ((), ())), preferred_element_type=F32)


def features_t(logits):
    top = jnp.max(logits, axis=0, keepdims=True)
    low = jnp.min(logits, axis=0, keepdims=True)
    up = jnp.exp(logits - top)
    down = jnp.exp(low - logits)
    up = up * (1.0 / jnp.sum(up, axis=0, keepdims=True))
    down = down * (1.0 / jnp.sum(down, axis=0, keepdims=True))
    return jnp.concatenate([up.astype(BF16), down.astype(BF16)], axis=0)


def mix_kernel(
    place_ref, q_ref, k_ref, v_ref, wq_ref, wk_ref, ratio_ref, out_ref, fk_scr, state_scr
):
    tok = q_ref.shape[0]
    heads, feat, dh = wq_ref.shape
    seen = fk_scr.shape[1]
    place = place_ref[0]
    first_head = pl.program_id(0) * heads

    weights = wk_ref[...].reshape(heads * feat, dh)
    for start in range(0, seen, 256):
        size = min(256, seen - start)
        logits = dot_t(weights, k_ref[start : start + size, :])
        for h in range(heads):
            fk_scr[h * 2 * feat : (h + 1) * 2 * feat, start : start + size] = features_t(
                logits[h * feat : (h + 1) * feat]
            )
    row = lax.broadcasted_iota(jnp.int32, (seen, dh), 0)
    kept = row < (place - 1) * tok
    v_seen = jnp.where(kept, v_ref[:seen, :].astype(F32), 0.0).astype(BF16)
    ones_seen = jnp.where(kept, 1.0, 0.0).astype(BF16)
    v_seen = jnp.concatenate([v_seen, ones_seen], axis=1)
    state_scr[...] = jnp.dot(fk_scr[...], v_seen, preferred_element_type=F32).astype(BF16)

    before = pl.multiple_of(jnp.maximum(place - 1, 0) * tok, tok)
    own = pl.multiple_of(place * tok, tok)
    k_ext = jnp.concatenate([k_ref[pl.ds(before, tok), :], k_ref[pl.ds(own, tok), :]], axis=0)
    v_ext = jnp.concatenate([v_ref[pl.ds(before, tok), :], v_ref[pl.ds(own, tok), :]], axis=0)
    v_ext = jnp.concatenate([v_ext, jnp.ones_like(v_ext)], axis=1)
    row = lax.broadcasted_iota(jnp.int32, (tok, 2 * tok), 0)
    col = lax.broadcasted_iota(jnp.int32, (tok, 2 * tok), 1)
    valid = (col >= tok) | (place > 0)
    inside = (col > row) & (col <= row + WINDOW) & valid
    causal = (col <= row) & valid
    lane = lax.broadcasted_iota(jnp.int32, (tok, 2 * feat), 1)
    left = lane < feat
    side_r = lax.broadcasted_iota(jnp.int32, (2 * feat, 2 * feat), 0) < feat
    side_c = lax.broadcasted_iota(jnp.int32, (2 * feat, 2 * feat), 1) < feat
    halves = jnp.where(side_r == side_c, 1.0, 0.0).astype(BF16)

    for h in range(heads):
        q = q_ref[:, h * dh : (h + 1) * dh]
        wq = wq_ref[h]
        logits = dot_t(q, jnp.concatenate([wq, -wq], axis=0))
        top_l = jnp.max(jnp.where(left, logits, -jnp.inf), axis=1, keepdims=True)
        top_r = jnp.max(jnp.where(left, -jnp.inf, logits), axis=1, keepdims=True)
        expd = jnp.exp(logits - jnp.where(left, top_l, top_r)).astype(BF16)
        total = jnp.dot(expd, halves, preferred_element_type=F32)
        fq = (expd.astype(F32) / total).astype(BF16)
        fk = features_t(dot_t(wk_ref[h], k_ext))
        linear = jnp.dot(fq, fk, preferred_element_type=F32)
        scores = dot_t(q, k_ext) * (1.0 / math.sqrt(dh))
        masked = jnp.where(inside, scores, -jnp.inf)
        top = jnp.max(masked, axis=1, keepdims=True)
        soft = jnp.exp(masked - top) * ratio_ref[first_head + h]
        weight = jnp.where(causal, linear, soft).astype(BF16)
        both = jnp.dot(weight, v_ext, preferred_element_type=F32) + jnp.dot(
            fq, state_scr[h * 2 * feat : (h + 1) * 2 * feat, :], preferred_element_type=F32
        )
        out_ref[:, h * dh : (h + 1) * dh] = (both[:, :dh] / both[:, dh:]).astype(BF16)


def mix(place, queries, kv, wq, wk, ratio, group):
    tok = queries.shape[0]
    local_heads, feat, dh = wq.shape
    groups = local_heads // group
    tokens = kv.shape[0]
    seen = tokens - 2 * tok
    return pl.pallas_call(
        mix_kernel,
        grid_spec=pltpu.PrefetchScalarGridSpec(
            num_scalar_prefetch=1,
            grid=(groups,),
            in_specs=[
                pl.BlockSpec((tok, group * dh), lambda g, p: (0, g)),
                pl.BlockSpec((tokens, dh), lambda g, p: (0, g)),
                pl.BlockSpec((tokens, dh), lambda g, p: (0, groups + g)),
                pl.BlockSpec((group, feat, dh), lambda g, p: (g, 0, 0)),
                pl.BlockSpec((group, feat, dh), lambda g, p: (g, 0, 0)),
                pl.BlockSpec(memory_space=pltpu.SMEM),
            ],
            out_specs=pl.BlockSpec((tok, group * dh), lambda g, p: (0, g)),
            scratch_shapes=[
                pltpu.VMEM((group * 2 * feat, seen), BF16),
                pltpu.VMEM((group * 2 * feat, 2 * dh), BF16),
            ],
        ),
        out_shape=jax.ShapeDtypeStruct(queries.shape, BF16),
        compiler_params=pltpu.CompilerParams(vmem_limit_bytes=48 * 2**20),
        cost_estimate=pl.CostEstimate(
            flops=2 * local_heads * tokens * 3 * feat * 2 * dh,
            bytes_accessed=8 * 2**20,
            transcendentals=local_heads * tokens * 2 * feat,
        ),
    )(place, queries, kv, kv, wq, wk, ratio)


WAYS = 4

EARLY = pl.CostEstimate(flops=10**10, bytes_accessed=10**8, transcendentals=0)
EARLY_KERNELS = ("pack_kv", "pack_q", "pair_kv", "stack_kv")


SLOTS = (
    ((0, 0), (0, 0)),
    ((2, 1), (2, 1)),
    ((2, 0), (0, 1)),
    ((0, 1), (2, 0)),
    ((3, 1), (3, 1)),
    ((3, 0), (1, 1)),
    ((1, 1), (3, 0)),
    ((1, 0), (1, 0)),
)


def slot_of(n, odd):
    return [jnp.where(odd == 1, b, a) if a != b else a for a, b in zip(*SLOTS[n])]


def spot():
    at = lax.axis_index("seq")
    return lax.rem(at, WAYS), lax.div(at, WAYS)


def aligned(at, step):
    return pl.ds(pl.multiple_of(at * step, step), step)


def with_ones(values, kept=True):
    here = jnp.where(kept, 1.0, 0.0).astype(BF16)
    return jnp.concatenate([values, jnp.full(values.shape, here)], axis=1)


def pack_kv_kernel(k_ref, v_ref, k_away_ref, v_away_ref, own_ref, away_ref):
    odd = lax.rem(spot()[0], 2)
    for k, v, ref in ((k_ref, v_ref, own_ref), (k_away_ref, v_away_ref, away_ref)):
        for d in range(2):
            at = aligned(odd ^ d, DH)
            ref[:, 2 * d * DH : (2 * d + 1) * DH] = k[:, at]
            ref[:, (2 * d + 1) * DH : (2 * d + 2) * DH] = v[:, at]


def pair_kernel(own_ref, got_ref, out_ref):
    tok = own_ref.shape[0]
    out_ref[:tok, :] = own_ref[:, 2 * DH :]
    out_ref[tok:, :] = got_ref[:, 2 * DH :]


def stack_kernel(own_ref, got_ref, pair_ref, out_ref):
    tok = own_ref.shape[0]
    place = spot()[0]
    out_ref[aligned(place, tok), :] = own_ref[:, : 2 * DH]
    out_ref[aligned(place ^ 2, tok), :] = got_ref[:, : 2 * DH]
    out_ref[aligned(place ^ 1, tok), :] = pair_ref[:tok, :]
    out_ref[aligned(place ^ 3, tok), :] = pair_ref[tok:, :]


def pack_q_kernel(q_ref, *out_refs):
    place = spot()[0]
    for d, out in enumerate(out_refs):
        out[...] = q_ref[:, aligned(place ^ d, out.shape[1])]


def weights_kernel(wq_ref, factor_ref, both_ref, ratio_ref):
    heads = both_ref.shape[0]
    shape = (heads, factor_ref.shape[1])
    head = lax.broadcasted_iota(jnp.int32, shape, 0) + spot()[0] * heads
    ratio = jnp.broadcast_to((1.0 - factor_ref[...]) / factor_ref[...], shape)
    ratio = jnp.where(lax.broadcasted_iota(jnp.int32, shape, 1) == head, ratio, 0.0)
    ratio = jnp.sum(ratio, axis=1, keepdims=True)
    ratio_ref[...] = jnp.broadcast_to(ratio, ratio_ref.shape)
    for h in range(heads):
        wq = wq_ref[h].T
        both_ref[h] = jnp.concatenate([wq, -wq], axis=1)


def join_kernel(slots, *refs):
    got, out_ref, sems = refs[: len(slots)], *refs[-2:]
    width = got[0].shape[1]
    place, side = spot()[0], lax.axis_index("head")
    copies = []
    for n, ref in zip(slots, got):
        dr, dy = slot_of(n, lax.rem(place, 2) ^ (SLOTS[n][0][0] & 1))
        at = aligned((side ^ dy) * WAYS + (place ^ dr), width)
        copies.append(pltpu.make_async_copy(ref, out_ref.at[:, at], sems.at[len(copies)]))
    for copy in copies:
        copy.start()
    for copy in copies:
        copy.wait()


def write_key_features(keys, wk_ref, fk_ref):
    heads, feat, dh = wk_ref.shape
    logits = dot_t(wk_ref[...].reshape(heads * feat, dh), keys)
    for h in range(heads):
        part = logits[h * feat : (h + 1) * feat]
        top = jnp.max(part, axis=0, keepdims=True)
        low = jnp.min(part, axis=0, keepdims=True)
        for n, shifted in enumerate((part - top, low - part)):
            row = (2 * h + n) * feat
            expd = jnp.exp(shifted.astype(BF16))
            total = expd[: feat // 4]
            for q in range(1, 4):
                total = total + expd[q * feat // 4 : (q + 1) * feat // 4]
            total = jnp.sum(total.astype(F32), axis=0, keepdims=True)
            fk_ref[row : row + feat, :] = expd * pl.reciprocal(total).astype(BF16)


def own_features_kernel(own_ref, wk_ref, fk_ref):
    write_key_features(own_ref[:, :DH], wk_ref, fk_ref.at[:, own_ref.shape[0] :])


def last_features_kernel(last_ref, wk_ref, _, fk_ref, past_ref, step_ref):
    size = last_ref.shape[0]
    half = size // 2
    level = spot()[1]

    @pl.when(level == 0)
    def _():
        fk_ref[:, :size] = jnp.zeros((fk_ref.shape[0], size), BF16)
        for ref in (past_ref, step_ref):
            ref[...] = jnp.zeros_like(ref)

    @pl.when(level > 0)
    def _():
        write_key_features(last_ref[:, :DH], wk_ref, fk_ref.at[:, :size])
        for at, ref in ((0, past_ref), (half, step_ref)):
            ref[...] = jnp.dot(
                fk_ref[:, at : at + half],
                with_ones(last_ref[at : at + half, DH:]),
                preferred_element_type=F32,
            )


def past_kernel(first_ref, wk_ref, sum_ref, past_ref, fk_scr):
    level = spot()[1]

    @pl.when(level < 3)
    def _():
        past_ref[...] = sum_ref[...]

    @pl.when(level >= 3)
    def _():
        write_key_features(first_ref[:, :DH], wk_ref, fk_scr)
        past_ref[...] = sum_ref[...] + jnp.dot(
            fk_scr[...], with_ones(first_ref[:, DH:]), preferred_element_type=F32
        )


def query_features_kernel(a_ref, b_ref, w_ref, ratio_ref, q_out, fq_out, exp_scr):
    tok = a_ref.shape[0]
    heads, dh, both = w_ref.shape
    half = 2 * tok
    place = spot()[0]
    for d, ref in enumerate((a_ref, b_ref)):
        row = pl.multiple_of(lax.rem(place ^ d, 2) * tok, tok)
        for h in range(heads):
            q_out[pl.ds(h * half + row, tok), :] = ref[:, h * dh : (h + 1) * dh]
    rows_of = [slice(h * half, (h + 1) * half) for h in range(heads)]
    left = lax.broadcasted_iota(jnp.int32, (half, both), 1) < both // 2
    for h, rows in enumerate(rows_of):
        logits = jnp.dot(q_out[rows, :], w_ref[h], preferred_element_type=F32)
        top_l = jnp.max(jnp.where(left, logits, -jnp.inf), axis=1, keepdims=True)
        top_r = jnp.max(jnp.where(left, -jnp.inf, logits), axis=1, keepdims=True)
        exp_scr[rows, :] = jnp.exp((logits - jnp.where(left, top_l, top_r)).astype(BF16))
    side_r = lax.broadcasted_iota(jnp.int32, (both, both), 0) < both // 2
    side_c = lax.broadcasted_iota(jnp.int32, (both, both), 1) < both // 2
    halves = jnp.where(side_r == side_c, 1.0, 0.0).astype(BF16)
    total = jnp.dot(exp_scr[...], halves, preferred_element_type=F32)
    for h, rows in enumerate(rows_of):
        scale = pl.reciprocal(total[rows], approx=True) * ratio_ref[h : h + 1, :]
        fq_out[rows, :] = (exp_scr[rows, :].astype(F32) * scale).astype(BF16)


def near_kernel(other, q_ref, fq_ref, last_ref, own_ref, fk_ref, near_ref, kv_scr, w_scr):
    half, dh = last_ref.shape[0] // 2, q_ref.shape[1]
    heads = q_ref.shape[0] // half
    feats = fq_ref.shape[1]
    place, level = spot()
    u = lax.div(place, 2) ^ other
    kv_scr[:half, :] = last_ref[half:, :]
    kv_scr[half:, :] = own_ref[...]
    at = pl.ds(pl.multiple_of(u * half, half), 2 * half)
    keys, values = kv_scr[at, :dh], kv_scr[at, dh:]
    fk_at = pl.ds(pl.multiple_of((u + 1) * half, half), 2 * half)
    known = (level > 0) | (u > 0)
    cut = half - WINDOW
    row = lax.broadcasted_iota(jnp.int32, (WINDOW, 2 * half), 0)
    col = lax.broadcasted_iota(jnp.int32, (WINDOW, 2 * half), 1)
    inside = (col > row + cut) & (col <= row + half) & ((col >= half) | known)
    causal = (col <= row + cut)[:, :half]
    row, col = row[:, :half], col[:, :half]
    inside_low = (col > row) & (col <= row + WINDOW)
    causal_low = col <= row
    scores = dot_t(q_ref[...], keys)
    scale = math.log2(math.e) / math.sqrt(dh)

    def window(part, kept):
        masked = jnp.where(kept, part, -jnp.inf)
        top = jnp.max(masked, axis=1, keepdims=True)
        return jnp.exp2(((masked - top) * scale).astype(BF16))

    for h in range(heads):
        here = slice(h * half, (h + 1) * half)
        up, low = slice(h * half, h * half + cut), slice(h * half + cut, (h + 1) * half)
        linear = jnp.dot(
            fq_ref[here, :],
            fk_ref[h * feats : (h + 1) * feats, fk_at],
            preferred_element_type=F32,
        )
        soft = window(scores[up], inside)
        w_scr[up, :half] = soft[:, :half] + jnp.where(causal, linear[:cut, :half], 0.0).astype(BF16)
        w_scr[up, half:] = soft[:, half:]
        soft = window(scores[low, half:], inside_low)
        w_scr[low, :half] = linear[cut:, :half].astype(BF16)
        w_scr[low, half:] = soft + jnp.where(causal_low, linear[cut:, half:], 0.0).astype(BF16)
    values = jnp.concatenate(
        [with_ones(values[:half], known), with_ones(values[half:])], axis=0
    )
    near_ref[...] = jnp.dot(w_scr[...], values, preferred_element_type=F32)


def mix_kernel_of_level(*refs):
    near_refs, fq_refs, (past_ref, step_ref, wk_ref) = refs[:2], refs[2:4], refs[4:7]
    before_ref, refs = refs[7], refs[8:]
    out_refs, (fk_scr, state_scr, out_scr) = refs[:-3], refs[-3:]
    rows, dh = near_refs[0].shape[0], near_refs[0].shape[1] // 2
    feats = fq_refs[0].shape[1]
    heads = past_ref.shape[0] // feats
    half = rows // heads
    place, level = spot()
    side = lax.axis_index("head")
    u = lax.div(place, 2)

    @pl.when(level < 2)
    def _():
        state_scr[0] = past_ref[...].astype(BF16)
        state_scr[1] = (past_ref[...] + step_ref[...]).astype(BF16)

    @pl.when(level >= 2)
    def _():
        write_key_features(before_ref[:, :dh], wk_ref, fk_scr)
        state = past_ref[...] + jnp.dot(
            fk_scr[...], with_ones(before_ref[:, dh:]), preferred_element_type=F32
        )
        state_scr[0] = state.astype(BF16)
        state_scr[1] = (state + step_ref[...]).astype(BF16)

    part = out_refs[0].shape[0]
    for other in (1, 0):
        for h in range(heads):
            here = slice(h * half, (h + 1) * half)
            far = jnp.dot(
                fq_refs[other][here, :],
                state_scr[u ^ other, h * feats : (h + 1) * feats, :],
                preferred_element_type=F32,
            )
            both = near_refs[other][here, :] + far
            out_scr[aligned(u ^ other, half), h * dh : (h + 1) * dh] = (
                both[:, :dh] * pl.reciprocal(both[:, dh:], approx=True)
            ).astype(BF16)
    for n, ref in enumerate(out_refs):
        dr, dy = slot_of(n, lax.rem(place, 2))
        ref[...] = out_scr[aligned((place ^ dr) * 2 + (side ^ dy), part), :]


def whole_spec(space=pltpu.VMEM):
    return pl.BlockSpec(memory_space=space)


def call(kernel, ins, outs, name, scratch=(), limit=4, out_type=BF16, aliases={}):
    return pl.pallas_call(
        kernel,
        in_specs=[whole_spec() for _ in ins],
        out_specs=[whole_spec() for _ in outs],
        out_shape=[
            jax.ShapeDtypeStruct(s, out_type[n] if isinstance(out_type, list) else out_type)
            for n, s in enumerate(outs)
        ],
        scratch_shapes=list(scratch),
        input_output_aliases=aliases,
        cost_estimate=EARLY if name in EARLY_KERNELS else None,
        compiler_params=pltpu.CompilerParams(vmem_limit_bytes=limit * 2**20),
        name=name,
    )(*ins)


def by_levels(queries, keys, values, wq, wk, factor):
    tok, width = queries.shape
    local_heads, feat, dh = wq.shape
    heads = local_heads // WAYS
    seq, sides = lax.axis_size("seq"), lax.axis_size("head")
    half = 2 * tok
    rows, states = heads * half, heads * 2 * feat

    def partner(x, dr, dy=0):
        pairs = [
            (i * sides + j, (i // WAYS * WAYS + (i % WAYS ^ dr)) * sides + (j ^ dy))
            for i in range(seq)
            for j in range(sides)
        ]
        return lax.ppermute(x, ("seq", "head"), pairs)

    def levels_back(x, by):
        pairs = [(i, i + by * WAYS) for i in range(seq - by * WAYS)]
        return lax.ppermute(x, "seq", pairs)

    place = lax.rem(lax.axis_index("seq"), WAYS)
    ours = place // 2 * 2 * dh
    cuts = [
        lax.dynamic_slice_in_dim(x, at, 2 * dh, 1)
        for at in (ours, 2 * dh - ours)
        for x in (keys, values)
    ]
    own, away = call(pack_kv_kernel, cuts, [(tok, 4 * dh)] * 2, "pack_kv")
    got = partner(away, 2)
    queries, away = lax.optimization_barrier((queries, away))
    q = list(call(pack_q_kernel, [queries], [(tok, width // WAYS)] * WAYS, "pack_q"))
    q[2], q[3] = partner(q[2], 2), partner(q[3], 3)
    (pair,) = call(pair_kernel, [own, got], [(half, 2 * dh)], "pair_kv")
    pair, q[1], wq, wk = lax.optimization_barrier((pair, q[1], wq, wk))
    pair, q[1] = partner(pair, 1), partner(q[1], 1)
    wq, wk = [lax.dynamic_slice_in_dim(w, place * heads, heads) for w in (wq, wk)]
    pair, wq, wk = lax.optimization_barrier((pair, wq, wk))
    (kv,) = call(stack_kernel, [own, got, pair], [(2 * half, 2 * dh)], "stack_kv")
    last, first = levels_back(kv, 1), levels_back(kv, 3)
    wq, kv, q[1] = lax.optimization_barrier((wq, kv, q[1]))
    before = levels_back(kv, 2)
    (fk,) = call(own_features_kernel, [kv, wk], [(states, 4 * half)], "own_features", limit=16)
    wq, ratio = call(
        weights_kernel,
        [wq, factor.reshape(1, local_heads)],
        [(heads, dh, 2 * feat), (heads, 2 * feat)],
        "weights",
        out_type=[BF16, F32],
    )

    def query_features(a, b):
        return call(
            query_features_kernel,
            [a, b, wq, ratio],
            [(rows, dh), (rows, 2 * feat)],
            "query_features",
            [pltpu.VMEM((rows, 2 * feat), BF16)],
            12,
        )

    def near(other, q_rows, fq):
        return call(
            lambda *refs: near_kernel(other, *refs),
            [q_rows, fq, last, kv, fk],
            [(rows, 2 * dh)],
            "near",
            [
                pltpu.VMEM((3 * half, 2 * dh), BF16),
                pltpu.VMEM((rows, 2 * half), BF16),
            ],
            16,
            F32,
        )[0]

    q_own, fq_own = query_features(q[0], q[1])
    last, fq_own, fk = lax.optimization_barrier((last, fq_own, fk))
    fk, past, step = call(
        last_features_kernel,
        [last, wk, fk],
        [(states, 4 * half), (states, 2 * dh), (states, 2 * dh)],
        "last_features",
        limit=20,
        out_type=[BF16, F32, F32],
        aliases={2: 0},
    )
    near_own = near(0, q_own, fq_own)
    q[2], q[3], near_own = lax.optimization_barrier((q[2], q[3], near_own))
    q_other, fq_other = query_features(q[2], q[3])
    near_other = near(1, q_other, fq_other)
    first, near_other = lax.optimization_barrier((first, near_other))
    (past,) = call(
        past_kernel,
        [first, wk, past],
        [(states, 2 * dh)],
        "past",
        [pltpu.VMEM((states, 2 * half), BF16)],
        16,
        F32,
    )
    before, past = lax.optimization_barrier((before, past))
    part = tok // sides
    outs = call(
        mix_kernel_of_level,
        [near_own, near_other, fq_own, fq_other, past, step, wk, before],
        [(part, heads * dh)] * (WAYS * sides),
        "mix_level",
        [
            pltpu.VMEM((states, 2 * half), BF16),
            pltpu.VMEM((2, states, 2 * dh), BF16),
            pltpu.VMEM((2 * half, heads * dh), BF16),
        ],
        24,
    )

    def sent(x, slot):
        pairs = []
        for i in range(seq):
            dr, dy = slot[i % 2]
            to = i // WAYS * WAYS + (i % WAYS ^ dr)
            pairs += [(i * sides + j, to * sides + (j ^ dy)) for j in range(sides)]
        return lax.ppermute(x, ("seq", "head"), pairs)

    outs = list(outs)
    for n in range(1, 6):
        outs[n] = sent(outs[n], SLOTS[n])
    outs[6], outs[7], outs[1] = lax.optimization_barrier((outs[6], outs[7], outs[1]))
    outs[6], outs[7] = sent(outs[6], SLOTS[6]), sent(outs[7], SLOTS[7])

    def joined(slots, into):
        return pl.pallas_call(
            lambda *refs: join_kernel(slots, *refs),
            in_specs=[whole_spec()] * len(slots) + [whole_spec(pltpu.HBM)] * len(into),
            out_specs=whole_spec(pltpu.HBM),
            out_shape=jax.ShapeDtypeStruct((part, sides * WAYS * heads * dh), BF16),
            input_output_aliases={len(slots): 0} if into else {},
            scratch_shapes=[pltpu.SemaphoreType.DMA((len(slots),))],
            compiler_params=pltpu.CompilerParams(vmem_limit_bytes=4 * 2**20),
            name="join",
        )(*[outs[n] for n in slots], *into)

    return joined((4, 5, 6, 7), [joined((0, 1, 2, 3), [])])


def by_blocks(queries, keys, values, wq, wk, ratio):
    group = wq.shape[0] // (keys.shape[1] // DH)
    place = lax.axis_index("seq").astype(jnp.int32).reshape(1)
    kv = lax.all_gather(jnp.concatenate([keys, values], axis=1), "seq", tiled=True)
    out = mix(place, queries, kv, wq, wk, ratio, group)
    return lax.all_to_all(out, "head", split_axis=0, concat_axis=1, tiled=True)


def local(queries, keys, values, q_feature, k_feature, window_factor):
    tok = queries.shape[0]
    seq, sides = lax.axis_size("seq"), lax.axis_size("head")
    wq, wk = jnp.swapaxes(q_feature, 1, 2), jnp.swapaxes(k_feature, 1, 2)
    if keys.shape[1] == WAYS * DH and seq == 4 * WAYS and sides == 2 and tok == WINDOW:
        return by_levels(queries, keys, values, wq, wk, window_factor)
    ratio = window_factor / (1.0 - window_factor)
    return by_blocks(queries, keys, values, wq, wk, ratio)


def solution(mesh):
    return jax.shard_map(
        local,
        mesh=mesh,
        in_specs=(
            P("seq", "head"),
            P("seq", "head"),
            P("seq", "head"),
            P("head", None, None),
            P("head", None, None),
            P("head"),
        ),
        out_specs=P(("seq", "head"), None),
        check_vma=False,
    )
```

```python
import math

import jax
import jax.numpy as jnp
from jax import lax
from jax.experimental import pallas as pl
from jax.experimental.pallas import tpu as pltpu
from jax.sharding import PartitionSpec as P

DH = 128
WINDOW = 64
F32 = jnp.float32
BF16 = jnp.bfloat16


def dot_t(a, b):
    return lax.dot_general(a, b, (((1,), (1,)), ((), ())), preferred_element_type=F32)


def features_t(logits):
    top = jnp.max(logits, axis=0, keepdims=True)
    low = jnp.min(logits, axis=0, keepdims=True)
    up = jnp.exp(logits - top)
    down = jnp.exp(low - logits)
    up = up * (1.0 / jnp.sum(up, axis=0, keepdims=True))
    down = down * (1.0 / jnp.sum(down, axis=0, keepdims=True))
    return jnp.concatenate([up.astype(BF16), down.astype(BF16)], axis=0)


def mix_kernel(
    place_ref, q_ref, k_ref, v_ref, wq_ref, wk_ref, ratio_ref, out_ref, fk_scr, state_scr
):
    tok = q_ref.shape[0]
    heads, feat, dh = wq_ref.shape
    seen = fk_scr.shape[1]
    place = place_ref[0]
    first_head = pl.program_id(0) * heads

    weights = wk_ref[...].reshape(heads * feat, dh)
    for start in range(0, seen, 256):
        size = min(256, seen - start)
        logits = dot_t(weights, k_ref[start : start + size, :])
        for h in range(heads):
            fk_scr[h * 2 * feat : (h + 1) * 2 * feat, start : start + size] = features_t(
                logits[h * feat : (h + 1) * feat]
            )
    row = lax.broadcasted_iota(jnp.int32, (seen, dh), 0)
    kept = row < (place - 1) * tok
    v_seen = jnp.where(kept, v_ref[:seen, :].astype(F32), 0.0).astype(BF16)
    ones_seen = jnp.where(kept, 1.0, 0.0).astype(BF16)
    v_seen = jnp.concatenate([v_seen, ones_seen], axis=1)
    state_scr[...] = jnp.dot(fk_scr[...], v_seen, preferred_element_type=F32).astype(BF16)

    before = pl.multiple_of(jnp.maximum(place - 1, 0) * tok, tok)
    own = pl.multiple_of(place * tok, tok)
    k_ext = jnp.concatenate([k_ref[pl.ds(before, tok), :], k_ref[pl.ds(own, tok), :]], axis=0)
    v_ext = jnp.concatenate([v_ref[pl.ds(before, tok), :], v_ref[pl.ds(own, tok), :]], axis=0)
    v_ext = jnp.concatenate([v_ext, jnp.ones_like(v_ext)], axis=1)
    row = lax.broadcasted_iota(jnp.int32, (tok, 2 * tok), 0)
    col = lax.broadcasted_iota(jnp.int32, (tok, 2 * tok), 1)
    valid = (col >= tok) | (place > 0)
    inside = (col > row) & (col <= row + WINDOW) & valid
    causal = (col <= row) & valid
    lane = lax.broadcasted_iota(jnp.int32, (tok, 2 * feat), 1)
    left = lane < feat
    side_r = lax.broadcasted_iota(jnp.int32, (2 * feat, 2 * feat), 0) < feat
    side_c = lax.broadcasted_iota(jnp.int32, (2 * feat, 2 * feat), 1) < feat
    halves = jnp.where(side_r == side_c, 1.0, 0.0).astype(BF16)

    for h in range(heads):
        q = q_ref[:, h * dh : (h + 1) * dh]
        wq = wq_ref[h]
        logits = dot_t(q, jnp.concatenate([wq, -wq], axis=0))
        top_l = jnp.max(jnp.where(left, logits, -jnp.inf), axis=1, keepdims=True)
        top_r = jnp.max(jnp.where(left, -jnp.inf, logits), axis=1, keepdims=True)
        expd = jnp.exp(logits - jnp.where(left, top_l, top_r)).astype(BF16)
        total = jnp.dot(expd, halves, preferred_element_type=F32)
        fq = (expd.astype(F32) / total).astype(BF16)
        fk = features_t(dot_t(wk_ref[h], k_ext))
        linear = jnp.dot(fq, fk, preferred_element_type=F32)
        scores = dot_t(q, k_ext) * (1.0 / math.sqrt(dh))
        masked = jnp.where(inside, scores, -jnp.inf)
        top = jnp.max(masked, axis=1, keepdims=True)
        soft = jnp.exp(masked - top) * ratio_ref[first_head + h]
        weight = jnp.where(causal, linear, soft).astype(BF16)
        both = jnp.dot(weight, v_ext, preferred_element_type=F32) + jnp.dot(
            fq, state_scr[h * 2 * feat : (h + 1) * 2 * feat, :], preferred_element_type=F32
        )
        out_ref[:, h * dh : (h + 1) * dh] = (both[:, :dh] / both[:, dh:]).astype(BF16)


def mix(place, queries, kv, wq, wk, ratio, group):
    tok = queries.shape[0]
    local_heads, feat, dh = wq.shape
    groups = local_heads // group
    tokens = kv.shape[0]
    seen = tokens - 2 * tok
    return pl.pallas_call(
        mix_kernel,
        grid_spec=pltpu.PrefetchScalarGridSpec(
            num_scalar_prefetch=1,
            grid=(groups,),
            in_specs=[
                pl.BlockSpec((tok, group * dh), lambda g, p: (0, g)),
                pl.BlockSpec((tokens, dh), lambda g, p: (0, g)),
                pl.BlockSpec((tokens, dh), lambda g, p: (0, groups + g)),
                pl.BlockSpec((group, feat, dh), lambda g, p: (g, 0, 0)),
                pl.BlockSpec((group, feat, dh), lambda g, p: (g, 0, 0)),
                pl.BlockSpec(memory_space=pltpu.SMEM),
            ],
            out_specs=pl.BlockSpec((tok, group * dh), lambda g, p: (0, g)),
            scratch_shapes=[
                pltpu.VMEM((group * 2 * feat, seen), BF16),
                pltpu.VMEM((group * 2 * feat, 2 * dh), BF16),
            ],
        ),
        out_shape=jax.ShapeDtypeStruct(queries.shape, BF16),
        compiler_params=pltpu.CompilerParams(vmem_limit_bytes=48 * 2**20),
        cost_estimate=pl.CostEstimate(
            flops=2 * local_heads * tokens * 3 * feat * 2 * dh,
            bytes_accessed=8 * 2**20,
            transcendentals=local_heads * tokens * 2 * feat,
        ),
    )(place, queries, kv, kv, wq, wk, ratio)


WAYS = 4

EARLY = pl.CostEstimate(flops=10**10, bytes_accessed=10**8, transcendentals=0)
EARLY_KERNELS = ("pack_kv", "pack_q", "pair_kv", "stack_kv")


SLOTS = (
    ((0, 0), (0, 0)),
    ((2, 1), (2, 1)),
    ((2, 0), (0, 1)),
    ((0, 1), (2, 0)),
    ((3, 1), (3, 1)),
    ((3, 0), (1, 1)),
    ((1, 1), (3, 0)),
    ((1, 0), (1, 0)),
)


def slot_of(n, odd):
    return [jnp.where(odd == 1, b, a) if a != b else a for a, b in zip(*SLOTS[n])]


def spot():
    at = lax.axis_index("seq")
    return lax.rem(at, WAYS), lax.div(at, WAYS)


def aligned(at, step):
    return pl.ds(pl.multiple_of(at * step, step), step)


def with_ones(values, kept=True):
    here = jnp.where(kept, 1.0, 0.0).astype(BF16)
    return jnp.concatenate([values, jnp.full(values.shape, here)], axis=1)


def pack_kv_kernel(k_ref, v_ref, k_away_ref, v_away_ref, own_ref, away_ref):
    odd = lax.rem(spot()[0], 2)
    for k, v, ref in ((k_ref, v_ref, own_ref), (k_away_ref, v_away_ref, away_ref)):
        for d in range(2):
            at = aligned(odd ^ d, DH)
            ref[:, 2 * d * DH : (2 * d + 1) * DH] = k[:, at]
            ref[:, (2 * d + 1) * DH : (2 * d + 2) * DH] = v[:, at]


def pair_kernel(own_ref, got_ref, out_ref):
    tok = own_ref.shape[0]
    out_ref[:tok, :] = own_ref[:, 2 * DH :]
    out_ref[tok:, :] = got_ref[:, 2 * DH :]


def stack_kernel(own_ref, got_ref, pair_ref, out_ref):
    tok = own_ref.shape[0]
    place = spot()[0]
    out_ref[aligned(place, tok), :] = own_ref[:, : 2 * DH]
    out_ref[aligned(place ^ 2, tok), :] = got_ref[:, : 2 * DH]
    out_ref[aligned(place ^ 1, tok), :] = pair_ref[:tok, :]
    out_ref[aligned(place ^ 3, tok), :] = pair_ref[tok:, :]


def pack_q_kernel(q_ref, *out_refs):
    place = spot()[0]
    for d, out in enumerate(out_refs):
        out[...] = q_ref[:, aligned(place ^ d, out.shape[1])]


def weights_kernel(wq_ref, factor_ref, both_ref, ratio_ref):
    heads = both_ref.shape[0]
    shape = (heads, factor_ref.shape[1])
    head = lax.broadcasted_iota(jnp.int32, shape, 0) + spot()[0] * heads
    ratio = jnp.broadcast_to((1.0 - factor_ref[...]) / factor_ref[...], shape)
    ratio = jnp.where(lax.broadcasted_iota(jnp.int32, shape, 1) == head, ratio, 0.0)
    ratio = jnp.sum(ratio, axis=1, keepdims=True)
    ratio_ref[...] = jnp.broadcast_to(ratio, ratio_ref.shape)
    for h in range(heads):
        wq = wq_ref[h].T
        both_ref[h] = jnp.concatenate([wq, -wq], axis=1)


def join_kernel(slots, *refs):
    got, out_ref, sems = refs[: len(slots)], *refs[-2:]
    width = got[0].shape[1]
    place, side = spot()[0], lax.axis_index("head")
    copies = []
    for n, ref in zip(slots, got):
        dr, dy = slot_of(n, lax.rem(place, 2) ^ (SLOTS[n][0][0] & 1))
        at = aligned((side ^ dy) * WAYS + (place ^ dr), width)
        copies.append(pltpu.make_async_copy(ref, out_ref.at[:, at], sems.at[len(copies)]))
    for copy in copies:
        copy.start()
    for copy in copies:
        copy.wait()


def write_key_features(keys, wk_ref, fk_ref):
    heads, feat, dh = wk_ref.shape
    logits = dot_t(wk_ref[...].reshape(heads * feat, dh), keys)
    for h in range(heads):
        part = logits[h * feat : (h + 1) * feat]
        top = jnp.max(part, axis=0, keepdims=True)
        low = jnp.min(part, axis=0, keepdims=True)
        for n, shifted in enumerate((part - top, low - part)):
            row = (2 * h + n) * feat
            expd = jnp.exp(shifted.astype(BF16))
            total = expd[: feat // 4]
            for q in range(1, 4):
                total = total + expd[q * feat // 4 : (q + 1) * feat // 4]
            total = jnp.sum(total.astype(F32), axis=0, keepdims=True)
            fk_ref[row : row + feat, :] = expd * pl.reciprocal(total, approx=True).astype(BF16)


def own_features_kernel(own_ref, wk_ref, fk_ref):
    write_key_features(own_ref[:, :DH], wk_ref, fk_ref.at[:, own_ref.shape[0] :])


def last_features_kernel(last_ref, wk_ref, _, fk_ref, past_ref, step_ref):
    size = last_ref.shape[0]
    half = size // 2
    level = spot()[1]

    @pl.when(level == 0)
    def _():
        fk_ref[:, :size] = jnp.zeros((fk_ref.shape[0], size), BF16)
        for ref in (past_ref, step_ref):
            ref[...] = jnp.zeros_like(ref)

    @pl.when(level > 0)
    def _():
        write_key_features(last_ref[:, :DH], wk_ref, fk_ref.at[:, :size])
        for at, ref in ((0, past_ref), (half, step_ref)):
            ref[...] = jnp.dot(
                fk_ref[:, at : at + half],
                with_ones(last_ref[at : at + half, DH:]),
                preferred_element_type=F32,
            )


def past_kernel(first_ref, wk_ref, sum_ref, past_ref, fk_scr):
    level = spot()[1]

    @pl.when(level < 3)
    def _():
        past_ref[...] = sum_ref[...]

    @pl.when(level >= 3)
    def _():
        write_key_features(first_ref[:, :DH], wk_ref, fk_scr)
        past_ref[...] = sum_ref[...] + jnp.dot(
            fk_scr[...], with_ones(first_ref[:, DH:]), preferred_element_type=F32
        )


def query_features_kernel(a_ref, b_ref, w_ref, ratio_ref, q_out, fq_out, exp_scr):
    tok = a_ref.shape[0]
    heads, dh, both = w_ref.shape
    half = 2 * tok
    place = spot()[0]
    for d, ref in enumerate((a_ref, b_ref)):
        row = pl.multiple_of(lax.rem(place ^ d, 2) * tok, tok)
        for h in range(heads):
            q_out[pl.ds(h * half + row, tok), :] = ref[:, h * dh : (h + 1) * dh]
    rows_of = [slice(h * half, (h + 1) * half) for h in range(heads)]
    left = lax.broadcasted_iota(jnp.int32, (half, both), 1) < both // 2
    for h, rows in enumerate(rows_of):
        logits = jnp.dot(q_out[rows, :], w_ref[h], preferred_element_type=F32)
        top_l = jnp.max(jnp.where(left, logits, -jnp.inf), axis=1, keepdims=True)
        top_r = jnp.max(jnp.where(left, -jnp.inf, logits), axis=1, keepdims=True)
        exp_scr[rows, :] = jnp.exp((logits - jnp.where(left, top_l, top_r)).astype(BF16))
    side_r = lax.broadcasted_iota(jnp.int32, (both, both), 0) < both // 2
    side_c = lax.broadcasted_iota(jnp.int32, (both, both), 1) < both // 2
    halves = jnp.where(side_r == side_c, 1.0, 0.0).astype(BF16)
    total = jnp.dot(exp_scr[...], halves, preferred_element_type=F32)
    for h, rows in enumerate(rows_of):
        scale = pl.reciprocal(total[rows], approx=True) * ratio_ref[h : h + 1, :]
        fq_out[rows, :] = (exp_scr[rows, :].astype(F32) * scale).astype(BF16)


def near_kernel(other, q_ref, fq_ref, last_ref, own_ref, fk_ref, near_ref, kv_scr, w_scr):
    half, dh = last_ref.shape[0] // 2, q_ref.shape[1]
    heads = q_ref.shape[0] // half
    feats = fq_ref.shape[1]
    place, level = spot()
    u = lax.div(place, 2) ^ other
    kv_scr[:half, :] = last_ref[half:, :]
    kv_scr[half:, :] = own_ref[...]
    at = pl.ds(pl.multiple_of(u * half, half), 2 * half)
    keys, values = kv_scr[at, :dh], kv_scr[at, dh:]
    fk_at = pl.ds(pl.multiple_of((u + 1) * half, half), 2 * half)
    known = (level > 0) | (u > 0)
    cut = half - WINDOW
    row = lax.broadcasted_iota(jnp.int32, (WINDOW, 2 * half), 0)
    col = lax.broadcasted_iota(jnp.int32, (WINDOW, 2 * half), 1)
    inside = (col > row + cut) & (col <= row + half) & ((col >= half) | known)
    causal = (col <= row + cut)[:, :half]
    row, col = row[:, :half], col[:, :half]
    inside_low = (col > row) & (col <= row + WINDOW)
    causal_low = col <= row
    scores = dot_t(q_ref[...], keys)
    scale = math.log2(math.e) / math.sqrt(dh)

    def window(part, kept):
        masked = jnp.where(kept, part, -jnp.inf)
        top = jnp.max(masked, axis=1, keepdims=True)
        return jnp.exp2(((masked - top) * scale).astype(BF16))

    for h in range(heads):
        here = slice(h * half, (h + 1) * half)
        up, low = slice(h * half, h * half + cut), slice(h * half + cut, (h + 1) * half)
        linear = jnp.dot(
            fq_ref[here, :],
            fk_ref[h * feats : (h + 1) * feats, fk_at],
            preferred_element_type=F32,
        )
        soft = window(scores[up], inside)
        w_scr[up, :half] = soft[:, :half] + jnp.where(causal, linear[:cut, :half], 0.0).astype(BF16)
        w_scr[up, half:] = soft[:, half:]
        soft = window(scores[low, half:], inside_low)
        w_scr[low, :half] = linear[cut:, :half].astype(BF16)
        w_scr[low, half:] = soft + jnp.where(causal_low, linear[cut:, half:], 0.0).astype(BF16)
    values = jnp.concatenate(
        [with_ones(values[:half], known), with_ones(values[half:])], axis=0
    )
    near_ref[...] = jnp.dot(w_scr[...], values, preferred_element_type=F32)


def mix_kernel_of_level(*refs):
    near_refs, fq_refs, (past_ref, step_ref, wk_ref) = refs[:2], refs[2:4], refs[4:7]
    before_ref, refs = refs[7], refs[8:]
    out_refs, (fk_scr, state_scr, out_scr) = refs[:-3], refs[-3:]
    rows, dh = near_refs[0].shape[0], near_refs[0].shape[1] // 2
    feats = fq_refs[0].shape[1]
    heads = past_ref.shape[0] // feats
    half = rows // heads
    place, level = spot()
    side = lax.axis_index("head")
    u = lax.div(place, 2)

    @pl.when(level < 2)
    def _():
        state_scr[0] = past_ref[...].astype(BF16)
        state_scr[1] = (past_ref[...] + step_ref[...]).astype(BF16)

    @pl.when(level >= 2)
    def _():
        write_key_features(before_ref[:, :dh], wk_ref, fk_scr)
        state = past_ref[...] + jnp.dot(
            fk_scr[...], with_ones(before_ref[:, dh:]), preferred_element_type=F32
        )
        state_scr[0] = state.astype(BF16)
        state_scr[1] = (state + step_ref[...]).astype(BF16)

    part = out_refs[0].shape[0]
    for other in (1, 0):
        for h in range(heads):
            here = slice(h * half, (h + 1) * half)
            far = jnp.dot(
                fq_refs[other][here, :],
                state_scr[u ^ other, h * feats : (h + 1) * feats, :],
                preferred_element_type=F32,
            )
            both = near_refs[other][here, :] + far
            out_scr[aligned(u ^ other, half), h * dh : (h + 1) * dh] = (
                both[:, :dh] * pl.reciprocal(both[:, dh:], approx=True)
            ).astype(BF16)
    for n, ref in enumerate(out_refs):
        dr, dy = slot_of(n, lax.rem(place, 2))
        ref[...] = out_scr[aligned((place ^ dr) * 2 + (side ^ dy), part), :]


def whole_spec(space=pltpu.VMEM):
    return pl.BlockSpec(memory_space=space)


def call(kernel, ins, outs, name, scratch=(), limit=4, out_type=BF16, aliases={}):
    return pl.pallas_call(
        kernel,
        in_specs=[whole_spec() for _ in ins],
        out_specs=[whole_spec() for _ in outs],
        out_shape=[
            jax.ShapeDtypeStruct(s, out_type[n] if isinstance(out_type, list) else out_type)
            for n, s in enumerate(outs)
        ],
        scratch_shapes=list(scratch),
        input_output_aliases=aliases,
        cost_estimate=EARLY if name in EARLY_KERNELS else None,
        compiler_params=pltpu.CompilerParams(vmem_limit_bytes=limit * 2**20),
        name=name,
    )(*ins)


def by_levels(queries, keys, values, wq, wk, factor):
    tok, width = queries.shape
    local_heads, feat, dh = wq.shape
    heads = local_heads // WAYS
    seq, sides = lax.axis_size("seq"), lax.axis_size("head")
    half = 2 * tok
    rows, states = heads * half, heads * 2 * feat

    def partner(x, dr, dy=0):
        pairs = [
            (i * sides + j, (i // WAYS * WAYS + (i % WAYS ^ dr)) * sides + (j ^ dy))
            for i in range(seq)
            for j in range(sides)
        ]
        return lax.ppermute(x, ("seq", "head"), pairs)

    def levels_back(x, by):
        pairs = [(i, i + by * WAYS) for i in range(seq - by * WAYS)]
        return lax.ppermute(x, "seq", pairs)

    place = lax.rem(lax.axis_index("seq"), WAYS)
    ours = place // 2 * 2 * dh
    cuts = [
        lax.dynamic_slice_in_dim(x, at, 2 * dh, 1)
        for at in (ours, 2 * dh - ours)
        for x in (keys, values)
    ]
    own, away = call(pack_kv_kernel, cuts, [(tok, 4 * dh)] * 2, "pack_kv")
    got = partner(away, 2)
    queries, away = lax.optimization_barrier((queries, away))
    q = list(call(pack_q_kernel, [queries], [(tok, width // WAYS)] * WAYS, "pack_q"))
    q[2], q[3] = partner(q[2], 2), partner(q[3], 3)
    (pair,) = call(pair_kernel, [own, got], [(half, 2 * dh)], "pair_kv")
    pair, q[1], wq, wk = lax.optimization_barrier((pair, q[1], wq, wk))
    pair, q[1] = partner(pair, 1), partner(q[1], 1)
    wq, wk = [lax.dynamic_slice_in_dim(w, place * heads, heads) for w in (wq, wk)]
    pair, wq, wk = lax.optimization_barrier((pair, wq, wk))
    (kv,) = call(stack_kernel, [own, got, pair], [(2 * half, 2 * dh)], "stack_kv")
    last, first = levels_back(kv, 1), levels_back(kv, 3)
    wq, kv, q[1] = lax.optimization_barrier((wq, kv, q[1]))
    before = levels_back(kv, 2)
    (fk,) = call(own_features_kernel, [kv, wk], [(states, 4 * half)], "own_features", limit=16)
    wq, ratio = call(
        weights_kernel,
        [wq, factor.reshape(1, local_heads)],
        [(heads, dh, 2 * feat), (heads, 2 * feat)],
        "weights",
        out_type=[BF16, F32],
    )

    def query_features(a, b):
        return call(
            query_features_kernel,
            [a, b, wq, ratio],
            [(rows, dh), (rows, 2 * feat)],
            "query_features",
            [pltpu.VMEM((rows, 2 * feat), BF16)],
            12,
        )

    def near(other, q_rows, fq):
        return call(
            lambda *refs: near_kernel(other, *refs),
            [q_rows, fq, last, kv, fk],
            [(rows, 2 * dh)],
            "near",
            [
                pltpu.VMEM((3 * half, 2 * dh), BF16),
                pltpu.VMEM((rows, 2 * half), BF16),
            ],
            16,
            F32,
        )[0]

    q_own, fq_own = query_features(q[0], q[1])
    last, fq_own, fk = lax.optimization_barrier((last, fq_own, fk))
    fk, past, step = call(
        last_features_kernel,
        [last, wk, fk],
        [(states, 4 * half), (states, 2 * dh), (states, 2 * dh)],
        "last_features",
        limit=20,
        out_type=[BF16, F32, F32],
        aliases={2: 0},
    )
    near_own = near(0, q_own, fq_own)
    q[2], q[3], near_own = lax.optimization_barrier((q[2], q[3], near_own))
    q_other, fq_other = query_features(q[2], q[3])
    near_other = near(1, q_other, fq_other)
    first, near_other = lax.optimization_barrier((first, near_other))
    (past,) = call(
        past_kernel,
        [first, wk, past],
        [(states, 2 * dh)],
        "past",
        [pltpu.VMEM((states, 2 * half), BF16)],
        16,
        F32,
    )
    before, past = lax.optimization_barrier((before, past))
    part = tok // sides
    outs = call(
        mix_kernel_of_level,
        [near_own, near_other, fq_own, fq_other, past, step, wk, before],
        [(part, heads * dh)] * (WAYS * sides),
        "mix_level",
        [
            pltpu.VMEM((states, 2 * half), BF16),
            pltpu.VMEM((2, states, 2 * dh), BF16),
            pltpu.VMEM((2 * half, heads * dh), BF16),
        ],
        24,
    )

    def sent(x, slot):
        pairs = []
        for i in range(seq):
            dr, dy = slot[i % 2]
            to = i // WAYS * WAYS + (i % WAYS ^ dr)
            pairs += [(i * sides + j, to * sides + (j ^ dy)) for j in range(sides)]
        return lax.ppermute(x, ("seq", "head"), pairs)

    outs = list(outs)
    for n in range(1, 6):
        outs[n] = sent(outs[n], SLOTS[n])
    outs[6], outs[7], outs[1] = lax.optimization_barrier((outs[6], outs[7], outs[1]))
    outs[6], outs[7] = sent(outs[6], SLOTS[6]), sent(outs[7], SLOTS[7])

    def joined(slots, into):
        return pl.pallas_call(
            lambda *refs: join_kernel(slots, *refs),
            in_specs=[whole_spec()] * len(slots) + [whole_spec(pltpu.HBM)] * len(into),
            out_specs=whole_spec(pltpu.HBM),
            out_shape=jax.ShapeDtypeStruct((part, sides * WAYS * heads * dh), BF16),
            input_output_aliases={len(slots): 0} if into else {},
            scratch_shapes=[pltpu.SemaphoreType.DMA((len(slots),))],
            compiler_params=pltpu.CompilerParams(vmem_limit_bytes=4 * 2**20),
            name="join",
        )(*[outs[n] for n in slots], *into)

    return joined((4, 5, 6, 7), [joined((0, 1, 2, 3), [])])


def by_blocks(queries, keys, values, wq, wk, ratio):
    group = wq.shape[0] // (keys.shape[1] // DH)
    place = lax.axis_index("seq").astype(jnp.int32).reshape(1)
    kv = lax.all_gather(jnp.concatenate([keys, values], axis=1), "seq", tiled=True)
    out = mix(place, queries, kv, wq, wk, ratio, group)
    return lax.all_to_all(out, "head", split_axis=0, concat_axis=1, tiled=True)


def local(queries, keys, values, q_feature, k_feature, window_factor):
    tok = queries.shape[0]
    seq, sides = lax.axis_size("seq"), lax.axis_size("head")
    wq, wk = jnp.swapaxes(q_feature, 1, 2), jnp.swapaxes(k_feature, 1, 2)
    if keys.shape[1] == WAYS * DH and seq == 4 * WAYS and sides == 2 and tok == WINDOW:
        return by_levels(queries, keys, values, wq, wk, window_factor)
    ratio = window_factor / (1.0 - window_factor)
    return by_blocks(queries, keys, values, wq, wk, ratio)


def solution(mesh):
    return jax.shard_map(
        local,
        mesh=mesh,
        in_specs=(
            P("seq", "head"),
            P("seq", "head"),
            P("seq", "head"),
            P("head", None, None),
            P("head", None, None),
            P("head"),
        ),
        out_specs=P(("seq", "head"), None),
        check_vma=False,
    )
```

```python
import math

import jax
import jax.numpy as jnp
from jax import lax
from jax.experimental import pallas as pl
from jax.experimental.pallas import tpu as pltpu
from jax.sharding import PartitionSpec as P

DH = 128
WINDOW = 64
F32 = jnp.float32
BF16 = jnp.bfloat16


def dot_t(a, b):
    return lax.dot_general(a, b, (((1,), (1,)), ((), ())), preferred_element_type=F32)


def features_t(logits):
    top = jnp.max(logits, axis=0, keepdims=True)
    low = jnp.min(logits, axis=0, keepdims=True)
    up = jnp.exp(logits - top)
    down = jnp.exp(low - logits)
    up = up * (1.0 / jnp.sum(up, axis=0, keepdims=True))
    down = down * (1.0 / jnp.sum(down, axis=0, keepdims=True))
    return jnp.concatenate([up.astype(BF16), down.astype(BF16)], axis=0)


def mix_kernel(
    place_ref, q_ref, k_ref, v_ref, wq_ref, wk_ref, ratio_ref, out_ref, fk_scr, state_scr
):
    tok = q_ref.shape[0]
    heads, feat, dh = wq_ref.shape
    seen = fk_scr.shape[1]
    place = place_ref[0]
    first_head = pl.program_id(0) * heads

    weights = wk_ref[...].reshape(heads * feat, dh)
    for start in range(0, seen, 256):
        size = min(256, seen - start)
        logits = dot_t(weights, k_ref[start : start + size, :])
        for h in range(heads):
            fk_scr[h * 2 * feat : (h + 1) * 2 * feat, start : start + size] = features_t(
                logits[h * feat : (h + 1) * feat]
            )
    row = lax.broadcasted_iota(jnp.int32, (seen, dh), 0)
    kept = row < (place - 1) * tok
    v_seen = jnp.where(kept, v_ref[:seen, :].astype(F32), 0.0).astype(BF16)
    ones_seen = jnp.where(kept, 1.0, 0.0).astype(BF16)
    v_seen = jnp.concatenate([v_seen, ones_seen], axis=1)
    state_scr[...] = jnp.dot(fk_scr[...], v_seen, preferred_element_type=F32).astype(BF16)

    before = pl.multiple_of(jnp.maximum(place - 1, 0) * tok, tok)
    own = pl.multiple_of(place * tok, tok)
    k_ext = jnp.concatenate([k_ref[pl.ds(before, tok), :], k_ref[pl.ds(own, tok), :]], axis=0)
    v_ext = jnp.concatenate([v_ref[pl.ds(before, tok), :], v_ref[pl.ds(own, tok), :]], axis=0)
    v_ext = jnp.concatenate([v_ext, jnp.ones_like(v_ext)], axis=1)
    row = lax.broadcasted_iota(jnp.int32, (tok, 2 * tok), 0)
    col = lax.broadcasted_iota(jnp.int32, (tok, 2 * tok), 1)
    valid = (col >= tok) | (place > 0)
    inside = (col > row) & (col <= row + WINDOW) & valid
    causal = (col <= row) & valid
    lane = lax.broadcasted_iota(jnp.int32, (tok, 2 * feat), 1)
    left = lane < feat
    side_r = lax.broadcasted_iota(jnp.int32, (2 * feat, 2 * feat), 0) < feat
    side_c = lax.broadcasted_iota(jnp.int32, (2 * feat, 2 * feat), 1) < feat
    halves = jnp.where(side_r == side_c, 1.0, 0.0).astype(BF16)

    for h in range(heads):
        q = q_ref[:, h * dh : (h + 1) * dh]
        wq = wq_ref[h]
        logits = dot_t(q, jnp.concatenate([wq, -wq], axis=0))
        top_l = jnp.max(jnp.where(left, logits, -jnp.inf), axis=1, keepdims=True)
        top_r = jnp.max(jnp.where(left, -jnp.inf, logits), axis=1, keepdims=True)
        expd = jnp.exp(logits - jnp.where(left, top_l, top_r)).astype(BF16)
        total = jnp.dot(expd, halves, preferred_element_type=F32)
        fq = (expd.astype(F32) / total).astype(BF16)
        fk = features_t(dot_t(wk_ref[h], k_ext))
        linear = jnp.dot(fq, fk, preferred_element_type=F32)
        scores = dot_t(q, k_ext) * (1.0 / math.sqrt(dh))
        masked = jnp.where(inside, scores, -jnp.inf)
        top = jnp.max(masked, axis=1, keepdims=True)
        soft = jnp.exp(masked - top) * ratio_ref[first_head + h]
        weight = jnp.where(causal, linear, soft).astype(BF16)
        both = jnp.dot(weight, v_ext, preferred_element_type=F32) + jnp.dot(
            fq, state_scr[h * 2 * feat : (h + 1) * 2 * feat, :], preferred_element_type=F32
        )
        out_ref[:, h * dh : (h + 1) * dh] = (both[:, :dh] / both[:, dh:]).astype(BF16)


def mix(place, queries, kv, wq, wk, ratio, group):
    tok = queries.shape[0]
    local_heads, feat, dh = wq.shape
    groups = local_heads // group
    tokens = kv.shape[0]
    seen = tokens - 2 * tok
    return pl.pallas_call(
        mix_kernel,
        grid_spec=pltpu.PrefetchScalarGridSpec(
            num_scalar_prefetch=1,
            grid=(groups,),
            in_specs=[
                pl.BlockSpec((tok, group * dh), lambda g, p: (0, g)),
                pl.BlockSpec((tokens, dh), lambda g, p: (0, g)),
                pl.BlockSpec((tokens, dh), lambda g, p: (0, groups + g)),
                pl.BlockSpec((group, feat, dh), lambda g, p: (g, 0, 0)),
                pl.BlockSpec((group, feat, dh), lambda g, p: (g, 0, 0)),
                pl.BlockSpec(memory_space=pltpu.SMEM),
            ],
            out_specs=pl.BlockSpec((tok, group * dh), lambda g, p: (0, g)),
            scratch_shapes=[
                pltpu.VMEM((group * 2 * feat, seen), BF16),
                pltpu.VMEM((group * 2 * feat, 2 * dh), BF16),
            ],
        ),
        out_shape=jax.ShapeDtypeStruct(queries.shape, BF16),
        compiler_params=pltpu.CompilerParams(vmem_limit_bytes=48 * 2**20),
        cost_estimate=pl.CostEstimate(
            flops=2 * local_heads * tokens * 3 * feat * 2 * dh,
            bytes_accessed=8 * 2**20,
            transcendentals=local_heads * tokens * 2 * feat,
        ),
    )(place, queries, kv, kv, wq, wk, ratio)


WAYS = 4

EARLY = pl.CostEstimate(flops=10**10, bytes_accessed=10**8, transcendentals=0)
EARLY_KERNELS = ("pack_kv", "pack_q", "pair_kv", "stack_kv")


SLOTS = (
    ((0, 0), (0, 0)),
    ((2, 1), (2, 1)),
    ((2, 0), (0, 1)),
    ((0, 1), (2, 0)),
    ((3, 1), (3, 1)),
    ((3, 0), (1, 1)),
    ((1, 1), (3, 0)),
    ((1, 0), (1, 0)),
)


def slot_of(n, odd):
    return [jnp.where(odd == 1, b, a) if a != b else a for a, b in zip(*SLOTS[n])]


def spot():
    at = lax.axis_index("seq")
    return lax.rem(at, WAYS), lax.div(at, WAYS)


def aligned(at, step):
    return pl.ds(pl.multiple_of(at * step, step), step)


def with_ones(values, kept=True):
    here = jnp.where(kept, 1.0, 0.0).astype(BF16)
    return jnp.concatenate([values, jnp.full(values.shape, here)], axis=1)


def pack_kv_kernel(k_ref, v_ref, k_away_ref, v_away_ref, own_ref, away_ref):
    odd = lax.rem(spot()[0], 2)
    for k, v, ref in ((k_ref, v_ref, own_ref), (k_away_ref, v_away_ref, away_ref)):
        for d in range(2):
            at = aligned(odd ^ d, DH)
            ref[:, 2 * d * DH : (2 * d + 1) * DH] = k[:, at]
            ref[:, (2 * d + 1) * DH : (2 * d + 2) * DH] = v[:, at]


def pair_kernel(own_ref, got_ref, out_ref):
    tok = own_ref.shape[0]
    out_ref[:tok, :] = own_ref[:, 2 * DH :]
    out_ref[tok:, :] = got_ref[:, 2 * DH :]


def stack_kernel(own_ref, got_ref, pair_ref, out_ref):
    tok = own_ref.shape[0]
    place = spot()[0]
    out_ref[aligned(place, tok), :] = own_ref[:, : 2 * DH]
    out_ref[aligned(place ^ 2, tok), :] = got_ref[:, : 2 * DH]
    out_ref[aligned(place ^ 1, tok), :] = pair_ref[:tok, :]
    out_ref[aligned(place ^ 3, tok), :] = pair_ref[tok:, :]


def pack_q_kernel(q_ref, *out_refs):
    place = spot()[0]
    for d, out in enumerate(out_refs):
        out[...] = q_ref[:, aligned(place ^ d, out.shape[1])]


def weights_kernel(wq_ref, factor_ref, both_ref, ratio_ref):
    heads = both_ref.shape[0]
    shape = (heads, factor_ref.shape[1])
    head = lax.broadcasted_iota(jnp.int32, shape, 0) + spot()[0] * heads
    ratio = jnp.broadcast_to((1.0 - factor_ref[...]) / factor_ref[...], shape)
    ratio = jnp.where(lax.broadcasted_iota(jnp.int32, shape, 1) == head, ratio, 0.0)
    ratio = jnp.sum(ratio, axis=1, keepdims=True)
    ratio_ref[...] = jnp.broadcast_to(ratio, ratio_ref.shape)
    for h in range(heads):
        wq = wq_ref[h].T
        both_ref[h] = jnp.concatenate([wq, -wq], axis=1)


def join_kernel(slots, *refs):
    got, out_ref, sems = refs[: len(slots)], *refs[-2:]
    width = got[0].shape[1]
    place, side = spot()[0], lax.axis_index("head")
    copies = []
    for n, ref in zip(slots, got):
        dr, dy = slot_of(n, lax.rem(place, 2) ^ (SLOTS[n][0][0] & 1))
        at = aligned((side ^ dy) * WAYS + (place ^ dr), width)
        copies.append(pltpu.make_async_copy(ref, out_ref.at[:, at], sems.at[len(copies)]))
    for copy in copies:
        copy.start()
    for copy in copies:
        copy.wait()


def write_key_features(keys, wk_ref, fk_ref):
    heads, feat, dh = wk_ref.shape
    logits = dot_t(wk_ref[...].reshape(heads * feat, dh), keys)
    for h in range(heads):
        part = logits[h * feat : (h + 1) * feat] * math.log2(math.e)
        top = jnp.max(part, axis=0, keepdims=True)
        low = jnp.min(part, axis=0, keepdims=True)
        for n, shifted in enumerate((part - top, low - part)):
            row = (2 * h + n) * feat
            expd = jnp.exp2(shifted.astype(BF16))
            total = expd[: feat // 4]
            for q in range(1, 4):
                total = total + expd[q * feat // 4 : (q + 1) * feat // 4]
            total = jnp.sum(total.astype(F32), axis=0, keepdims=True)
            fk_ref[row : row + feat, :] = expd * pl.reciprocal(total, approx=True).astype(BF16)


def own_features_kernel(own_ref, wk_ref, fk_ref):
    write_key_features(own_ref[:, :DH], wk_ref, fk_ref.at[:, own_ref.shape[0] :])


def last_features_kernel(last_ref, wk_ref, _, fk_ref, past_ref, step_ref):
    size = last_ref.shape[0]
    half = size // 2
    level = spot()[1]

    @pl.when(level == 0)
    def _():
        fk_ref[:, :size] = jnp.zeros((fk_ref.shape[0], size), BF16)
        for ref in (past_ref, step_ref):
            ref[...] = jnp.zeros_like(ref)

    @pl.when(level > 0)
    def _():
        write_key_features(last_ref[:, :DH], wk_ref, fk_ref.at[:, :size])
        for at, ref in ((0, past_ref), (half, step_ref)):
            ref[...] = jnp.dot(
                fk_ref[:, at : at + half],
                with_ones(last_ref[at : at + half, DH:]),
                preferred_element_type=F32,
            )


def past_kernel(first_ref, wk_ref, sum_ref, past_ref, fk_scr):
    level = spot()[1]

    @pl.when(level < 3)
    def _():
        past_ref[...] = sum_ref[...]

    @pl.when(level >= 3)
    def _():
        write_key_features(first_ref[:, :DH], wk_ref, fk_scr)
        past_ref[...] = sum_ref[...] + jnp.dot(
            fk_scr[...], with_ones(first_ref[:, DH:]), preferred_element_type=F32
        )


def query_features_kernel(a_ref, b_ref, w_ref, ratio_ref, q_out, fq_out, exp_scr):
    tok = a_ref.shape[0]
    heads, dh, both = w_ref.shape
    half = 2 * tok
    place = spot()[0]
    for d, ref in enumerate((a_ref, b_ref)):
        row = pl.multiple_of(lax.rem(place ^ d, 2) * tok, tok)
        for h in range(heads):
            q_out[pl.ds(h * half + row, tok), :] = ref[:, h * dh : (h + 1) * dh]
    rows_of = [slice(h * half, (h + 1) * half) for h in range(heads)]
    left = lax.broadcasted_iota(jnp.int32, (half, both), 1) < both // 2
    for h, rows in enumerate(rows_of):
        logits = jnp.dot(q_out[rows, :], w_ref[h], preferred_element_type=F32)
        top_l = jnp.max(jnp.where(left, logits, -jnp.inf), axis=1, keepdims=True)
        top_r = jnp.max(jnp.where(left, -jnp.inf, logits), axis=1, keepdims=True)
        exp_scr[rows, :] = jnp.exp((logits - jnp.where(left, top_l, top_r)).astype(BF16))
    side_r = lax.broadcasted_iota(jnp.int32, (both, both), 0) < both // 2
    side_c = lax.broadcasted_iota(jnp.int32, (both, both), 1) < both // 2
    halves = jnp.where(side_r == side_c, 1.0, 0.0).astype(BF16)
    total = jnp.dot(exp_scr[...], halves, preferred_element_type=F32)
    for h, rows in enumerate(rows_of):
        scale = pl.reciprocal(total[rows], approx=True) * ratio_ref[h : h + 1, :]
        fq_out[rows, :] = (exp_scr[rows, :].astype(F32) * scale).astype(BF16)


def near_kernel(other, q_ref, fq_ref, last_ref, own_ref, fk_ref, near_ref, kv_scr, w_scr):
    half, dh = last_ref.shape[0] // 2, q_ref.shape[1]
    heads = q_ref.shape[0] // half
    feats = fq_ref.shape[1]
    place, level = spot()
    u = lax.div(place, 2) ^ other
    kv_scr[:half, :] = last_ref[half:, :]
    kv_scr[half:, :] = own_ref[...]
    at = pl.ds(pl.multiple_of(u * half, half), 2 * half)
    keys, values = kv_scr[at, :dh], kv_scr[at, dh:]
    fk_at = pl.ds(pl.multiple_of((u + 1) * half, half), 2 * half)
    known = (level > 0) | (u > 0)
    cut = half - WINDOW
    row = lax.broadcasted_iota(jnp.int32, (WINDOW, 2 * half), 0)
    col = lax.broadcasted_iota(jnp.int32, (WINDOW, 2 * half), 1)
    inside = (col > row + cut) & (col <= row + half) & ((col >= half) | known)
    causal = (col <= row + cut)[:, :half]
    row, col = row[:, :half], col[:, :half]
    inside_low = (col > row) & (col <= row + WINDOW)
    causal_low = col <= row
    scores = dot_t(q_ref[...], keys)
    scale = math.log2(math.e) / math.sqrt(dh)

    def window(part, kept):
        masked = jnp.where(kept, part, -jnp.inf)
        top = jnp.max(masked, axis=1, keepdims=True)
        return jnp.exp2(((masked - top) * scale).astype(BF16))

    for h in range(heads):
        here = slice(h * half, (h + 1) * half)
        up, low = slice(h * half, h * half + cut), slice(h * half + cut, (h + 1) * half)
        linear = jnp.dot(
            fq_ref[here, :],
            fk_ref[h * feats : (h + 1) * feats, fk_at],
            preferred_element_type=F32,
        )
        soft = window(scores[up], inside)
        w_scr[up, :half] = soft[:, :half] + jnp.where(causal, linear[:cut, :half], 0.0).astype(BF16)
        w_scr[up, half:] = soft[:, half:]
        soft = window(scores[low, half:], inside_low)
        w_scr[low, :half] = linear[cut:, :half].astype(BF16)
        w_scr[low, half:] = soft + jnp.where(causal_low, linear[cut:, half:], 0.0).astype(BF16)
    values = jnp.concatenate(
        [with_ones(values[:half], known), with_ones(values[half:])], axis=0
    )
    near_ref[...] = jnp.dot(w_scr[...], values, preferred_element_type=F32)


def mix_kernel_of_level(*refs):
    near_refs, fq_refs, (past_ref, step_ref, wk_ref) = refs[:2], refs[2:4], refs[4:7]
    before_ref, refs = refs[7], refs[8:]
    out_refs, (fk_scr, state_scr, out_scr) = refs[:-3], refs[-3:]
    rows, dh = near_refs[0].shape[0], near_refs[0].shape[1] // 2
    feats = fq_refs[0].shape[1]
    heads = past_ref.shape[0] // feats
    half = rows // heads
    place, level = spot()
    side = lax.axis_index("head")
    u = lax.div(place, 2)

    @pl.when(level < 2)
    def _():
        state_scr[0] = past_ref[...].astype(BF16)
        state_scr[1] = (past_ref[...] + step_ref[...]).astype(BF16)

    @pl.when(level >= 2)
    def _():
        write_key_features(before_ref[:, :dh], wk_ref, fk_scr)
        state = past_ref[...] + jnp.dot(
            fk_scr[...], with_ones(before_ref[:, dh:]), preferred_element_type=F32
        )
        state_scr[0] = state.astype(BF16)
        state_scr[1] = (state + step_ref[...]).astype(BF16)

    part = out_refs[0].shape[0]
    for other in (1, 0):
        for h in range(heads):
            here = slice(h * half, (h + 1) * half)
            far = jnp.dot(
                fq_refs[other][here, :],
                state_scr[u ^ other, h * feats : (h + 1) * feats, :],
                preferred_element_type=F32,
            )
            both = near_refs[other][here, :] + far
            out_scr[aligned(u ^ other, half), h * dh : (h + 1) * dh] = (
                both[:, :dh] * pl.reciprocal(both[:, dh:], approx=True)
            ).astype(BF16)
    for n, ref in enumerate(out_refs):
        dr, dy = slot_of(n, lax.rem(place, 2))
        ref[...] = out_scr[aligned((place ^ dr) * 2 + (side ^ dy), part), :]


def whole_spec(space=pltpu.VMEM):
    return pl.BlockSpec(memory_space=space)


def call(kernel, ins, outs, name, scratch=(), limit=4, out_type=BF16, aliases={}):
    return pl.pallas_call(
        kernel,
        in_specs=[whole_spec() for _ in ins],
        out_specs=[whole_spec() for _ in outs],
        out_shape=[
            jax.ShapeDtypeStruct(s, out_type[n] if isinstance(out_type, list) else out_type)
            for n, s in enumerate(outs)
        ],
        scratch_shapes=list(scratch),
        input_output_aliases=aliases,
        cost_estimate=EARLY if name in EARLY_KERNELS else None,
        compiler_params=pltpu.CompilerParams(vmem_limit_bytes=limit * 2**20),
        name=name,
    )(*ins)


def by_levels(queries, keys, values, wq, wk, factor):
    tok, width = queries.shape
    local_heads, feat, dh = wq.shape
    heads = local_heads // WAYS
    seq, sides = lax.axis_size("seq"), lax.axis_size("head")
    half = 2 * tok
    rows, states = heads * half, heads * 2 * feat

    def partner(x, dr, dy=0):
        pairs = [
            (i * sides + j, (i // WAYS * WAYS + (i % WAYS ^ dr)) * sides + (j ^ dy))
            for i in range(seq)
            for j in range(sides)
        ]
        return lax.ppermute(x, ("seq", "head"), pairs)

    def levels_back(x, by):
        pairs = [(i, i + by * WAYS) for i in range(seq - by * WAYS)]
        return lax.ppermute(x, "seq", pairs)

    place = lax.rem(lax.axis_index("seq"), WAYS)
    ours = place // 2 * 2 * dh
    cuts = [
        lax.dynamic_slice_in_dim(x, at, 2 * dh, 1)
        for at in (ours, 2 * dh - ours)
        for x in (keys, values)
    ]
    own, away = call(pack_kv_kernel, cuts, [(tok, 4 * dh)] * 2, "pack_kv")
    got = partner(away, 2)
    queries, away = lax.optimization_barrier((queries, away))
    q = list(call(pack_q_kernel, [queries], [(tok, width // WAYS)] * WAYS, "pack_q"))
    q[2], q[3] = partner(q[2], 2), partner(q[3], 3)
    (pair,) = call(pair_kernel, [own, got], [(half, 2 * dh)], "pair_kv")
    pair, q[1], wq, wk = lax.optimization_barrier((pair, q[1], wq, wk))
    pair, q[1] = partner(pair, 1), partner(q[1], 1)
    wq, wk = [lax.dynamic_slice_in_dim(w, place * heads, heads) for w in (wq, wk)]
    pair, wq, wk = lax.optimization_barrier((pair, wq, wk))
    (kv,) = call(stack_kernel, [own, got, pair], [(2 * half, 2 * dh)], "stack_kv")
    last, first = levels_back(kv, 1), levels_back(kv, 3)
    wq, kv, q[1] = lax.optimization_barrier((wq, kv, q[1]))
    before = levels_back(kv, 2)
    (fk,) = call(own_features_kernel, [kv, wk], [(states, 4 * half)], "own_features", limit=16)
    wq, ratio = call(
        weights_kernel,
        [wq, factor.reshape(1, local_heads)],
        [(heads, dh, 2 * feat), (heads, 2 * feat)],
        "weights",
        out_type=[BF16, F32],
    )

    def query_features(a, b):
        return call(
            query_features_kernel,
            [a, b, wq, ratio],
            [(rows, dh), (rows, 2 * feat)],
            "query_features",
            [pltpu.VMEM((rows, 2 * feat), BF16)],
            12,
        )

    def near(other, q_rows, fq):
        return call(
            lambda *refs: near_kernel(other, *refs),
            [q_rows, fq, last, kv, fk],
            [(rows, 2 * dh)],
            "near",
            [
                pltpu.VMEM((3 * half, 2 * dh), BF16),
                pltpu.VMEM((rows, 2 * half), BF16),
            ],
            16,
            F32,
        )[0]

    q_own, fq_own = query_features(q[0], q[1])
    last, fq_own, fk = lax.optimization_barrier((last, fq_own, fk))
    fk, past, step = call(
        last_features_kernel,
        [last, wk, fk],
        [(states, 4 * half), (states, 2 * dh), (states, 2 * dh)],
        "last_features",
        limit=20,
        out_type=[BF16, F32, F32],
        aliases={2: 0},
    )
    near_own = near(0, q_own, fq_own)
    q[2], q[3], near_own = lax.optimization_barrier((q[2], q[3], near_own))
    q_other, fq_other = query_features(q[2], q[3])
    near_other = near(1, q_other, fq_other)
    first, near_other = lax.optimization_barrier((first, near_other))
    (past,) = call(
        past_kernel,
        [first, wk, past],
        [(states, 2 * dh)],
        "past",
        [pltpu.VMEM((states, 2 * half), BF16)],
        16,
        F32,
    )
    before, past = lax.optimization_barrier((before, past))
    part = tok // sides
    outs = call(
        mix_kernel_of_level,
        [near_own, near_other, fq_own, fq_other, past, step, wk, before],
        [(part, heads * dh)] * (WAYS * sides),
        "mix_level",
        [
            pltpu.VMEM((states, 2 * half), BF16),
            pltpu.VMEM((2, states, 2 * dh), BF16),
            pltpu.VMEM((2 * half, heads * dh), BF16),
        ],
        24,
    )

    def sent(x, slot):
        pairs = []
        for i in range(seq):
            dr, dy = slot[i % 2]
            to = i // WAYS * WAYS + (i % WAYS ^ dr)
            pairs += [(i * sides + j, to * sides + (j ^ dy)) for j in range(sides)]
        return lax.ppermute(x, ("seq", "head"), pairs)

    outs = list(outs)
    for n in range(1, 6):
        outs[n] = sent(outs[n], SLOTS[n])
    outs[6], outs[7], outs[1] = lax.optimization_barrier((outs[6], outs[7], outs[1]))
    outs[6], outs[7] = sent(outs[6], SLOTS[6]), sent(outs[7], SLOTS[7])

    def joined(slots, into):
        return pl.pallas_call(
            lambda *refs: join_kernel(slots, *refs),
            in_specs=[whole_spec()] * len(slots) + [whole_spec(pltpu.HBM)] * len(into),
            out_specs=whole_spec(pltpu.HBM),
            out_shape=jax.ShapeDtypeStruct((part, sides * WAYS * heads * dh), BF16),
            input_output_aliases={len(slots): 0} if into else {},
            scratch_shapes=[pltpu.SemaphoreType.DMA((len(slots),))],
            compiler_params=pltpu.CompilerParams(vmem_limit_bytes=4 * 2**20),
            name="join",
        )(*[outs[n] for n in slots], *into)

    return joined((4, 5, 6, 7), [joined((0, 1, 2, 3), [])])


def by_blocks(queries, keys, values, wq, wk, ratio):
    group = wq.shape[0] // (keys.shape[1] // DH)
    place = lax.axis_index("seq").astype(jnp.int32).reshape(1)
    kv = lax.all_gather(jnp.concatenate([keys, values], axis=1), "seq", tiled=True)
    out = mix(place, queries, kv, wq, wk, ratio, group)
    return lax.all_to_all(out, "head", split_axis=0, concat_axis=1, tiled=True)


def local(queries, keys, values, q_feature, k_feature, window_factor):
    tok = queries.shape[0]
    seq, sides = lax.axis_size("seq"), lax.axis_size("head")
    wq, wk = jnp.swapaxes(q_feature, 1, 2), jnp.swapaxes(k_feature, 1, 2)
    if keys.shape[1] == WAYS * DH and seq == 4 * WAYS and sides == 2 and tok == WINDOW:
        return by_levels(queries, keys, values, wq, wk, window_factor)
    ratio = window_factor / (1.0 - window_factor)
    return by_blocks(queries, keys, values, wq, wk, ratio)


def solution(mesh):
    return jax.shard_map(
        local,
        mesh=mesh,
        in_specs=(
            P("seq", "head"),
            P("seq", "head"),
            P("seq", "head"),
            P("head", None, None),
            P("head", None, None),
            P("head"),
        ),
        out_specs=P(("seq", "head"), None),
        check_vma=False,
    )
```
